32 devices in a mesh: seq: 16 (over z, y, x), fsdp: 2 (over core).
Axes of the slice: x: 2, y: 2, z: 4, core: 2. Of those that a mesh axis runs over, the one named last changes fastest.
Arguments:
- tokens: bfloat16 [4096, 2048], P(('fsdp', 'seq')), may hold values from -6 to 6
- cotangent: bfloat16 [4096, 2048], P(('fsdp', 'seq')), may hold values from -6 to 6
- lengths: int32 [2, 4], P('fsdp'), may hold values from 1 to 2045, as said below
- routes: int32 [4096, 6], P(('fsdp', 'seq')), may hold values from 0 to 15, all different within a row; in each aligned block of 128 rows (0 to 127, 128 to 255, ...) at most 96 rows name the same one
- g_attn: bfloat16 [2048], P('fsdp'), may hold values from 0.5 to 1.5
- w_q: bfloat16 [2048, 3072], P('fsdp')
- w_kva: bfloat16 [2048, 576], P('fsdp'), may hold values from -0.125 to 0.125
- g_kv: bfloat16 [512], P('fsdp'), may hold values from 0.5 to 1.5
- w_kvb: bfloat16 [512, 4096], P('fsdp'), may hold values from -0.25 to 0.25
- w_o: bfloat16 [2048, 2048], P('fsdp'), may hold values from -1 to 1
- g_ffn: bfloat16 [2048], P('fsdp'), may hold values from 0.5 to 1.5
- w_router: bfloat16 [2048, 16], P('fsdp'), may hold values from -0.0625 to 0.0625
- w_shared_in: bfloat16 [2048, 5632], P('fsdp'), may hold values from -0.125 to 0.125
- w_shared_out: bfloat16 [2816, 2048], P('fsdp'), may hold values from -0.109375 to 0.109375
- w_expert_in: bfloat16 [16, 2048, 2816], P('seq', 'fsdp'), may hold values from -0.125 to 0.125
- w_expert_out: bfloat16 [16, 1408, 2048], P('seq', 'fsdp'), may hold values from -1.25 to 1.25
Outputs:
- mixed: bfloat16 [4096, 2048], P(('fsdp', 'seq'))
- grad_tokens: float32 [4096, 2048], P(('fsdp', 'seq'))
- grad_g_attn: float32 [2048], P('fsdp')
- grad_w_q: float32 [2048, 3072], P('fsdp')
- grad_w_kva: float32 [2048, 576], P('fsdp')
- grad_g_kv: float32 [512], P('fsdp')
- grad_w_kvb: float32 [512, 4096], P('fsdp')
- grad_w_o: float32 [2048, 2048], P('fsdp')
- grad_g_ffn: float32 [2048], P('fsdp')
- grad_w_router: float32 [2048, 16], P('fsdp')
- grad_w_shared_in: float32 [2048, 5632], P('fsdp')
- grad_w_shared_out: float32 [2816, 2048], P('fsdp')
- grad_w_expert_in: float32 [16, 2048, 2816], P('seq', 'fsdp')
- grad_w_expert_out: float32 [16, 1408, 2048], P('seq', 'fsdp')
- clipped_w_q: bfloat16 [2048, 3072], P('fsdp')
The draws below stay inside these ranges and needn't reach their ends.
Inputs may be any that keep to these rules, and one draw needn't show every extreme that they name: Row f holds the lengths of the 4 sequences of group f, which sum to at most 2048. One sequence of each group begins on the group's first device and ends on its last. Some group in every draw is filled with no padding, all its other sequences of length 1. `routes`: the rows of one device (128 aligned rows) name no expert more than 96 times, a bound that some block reaches.
All inputs are finite; a program needn't handle non-finite values.
Results may differ from the reference program's by a relative error of at most 0.025.
Values may be sent and summed in bfloat16 or wider, within the bound.
A program may use at most 384 MiB of HBM per device.

```python
import math
from functools import partial
import jax
import jax.numpy as jnp
import numpy as np
from jax import lax

D = 2048
H = 16
DN = 128
DR = 64
DV = 128
KVR = 512
FF = 1408
TOP = 6
SH = 2816
EXPERTS = 16
TOK_DEV = 128
NSEQ = 4
TOKENS = 4096
CAP = 96
N_SEQ = 16
N_FSDP = 2


def draw_lengths(key, part):
    key = jax.random.fold_in(key, 7)
    first_key, second_key, third_key, fourth_key = jax.random.split(key, 4)
    short_most = TOK_DEV // (NSEQ + 1)
    group_size = TOK_DEV * N_SEQ
    full_group = jax.random.randint(fourth_key, (1, 1), 0, N_FSDP, dtype=jnp.int32)
    is_full = jnp.arange(N_FSDP, dtype=jnp.int32)[:, None] == full_group
    shorts = jax.random.randint(first_key, (N_FSDP, NSEQ), 1, short_most + 1, dtype=jnp.int32)
    shorts = jnp.where(is_full, 1, shorts).astype(jnp.int32)
    padding = jax.random.randint(second_key, (N_FSDP, 1), 0, short_most + 1, dtype=jnp.int32)
    padding = jnp.where(is_full, 0, padding).astype(jnp.int32)
    chosen = jax.random.randint(third_key, (N_FSDP, 1), 0, NSEQ, dtype=jnp.int32)
    is_long = jnp.arange(NSEQ, dtype=jnp.int32)[None, :] == chosen
    short_total = jnp.sum(jnp.where(is_long, 0, shorts), axis=1, keepdims=True).astype(jnp.int32)
    return jnp.where(is_long, group_size - short_total - padding, shorts).astype(jnp.int32)


def draw_w_q(key, part):
    key = jax.random.fold_in(key, 11)
    scale_key, value_key = jax.random.split(key)
    head_scale = jnp.exp(jax.random.uniform(scale_key, (1, H, 1), jnp.float32, math.log(0.7), math.log(3.0)))
    entries = jax.random.normal(value_key, (D, H, DN + DR), jnp.float32)
    return (entries * head_scale * D ** (-0.5)).reshape(D, H * (DN + DR)).astype(jnp.bfloat16)


def block_levels(key, shape, shards, smallest, top_value):
    def one(dim, blocks):
        draws = jax.random.uniform(jax.random.fold_in(jax.random.fold_in(key, 6), dim), (blocks,), jnp.float32, smallest / len(shards), top_value / len(shards))
        return jnp.repeat(jnp.exp(draws), shape[dim] // blocks).reshape((-1,) + (1,) * (len(shape) - dim - 1))

    factor_of = one(*shards[0])
    for cut in shards[1:]:
        factor_of = factor_of * one(*cut)
    return factor_of


def assign_block(stream_key, own, number, rows, count, top, reach, skew):
    order = jax.random.permutation(stream_key, count)
    heavy_load, common = portions_of(count, rows * top, reach, skew, True), portions_of(count, rows * top, reach, skew, False)
    places = jnp.arange(count)

    def named(sizes, turn):
        used = int((sizes > 0).sum())
        fixed = max(1, used // 4)
        shifted = fixed + (places - fixed + turn * (used - fixed)) % max(1, count - fixed)
        return jnp.zeros((count,), jnp.int32).at[order[jnp.where(places < fixed, places, shifted)]].set(jnp.asarray(sizes, jnp.int32))

    sizes = jnp.where(number % 4 == 0, named(heavy_load, number // 4), named(common, number - number // 4 - 1))
    mixed = jax.random.permutation(jax.random.fold_in(own, 3), count)
    giver, taker = mixed[0:count // 2 * 2:2], mixed[1:count // 2 * 2:2]
    margin = jnp.minimum(sizes[giver] - 1, reach - sizes[taker]) // 2
    margin = jnp.where((giver == order[0]) | (taker == order[0]) | (sizes[taker] == 0), 0, jnp.maximum(margin, 0))
    shifted = jax.random.randint(jax.random.fold_in(own, 4), (count // 2,), 0, 1 << 20) % (margin + 1)
    sizes = sizes.at[giver].add(-shifted).at[taker].add(shifted)
    members = jnp.searchsorted(jnp.cumsum(sizes), jnp.arange(rows * top), side="right").astype(jnp.int32)
    grid = members.reshape(top, rows).T
    grid = grid[jax.random.permutation(jax.random.fold_in(own, 1), rows)]
    turn = jax.random.randint(jax.random.fold_in(own, 2), (rows, 1), 0, top)
    return jnp.take_along_axis(grid, (jnp.arange(top)[None, :] + turn) % top, axis=1)


def portions_of(number_of, total, most, lean, full):
    portions = [(1 << 20) // math.isqrt(rank ** lean) + 1 for rank in range(1, number_of + 1)]
    largest = most if full else min(most, max(-(-total // number_of), total * portions[0] // sum(portions)))
    least = 1 if total - largest >= number_of - 1 else 0
    counts, rest = [largest] + [least] * (number_of - 1), total - largest - least * (number_of - 1)
    while rest > 0:
        free = [i for i in range(1, number_of) if counts[i] < largest] or [i for i in range(1, number_of) if counts[i] < most]
        pool, left = sum([portions[i] for i in free]), rest
        for i in free:
            extra = min(most - counts[i], max(1, left * portions[i] // pool), rest)
            counts[i] = counts[i] + extra
            rest = rest - extra
    return np.array(counts)


def bell_draw(own_key, dims, deviation, reach, cuts=(), kind=jnp.bfloat16):
    values = jax.random.normal(own_key, dims, jnp.float32) * deviation
    if len(cuts) > 0:
        values = block_levels(own_key, dims, cuts, -0.22, 0.18) * values
    return jnp.clip(values, min=-reach, max=reach).astype(kind)


def setup_inputs(seed: int = 0) -> dict:
    key_of = jax.random.split(jax.random.key(seed), 17)
    tokens = bell_draw(key_of[0], (TOKENS, D), 1.0, 6.0, ((0, 32),))
    cotangent = bell_draw(key_of[1], (TOKENS, D), 1.0, 6.0, ((0, 32),))
    lengths = draw_lengths(jax.random.fold_in(key_of[16], 71), 0)
    routes_keys = jax.random.split(jax.random.fold_in(key_of[3], 1), TOKENS // TOK_DEV)
    routes_turns = jax.random.permutation(jax.random.fold_in(key_of[3], 3), TOKENS // TOK_DEV)
    routes = jax.vmap(lambda own, number: assign_block(jax.random.fold_in(key_of[3], 2), own, number, TOK_DEV, EXPERTS, TOP, CAP, 1))(routes_keys, routes_turns).reshape((TOKENS, TOP))
    g_attn = jnp.clip(1.0 + 0.1 * jax.random.normal(key_of[4], (D,), jnp.float32), 0.5, 1.5).astype(jnp.bfloat16)
    w_q = draw_w_q(jax.random.fold_in(key_of[16], 71), 0)
    w_kva = bell_draw(key_of[6], (D, KVR + DR), D ** -0.5, 0.125, ((0, 2),))
    g_kv = jnp.clip(1.0 + 0.1 * jax.random.normal(key_of[7], (KVR,), jnp.float32), 0.5, 1.5).astype(jnp.bfloat16)
    w_kvb = bell_draw(key_of[8], (KVR, H * (DN + DV)), KVR ** -0.5, 0.25, ((0, 2),))
    w_o = bell_draw(key_of[9], (H * DV, D), (H * DV // 64) ** -0.5, 1.0, ((0, 2),))
    g_ffn = jnp.clip(1.0 + 0.1 * jax.random.normal(key_of[10], (D,), jnp.float32), 0.5, 1.5).astype(jnp.bfloat16)
    w_router = bell_draw(key_of[11], (D, EXPERTS), (4 * D) ** -0.5, 0.0625, ((0, 2),))
    w_shared_in = bell_draw(key_of[12], (D, 2 * SH), D ** -0.5, 0.125, ((0, 2),))
    w_shared_out = bell_draw(key_of[13], (SH, D), SH ** -0.5, 0.109375, ((0, 2),))
    w_expert_in = bell_draw(key_of[14], (EXPERTS, D, 2 * FF), D ** -0.5, 0.125, ((0, 16), (1, 2)))
    w_expert_out = bell_draw(key_of[15], (EXPERTS, FF, D), (max(FF // 64, 1)) ** -0.5, 1.25, ((0, 16), (1, 2)))
    return dict(tokens=tokens, cotangent=cotangent, lengths=lengths, routes=routes, g_attn=g_attn, w_q=w_q, w_kva=w_kva, g_kv=g_kv, w_kvb=w_kvb, w_o=w_o, g_ffn=g_ffn, w_router=w_router, w_shared_in=w_shared_in, w_shared_out=w_shared_out, w_expert_in=w_expert_in, w_expert_out=w_expert_out)


@jax.custom_vjp
def low(v):
    return lax.optimization_barrier(v.astype(jnp.bfloat16)).astype(jnp.float32)

@jax.custom_vjp
def low_back(v):
    return v

def low_keep(v):
    return (low(v), None)

def low_pass(kept, grad):
    return (grad,)

def back_keep(v):
    return (v, None)

def back_low(kept, grad):
    return (low(grad),)
low.defvjp(low_keep, low_pass)
low_back.defvjp(back_keep, back_low)
EPSILON = 1e-06
CLIP_LIMIT = 8.0
ROPE_BASE = 10000.0
MASK_VALUE = -1e+30

def product(left, right):
    return jnp.dot(left, right, precision=lax.Precision.HIGHEST)

def rms_norm(values, gain_vector):
    return values * lax.rsqrt(lax.optimization_barrier(jnp.mean(values * values, axis=-1, keepdims=True)) + EPSILON) * gain_vector

def rotate(values, angles):
    half_width = values.shape[-1] // 2
    first_half = values[..., :half_width]
    second_half = values[..., half_width:]
    cosine = jnp.cos(angles)
    sine_part = jnp.sin(angles)
    return jnp.concatenate([first_half * cosine - second_half * sine_part, second_half * cosine + first_half * sine_part], axis=-1)

def frequencies(count):
    exponent = jnp.arange(count // 2, dtype=jnp.float32) * 2.0 / count
    return ROPE_BASE ** (-exponent)

def layout(lengths_row, slot_ids):
    seq_ends = jnp.cumsum(lengths_row).astype(jnp.int32)
    seq_starts = (seq_ends - lengths_row).astype(jnp.int32)
    inside = (slot_ids[:, None] >= seq_starts[None, :]) & (slot_ids[:, None] < seq_ends[None, :])
    is_valid = jnp.any(inside, axis=1)
    numbers = jnp.arange(lengths_row.shape[0], dtype=jnp.int32)
    seq_number = lax.optimization_barrier(jnp.sum(jnp.where(inside, numbers[None, :], 0), axis=1)).astype(jnp.int32)
    first_slot = lax.optimization_barrier(jnp.sum(jnp.where(inside, seq_starts[None, :], 0), axis=1)).astype(jnp.int32)
    segment = jnp.where(is_valid, seq_number, lengths_row.shape[0] + slot_ids).astype(jnp.int32)
    position = jnp.where(is_valid, slot_ids - first_slot, 0).astype(jnp.int32)
    return (segment, position, is_valid)

def group_layout(lengths):
    slot_ids = jnp.arange(TOK_DEV * N_SEQ, dtype=jnp.int32)
    segment, position, is_valid = jax.vmap(partial(layout, slot_ids=slot_ids))(lengths)
    return (segment.reshape(-1), position.reshape(-1), is_valid.reshape(-1))

def attend_group(operands):
    query, key, value, segment, is_valid = operands
    length = query.shape[0]
    block_rows = 512 if length % 512 == 0 else length
    score_scale = query.shape[-1] ** (-0.5)
    key_slots = jnp.arange(length, dtype=jnp.int32)

    @jax.checkpoint
    def one_block(first_row):
        row_query = lax.dynamic_slice_in_dim(query, first_row, block_rows, 0)
        raw_scores = jnp.einsum('qhd,khd->hqk', row_query, key, precision=lax.Precision.HIGHEST)
        scores = low_back(score_scale * raw_scores)
        row_slots = first_row + jnp.arange(block_rows, dtype=jnp.int32)
        row_segment = lax.dynamic_slice_in_dim(segment, first_row, block_rows, 0)
        row_valid = lax.dynamic_slice_in_dim(is_valid, first_row, block_rows, 0)
        allowed = (row_segment[:, None] == segment[None, :]) & (key_slots[None, :] <= row_slots[:, None])
        probs = jax.nn.softmax(jnp.where(allowed[None], scores, MASK_VALUE), axis=-1)
        context = jnp.einsum('hqk,khd->qhd', low(probs), value, precision=lax.Precision.HIGHEST)
        largest = lax.optimization_barrier(jnp.max(jnp.where((allowed & row_valid[:, None])[None], scores, MASK_VALUE), axis=(1, 2)))
        return (context, largest)
    starts = jnp.arange(length // block_rows, dtype=jnp.int32) * block_rows
    context, largest = lax.map(one_block, starts)
    return (context.reshape(length, query.shape[1], value.shape[-1]), lax.optimization_barrier(jnp.max(largest, axis=0)))

def expert_sum(ffn_in, gate_values, routes, w_expert_in, w_expert_out):
    count = ffn_in.shape[0]
    block_count = count // TOK_DEV
    buffer_rows = block_count * CAP
    expert_ids = jnp.arange(EXPERTS, dtype=jnp.int32)
    onehot = (routes.reshape(block_count, TOK_DEV * TOP)[:, :, None] == expert_ids[None, None, :]).astype(jnp.int32)
    slot_rank = lax.optimization_barrier(jnp.sum((jnp.cumsum(onehot, axis=1).astype(jnp.int32) - 1) * onehot, axis=2)).astype(jnp.int32)
    source = jnp.arange(block_count, dtype=jnp.int32)[:, None]
    buffer_row = (source * CAP + slot_rank).reshape(count, TOP).astype(jnp.int32)

    @jax.checkpoint
    def one_expert(running, operands):
        expert_number, weight_in, weight_out = operands
        matched = routes == expert_number
        chosen = jnp.any(matched, axis=1)
        target = jnp.where(chosen, lax.optimization_barrier(jnp.sum(jnp.where(matched, buffer_row, 0), axis=1)), buffer_rows).astype(jnp.int32)
        buffer = jnp.zeros((buffer_rows, ffn_in.shape[1]), jnp.float32).at[target].set(low_back(ffn_in), mode='drop')
        gate_up = low_back(product(buffer, weight_in))
        hidden = low(jax.nn.silu(gate_up[:, :FF]) * gate_up[:, FF:])
        result = low_back(low(product(hidden, weight_out)))
        picked = jnp.take(result, target, axis=0, mode='fill', fill_value=0.0)
        weight = lax.optimization_barrier(jnp.sum(jnp.where(matched, gate_values, 0.0), axis=1))
        return (running + weight[:, None] * picked, None)
    routed, unused = lax.scan(one_expert, jnp.zeros(ffn_in.shape, jnp.float32), (expert_ids, w_expert_in, w_expert_out))
    return routed

def forward(tokens, g_attn, w_q, w_kva, g_kv, w_kvb, w_o, g_ffn, w_router, w_shared_in, w_shared_out, w_expert_in, w_expert_out, lengths, routes):
    count = tokens.shape[0]
    group_size = TOK_DEV * N_SEQ
    group_count = count // group_size
    segment, position, is_valid = group_layout(lengths)
    angles = position[:, None].astype(jnp.float32) * frequencies(DR)[None, :]
    normed = low(rms_norm(tokens, g_attn))
    query_pre = low_back(product(normed, w_q)).reshape(count, H, DN + DR)
    latent_full = low_back(product(normed, w_kva))
    latent = low(rms_norm(latent_full[:, :KVR], g_kv))
    expanded = product(latent, w_kvb).reshape(count, H, DN + DV)
    query = low_back(low(jnp.concatenate([query_pre[..., :DN], rotate(query_pre[..., DN:], angles[:, None, :])], axis=-1)))
    key_rope = rotate(latent_full[:, KVR:], angles)
    key = low_back(low(jnp.concatenate([expanded[..., :DN], jnp.broadcast_to(key_rope[:, None, :], (count, H, DR))], axis=-1)))
    value = low_back(low(expanded[..., DN:]))
    context, head_max = lax.map(attend_group, (query.reshape(group_count, group_size, H, DN + DR), key.reshape(group_count, group_size, H, DN + DR), value.reshape(group_count, group_size, H, DV), segment.reshape(group_count, group_size), is_valid.reshape(group_count, group_size)))
    context = low_back(low(context.reshape(count, H * DV)))
    attended = low_back(product(context, w_o))
    middle = tokens + attended
    ffn_in = low(rms_norm(middle, g_ffn))
    logits = low_back(product(ffn_in, w_router))
    router_probs = jax.nn.softmax(logits, axis=-1)
    gate_values = jnp.take_along_axis(router_probs, routes, axis=1)
    shared_gate_up = low_back(product(ffn_in, w_shared_in))
    shared_hidden = low(jax.nn.silu(shared_gate_up[:, :SH]) * shared_gate_up[:, SH:])
    shared_result = product(shared_hidden, w_shared_out)
    routed = expert_sum(ffn_in, gate_values, routes, w_expert_in, w_expert_out)
    return (middle + shared_result + routed, lax.optimization_barrier(jnp.max(head_max, axis=0)))

def reference(tokens, cotangent, lengths, routes, g_attn, w_q, w_kva, g_kv, w_kvb, w_o, g_ffn, w_router, w_shared_in, w_shared_out, w_expert_in, w_expert_out):
    floats = (tokens.astype(jnp.float32), g_attn.astype(jnp.float32), w_q.astype(jnp.float32), w_kva.astype(jnp.float32), g_kv.astype(jnp.float32), w_kvb.astype(jnp.float32), w_o.astype(jnp.float32), g_ffn.astype(jnp.float32), w_router.astype(jnp.float32), w_shared_in.astype(jnp.float32), w_shared_out.astype(jnp.float32), w_expert_in.astype(jnp.float32), w_expert_out.astype(jnp.float32))
    run = partial(forward, lengths=lengths, routes=routes)
    mixed, pull, head_max = jax.vjp(run, *floats, has_aux=True)
    segment, position, is_valid = group_layout(lengths)
    grads = pull(cotangent.astype(jnp.float32) * is_valid[:, None].astype(jnp.float32))
    clip_gamma = CLIP_LIMIT / jnp.maximum(head_max, CLIP_LIMIT)
    clip_root = jnp.sqrt(clip_gamma)
    query_factor = jnp.concatenate([jnp.broadcast_to(clip_root[:, None], (H, DN)), jnp.broadcast_to(clip_gamma[:, None], (H, DR))], axis=1).reshape(1, -1)
    clipped_query = (w_q.astype(jnp.float32) * query_factor).astype(jnp.bfloat16)
    return (mixed.astype(jnp.bfloat16), grads[0], grads[1], grads[2], grads[3], grads[4], grads[5], grads[6], grads[7], grads[8], grads[9], grads[10], grads[11], grads[12], clipped_query)
```

```python
import functools

import jax
import jax.numpy as jnp
from jax import lax
from jax.experimental import pallas as pl
from jax.experimental.pallas import tpu as pltpu
from jax.sharding import PartitionSpec as P

D = 2048
H = 16
DN = 128
DR = 64
DV = 128
KVR = 512
FF = 1408
TOP = 6
SH = 2816

EPSILON = 1e-06
CLIP_LIMIT = 8.0
ROPE_BASE = 10000.0
MASK_VALUE = -1e30
BF16 = jnp.bfloat16
F32 = jnp.float32


def rms_norm(values, gain_vector):
    return (
        values
        * lax.rsqrt(jnp.mean(values * values, axis=-1, keepdims=True) + EPSILON)
        * gain_vector
    )


def rotate(values, angles):
    half_width = values.shape[-1] // 2
    first_half = values[..., :half_width]
    second_half = values[..., half_width:]
    cosine = jnp.cos(angles)
    sine_part = jnp.sin(angles)
    return jnp.concatenate(
        [
            first_half * cosine - second_half * sine_part,
            second_half * cosine + first_half * sine_part,
        ],
        axis=-1,
    )


def frequencies(count):
    exponent = jnp.arange(count // 2, dtype=jnp.float32) * 2.0 / count
    return ROPE_BASE ** (-exponent)


def layout(lengths_row, slot_ids):
    seq_ends = jnp.cumsum(lengths_row)
    seq_starts = seq_ends - lengths_row
    inside = (slot_ids[:, None] >= seq_starts[None, :]) & (slot_ids[:, None] < seq_ends[None, :])
    is_valid = jnp.any(inside, axis=1)
    numbers = jnp.arange(lengths_row.shape[0], dtype=jnp.int32)
    seq_number = jnp.sum(jnp.where(inside, numbers[None, :], 0), axis=1)
    first_slot = jnp.sum(jnp.where(inside, seq_starts[None, :], 0), axis=1)
    segment = jnp.where(is_valid, seq_number, lengths_row.shape[0] + slot_ids)
    position = jnp.where(is_valid, slot_ids - first_slot, 0)
    return (segment, position, is_valid)


def silu_back(gate_part, up_part, hidden_grad):
    sigmoid_gate = jax.nn.sigmoid(gate_part)
    gate_grad = hidden_grad * up_part * sigmoid_gate * (1.0 + gate_part * (1.0 - sigmoid_gate))
    up_grad = hidden_grad * gate_part * sigmoid_gate
    return jnp.concatenate([gate_grad, up_grad], axis=1)


def dot(left, right):
    return jnp.dot(left, right, preferred_element_type=F32)


def dot_tn(left, right):
    return lax.dot_general(left, right, (((0,), (0,)), ((), ())), preferred_element_type=F32)


def dot_nt(left, right):
    return lax.dot_general(left, right, (((1,), (1,)), ((), ())), preferred_element_type=F32)


ROWS = 256


def masked_scores(query, key, seg_col, seg_row, first, scale):
    scores = dot_nt(query, key) * scale
    shape = scores.shape
    row_slot = first + lax.broadcasted_iota(jnp.int32, shape, 0)
    key_slot = lax.broadcasted_iota(jnp.int32, shape, 1)
    allowed = (seg_col == seg_row) & (key_slot <= row_slot)
    return jnp.where(allowed, scores, MASK_VALUE)


def attention_forward_kernel(scale, q_ref, k_ref, v_ref, segc_ref, segr_ref, valid_ref, ctx_ref, lse_ref, max_ref):
    count = q_ref.shape[0]
    best = jnp.full((1, 1), MASK_VALUE, F32)
    for first in range(0, count, ROWS):
        rows, keys = pl.ds(first, ROWS), pl.ds(0, first + ROWS)
        masked = masked_scores(q_ref[rows, :], k_ref[keys, :], segc_ref[rows, :], segr_ref[:, keys], first, scale)
        row_max = jnp.max(masked, axis=1, keepdims=True)
        exponent = jnp.exp(masked - row_max)
        row_sum = jnp.sum(exponent, axis=1, keepdims=True)
        probs = (exponent * (1.0 / row_sum)).astype(BF16)
        ctx_ref[rows, :] = dot(probs, v_ref[keys, :]).astype(BF16)
        lse_ref[rows, :] = row_max + jnp.log(row_sum)
        counted = jnp.where(valid_ref[rows, :] > 0, row_max, MASK_VALUE)
        best = jnp.maximum(best, jnp.max(counted, axis=0, keepdims=True))
    max_ref[...] = jnp.broadcast_to(best, max_ref.shape)


def attention_forward(query, key, value, segment, valid):
    count, width = query.shape
    return pl.pallas_call(
        functools.partial(attention_forward_kernel, width ** (-0.5)),
        out_shape=(
            jax.ShapeDtypeStruct((count, value.shape[1]), BF16),
            jax.ShapeDtypeStruct((count, 1), F32),
            jax.ShapeDtypeStruct((8, 128), F32),
        ),
        compiler_params=pltpu.CompilerParams(vmem_limit_bytes=48 * 2**20),
        cost_estimate=pl.CostEstimate(flops=count * count * 320, bytes_accessed=4 * 2**20, transcendentals=count * count // 2),
        name="attention_forward",
    )(query, key, value, segment[:, None], segment[None, :], valid[:, None].astype(jnp.int32))


def attention_backward_kernel(scale, q_ref, k_ref, v_ref, g_ref, segc_ref, segr_ref, lse_ref, dq_ref, dk_ref, dv_ref, dk_sum, dv_sum):
    count = q_ref.shape[0]
    dk_sum[...] = jnp.zeros_like(dk_sum)
    dv_sum[...] = jnp.zeros_like(dv_sum)
    for first in range(0, count, ROWS):
        rows, keys = pl.ds(first, ROWS), pl.ds(0, first + ROWS)
        query, grad = q_ref[rows, :], g_ref[rows, :]
        masked = masked_scores(query, k_ref[keys, :], segc_ref[rows, :], segr_ref[:, keys], first, scale)
        probs = jnp.exp(masked - lse_ref[rows, :])
        prob_grad = dot_nt(grad, v_ref[keys, :])
        mean = jnp.sum(probs * prob_grad, axis=1, keepdims=True)
        score_grad = (probs * (prob_grad - mean)).astype(BF16)
        dq_ref[rows, :] = (dot(score_grad, k_ref[keys, :]) * scale).astype(BF16)
        dk_sum[keys, :] += dot_tn(score_grad, query)
        dv_sum[keys, :] += dot_tn(probs.astype(BF16), grad)
    dk_ref[...] = (dk_sum[...] * scale).astype(BF16)
    dv_ref[...] = dv_sum[...].astype(BF16)


def attention_backward(query, key, value, grad, segment, log_total):
    count, width = query.shape
    return pl.pallas_call(
        functools.partial(attention_backward_kernel, width ** (-0.5)),
        out_shape=(
            jax.ShapeDtypeStruct(query.shape, BF16),
            jax.ShapeDtypeStruct(key.shape, BF16),
            jax.ShapeDtypeStruct(value.shape, BF16),
        ),
        scratch_shapes=[pltpu.VMEM(key.shape, F32), pltpu.VMEM(value.shape, F32)],
        compiler_params=pltpu.CompilerParams(vmem_limit_bytes=48 * 2**20),
        cost_estimate=pl.CostEstimate(flops=count * count * 832, bytes_accessed=6 * 2**20, transcendentals=count * count // 2),
        name="attention_backward",
    )(query, key, value, grad, segment[:, None], segment[None, :], log_total)


def gather_seq(rows):
    return lax.all_gather(rows, "seq", axis=0, tiled=True)


def scatter_seq(partial):
    return lax.psum_scatter(partial, "seq", scatter_dimension=0, tiled=True)


def gather_fsdp(rows, axis=0):
    return lax.all_gather(rows, "fsdp", axis=axis, tiled=True)


def scatter_fsdp(partial, axis=0):
    return lax.psum_scatter(partial, "fsdp", scatter_dimension=axis, tiled=True)


def on_device(
    tokens,
    cotangent,
    lengths,
    routes,
    g_attn,
    w_q,
    w_kva,
    g_kv,
    w_kvb,
    w_o,
    g_ffn,
    w_router,
    w_shared_in,
    w_shared_out,
    w_expert_in,
    w_expert_out,
):
    seq_count = lax.axis_size("seq")
    fsdp_count = lax.axis_size("fsdp")
    rank = lax.axis_index("seq")
    tok_count = tokens.shape[0]
    group_size = tok_count * seq_count
    query_width = DN + DR
    kv_width = DN + DV
    experts = seq_count
    capacity = min(tok_count, 2 * tok_count * TOP // experts)
    buffer_rows = seq_count * capacity
    unit = SH // (seq_count * fsdp_count)
    units = unit * fsdp_count
    row_part = w_q.shape[0]

    def own(rows, axis=0):
        return lax.dynamic_slice_in_dim(rows, rank * tok_count, tok_count, axis)

    token_all = gather_seq(tokens)
    routes_all = gather_seq(routes)
    cotangent_all = gather_seq(cotangent)

    small = gather_fsdp(jnp.concatenate([g_attn, g_kv, g_ffn, w_router.reshape(-1)])[None])
    cuts = [0, g_attn.size, g_kv.size, g_ffn.size, w_router.size]
    ends = [sum(cuts[: i + 1]) for i in range(len(cuts))]
    gain_attn = small[:, ends[0] : ends[1]].reshape(-1).astype(F32)
    gain_latent = small[:, ends[1] : ends[2]].reshape(-1).astype(F32)
    gain_ffn = small[:, ends[2] : ends[3]].reshape(-1).astype(F32)
    router_weight = small[:, ends[3] : ends[4]].reshape(D, experts)
    head_query_part = lax.dynamic_slice_in_dim(w_q, rank * query_width, query_width, 1)
    shared_in_part = lax.dynamic_slice_in_dim(
        w_shared_in.reshape(row_part, 2, fsdp_count, seq_count, unit), rank, 1, 3
    ).reshape(row_part, 2 * units)
    head_expand = gather_fsdp(lax.dynamic_slice_in_dim(w_kvb, rank * kv_width, kv_width, 1))
    head_weights = gather_fsdp(jnp.concatenate([w_kva, head_query_part], axis=1))
    latent_weight = head_weights[:, : KVR + DR]
    head_query = head_weights[:, KVR + DR :]
    shared_in = gather_fsdp(shared_in_part)
    shared_out = gather_fsdp(lax.dynamic_slice_in_dim(w_shared_out, rank * unit, unit, 0))
    output_weight = gather_fsdp(w_o)
    expert_in = gather_fsdp(w_expert_in[0])
    expert_out = gather_fsdp(w_expert_out[0])
    query_weight = gather_fsdp(w_q)
    expand_weight = gather_fsdp(w_kvb)

    slot_ids = jnp.arange(group_size, dtype=jnp.int32)
    segment, position, valid_all = layout(lengths[0], slot_ids)
    angles_all = position[:, None].astype(F32) * frequencies(DR)[None, :]
    angles = own(angles_all)

    normed_all = rms_norm(token_all.astype(F32), gain_attn).astype(BF16)
    query_pre = dot(normed_all, head_query)
    latent_full = dot(normed_all, latent_weight)
    latent_all = rms_norm(latent_full[:, :KVR], gain_latent).astype(BF16)
    expanded = dot(latent_all, head_expand)
    query = jnp.concatenate([query_pre[:, :DN], rotate(query_pre[:, DN:], angles_all)], axis=1).astype(BF16)
    key_rope = rotate(latent_full[:, KVR:], angles_all)
    key = jnp.concatenate([expanded[:, :DN], key_rope], axis=1).astype(BF16)
    value = expanded[:, DN:].astype(BF16)
    context, log_total, head_largest = attention_forward(query, key, value, segment, valid_all)
    largest_all = lax.all_gather(head_largest[:1], ("fsdp", "seq"), axis=0, tiled=False)
    global_max = jnp.max(largest_all.reshape(fsdp_count, seq_count, -1)[:, :, 0], axis=0)

    context_low = lax.all_to_all(context, "seq", split_axis=0, concat_axis=1, tiled=True)
    inputs = tokens.astype(F32)
    middle = inputs + dot(context_low, output_weight)
    ffn_low = rms_norm(middle, gain_ffn).astype(BF16)
    ffn_all = gather_seq(ffn_low)

    router_probs = jax.nn.softmax(dot(ffn_all, router_weight), axis=-1)
    chosen = jnp.any(routes_all == rank, axis=1).reshape(seq_count, tok_count)
    gates = lax.dynamic_slice_in_dim(router_probs, rank, 1, 1).reshape(seq_count, tok_count)
    place = jnp.cumsum(chosen.astype(jnp.int32), axis=1) - 1
    place = jnp.where(chosen, place, capacity)
    picks = lax.broadcasted_iota(jnp.int32, (seq_count, capacity, tok_count), 1) == place[:, None, :]
    pick = picks.astype(BF16)
    row_gate = jnp.sum(jnp.where(picks, gates[:, None, :], 0.0), axis=2).reshape(buffer_rows, 1)

    def to_slots(rows):
        return lax.dot_general(
            pick,
            rows.reshape(seq_count, tok_count, D),
            (((2,), (1,)), ((0,), (0,))),
            preferred_element_type=F32,
        ).reshape(buffer_rows, D)

    def to_tokens(rows):
        return lax.dot_general(
            pick,
            rows.reshape(seq_count, capacity, D),
            (((1,), (1,)), ((0,), (0,))),
            preferred_element_type=F32,
        ).reshape(group_size, D)

    arrived = to_slots(ffn_all).astype(BF16)
    gate_up = dot(arrived, expert_in)
    hidden = (jax.nn.silu(gate_up[:, :FF]) * gate_up[:, FF:]).astype(BF16)
    result = dot(hidden, expert_out).astype(BF16).astype(F32)
    shared_both = dot(ffn_all, shared_in)
    shared_hidden = (jax.nn.silu(shared_both[:, :units]) * shared_both[:, units:]).astype(BF16)
    mixed_part = to_tokens((row_gate * result).astype(BF16)) + dot(shared_hidden, shared_out)
    mixed_sum = scatter_seq(mixed_part.astype(BF16))
    mixed = (middle + mixed_sum.astype(F32)).astype(BF16)

    upstream_all = jnp.where(valid_all[:, None], cotangent_all, 0).astype(BF16)
    upstream_rows = to_slots(upstream_all)
    row_gate_grad = jnp.sum(upstream_rows * result, axis=1).reshape(seq_count, capacity)
    gate_grad = jnp.sum(jnp.where(picks, row_gate_grad[:, :, None], 0.0), axis=1).reshape(1, group_size)
    prob_grads = gather_seq(gate_grad).T
    result_grad = (row_gate * upstream_rows).astype(BF16)
    d_hidden = dot_nt(result_grad, expert_out)
    grad_expert_out = dot_tn(hidden, result_grad)
    d_gate_up = silu_back(gate_up[:, :FF], gate_up[:, FF:], d_hidden).astype(BF16)
    grad_expert_in = dot_tn(arrived, d_gate_up)
    row_grad = dot_nt(d_gate_up, expert_in).astype(BF16)
    shared_hidden_grad = dot_nt(upstream_all, shared_out)
    shared_grad = silu_back(shared_both[:, :units], shared_both[:, units:], shared_hidden_grad).astype(BF16)
    ffn_part = to_tokens(row_grad) + dot_nt(shared_grad, shared_in)
    ffn_sum = scatter_seq(ffn_part.astype(BF16))
    grad_shared_out = dot_tn(shared_hidden, upstream_all)
    grad_shared_in = dot_tn(shared_grad, ffn_all)
    sum_expert_in = scatter_fsdp(grad_expert_in.astype(BF16)).astype(F32)[None]
    sum_expert_out = scatter_fsdp(grad_expert_out.astype(BF16)).astype(F32)[None]
    sum_shared_out = gather_seq(scatter_fsdp(grad_shared_out.astype(BF16))).astype(F32)
    sum_shared_in = gather_seq(scatter_fsdp(grad_shared_in.astype(BF16), 1))
    sum_shared_in = (
        sum_shared_in.reshape(seq_count, 2, fsdp_count, unit, row_part)
        .transpose(4, 1, 2, 0, 3)
        .reshape(row_part, 2 * SH)
        .astype(F32)
    )

    logit_grads = (
        router_probs * (prob_grads - jnp.sum(router_probs * prob_grads, axis=-1, keepdims=True))
    ).astype(BF16)
    grad_router = dot_tn(ffn_all, logit_grads)
    sum_router = scatter_fsdp(grad_router.astype(BF16)).astype(F32)
    ffn_grad = ffn_sum.astype(F32) + dot_nt(own(logit_grads), router_weight)

    ffn_pull = jax.vjp(rms_norm, middle, gain_ffn)[1]
    middle_norm_grad, grad_gain_ffn = ffn_pull(ffn_grad)
    upstream = own(upstream_all).astype(F32)
    middle_grad = upstream + middle_norm_grad
    middle_low = middle_grad.astype(BF16)
    context_grad = dot_nt(middle_low, output_weight).astype(BF16)
    head_grad = lax.all_to_all(context_grad, "seq", split_axis=1, concat_axis=0, tiled=True)
    grad_output = scatter_fsdp(dot_tn(context_low, middle_low).astype(BF16))
    sum_output = lax.psum(grad_output, "seq").astype(F32)

    query_grad, key_grad, value_grad = attention_backward(query, key, value, head_grad, segment, log_total)
    back = lax.all_to_all(
        jnp.concatenate([query_grad, key_grad, value_grad], axis=1).reshape(seq_count, tok_count, -1),
        "seq",
        split_axis=0,
        concat_axis=0,
        tiled=True,
    )
    query_grad_32 = query_grad.astype(F32)
    head_pre_grad = jnp.concatenate(
        [query_grad_32[:, :DN], rotate(query_grad_32[:, DN:], -angles_all)], axis=1
    ).astype(BF16)
    grad_query = scatter_fsdp(dot_tn(head_pre_grad, normed_all).astype(BF16), 1)
    sum_query = gather_seq(grad_query).T.astype(F32)
    head_expand_grad = jnp.concatenate([key_grad[:, :DN], value_grad], axis=1)
    grad_expand = scatter_fsdp(dot_tn(head_expand_grad, latent_all).astype(BF16), 1)
    sum_expand = gather_seq(grad_expand).T.astype(F32)

    back = back.transpose(1, 0, 2)
    back_query = back[..., :query_width].astype(F32)
    back_key = back[..., query_width : 2 * query_width]
    back_value = back[..., 2 * query_width :]
    pre_grad = (
        jnp.concatenate([back_query[..., :DN], rotate(back_query[..., DN:], -angles[:, None, :])], axis=-1)
        .reshape(tok_count, H * query_width)
        .astype(BF16)
    )
    expand_grad = jnp.concatenate([back_key[..., :DN], back_value], axis=-1).reshape(tok_count, H * kv_width)
    latent_grad = dot_nt(expand_grad, expand_weight)
    rope_grad = rotate(jnp.sum(back_key[..., DN:].astype(F32), axis=1), -angles)
    latent_pull = jax.vjp(rms_norm, own(latent_full)[:, :KVR], gain_latent)[1]
    compressed_grad, grad_gain_latent = latent_pull(latent_grad)
    full_grad = jnp.concatenate([compressed_grad, rope_grad], axis=1).astype(BF16)
    full_all = gather_seq(full_grad)
    sum_latent = scatter_fsdp(dot_tn(normed_all, full_all).astype(BF16)).astype(F32)
    normed_grad = dot_nt(pre_grad, query_weight) + dot_nt(full_grad, latent_weight)
    input_pull = jax.vjp(rms_norm, inputs, gain_attn)[1]
    input_norm_grad, grad_gain_attn = input_pull(normed_grad)
    grad_inputs = middle_grad + input_norm_grad

    gain_grads = jnp.concatenate([grad_gain_attn, grad_gain_latent, grad_gain_ffn])
    gain_sum = jnp.sum(lax.all_gather(gain_grads[None], ("fsdp", "seq"), axis=0, tiled=True), axis=0)
    fsdp_rank = lax.axis_index("fsdp")

    def own_part(first, like):
        return lax.dynamic_slice_in_dim(gain_sum, first + fsdp_rank * like.size, like.size, 0)

    sum_gain_attn = own_part(0, g_attn)
    sum_gain_latent = own_part(D, g_kv)
    sum_gain_ffn = own_part(D + KVR, g_ffn)

    clip_gamma = CLIP_LIMIT / jnp.maximum(global_max, CLIP_LIMIT)
    clip_root = jnp.sqrt(clip_gamma)
    query_factor = jnp.concatenate(
        [
            jnp.broadcast_to(clip_root[:, None], (H, DN)),
            jnp.broadcast_to(clip_gamma[:, None], (H, DR)),
        ],
        axis=1,
    ).reshape(1, -1)
    clipped_query = (w_q.astype(F32) * query_factor).astype(BF16)
    return (
        mixed,
        grad_inputs,
        sum_gain_attn,
        sum_query,
        sum_latent,
        sum_gain_latent,
        sum_expand,
        sum_output,
        sum_gain_ffn,
        sum_router,
        sum_shared_in,
        sum_shared_out,
        sum_expert_in,
        sum_expert_out,
        clipped_query,
    )


def solution(mesh):
    in_specs = (
        P(("fsdp", "seq"), None),
        P(("fsdp", "seq"), None),
        P("fsdp", None),
        P(("fsdp", "seq"), None),
        P("fsdp"),
        P("fsdp", None),
        P("fsdp", None),
        P("fsdp"),
        P("fsdp", None),
        P("fsdp", None),
        P("fsdp"),
        P("fsdp", None),
        P("fsdp", None),
        P("fsdp", None),
        P("seq", "fsdp", None),
        P("seq", "fsdp", None),
    )
    out_specs = (
        P(("fsdp", "seq"), None),
        P(("fsdp", "seq"), None),
        P("fsdp"),
        P("fsdp", None),
        P("fsdp", None),
        P("fsdp"),
        P("fsdp", None),
        P("fsdp", None),
        P("fsdp"),
        P("fsdp", None),
        P("fsdp", None),
        P("fsdp", None),
        P("seq", "fsdp", None),
        P("seq", "fsdp", None),
        P("fsdp", None),
    )
    return jax.shard_map(
        on_device, mesh=mesh, in_specs=in_specs, out_specs=out_specs, check_vma=False
    )
```

```python
import functools

import jax
import jax.numpy as jnp
from jax import lax
from jax.experimental import pallas as pl
from jax.experimental.pallas import tpu as pltpu
from jax.sharding import PartitionSpec as P

D = 2048
H = 16
DN = 128
DR = 64
DV = 128
KVR = 512
FF = 1408
TOP = 6
SH = 2816

EPSILON = 1e-06
CLIP_LIMIT = 8.0
ROPE_BASE = 10000.0
MASK_VALUE = -1e30
BF16 = jnp.bfloat16
F32 = jnp.float32


def rms_norm(values, gain_vector):
    return (
        values
        * lax.rsqrt(jnp.mean(values * values, axis=-1, keepdims=True) + EPSILON)
        * gain_vector
    )


def rotate(values, angles):
    half_width = values.shape[-1] // 2
    first_half = values[..., :half_width]
    second_half = values[..., half_width:]
    cosine = jnp.cos(angles)
    sine_part = jnp.sin(angles)
    return jnp.concatenate(
        [
            first_half * cosine - second_half * sine_part,
            second_half * cosine + first_half * sine_part,
        ],
        axis=-1,
    )


def frequencies(count):
    exponent = jnp.arange(count // 2, dtype=jnp.float32) * 2.0 / count
    return ROPE_BASE ** (-exponent)


def layout(lengths_row, slot_ids):
    seq_ends = jnp.cumsum(lengths_row)
    seq_starts = seq_ends - lengths_row
    inside = (slot_ids[:, None] >= seq_starts[None, :]) & (slot_ids[:, None] < seq_ends[None, :])
    is_valid = jnp.any(inside, axis=1)
    numbers = jnp.arange(lengths_row.shape[0], dtype=jnp.int32)
    seq_number = jnp.sum(jnp.where(inside, numbers[None, :], 0), axis=1)
    first_slot = jnp.sum(jnp.where(inside, seq_starts[None, :], 0), axis=1)
    segment = jnp.where(is_valid, seq_number, lengths_row.shape[0] + slot_ids)
    position = jnp.where(is_valid, slot_ids - first_slot, 0)
    return (segment, position, is_valid)


def silu_back(gate_part, up_part, hidden_grad):
    sigmoid_gate = jax.nn.sigmoid(gate_part)
    gate_grad = hidden_grad * up_part * sigmoid_gate * (1.0 + gate_part * (1.0 - sigmoid_gate))
    up_grad = hidden_grad * gate_part * sigmoid_gate
    return jnp.concatenate([gate_grad, up_grad], axis=1)


def dot(left, right):
    return jnp.dot(left, right, preferred_element_type=F32)


def dot_tn(left, right):
    return lax.dot_general(left, right, (((0,), (0,)), ((), ())), preferred_element_type=F32)


def dot_nt(left, right):
    return lax.dot_general(left, right, (((1,), (1,)), ((), ())), preferred_element_type=F32)


ROWS = 256


def masked_scores(query, key, seg_col, seg_row, first, scale):
    scores = dot_nt(query, key) * scale
    shape = scores.shape
    row_slot = first + lax.broadcasted_iota(jnp.int32, shape, 0)
    key_slot = lax.broadcasted_iota(jnp.int32, shape, 1)
    allowed = (seg_col == seg_row) & (key_slot <= row_slot)
    return jnp.where(allowed, scores, MASK_VALUE)


def attention_forward_kernel(scale, q_ref, k_ref, v_ref, segc_ref, segr_ref, valid_ref, ctx_ref, lse_ref, max_ref):
    count = q_ref.shape[0]
    best = jnp.full((1, 1), MASK_VALUE, F32)
    for first in range(0, count, ROWS):
        rows, keys = pl.ds(first, ROWS), pl.ds(0, first + ROWS)
        masked = masked_scores(q_ref[rows, :], k_ref[keys, :], segc_ref[rows, :], segr_ref[:, keys], first, scale)
        row_max = jnp.max(masked, axis=1, keepdims=True)
        exponent = jnp.exp(masked - row_max)
        row_sum = jnp.sum(exponent, axis=1, keepdims=True)
        probs = (exponent * (1.0 / row_sum)).astype(BF16)
        ctx_ref[rows, :] = dot(probs, v_ref[keys, :]).astype(BF16)
        lse_ref[rows, :] = row_max + jnp.log(row_sum)
        counted = jnp.where(valid_ref[rows, :] > 0, row_max, MASK_VALUE)
        best = jnp.maximum(best, jnp.max(counted, axis=0, keepdims=True))
    max_ref[...] = jnp.broadcast_to(best, max_ref.shape)


def attention_forward(query, key, value, segment, valid):
    count, width = query.shape
    return pl.pallas_call(
        functools.partial(attention_forward_kernel, width ** (-0.5)),
        out_shape=(
            jax.ShapeDtypeStruct((count, value.shape[1]), BF16),
            jax.ShapeDtypeStruct((count, 1), F32),
            jax.ShapeDtypeStruct((8, 128), F32),
        ),
        compiler_params=pltpu.CompilerParams(vmem_limit_bytes=48 * 2**20),
        cost_estimate=pl.CostEstimate(flops=count * count * 320, bytes_accessed=4 * 2**20, transcendentals=count * count // 2),
        name="attention_forward",
    )(query, key, value, segment[:, None], segment[None, :], valid[:, None].astype(jnp.int32))


def attention_backward_kernel(scale, q_ref, k_ref, v_ref, g_ref, segc_ref, segr_ref, lse_ref, dq_ref, dk_ref, dv_ref, dk_sum, dv_sum):
    count = q_ref.shape[0]
    dk_sum[...] = jnp.zeros_like(dk_sum)
    dv_sum[...] = jnp.zeros_like(dv_sum)
    for first in range(0, count, ROWS):
        rows, keys = pl.ds(first, ROWS), pl.ds(0, first + ROWS)
        query, grad = q_ref[rows, :], g_ref[rows, :]
        masked = masked_scores(query, k_ref[keys, :], segc_ref[rows, :], segr_ref[:, keys], first, scale)
        probs = jnp.exp(masked - lse_ref[rows, :])
        prob_grad = dot_nt(grad, v_ref[keys, :])
        mean = jnp.sum(probs * prob_grad, axis=1, keepdims=True)
        score_grad = (probs * (prob_grad - mean)).astype(BF16)
        dq_ref[rows, :] = (dot(score_grad, k_ref[keys, :]) * scale).astype(BF16)
        dk_sum[keys, :] += dot_tn(score_grad, query)
        dv_sum[keys, :] += dot_tn(probs.astype(BF16), grad)
    dk_ref[...] = (dk_sum[...] * scale).astype(BF16)
    dv_ref[...] = dv_sum[...].astype(BF16)


def attention_backward(query, key, value, grad, segment, log_total):
    count, width = query.shape
    return pl.pallas_call(
        functools.partial(attention_backward_kernel, width ** (-0.5)),
        out_shape=(
            jax.ShapeDtypeStruct(query.shape, BF16),
            jax.ShapeDtypeStruct(key.shape, BF16),
            jax.ShapeDtypeStruct(value.shape, BF16),
        ),
        scratch_shapes=[pltpu.VMEM(key.shape, F32), pltpu.VMEM(value.shape, F32)],
        compiler_params=pltpu.CompilerParams(vmem_limit_bytes=48 * 2**20),
        cost_estimate=pl.CostEstimate(flops=count * count * 832, bytes_accessed=6 * 2**20, transcendentals=count * count // 2),
        name="attention_backward",
    )(query, key, value, grad, segment[:, None], segment[None, :], log_total)


LINE = 4
MESH = pl.DeviceIdType.MESH


def place():
    rank = lax.axis_index("seq")
    return rank, lax.div(rank, 4), lax.rem(lax.div(rank, 2), 2), lax.rem(rank, 2)


def rank_at(z, y, x, dz, dy, dx):
    across = y + dy * (1 - 2 * y)
    along = x + dx * (1 - 2 * x)
    return (z + dz) * 4 + across * 2 + along


OFFSETS = [(dz, dy, dx) for dz in (0, -1, 1, -2, 2, -3, 3) for dy in (0, 1) for dx in (0, 1)]


def hops(offset):
    return abs(offset[0]) + offset[1] + offset[2]


def onward(order, offset):
    rel = dict(zip("zyx", offset))
    moved = [i for i, dim in enumerate(order) if rel[dim]]
    last = moved[-1] if moved else -1
    steps = []
    if last >= 0 and order[last] == "z":
        steps.append((1 if rel["z"] < 0 else -1, 0, 0))
    for dim in order[last + 1 :]:
        steps += {"z": [(1, 0, 0), (-1, 0, 0)], "y": [(0, 1, 0)], "x": [(0, 0, 1)]}[dim]
    return [s for s in steps if any(0 <= z + offset[0] < LINE and 0 <= z + s[0] < LINE for z in range(LINE))]


def inside(z, dz):
    return (z + dz >= 0) & (z + dz < LINE)


def guarded(z, steps, body):
    steps = [dz for dz in steps if dz]
    if not steps:
        body()
        return
    good = inside(z, steps[0])
    for dz in steps[1:]:
        good = good & inside(z, dz)
    pl.when(good)(body)


def greet_all():
    rank = lax.axis_index("seq")
    count = lax.axis_size("seq")
    barrier = pltpu.get_barrier_semaphore()
    for k in range(1, count):
        peer = lax.rem(rank + k, count)
        pl.semaphore_signal(barrier, inc=1, device_id={"seq": peer}, device_id_type=MESH)
    pl.semaphore_wait(barrier, count - 1)


def gather_kernel(streams, n_main, n_small, *refs):
    n = n_main + n_small
    ins, outs = refs[:n], refs[n : 2 * n]
    send_sems, recv_sems, small_send, small_recv, local_sems = refs[2 * n :]
    rank, z, y, x = place()
    count = lax.axis_size("seq")
    greet_all()
    locals_ = [pltpu.make_async_copy(ins[i], outs[i].at[rank], local_sems.at[i]) for i in range(n)]
    slots = {}

    def copy(stream, offset, step):
        index, first, rows, order = streams[stream]
        part = pl.ds(first, rows)
        source = rank_at(z, y, x, *offset)
        slot = slots.setdefault((stream, offset, step), len(slots))
        block = outs[index].at[source, part]
        own = offset == (0, 0, 0)
        return pltpu.make_async_remote_copy(
            src_ref=ins[index].at[part] if own else block,
            dst_ref=block,
            send_sem=send_sems.at[slot],
            recv_sem=recv_sems.at[stream * count + source],
            device_id={"seq": rank_at(z, y, x, *step)},
            device_id_type=MESH,
        )

    def small_copy(i, k):
        peer = lax.rem(rank + k, count)
        return pltpu.make_async_remote_copy(
            src_ref=ins[n_main + i],
            dst_ref=outs[n_main + i].at[rank],
            send_sem=small_send.at[i * count + k],
            recv_sem=small_recv.at[i * count + rank],
            device_id={"seq": peer},
            device_id_type=MESH,
        )

    def arrived(stream, offset):
        index, first, rows, order = streams[stream]
        source = rank_at(z, y, x, *offset)
        block = outs[index].at[source, pl.ds(first, rows)]
        pltpu.make_async_remote_copy(
            src_ref=block,
            dst_ref=block,
            send_sem=send_sems.at[0],
            recv_sem=recv_sems.at[stream * count + source],
            device_id={"seq": rank},
            device_id_type=MESH,
        ).wait_recv()

    todo = sorted(
        ((stream, offset) for stream in range(len(streams)) for offset in OFFSETS),
        key=lambda it: (hops(it[1]), it[0]),
    )
    for stream, offset in todo:
        def forward(stream=stream, offset=offset):
            if hops(offset):
                arrived(stream, offset)
            for step in onward(streams[stream][3], offset):
                guarded(z, [step[0]], lambda: copy(stream, offset, step).start())
        guarded(z, [offset[0]], forward)
        if stream == len(streams) - 1 and offset == (0, 0, 0):
            for c in locals_:
                c.start()
            for i in range(n_small):
                for k in range(1, count):
                    small_copy(i, k).start()
    for stream, offset in todo:
        for step in onward(streams[stream][3], offset):
            guarded(z, [offset[0], step[0]], lambda: copy(stream, offset, step).wait_send())
    for i in range(n_small):
        for k in range(1, count):
            small_copy(i, k).wait_send()
        for k in range(1, count):
            source = lax.rem(rank + k, count)
            block = outs[n_main + i].at[source]
            pltpu.make_async_remote_copy(
                src_ref=block, dst_ref=block, send_sem=small_send.at[0],
                recv_sem=small_recv.at[i * count + source], device_id={"seq": rank}, device_id_type=MESH,
            ).wait_recv()
    for c in locals_:
        c.wait()


def n_sends(streams):
    return sum(len(onward(s[3], o)) for s in streams for o in OFFSETS)


def gather_all(main, parts, small, collective_id, count=16):
    streams = []
    for i, pieces in enumerate(parts):
        first = 0
        for rows, order in pieces:
            streams.append((i, first, rows, order))
            first += rows
        assert first == main[i].shape[0]
    arrays = list(main) + list(small)
    any_spec = pl.BlockSpec(memory_space=pl.ANY)
    return pl.pallas_call(
        functools.partial(gather_kernel, streams, len(main), len(small)),
        out_shape=tuple(jax.ShapeDtypeStruct((count,) + a.shape, a.dtype) for a in arrays),
        in_specs=[any_spec] * len(arrays),
        out_specs=tuple([any_spec] * len(arrays)),
        scratch_shapes=[
            pltpu.SemaphoreType.DMA((n_sends(streams),)),
            pltpu.SemaphoreType.DMA((len(streams) * count,)),
            pltpu.SemaphoreType.DMA((max(1, len(small)) * count,)),
            pltpu.SemaphoreType.DMA((max(1, len(small)) * count,)),
            pltpu.SemaphoreType.DMA((len(arrays),)),
        ],
        compiler_params=pltpu.CompilerParams(collective_id=collective_id, has_side_effects=True),
        name="gather_all",
    )(*arrays)


def toward(order, offset):
    rel = dict(zip("zyx", offset))
    dim = [d for d in order if rel[d]][-1]
    return {"z": (1 if rel["z"] > 0 else -1, 0, 0), "y": (0, 1, 0), "x": (0, 0, 1)}[dim]


def seen_from(offset, step):
    return (offset[0] - step[0], offset[1] ^ step[1], offset[2] ^ step[2])


def back(step):
    return (-step[0], step[1], step[2])


ADD_ROWS = 16


def scatter_kernel(streams, n_main, n_small, *refs):
    n = n_main + n_small
    ins, outs = refs[:n], refs[n : 2 * n]
    scratch = refs[2 * n :]
    bufs, accs = scratch[: len(streams)], scratch[len(streams) : 2 * len(streams)]
    send_sems, recv_sems, small_send, small_recv, local_sems = scratch[2 * len(streams) :]
    rank, z, y, x = place()
    count = lax.axis_size("seq")
    slot_of, acc_of = {}, {}
    for s, stream in enumerate(streams):
        k = 0
        a = 0
        for offset in OFFSETS:
            for step in onward(stream[3], offset):
                slot_of[s, offset, step] = (k, len(slot_of))
                k += 1
            if hops(offset) and onward(stream[3], offset):
                acc_of[s, offset] = a
                a += 1
    greet_all()

    def small_copy(i, k):
        peer = lax.rem(rank + k, count)
        return pltpu.make_async_remote_copy(
            src_ref=ins[n_main + i],
            dst_ref=outs[n_main + i].at[rank],
            send_sem=small_send.at[i * count + k],
            recv_sem=small_recv.at[i * count + rank],
            device_id={"seq": peer},
            device_id_type=MESH,
        )

    todo = sorted(
        ((s, offset) for s in range(len(streams)) for offset in OFFSETS),
        key=lambda it: (-hops(it[1]), it[0]),
    )
    send_slot = {key: i for i, key in enumerate(k for k in todo if hops(k[1]))}

    def send_copy(s, offset, source):
        order = streams[s][3]
        step = toward(order, offset)
        k, sem = slot_of[s, seen_from(offset, step), back(step)]
        return pltpu.make_async_remote_copy(
            src_ref=source,
            dst_ref=bufs[s].at[k],
            send_sem=send_sems.at[send_slot[s, offset]],
            recv_sem=recv_sems.at[sem],
            device_id={"seq": rank_at(z, y, x, *step)},
            device_id_type=MESH,
        )

    def wait_child(s, offset, step):
        k, sem = slot_of[s, offset, step]
        pltpu.make_async_remote_copy(
            src_ref=bufs[s].at[k],
            dst_ref=bufs[s].at[k],
            send_sem=send_sems.at[0],
            recv_sem=recv_sems.at[sem],
            device_id={"seq": rank},
            device_id_type=MESH,
        ).wait_recv()

    for s, offset in todo:
        index, first, rows, order = streams[s]
        children = onward(order, offset)
        dest = rank_at(z, y, x, *offset)
        always = [c for c in children if not c[0]]
        sometimes = [c for c in children if c[0]]

        def run(present, s=s, offset=offset, index=index, first=first, rows=rows, dest=dest):
            own = ins[index].at[dest, pl.ds(first, rows)]
            if not present:
                send_copy(s, offset, own).start()
                return
            for step in present:
                wait_child(s, offset, step)
            final = not hops(offset)
            target = outs[index].at[pl.ds(first, rows)] if final else accs[s].at[acc_of[s, offset]]
            slots = [slot_of[s, offset, step][0] for step in present]

            def add(i, carry):
                part = pl.ds(pl.multiple_of(i * ADD_ROWS, ADD_ROWS), ADD_ROWS)
                total = own[part, :].astype(F32)
                for k in slots:
                    total = total + bufs[s][k, part, :].astype(F32)
                target[part, :] = total.astype(target.dtype)
                return carry

            lax.fori_loop(0, rows // ADD_ROWS, add, 0)
            if not final:
                send_copy(s, offset, target).start()

        def cases(run=run, always=always, sometimes=sometimes):
            if not sometimes:
                run(always)
                return
            for mask in range(2 ** len(sometimes)):
                present = [c for i, c in enumerate(sometimes) if mask >> i & 1]
                good = None
                for i, c in enumerate(sometimes):
                    here = inside(z, c[0]) if mask >> i & 1 else jnp.logical_not(inside(z, c[0]))
                    good = here if good is None else good & here
                pl.when(good)(functools.partial(run, present + always))

        guarded(z, [offset[0]], cases)
        if (s, offset) == todo[0]:
            for i in range(n_small):
                for k in range(1, count):
                    small_copy(i, k).start()
                pltpu.make_async_copy(ins[n_main + i], outs[n_main + i].at[rank], local_sems.at[i]).start()
    for s, offset in todo:
        if hops(offset):
            index, first, rows, order = streams[s]
            own = ins[index].at[rank_at(z, y, x, *offset), pl.ds(first, rows)]
            guarded(z, [offset[0]], lambda: send_copy(s, offset, own).wait_send())
    for i in range(n_small):
        for k in range(1, count):
            small_copy(i, k).wait_send()
        for k in range(1, count):
            source = lax.rem(rank + k, count)
            block = outs[n_main + i].at[source]
            pltpu.make_async_remote_copy(
                src_ref=block, dst_ref=block, send_sem=small_send.at[0],
                recv_sem=small_recv.at[i * count + source], device_id={"seq": rank}, device_id_type=MESH,
            ).wait_recv()
        pltpu.make_async_copy(ins[n_main + i], outs[n_main + i].at[rank], local_sems.at[i]).wait()


def scatter_sum(main, parts, small, collective_id, count=16):
    streams = []
    for i, pieces in enumerate(parts):
        first = 0
        for rows, order in pieces:
            streams.append((i, first, rows, order))
            first += rows
        assert first == main[i].shape[1]
    arrays = list(main) + list(small)
    any_spec = pl.BlockSpec(memory_space=pl.ANY)
    vmem = pl.BlockSpec(memory_space=pltpu.VMEM)
    buffers, sums = [], []
    for index, first, rows, order in streams:
        columns = main[index].shape[2]
        slots = sum(len(onward(order, o)) for o in OFFSETS)
        held = sum(1 for o in OFFSETS if hops(o) and onward(order, o))
        buffers.append(pltpu.VMEM((slots, rows, columns), main[index].dtype))
        sums.append(pltpu.VMEM((held, rows, columns), main[index].dtype))
    return pl.pallas_call(
        functools.partial(scatter_kernel, streams, len(main), len(small)),
        out_shape=tuple([jax.ShapeDtypeStruct(a.shape[1:], F32) for a in main] + [jax.ShapeDtypeStruct((count,) + a.shape, a.dtype) for a in small]),
        in_specs=[vmem] * len(main) + [any_spec] * len(small),
        out_specs=tuple([vmem] * len(main) + [any_spec] * len(small)),
        scratch_shapes=buffers + sums + [
            pltpu.SemaphoreType.DMA((len(streams) * len(OFFSETS),)),
            pltpu.SemaphoreType.DMA((n_sends(streams),)),
            pltpu.SemaphoreType.DMA((max(1, len(small)) * count,)),
            pltpu.SemaphoreType.DMA((max(1, len(small)) * count,)),
            pltpu.SemaphoreType.DMA((max(1, len(small)),)),
        ],
        compiler_params=pltpu.CompilerParams(collective_id=collective_id, has_side_effects=True, vmem_limit_bytes=60 * 2**20),
        name="scatter_sum",
    )(*arrays)


def gather_seq(rows):
    return lax.all_gather(rows, "seq", axis=0, tiled=True)


def scatter_seq(partial):
    return lax.psum_scatter(partial, "seq", scatter_dimension=0, tiled=True)


def gather_fsdp(rows, axis=0):
    return lax.all_gather(rows, "fsdp", axis=axis, tiled=True)


def scatter_fsdp(partial, axis=0):
    return lax.psum_scatter(partial, "fsdp", scatter_dimension=axis, tiled=True)


def shift_fsdp(rows, k):
    count = lax.axis_size("fsdp")
    return lax.ppermute(rows, "fsdp", [(i, (i + k) % count) for i in range(count)])


ROW_PARTS = [(48, "zxy"), (48, "zyx"), (16, "xyz"), (16, "yxz")]


def split_rows(rows):
    tile = 16
    tiles = rows // tile
    short = tiles // 8
    long = (tiles - 2 * short) // 2
    sizes = [tiles - 2 * short - long, long, short, short]
    orders = ["zxy", "zyx", "xyz", "yxz"]
    return [(n * tile, order) for n, order in zip(sizes, orders) if n]


def on_device(
    tokens,
    cotangent,
    lengths,
    routes,
    g_attn,
    w_q,
    w_kva,
    g_kv,
    w_kvb,
    w_o,
    g_ffn,
    w_router,
    w_shared_in,
    w_shared_out,
    w_expert_in,
    w_expert_out,
):
    seq_count = lax.axis_size("seq")
    fsdp_count = lax.axis_size("fsdp")
    rank = lax.axis_index("seq")
    tok_count = tokens.shape[0]
    group_size = tok_count * seq_count
    query_width = DN + DR
    kv_width = DN + DV
    experts = seq_count
    capacity = min(tok_count, 2 * tok_count * TOP // experts)
    buffer_rows = seq_count * capacity
    unit = SH // (seq_count * fsdp_count)
    units = unit * fsdp_count
    row_part = w_q.shape[0]

    def own(rows, axis=0):
        return lax.dynamic_slice_in_dim(rows, rank * tok_count, tok_count, axis)

    expert_ids = jnp.arange(experts, dtype=jnp.int32)
    route_mask = jnp.any(routes[None] == expert_ids[:, None, None], axis=2).astype(BF16)
    token_all, mask_all = gather_all([tokens], [ROW_PARTS], [route_mask], 1)
    token_all = token_all.reshape(group_size, D)
    cotangent_all = gather_seq(cotangent)

    small = gather_fsdp(jnp.concatenate([g_attn, g_kv, g_ffn, w_router.reshape(-1)])[None])
    cuts = [0, g_attn.size, g_kv.size, g_ffn.size, w_router.size]
    ends = [sum(cuts[: i + 1]) for i in range(len(cuts))]
    gain_attn = small[:, ends[0] : ends[1]].reshape(-1).astype(F32)
    gain_latent = small[:, ends[1] : ends[2]].reshape(-1).astype(F32)
    gain_ffn = small[:, ends[2] : ends[3]].reshape(-1).astype(F32)
    router_weight = small[:, ends[3] : ends[4]].reshape(D, experts)
    head_query_part = lax.dynamic_slice_in_dim(w_q, rank * query_width, query_width, 1)
    shared_in_part = jnp.concatenate(
        [
            lax.dynamic_slice_in_dim(w_shared_in, i * (SH // fsdp_count) + rank * unit, unit, 1)
            for i in range(2 * fsdp_count)
        ],
        axis=1,
    )
    head_expand = gather_fsdp(lax.dynamic_slice_in_dim(w_kvb, rank * kv_width, kv_width, 1))
    head_weights = gather_fsdp(jnp.concatenate([w_kva, head_query_part], axis=1))
    latent_weight = head_weights[:, : KVR + DR]
    head_query = head_weights[:, KVR + DR :]
    shared_in = gather_fsdp(shared_in_part)
    shared_out = gather_fsdp(lax.dynamic_slice_in_dim(w_shared_out, rank * unit, unit, 0))
    output_weight = gather_fsdp(w_o)
    expert_in = gather_fsdp(w_expert_in[0])
    expert_out = gather_fsdp(w_expert_out[0])
    query_weight = gather_fsdp(w_q)
    expand_weight = gather_fsdp(w_kvb)

    slot_ids = jnp.arange(group_size, dtype=jnp.int32)
    segment, position, valid_all = layout(lengths[0], slot_ids)
    angles_all = position[:, None].astype(F32) * frequencies(DR)[None, :]
    angles = own(angles_all)

    normed_all = rms_norm(token_all.astype(F32), gain_attn).astype(BF16)
    query_pre = dot(normed_all, head_query)
    latent_full = dot(normed_all, latent_weight)
    latent_all = rms_norm(latent_full[:, :KVR], gain_latent).astype(BF16)
    expanded = dot(latent_all, head_expand)
    query = jnp.concatenate([query_pre[:, :DN], rotate(query_pre[:, DN:], angles_all)], axis=1).astype(BF16)
    key_rope = rotate(latent_full[:, KVR:], angles_all)
    key = jnp.concatenate([expanded[:, :DN], key_rope], axis=1).astype(BF16)
    value = expanded[:, DN:].astype(BF16)
    context, log_total, head_largest = attention_forward(query, key, value, segment, valid_all)
    context_low = lax.all_to_all(context, "seq", split_axis=0, concat_axis=1, tiled=True)
    inputs = tokens.astype(F32)
    middle = inputs + dot(context_low, output_weight)
    ffn_low = rms_norm(middle, gain_ffn).astype(BF16)
    ffn_all, largest_all = gather_all([ffn_low], [ROW_PARTS], [head_largest], 2)
    ffn_all = ffn_all.reshape(group_size, D)
    head_max = largest_all[:, 0, :]
    for k in range(1, fsdp_count):
        head_max = jnp.maximum(head_max, shift_fsdp(largest_all[:, 0, :], k))
    global_max = head_max[:, 0]

    router_probs = jax.nn.softmax(dot(ffn_all, router_weight), axis=-1)
    chosen = lax.dynamic_slice_in_dim(mask_all, rank, 1, 1).reshape(seq_count, tok_count) > 0
    gates = lax.dynamic_slice_in_dim(router_probs, rank, 1, 1).reshape(seq_count, tok_count)
    place = jnp.cumsum(chosen.astype(jnp.int32), axis=1) - 1
    place = jnp.where(chosen, place, capacity)
    picks = lax.broadcasted_iota(jnp.int32, (seq_count, capacity, tok_count), 1) == place[:, None, :]
    pick = picks.astype(BF16)
    row_gate = jnp.sum(jnp.where(picks, gates[:, None, :], 0.0), axis=2).reshape(buffer_rows, 1)

    def to_slots(rows):
        return lax.dot_general(
            pick,
            rows.reshape(seq_count, tok_count, D),
            (((2,), (1,)), ((0,), (0,))),
            preferred_element_type=F32,
        ).reshape(buffer_rows, D)

    def to_tokens(rows):
        return lax.dot_general(
            pick,
            rows.reshape(seq_count, capacity, D),
            (((1,), (1,)), ((0,), (0,))),
            preferred_element_type=F32,
        ).reshape(group_size, D)

    arrived = to_slots(ffn_all).astype(BF16)
    gate_up = dot(arrived, expert_in)
    hidden = (jax.nn.silu(gate_up[:, :FF]) * gate_up[:, FF:]).astype(BF16)
    result = dot(hidden, expert_out).astype(BF16).astype(F32)
    shared_both = dot(ffn_all, shared_in)
    shared_hidden = (jax.nn.silu(shared_both[:, :units]) * shared_both[:, units:]).astype(BF16)
    mixed_part = to_tokens((row_gate * result).astype(BF16)) + dot(shared_hidden, shared_out)
    mixed_sum = scatter_seq(mixed_part.astype(BF16))
    mixed = (middle + mixed_sum.astype(F32)).astype(BF16)

    upstream_all = jnp.where(valid_all[:, None], cotangent_all, 0).astype(BF16)
    upstream_rows = to_slots(upstream_all)
    row_gate_grad = jnp.sum(upstream_rows * result, axis=1).reshape(seq_count, capacity)
    gate_grad = jnp.sum(jnp.where(picks, row_gate_grad[:, :, None], 0.0), axis=1)
    result_grad = (row_gate * upstream_rows).astype(BF16)
    d_hidden = dot_nt(result_grad, expert_out)
    grad_expert_out = dot_tn(hidden, result_grad)
    d_gate_up = silu_back(gate_up[:, :FF], gate_up[:, FF:], d_hidden).astype(BF16)
    grad_expert_in = dot_tn(arrived, d_gate_up)
    row_grad = dot_nt(d_gate_up, expert_in).astype(BF16)
    shared_hidden_grad = dot_nt(upstream_all, shared_out)
    shared_grad = silu_back(shared_both[:, :units], shared_both[:, units:], shared_hidden_grad).astype(BF16)
    ffn_part = to_tokens(row_grad) + dot_nt(shared_grad, shared_in)
    ffn_sum, prob_grads = scatter_sum(
        [ffn_part.astype(BF16).reshape(seq_count, tok_count, D)], [ROW_PARTS], [gate_grad], 3
    )
    prob_grads = prob_grads.reshape(experts, group_size).T
    grad_shared_out = dot_tn(shared_hidden, upstream_all)
    grad_shared_in = dot_tn(shared_grad, ffn_all)
    sum_expert_in = scatter_fsdp(grad_expert_in.astype(BF16)).astype(F32)[None]
    sum_expert_out = scatter_fsdp(grad_expert_out.astype(BF16)).astype(F32)[None]
    part_shared_out = scatter_fsdp(grad_shared_out.astype(BF16))
    part_shared_in = scatter_fsdp(grad_shared_in.astype(BF16), 1)

    logit_grads = (
        router_probs * (prob_grads - jnp.sum(router_probs * prob_grads, axis=-1, keepdims=True))
    ).astype(BF16)
    grad_router = dot_tn(ffn_all, logit_grads)
    sum_router = scatter_fsdp(grad_router.astype(BF16)).astype(F32)
    ffn_grad = ffn_sum + dot_nt(own(logit_grads), router_weight)

    ffn_pull = jax.vjp(rms_norm, middle, gain_ffn)[1]
    middle_norm_grad, grad_gain_ffn = ffn_pull(ffn_grad)
    upstream = own(upstream_all).astype(F32)
    middle_grad = upstream + middle_norm_grad
    middle_low = middle_grad.astype(BF16)
    context_grad = dot_nt(middle_low, output_weight).astype(BF16)
    head_grad = lax.all_to_all(context_grad, "seq", split_axis=1, concat_axis=0, tiled=True)
    grad_output = scatter_fsdp(dot_tn(context_low, middle_low).astype(BF16))
    part_output = scatter_seq(grad_output)

    query_grad, key_grad, value_grad = attention_backward(query, key, value, head_grad, segment, log_total)
    back = lax.all_to_all(
        jnp.concatenate([query_grad, key_grad, value_grad], axis=1).reshape(seq_count, tok_count, -1),
        "seq",
        split_axis=0,
        concat_axis=0,
        tiled=True,
    )
    query_grad_32 = query_grad.astype(F32)
    head_pre_grad = jnp.concatenate(
        [query_grad_32[:, :DN], rotate(query_grad_32[:, DN:], -angles_all)], axis=1
    ).astype(BF16)
    part_query = scatter_fsdp(dot_tn(head_pre_grad, normed_all).astype(BF16), 1)
    head_expand_grad = jnp.concatenate([key_grad[:, :DN], value_grad], axis=1)
    part_expand = scatter_fsdp(dot_tn(head_expand_grad, latent_all).astype(BF16), 1)

    back = back.transpose(1, 0, 2)
    back_query = back[..., :query_width].astype(F32)
    back_key = back[..., query_width : 2 * query_width]
    back_value = back[..., 2 * query_width :]
    pre_grad = (
        jnp.concatenate([back_query[..., :DN], rotate(back_query[..., DN:], -angles[:, None, :])], axis=-1)
        .reshape(tok_count, H * query_width)
        .astype(BF16)
    )
    expand_grad = jnp.concatenate([back_key[..., :DN], back_value], axis=-1).reshape(tok_count, H * kv_width)
    latent_grad = dot_nt(expand_grad, expand_weight)
    rope_grad = rotate(jnp.sum(back_key[..., DN:].astype(F32), axis=1), -angles)
    latent_pull = jax.vjp(rms_norm, own(latent_full)[:, :KVR], gain_latent)[1]
    compressed_grad, grad_gain_latent = latent_pull(latent_grad)
    full_grad = jnp.concatenate([compressed_grad, rope_grad], axis=1).astype(BF16)
    full_all = gather_seq(full_grad)
    sum_latent = scatter_fsdp(dot_tn(normed_all, full_all).astype(BF16)).astype(F32)
    normed_grad = dot_nt(pre_grad, query_weight) + dot_nt(full_grad, latent_weight)
    input_pull = jax.vjp(rms_norm, inputs, gain_attn)[1]
    input_norm_grad, grad_gain_attn = input_pull(normed_grad)
    grad_inputs = middle_grad + input_norm_grad

    gain_grads = jnp.concatenate([grad_gain_attn, grad_gain_latent, grad_gain_ffn]).reshape(-1, 128)
    gain_grads = jnp.pad(gain_grads, ((0, -gain_grads.shape[0] % 8), (0, 0)))
    part_shared_out = jnp.pad(part_shared_out, ((0, -unit % 16), (0, 0)))
    weight_parts = [part_shared_in, part_query, part_shared_out, part_output, part_expand]
    *sums, gain_all = gather_all(weight_parts, [split_rows(p.shape[0]) for p in weight_parts], [gain_grads], 4)
    sum_shared_in = (
        sums[0]
        .reshape(seq_count, 2, fsdp_count, unit, row_part)
        .transpose(4, 1, 2, 0, 3)
        .reshape(row_part, 2 * SH)
        .astype(F32)
    )
    sum_query = sums[1].reshape(-1, row_part).T.astype(F32)
    sum_shared_out = sums[2][:, :unit].reshape(w_shared_out.shape).astype(F32)
    sum_output = sums[3].reshape(w_o.shape).astype(F32)
    sum_expand = sums[4].reshape(-1, w_kvb.shape[0]).T.astype(F32)
    gain_seq = jnp.sum(gain_all, axis=0)
    gain_sum = gain_seq
    for k in range(1, fsdp_count):
        gain_sum = gain_sum + shift_fsdp(gain_seq, k)
    gain_sum = gain_sum.reshape(-1)
    fsdp_rank = lax.axis_index("fsdp")

    def own_part(first, like):
        return lax.dynamic_slice_in_dim(gain_sum, first + fsdp_rank * like.size, like.size, 0)

    sum_gain_attn = own_part(0, g_attn)
    sum_gain_latent = own_part(D, g_kv)
    sum_gain_ffn = own_part(D + KVR, g_ffn)

    clip_gamma = CLIP_LIMIT / jnp.maximum(global_max, CLIP_LIMIT)
    clip_root = jnp.sqrt(clip_gamma)
    query_factor = jnp.concatenate(
        [
            jnp.broadcast_to(clip_root[:, None], (H, DN)),
            jnp.broadcast_to(clip_gamma[:, None], (H, DR)),
        ],
        axis=1,
    ).reshape(1, -1)
    clipped_query = (w_q.astype(F32) * query_factor).astype(BF16)
    return (
        mixed,
        grad_inputs,
        sum_gain_attn,
        sum_query,
        sum_latent,
        sum_gain_latent,
        sum_expand,
        sum_output,
        sum_gain_ffn,
        sum_router,
        sum_shared_in,
        sum_shared_out,
        sum_expert_in,
        sum_expert_out,
        clipped_query,
    )


def solution(mesh):
    in_specs = (
        P(("fsdp", "seq"), None),
        P(("fsdp", "seq"), None),
        P("fsdp", None),
        P(("fsdp", "seq"), None),
        P("fsdp"),
        P("fsdp", None),
        P("fsdp", None),
        P("fsdp"),
        P("fsdp", None),
        P("fsdp", None),
        P("fsdp"),
        P("fsdp", None),
        P("fsdp", None),
        P("fsdp", None),
        P("seq", "fsdp", None),
        P("seq", "fsdp", None),
    )
    out_specs = (
        P(("fsdp", "seq"), None),
        P(("fsdp", "seq"), None),
        P("fsdp"),
        P("fsdp", None),
        P("fsdp", None),
        P("fsdp"),
        P("fsdp", None),
        P("fsdp", None),
        P("fsdp"),
        P("fsdp", None),
        P("fsdp", None),
        P("fsdp", None),
        P("seq", "fsdp", None),
        P("seq", "fsdp", None),
        P("fsdp", None),
    )
    return jax.shard_map(
        on_device, mesh=mesh, in_specs=in_specs, out_specs=out_specs, check_vma=False
    )
```

```python
import functools

import jax
import jax.numpy as jnp
from jax import lax
from jax.experimental import pallas as pl
from jax.experimental.pallas import tpu as pltpu
from jax.sharding import PartitionSpec as P

D = 2048
H = 16
DN = 128
DR = 64
DV = 128
KVR = 512
FF = 1408
TOP = 6
SH = 2816

EPSILON = 1e-06
CLIP_LIMIT = 8.0
ROPE_BASE = 10000.0
MASK_VALUE = -1e30
BF16 = jnp.bfloat16
F32 = jnp.float32


def rms_norm(values, gain_vector):
    return (
        values
        * lax.rsqrt(jnp.mean(values * values, axis=-1, keepdims=True) + EPSILON)
        * gain_vector
    )


def rotate(values, angles):
    half_width = values.shape[-1] // 2
    first_half = values[..., :half_width]
    second_half = values[..., half_width:]
    cosine = jnp.cos(angles)
    sine_part = jnp.sin(angles)
    return jnp.concatenate(
        [
            first_half * cosine - second_half * sine_part,
            second_half * cosine + first_half * sine_part,
        ],
        axis=-1,
    )


def frequencies(count):
    exponent = jnp.arange(count // 2, dtype=jnp.float32) * 2.0 / count
    return ROPE_BASE ** (-exponent)


def layout(lengths_row, slot_ids):
    seq_ends = jnp.cumsum(lengths_row)
    seq_starts = seq_ends - lengths_row
    inside = (slot_ids[:, None] >= seq_starts[None, :]) & (slot_ids[:, None] < seq_ends[None, :])
    is_valid = jnp.any(inside, axis=1)
    numbers = jnp.arange(lengths_row.shape[0], dtype=jnp.int32)
    seq_number = jnp.sum(jnp.where(inside, numbers[None, :], 0), axis=1)
    first_slot = jnp.sum(jnp.where(inside, seq_starts[None, :], 0), axis=1)
    segment = jnp.where(is_valid, seq_number, lengths_row.shape[0] + slot_ids)
    position = jnp.where(is_valid, slot_ids - first_slot, 0)
    return (segment, position, is_valid)


def silu_back(gate_part, up_part, hidden_grad):
    sigmoid_gate = jax.nn.sigmoid(gate_part)
    gate_grad = hidden_grad * up_part * sigmoid_gate * (1.0 + gate_part * (1.0 - sigmoid_gate))
    up_grad = hidden_grad * gate_part * sigmoid_gate
    return jnp.concatenate([gate_grad, up_grad], axis=1)


def dot(left, right):
    return jnp.dot(left, right, preferred_element_type=F32)


def dot_tn(left, right):
    return lax.dot_general(left, right, (((0,), (0,)), ((), ())), preferred_element_type=F32)


def dot_nt(left, right):
    return lax.dot_general(left, right, (((1,), (1,)), ((), ())), preferred_element_type=F32)


ROWS = 256


def masked_scores(query, key, seg_col, seg_row, first, scale):
    scores = dot_nt(query, key) * scale
    shape = scores.shape
    row_slot = first + lax.broadcasted_iota(jnp.int32, shape, 0)
    key_slot = lax.broadcasted_iota(jnp.int32, shape, 1)
    allowed = (seg_col == seg_row) & (key_slot <= row_slot)
    return jnp.where(allowed, scores, MASK_VALUE)


def attention_forward_kernel(scale, q_ref, k_ref, v_ref, segc_ref, segr_ref, valid_ref, ctx_ref, lse_ref, max_ref):
    count = q_ref.shape[0]
    best = jnp.full((1, 1), MASK_VALUE, F32)
    for first in range(0, count, ROWS):
        rows, keys = pl.ds(first, ROWS), pl.ds(0, first + ROWS)
        masked = masked_scores(q_ref[rows, :], k_ref[keys, :], segc_ref[rows, :], segr_ref[:, keys], first, scale)
        row_max = jnp.max(masked, axis=1, keepdims=True)
        exponent = jnp.exp(masked - row_max)
        row_sum = jnp.sum(exponent, axis=1, keepdims=True)
        probs = (exponent * (1.0 / row_sum)).astype(BF16)
        ctx_ref[rows, :] = dot(probs, v_ref[keys, :]).astype(BF16)
        lse_ref[rows, :] = row_max + jnp.log(row_sum)
        counted = jnp.where(valid_ref[rows, :] > 0, row_max, MASK_VALUE)
        best = jnp.maximum(best, jnp.max(counted, axis=0, keepdims=True))
    max_ref[...] = jnp.broadcast_to(best, max_ref.shape)


def attention_forward(query, key, value, segment, valid):
    count, width = query.shape
    return pl.pallas_call(
        functools.partial(attention_forward_kernel, width ** (-0.5)),
        out_shape=(
            jax.ShapeDtypeStruct((count, value.shape[1]), BF16),
            jax.ShapeDtypeStruct((count, 1), F32),
            jax.ShapeDtypeStruct((8, 128), F32),
        ),
        compiler_params=pltpu.CompilerParams(vmem_limit_bytes=48 * 2**20),
        cost_estimate=pl.CostEstimate(flops=count * count * 320, bytes_accessed=4 * 2**20, transcendentals=count * count // 2),
        name="attention_forward",
    )(query, key, value, segment[:, None], segment[None, :], valid[:, None].astype(jnp.int32))


def attention_backward_kernel(scale, q_ref, k_ref, v_ref, g_ref, segc_ref, segr_ref, lse_ref, dq_ref, dk_ref, dv_ref, dk_sum, dv_sum):
    count = q_ref.shape[0]
    dk_sum[...] = jnp.zeros_like(dk_sum)
    dv_sum[...] = jnp.zeros_like(dv_sum)
    for first in range(0, count, ROWS):
        rows, keys = pl.ds(first, ROWS), pl.ds(0, first + ROWS)
        query, grad = q_ref[rows, :], g_ref[rows, :]
        masked = masked_scores(query, k_ref[keys, :], segc_ref[rows, :], segr_ref[:, keys], first, scale)
        probs = jnp.exp(masked - lse_ref[rows, :])
        prob_grad = dot_nt(grad, v_ref[keys, :])
        mean = jnp.sum(probs * prob_grad, axis=1, keepdims=True)
        score_grad = (probs * (prob_grad - mean)).astype(BF16)
        dq_ref[rows, :] = (dot(score_grad, k_ref[keys, :]) * scale).astype(BF16)
        dk_sum[keys, :] += dot_tn(score_grad, query)
        dv_sum[keys, :] += dot_tn(probs.astype(BF16), grad)
    dk_ref[...] = (dk_sum[...] * scale).astype(BF16)
    dv_ref[...] = dv_sum[...].astype(BF16)


def attention_backward(query, key, value, grad, segment, log_total):
    count, width = query.shape
    return pl.pallas_call(
        functools.partial(attention_backward_kernel, width ** (-0.5)),
        out_shape=(
            jax.ShapeDtypeStruct(query.shape, BF16),
            jax.ShapeDtypeStruct(key.shape, BF16),
            jax.ShapeDtypeStruct(value.shape, BF16),
        ),
        scratch_shapes=[pltpu.VMEM(key.shape, F32), pltpu.VMEM(value.shape, F32)],
        compiler_params=pltpu.CompilerParams(vmem_limit_bytes=48 * 2**20),
        cost_estimate=pl.CostEstimate(flops=count * count * 832, bytes_accessed=6 * 2**20, transcendentals=count * count // 2),
        name="attention_backward",
    )(query, key, value, grad, segment[:, None], segment[None, :], log_total)


def swap_halves(values):
    half = DR // 2
    pieces = [values[:, i * half : (i + 1) * half] for i in (1, 0, 3, 2)]
    return jnp.concatenate(pieces, axis=1)


def project_kernel(x_ref, gain_ref, w_ref, gain_kv_ref, expand_ref, cos_ref, sin_ref, normed_ref, q_ref, k_ref, v_ref, raw_ref, latent_ref):
    normed = rms_norm(x_ref[...].astype(F32), gain_ref[...]).astype(BF16)
    normed_ref[...] = normed
    both = dot(normed, w_ref[...])
    raw = both[:, :KVR]
    raw_ref[...] = raw
    latent = rms_norm(raw, gain_kv_ref[...]).astype(BF16)
    latent_ref[...] = latent
    expanded = dot(latent, expand_ref[...])
    rope = both[:, KVR + DN :]
    rope = rope * cos_ref[...] + swap_halves(rope) * sin_ref[...]
    q_ref[...] = jnp.concatenate([both[:, KVR : KVR + DN], rope[:, :DR]], axis=1).astype(BF16)
    k_ref[...] = jnp.concatenate([expanded[:, :DN], rope[:, DR:]], axis=1).astype(BF16)
    v_ref[...] = expanded[:, DN:].astype(BF16)


def project(rows, gain, weight, gain_kv, expand, angles):
    count = rows.shape[0]
    tile = 256
    cosine, sine = jnp.cos(angles), jnp.sin(angles)
    cosines = jnp.concatenate([cosine] * 4, axis=1)
    sines = jnp.concatenate([-sine, sine] * 2, axis=1)

    def by_rows(columns):
        return pl.BlockSpec((tile, columns), lambda i: (i, 0))

    def whole(array):
        return pl.BlockSpec(array.shape, lambda i: (0, 0))

    outs = [(D, BF16), (DN + DR, BF16), (DN + DR, BF16), (DV, BF16), (KVR, F32), (KVR, BF16)]
    return pl.pallas_call(
        project_kernel,
        grid=(count // tile,),
        in_specs=[
            by_rows(D),
            whole(gain[None]),
            whole(weight),
            whole(gain_kv[None]),
            whole(expand),
            by_rows(2 * DR),
            by_rows(2 * DR),
        ],
        out_specs=tuple(by_rows(c) for c, _ in outs),
        out_shape=tuple(jax.ShapeDtypeStruct((count, c), t) for c, t in outs),
        compiler_params=pltpu.CompilerParams(vmem_limit_bytes=48 * 2**20),
        cost_estimate=pl.CostEstimate(flops=2 * count * D * 900, bytes_accessed=24 * 2**20, transcendentals=count),
        name="project",
    )(rows, gain[None], weight, gain_kv[None], expand, cosines, sines)


def turn_kernel(in_ref, out_ref):
    block = in_ref[...].astype(F32)
    out_ref[...] = block.reshape(-1, block.shape[-1]).T


def turn_rows(rows, tile):
    count, columns = rows.shape
    return pl.pallas_call(
        turn_kernel,
        grid=(count // tile,),
        in_specs=[pl.BlockSpec((tile, columns), lambda i: (i, 0))],
        out_specs=pl.BlockSpec((columns, tile), lambda i: (0, i)),
        out_shape=jax.ShapeDtypeStruct((columns, count), F32),
        compiler_params=pltpu.CompilerParams(vmem_limit_bytes=48 * 2**20),
        cost_estimate=pl.CostEstimate(flops=0, bytes_accessed=6 * rows.size, transcendentals=0),
        name="turn_rows",
    )(rows)


def turn_units(parts):
    seq_count, groups, unit, columns = parts.shape
    if unit % 8 or (seq_count * unit) % 128:
        return parts.transpose(3, 1, 0, 2).reshape(columns, -1).astype(F32)
    wide = seq_count * unit
    tile = 256
    return pl.pallas_call(
        turn_kernel,
        grid=(groups, columns // tile),
        in_specs=[pl.BlockSpec((seq_count, None, unit, tile), lambda g, i: (0, g, 0, i))],
        out_specs=pl.BlockSpec((tile, wide), lambda g, i: (i, g)),
        out_shape=jax.ShapeDtypeStruct((columns, groups * wide), F32),
        compiler_params=pltpu.CompilerParams(vmem_limit_bytes=48 * 2**20),
        cost_estimate=pl.CostEstimate(flops=0, bytes_accessed=6 * parts.size, transcendentals=0),
        name="turn_units",
    )(parts)


LINE = 4
MESH = pl.DeviceIdType.MESH


def place():
    rank = lax.axis_index("seq")
    return rank, lax.div(rank, 4), lax.rem(lax.div(rank, 2), 2), lax.rem(rank, 2)


def rank_at(z, y, x, dz, dy, dx):
    across = y + dy * (1 - 2 * y)
    along = x + dx * (1 - 2 * x)
    return (z + dz) * 4 + across * 2 + along


OFFSETS = [(dz, dy, dx) for dz in (0, -1, 1, -2, 2, -3, 3) for dy in (0, 1) for dx in (0, 1)]


def hops(offset):
    return abs(offset[0]) + offset[1] + offset[2]


def onward(order, offset):
    rel = dict(zip("zyx", offset))
    moved = [i for i, dim in enumerate(order) if rel[dim]]
    last = moved[-1] if moved else -1
    steps = []
    if last >= 0 and order[last] == "z":
        steps.append((1 if rel["z"] < 0 else -1, 0, 0))
    for dim in order[last + 1 :]:
        steps += {"z": [(1, 0, 0), (-1, 0, 0)], "y": [(0, 1, 0)], "x": [(0, 0, 1)]}[dim]
    return [s for s in steps if any(0 <= z + offset[0] < LINE and 0 <= z + s[0] < LINE for z in range(LINE))]


def inside(z, dz):
    return (z + dz >= 0) & (z + dz < LINE)


def guarded(z, steps, body):
    steps = [dz for dz in steps if dz]
    if not steps:
        body()
        return
    good = inside(z, steps[0])
    for dz in steps[1:]:
        good = good & inside(z, dz)
    pl.when(good)(body)


def greet_all():
    rank = lax.axis_index("seq")
    count = lax.axis_size("seq")
    barrier = pltpu.get_barrier_semaphore()
    for k in range(1, count):
        peer = lax.rem(rank + k, count)
        pl.semaphore_signal(barrier, inc=1, device_id={"seq": peer}, device_id_type=MESH)
    pl.semaphore_wait(barrier, count - 1)


def gather_kernel(streams, n_main, n_small, *refs):
    n = n_main + n_small
    ins, outs = refs[:n], refs[n : 2 * n]
    send_sems, recv_sems, small_send, small_recv, local_sems = refs[2 * n :]
    rank, z, y, x = place()
    count = lax.axis_size("seq")
    greet_all()
    locals_ = [pltpu.make_async_copy(ins[i], outs[i].at[rank], local_sems.at[i]) for i in range(n)]
    slots = {}

    def copy(stream, offset, step):
        index, first, rows, order = streams[stream]
        part = pl.ds(first, rows)
        source = rank_at(z, y, x, *offset)
        slot = slots.setdefault((stream, offset, step), len(slots))
        block = outs[index].at[source, part]
        own = offset == (0, 0, 0)
        return pltpu.make_async_remote_copy(
            src_ref=ins[index].at[part] if own else block,
            dst_ref=block,
            send_sem=send_sems.at[slot],
            recv_sem=recv_sems.at[stream * count + source],
            device_id={"seq": rank_at(z, y, x, *step)},
            device_id_type=MESH,
        )

    def small_copy(i, k):
        peer = lax.rem(rank + k, count)
        return pltpu.make_async_remote_copy(
            src_ref=ins[n_main + i],
            dst_ref=outs[n_main + i].at[rank],
            send_sem=small_send.at[i * count + k],
            recv_sem=small_recv.at[i * count + rank],
            device_id={"seq": peer},
            device_id_type=MESH,
        )

    def arrived(stream, offset):
        index, first, rows, order = streams[stream]
        source = rank_at(z, y, x, *offset)
        block = outs[index].at[source, pl.ds(first, rows)]
        pltpu.make_async_remote_copy(
            src_ref=block,
            dst_ref=block,
            send_sem=send_sems.at[0],
            recv_sem=recv_sems.at[stream * count + source],
            device_id={"seq": rank},
            device_id_type=MESH,
        ).wait_recv()

    todo = sorted(
        ((stream, offset) for stream in range(len(streams)) for offset in OFFSETS),
        key=lambda it: (hops(it[1]), it[0]),
    )
    for stream, offset in todo:
        def forward(stream=stream, offset=offset):
            if hops(offset):
                arrived(stream, offset)
            for step in onward(streams[stream][3], offset):
                guarded(z, [step[0]], lambda: copy(stream, offset, step).start())
        guarded(z, [offset[0]], forward)
        if stream == len(streams) - 1 and offset == (0, 0, 0):
            for c in locals_:
                c.start()
            for i in range(n_small):
                for k in range(1, count):
                    small_copy(i, k).start()
    for stream, offset in todo:
        for step in onward(streams[stream][3], offset):
            guarded(z, [offset[0], step[0]], lambda: copy(stream, offset, step).wait_send())
    for i in range(n_small):
        for k in range(1, count):
            small_copy(i, k).wait_send()
        for k in range(1, count):
            source = lax.rem(rank + k, count)
            block = outs[n_main + i].at[source]
            pltpu.make_async_remote_copy(
                src_ref=block, dst_ref=block, send_sem=small_send.at[0],
                recv_sem=small_recv.at[i * count + source], device_id={"seq": rank}, device_id_type=MESH,
            ).wait_recv()
    for c in locals_:
        c.wait()


def n_sends(streams):
    return sum(len(onward(s[3], o)) for s in streams for o in OFFSETS)


def gather_all(main, parts, small, collective_id, count=16):
    streams = []
    for i, pieces in enumerate(parts):
        first = 0
        for rows, order in pieces:
            streams.append((i, first, rows, order))
            first += rows
        assert first == main[i].shape[0]
    arrays = list(main) + list(small)
    any_spec = pl.BlockSpec(memory_space=pl.ANY)
    return pl.pallas_call(
        functools.partial(gather_kernel, streams, len(main), len(small)),
        out_shape=tuple(jax.ShapeDtypeStruct((count,) + a.shape, a.dtype) for a in arrays),
        in_specs=[any_spec] * len(arrays),
        out_specs=tuple([any_spec] * len(arrays)),
        scratch_shapes=[
            pltpu.SemaphoreType.DMA((n_sends(streams),)),
            pltpu.SemaphoreType.DMA((len(streams) * count,)),
            pltpu.SemaphoreType.DMA((max(1, len(small)) * count,)),
            pltpu.SemaphoreType.DMA((max(1, len(small)) * count,)),
            pltpu.SemaphoreType.DMA((len(arrays),)),
        ],
        compiler_params=pltpu.CompilerParams(collective_id=collective_id, has_side_effects=True),
        name="gather_all",
    )(*arrays)


def toward(order, offset):
    rel = dict(zip("zyx", offset))
    dim = [d for d in order if rel[d]][-1]
    return {"z": (1 if rel["z"] > 0 else -1, 0, 0), "y": (0, 1, 0), "x": (0, 0, 1)}[dim]


def seen_from(offset, step):
    return (offset[0] - step[0], offset[1] ^ step[1], offset[2] ^ step[2])


def back(step):
    return (-step[0], step[1], step[2])


ADD_ROWS = 16


def scatter_kernel(streams, n_main, n_small, *refs):
    n = n_main + n_small
    ins, outs = refs[:n], refs[n : 2 * n]
    scratch = refs[2 * n :]
    bufs, accs = scratch[: len(streams)], scratch[len(streams) : 2 * len(streams)]
    send_sems, recv_sems, small_send, small_recv, local_sems = scratch[2 * len(streams) :]
    rank, z, y, x = place()
    count = lax.axis_size("seq")
    slot_of, acc_of = {}, {}
    for s, stream in enumerate(streams):
        k = 0
        a = 0
        for offset in OFFSETS:
            for step in onward(stream[3], offset):
                slot_of[s, offset, step] = (k, len(slot_of))
                k += 1
            if hops(offset) and onward(stream[3], offset):
                acc_of[s, offset] = a
                a += 1
    greet_all()

    def small_copy(i, k):
        peer = lax.rem(rank + k, count)
        return pltpu.make_async_remote_copy(
            src_ref=ins[n_main + i],
            dst_ref=outs[n_main + i].at[rank],
            send_sem=small_send.at[i * count + k],
            recv_sem=small_recv.at[i * count + rank],
            device_id={"seq": peer},
            device_id_type=MESH,
        )

    todo = sorted(
        ((s, offset) for s in range(len(streams)) for offset in OFFSETS),
        key=lambda it: (-hops(it[1]), it[0]),
    )
    send_slot = {key: i for i, key in enumerate(k for k in todo if hops(k[1]))}

    def send_copy(s, offset, source):
        order = streams[s][3]
        step = toward(order, offset)
        k, sem = slot_of[s, seen_from(offset, step), back(step)]
        return pltpu.make_async_remote_copy(
            src_ref=source,
            dst_ref=bufs[s].at[k],
            send_sem=send_sems.at[send_slot[s, offset]],
            recv_sem=recv_sems.at[sem],
            device_id={"seq": rank_at(z, y, x, *step)},
            device_id_type=MESH,
        )

    def wait_child(s, offset, step):
        k, sem = slot_of[s, offset, step]
        pltpu.make_async_remote_copy(
            src_ref=bufs[s].at[k],
            dst_ref=bufs[s].at[k],
            send_sem=send_sems.at[0],
            recv_sem=recv_sems.at[sem],
            device_id={"seq": rank},
            device_id_type=MESH,
        ).wait_recv()

    for s, offset in todo:
        index, first, rows, order = streams[s]
        children = onward(order, offset)
        dest = rank_at(z, y, x, *offset)
        always = [c for c in children if not c[0]]
        sometimes = [c for c in children if c[0]]

        def run(present, s=s, offset=offset, index=index, first=first, rows=rows, dest=dest):
            own = ins[index].at[dest, pl.ds(first, rows)]
            if not present:
                send_copy(s, offset, own).start()
                return
            for step in present:
                wait_child(s, offset, step)
            final = not hops(offset)
            target = outs[index].at[pl.ds(first, rows)] if final else accs[s].at[acc_of[s, offset]]
            slots = [slot_of[s, offset, step][0] for step in present]

            def add(i, carry):
                part = pl.ds(pl.multiple_of(i * ADD_ROWS, ADD_ROWS), ADD_ROWS)
                total = own[part, :].astype(F32)
                for k in slots:
                    total = total + bufs[s][k, part, :].astype(F32)
                target[part, :] = total.astype(target.dtype)
                return carry

            lax.fori_loop(0, rows // ADD_ROWS, add, 0)
            if not final:
                send_copy(s, offset, target).start()

        def cases(run=run, always=always, sometimes=sometimes):
            if not sometimes:
                run(always)
                return
            for mask in range(2 ** len(sometimes)):
                present = [c for i, c in enumerate(sometimes) if mask >> i & 1]
                good = None
                for i, c in enumerate(sometimes):
                    here = inside(z, c[0]) if mask >> i & 1 else jnp.logical_not(inside(z, c[0]))
                    good = here if good is None else good & here
                pl.when(good)(functools.partial(run, present + always))

        guarded(z, [offset[0]], cases)
        if (s, offset) == todo[0]:
            for i in range(n_small):
                for k in range(1, count):
                    small_copy(i, k).start()
                pltpu.make_async_copy(ins[n_main + i], outs[n_main + i].at[rank], local_sems.at[i]).start()
    for s, offset in todo:
        if hops(offset):
            index, first, rows, order = streams[s]
            own = ins[index].at[rank_at(z, y, x, *offset), pl.ds(first, rows)]
            guarded(z, [offset[0]], lambda: send_copy(s, offset, own).wait_send())
    for i in range(n_small):
        for k in range(1, count):
            small_copy(i, k).wait_send()
        for k in range(1, count):
            source = lax.rem(rank + k, count)
            block = outs[n_main + i].at[source]
            pltpu.make_async_remote_copy(
                src_ref=block, dst_ref=block, send_sem=small_send.at[0],
                recv_sem=small_recv.at[i * count + source], device_id={"seq": rank}, device_id_type=MESH,
            ).wait_recv()
        pltpu.make_async_copy(ins[n_main + i], outs[n_main + i].at[rank], local_sems.at[i]).wait()


def scatter_sum(main, parts, small, collective_id, count=16):
    streams = []
    for i, pieces in enumerate(parts):
        first = 0
        for rows, order in pieces:
            streams.append((i, first, rows, order))
            first += rows
        assert first == main[i].shape[1]
    arrays = list(main) + list(small)
    any_spec = pl.BlockSpec(memory_space=pl.ANY)
    vmem = pl.BlockSpec(memory_space=pltpu.VMEM)
    buffers, sums = [], []
    for index, first, rows, order in streams:
        columns = main[index].shape[2]
        slots = sum(len(onward(order, o)) for o in OFFSETS)
        held = sum(1 for o in OFFSETS if hops(o) and onward(order, o))
        buffers.append(pltpu.VMEM((slots, rows, columns), main[index].dtype))
        sums.append(pltpu.VMEM((held, rows, columns), main[index].dtype))
    return pl.pallas_call(
        functools.partial(scatter_kernel, streams, len(main), len(small)),
        out_shape=tuple([jax.ShapeDtypeStruct(a.shape[1:], F32) for a in main] + [jax.ShapeDtypeStruct((count,) + a.shape, a.dtype) for a in small]),
        in_specs=[vmem] * len(main) + [any_spec] * len(small),
        out_specs=tuple([vmem] * len(main) + [any_spec] * len(small)),
        scratch_shapes=buffers + sums + [
            pltpu.SemaphoreType.DMA((len(streams) * len(OFFSETS),)),
            pltpu.SemaphoreType.DMA((n_sends(streams),)),
            pltpu.SemaphoreType.DMA((max(1, len(small)) * count,)),
            pltpu.SemaphoreType.DMA((max(1, len(small)) * count,)),
            pltpu.SemaphoreType.DMA((max(1, len(small)),)),
        ],
        compiler_params=pltpu.CompilerParams(collective_id=collective_id, has_side_effects=True, vmem_limit_bytes=60 * 2**20),
        name="scatter_sum",
    )(*arrays)


def gather_seq(rows):
    return lax.all_gather(rows, "seq", axis=0, tiled=True)


def scatter_seq(partial):
    return lax.psum_scatter(partial, "seq", scatter_dimension=0, tiled=True)


def gather_fsdp(rows, axis=0):
    return lax.all_gather(rows, "fsdp", axis=axis, tiled=True)


def scatter_fsdp(partial, axis=0):
    count, me = lax.axis_size("fsdp"), lax.axis_index("fsdp")
    size = partial.shape[axis] // count
    total = lax.dynamic_slice_in_dim(partial, me * size, size, axis).astype(F32)
    for k in range(1, count):
        piece = lax.dynamic_slice_in_dim(partial, lax.rem(me + k, count) * size, size, axis)
        total = total + shift_fsdp(piece, k).astype(F32)
    return total


def shift_fsdp(rows, k):
    count = lax.axis_size("fsdp")
    return lax.ppermute(rows, "fsdp", [(i, (i + k) % count) for i in range(count)])


ROW_PARTS = [(48, "zxy"), (48, "zyx"), (16, "xyz"), (16, "yxz")]


def split_rows(rows):
    tile = 16
    tiles = rows // tile
    short = tiles // 8
    long = (tiles - 2 * short) // 2
    sizes = [tiles - 2 * short - long, long, short, short]
    orders = ["zxy", "zyx", "xyz", "yxz"]
    return [(n * tile, order) for n, order in zip(sizes, orders) if n]


def on_device(
    tokens,
    cotangent,
    lengths,
    routes,
    g_attn,
    w_q,
    w_kva,
    g_kv,
    w_kvb,
    w_o,
    g_ffn,
    w_router,
    w_shared_in,
    w_shared_out,
    w_expert_in,
    w_expert_out,
):
    seq_count = lax.axis_size("seq")
    fsdp_count = lax.axis_size("fsdp")
    rank = lax.axis_index("seq")
    tok_count = tokens.shape[0]
    group_size = tok_count * seq_count
    query_width = DN + DR
    kv_width = DN + DV
    experts = seq_count
    capacity = min(tok_count, 2 * tok_count * TOP // experts)
    buffer_rows = seq_count * capacity
    unit = SH // (seq_count * fsdp_count)
    units = unit * fsdp_count
    row_part = w_q.shape[0]

    def own(rows, axis=0):
        return lax.dynamic_slice_in_dim(rows, rank * tok_count, tok_count, axis)

    expert_ids = jnp.arange(experts, dtype=jnp.int32)
    route_mask = jnp.any(routes[None] == expert_ids[:, None, None], axis=2).astype(BF16)
    token_all, mask_all = gather_all([tokens], [ROW_PARTS], [route_mask], 1)
    token_all = token_all.reshape(group_size, D)

    small = gather_fsdp(jnp.concatenate([g_attn, g_kv, g_ffn, w_router.reshape(-1)])[None])
    cuts = [0, g_attn.size, g_kv.size, g_ffn.size, w_router.size]
    ends = [sum(cuts[: i + 1]) for i in range(len(cuts))]
    gain_attn = small[:, ends[0] : ends[1]].reshape(-1).astype(F32)
    gain_latent = small[:, ends[1] : ends[2]].reshape(-1).astype(F32)
    gain_ffn = small[:, ends[2] : ends[3]].reshape(-1).astype(F32)
    router_weight = small[:, ends[3] : ends[4]].reshape(D, experts)
    head_query_part = lax.dynamic_slice_in_dim(w_q, rank * query_width, query_width, 1)
    shared_in_part = jnp.concatenate(
        [
            lax.dynamic_slice_in_dim(w_shared_in, i * (SH // fsdp_count) + rank * unit, unit, 1)
            for i in range(2 * fsdp_count)
        ],
        axis=1,
    )
    head_expand = gather_fsdp(lax.dynamic_slice_in_dim(w_kvb, rank * kv_width, kv_width, 1))
    head_weights = gather_fsdp(
        jnp.concatenate([w_kva[:, :KVR], head_query_part, w_kva[:, KVR:]], axis=1)
    )
    shared_in = gather_fsdp(shared_in_part)
    shared_out = gather_fsdp(lax.dynamic_slice_in_dim(w_shared_out, rank * unit, unit, 0))
    output_weight = gather_fsdp(w_o)
    expert_in = gather_fsdp(w_expert_in[0])
    expert_out = gather_fsdp(w_expert_out[0])
    query_weight = gather_fsdp(w_q)
    expand_weight = gather_fsdp(w_kvb)

    slot_ids = jnp.arange(group_size, dtype=jnp.int32)
    segment, position, valid_all = layout(lengths[0], slot_ids)
    angles_all = position[:, None].astype(F32) * frequencies(DR)[None, :]
    angles = own(angles_all)

    upstream_own = jnp.where(own(valid_all)[:, None], cotangent, 0).astype(BF16)
    upstream_all = gather_seq(upstream_own)

    normed_all, query, key, value, latent_full, latent_all = project(
        token_all, gain_attn, head_weights, gain_latent, head_expand, angles_all
    )
    context, log_total, head_largest = attention_forward(query, key, value, segment, valid_all)
    context_low = lax.all_to_all(context, "seq", split_axis=0, concat_axis=1, tiled=True)
    inputs = tokens.astype(F32)
    middle = inputs + dot(context_low, output_weight)
    ffn_low = rms_norm(middle, gain_ffn).astype(BF16)
    ffn_all, largest_all = gather_all([ffn_low], [ROW_PARTS], [head_largest], 2)
    ffn_all = ffn_all.reshape(group_size, D)
    head_max = largest_all[:, 0, :]
    for k in range(1, fsdp_count):
        head_max = jnp.maximum(head_max, shift_fsdp(largest_all[:, 0, :], k))
    global_max = head_max[:, 0]

    router_probs = jax.nn.softmax(dot(ffn_all, router_weight), axis=-1)
    chosen = lax.dynamic_slice_in_dim(mask_all, rank, 1, 1).reshape(seq_count, tok_count) > 0
    gates = lax.dynamic_slice_in_dim(router_probs, rank, 1, 1).reshape(seq_count, tok_count)
    place = jnp.cumsum(chosen.astype(jnp.int32), axis=1) - 1
    place = jnp.where(chosen, place, capacity)
    picks = lax.broadcasted_iota(jnp.int32, (seq_count, capacity, tok_count), 1) == place[:, None, :]
    pick = picks.astype(BF16)
    row_gate = jnp.sum(jnp.where(picks, gates[:, None, :], 0.0), axis=2).reshape(buffer_rows, 1)

    def to_slots(rows):
        return lax.dot_general(
            pick,
            rows.reshape(seq_count, tok_count, D),
            (((2,), (1,)), ((0,), (0,))),
            preferred_element_type=F32,
        ).reshape(buffer_rows, D)

    def to_tokens(rows):
        return lax.dot_general(
            pick,
            rows.reshape(seq_count, capacity, D),
            (((1,), (1,)), ((0,), (0,))),
            preferred_element_type=F32,
        ).reshape(group_size, D)

    arrived = to_slots(ffn_all).astype(BF16)
    gate_up = dot(arrived, expert_in)
    hidden = (jax.nn.silu(gate_up[:, :FF]) * gate_up[:, FF:]).astype(BF16)
    result = dot(hidden, expert_out).astype(BF16).astype(F32)
    shared_both = dot(ffn_all, shared_in)
    shared_hidden = (jax.nn.silu(shared_both[:, :units]) * shared_both[:, units:]).astype(BF16)
    mixed_part = to_tokens((row_gate * result).astype(BF16)) + dot(shared_hidden, shared_out)
    mixed_sum = scatter_seq(mixed_part.astype(BF16))
    mixed = (middle + mixed_sum.astype(F32)).astype(BF16)

    upstream_rows = to_slots(upstream_all)
    row_gate_grad = jnp.sum(upstream_rows * result, axis=1).reshape(seq_count, capacity)
    gate_grad = jnp.sum(jnp.where(picks, row_gate_grad[:, :, None], 0.0), axis=1)
    result_grad = (row_gate * upstream_rows).astype(BF16)
    d_hidden = dot_nt(result_grad, expert_out)
    grad_expert_out = dot_tn(hidden, result_grad)
    d_gate_up = silu_back(gate_up[:, :FF], gate_up[:, FF:], d_hidden).astype(BF16)
    grad_expert_in = dot_tn(arrived, d_gate_up)
    row_grad = dot_nt(d_gate_up, expert_in).astype(BF16)
    shared_hidden_grad = dot_nt(upstream_all, shared_out)
    shared_grad = silu_back(shared_both[:, :units], shared_both[:, units:], shared_hidden_grad).astype(BF16)
    ffn_part = to_tokens(row_grad) + dot_nt(shared_grad, shared_in)
    ffn_sum, prob_grads = scatter_sum(
        [ffn_part.astype(BF16).reshape(seq_count, tok_count, D)], [ROW_PARTS], [gate_grad], 3
    )
    prob_grads = prob_grads.reshape(experts, group_size).T
    grad_shared_out = dot_tn(shared_hidden, upstream_all)
    grad_shared_in = dot_tn(shared_grad, ffn_all)
    sum_expert_in = scatter_fsdp(grad_expert_in.astype(BF16))[None]
    sum_expert_out = scatter_fsdp(grad_expert_out.astype(BF16))[None]
    part_shared_out = scatter_fsdp(grad_shared_out.astype(BF16)).astype(BF16)
    part_shared_in = scatter_fsdp(grad_shared_in.astype(BF16), 1).astype(BF16)
    sum_shared_out = gather_seq(part_shared_out).astype(F32)
    sum_shared_in = turn_units(
        gather_seq(part_shared_in).reshape(seq_count, 2 * fsdp_count, unit, row_part)
    )

    logit_grads = (
        router_probs * (prob_grads - jnp.sum(router_probs * prob_grads, axis=-1, keepdims=True))
    ).astype(BF16)
    grad_router = dot_tn(ffn_all, logit_grads)
    sum_router = scatter_fsdp(grad_router.astype(BF16))
    ffn_grad = ffn_sum + dot_nt(own(logit_grads), router_weight)

    ffn_pull = jax.vjp(rms_norm, middle, gain_ffn)[1]
    middle_norm_grad, grad_gain_ffn = ffn_pull(ffn_grad)
    middle_grad = upstream_own.astype(F32) + middle_norm_grad
    middle_low = middle_grad.astype(BF16)
    context_grad = dot_nt(middle_low, output_weight).astype(BF16)
    head_grad = lax.all_to_all(context_grad, "seq", split_axis=1, concat_axis=0, tiled=True)
    grad_output = scatter_fsdp(dot_tn(context_low, middle_low).astype(BF16)).astype(BF16)
    output_rows = row_part // seq_count
    (part_output,) = scatter_sum(
        [grad_output.reshape(seq_count, output_rows, D)], [split_rows(output_rows)], [], 5
    )

    query_grad, key_grad, value_grad = attention_backward(query, key, value, head_grad, segment, log_total)
    back = lax.all_to_all(
        jnp.concatenate([query_grad, key_grad, value_grad], axis=1).reshape(seq_count, tok_count, -1),
        "seq",
        split_axis=0,
        concat_axis=0,
        tiled=True,
    )
    query_grad_32 = query_grad.astype(F32)
    head_pre_grad = jnp.concatenate(
        [query_grad_32[:, :DN], rotate(query_grad_32[:, DN:], -angles_all)], axis=1
    ).astype(BF16)
    part_query = scatter_fsdp(dot_tn(head_pre_grad, normed_all).astype(BF16), 1).astype(BF16)
    head_expand_grad = jnp.concatenate([key_grad[:, :DN], value_grad], axis=1)
    part_expand = scatter_fsdp(dot_tn(head_expand_grad, latent_all).astype(BF16), 1).astype(BF16)

    back = back.transpose(1, 0, 2)
    back_query = back[..., :query_width].astype(F32)
    back_key = back[..., query_width : 2 * query_width]
    back_value = back[..., 2 * query_width :]
    pre_grad = (
        jnp.concatenate([back_query[..., :DN], rotate(back_query[..., DN:], -angles[:, None, :])], axis=-1)
        .reshape(tok_count, H * query_width)
        .astype(BF16)
    )
    expand_grad = jnp.concatenate([back_key[..., :DN], back_value], axis=-1).reshape(tok_count, H * kv_width)
    latent_grad = dot_nt(expand_grad, expand_weight)
    rope_grad = rotate(jnp.sum(back_key[..., DN:].astype(F32), axis=1), -angles)
    latent_pull = jax.vjp(rms_norm, own(latent_full)[:, :KVR], gain_latent)[1]
    compressed_grad, grad_gain_latent = latent_pull(latent_grad)
    full_grad = jnp.concatenate([compressed_grad, rope_grad], axis=1).astype(BF16)
    full_all = gather_seq(full_grad)
    sum_latent = scatter_fsdp(dot_tn(normed_all, full_all).astype(BF16))
    spread_grad = jnp.pad(full_grad[:, :KVR], ((0, 0), (0, query_width + DR)))
    spread_grad = spread_grad + jnp.pad(full_grad[:, KVR:], ((0, 0), (KVR + query_width, 0)))
    normed_grad = dot_nt(pre_grad, query_weight) + dot_nt(spread_grad, head_weights)
    input_pull = jax.vjp(rms_norm, inputs, gain_attn)[1]
    input_norm_grad, grad_gain_attn = input_pull(normed_grad)
    grad_inputs = middle_grad + input_norm_grad

    gain_grads = jnp.concatenate([grad_gain_attn, grad_gain_latent, grad_gain_ffn]).reshape(-1, 128)
    gain_grads = jnp.pad(gain_grads, ((0, -gain_grads.shape[0] % 8), (0, 0)))
    weight_parts = [part_query, part_output.astype(BF16), part_expand]
    *sums, gain_all = gather_all(weight_parts, [split_rows(p.shape[0]) for p in weight_parts], [gain_grads], 4)
    sum_query = turn_rows(sums[0].reshape(-1, row_part), 384)
    sum_output = sums[1].reshape(w_o.shape).astype(F32)
    sum_expand = turn_rows(sums[2].reshape(-1, w_kvb.shape[0]), 512)
    gain_seq = jnp.sum(gain_all, axis=0)
    gain_sum = gain_seq
    for k in range(1, fsdp_count):
        gain_sum = gain_sum + shift_fsdp(gain_seq, k)
    gain_sum = gain_sum.reshape(-1)
    fsdp_rank = lax.axis_index("fsdp")

    def own_part(first, like):
        return lax.dynamic_slice_in_dim(gain_sum, first + fsdp_rank * like.size, like.size, 0)

    sum_gain_attn = own_part(0, g_attn)
    sum_gain_latent = own_part(D, g_kv)
    sum_gain_ffn = own_part(D + KVR, g_ffn)

    clip_gamma = CLIP_LIMIT / jnp.maximum(global_max, CLIP_LIMIT)
    clip_root = jnp.sqrt(clip_gamma)
    query_factor = jnp.concatenate(
        [
            jnp.broadcast_to(clip_root[:, None], (H, DN)),
            jnp.broadcast_to(clip_gamma[:, None], (H, DR)),
        ],
        axis=1,
    ).reshape(1, -1)
    clipped_query = (w_q.astype(F32) * query_factor).astype(BF16)
    return (
        mixed,
        grad_inputs,
        sum_gain_attn,
        sum_query,
        sum_latent,
        sum_gain_latent,
        sum_expand,
        sum_output,
        sum_gain_ffn,
        sum_router,
        sum_shared_in,
        sum_shared_out,
        sum_expert_in,
        sum_expert_out,
        clipped_query,
    )


def solution(mesh):
    in_specs = (
        P(("fsdp", "seq"), None),
        P(("fsdp", "seq"), None),
        P("fsdp", None),
        P(("fsdp", "seq"), None),
        P("fsdp"),
        P("fsdp", None),
        P("fsdp", None),
        P("fsdp"),
        P("fsdp", None),
        P("fsdp", None),
        P("fsdp"),
        P("fsdp", None),
        P("fsdp", None),
        P("fsdp", None),
        P("seq", "fsdp", None),
        P("seq", "fsdp", None),
    )
    out_specs = (
        P(("fsdp", "seq"), None),
        P(("fsdp", "seq"), None),
        P("fsdp"),
        P("fsdp", None),
        P("fsdp", None),
        P("fsdp"),
        P("fsdp", None),
        P("fsdp", None),
        P("fsdp"),
        P("fsdp", None),
        P("fsdp", None),
        P("fsdp", None),
        P("seq", "fsdp", None),
        P("seq", "fsdp", None),
        P("fsdp", None),
    )
    return jax.shard_map(
        on_device, mesh=mesh, in_specs=in_specs, out_specs=out_specs, check_vma=False
    )
```

```python
import functools

import jax
import jax.numpy as jnp
from jax import lax
from jax.experimental import pallas as pl
from jax.experimental.pallas import tpu as pltpu
from jax.sharding import PartitionSpec as P

D = 2048
H = 16
DN = 128
DR = 64
DV = 128
KVR = 512
FF = 1408
TOP = 6
SH = 2816

EPSILON = 1e-06
CLIP_LIMIT = 8.0
ROPE_BASE = 10000.0
MASK_VALUE = -1e30
BF16 = jnp.bfloat16
F32 = jnp.float32


def rms_norm(values, gain_vector):
    return (
        values
        * lax.rsqrt(jnp.mean(values * values, axis=-1, keepdims=True) + EPSILON)
        * gain_vector
    )


def rotate(values, angles):
    half_width = values.shape[-1] // 2
    first_half = values[..., :half_width]
    second_half = values[..., half_width:]
    cosine = jnp.cos(angles)
    sine_part = jnp.sin(angles)
    return jnp.concatenate(
        [
            first_half * cosine - second_half * sine_part,
            second_half * cosine + first_half * sine_part,
        ],
        axis=-1,
    )


def frequencies(count):
    exponent = jnp.arange(count // 2, dtype=jnp.float32) * 2.0 / count
    return ROPE_BASE ** (-exponent)


def layout(lengths_row, slot_ids):
    seq_ends = jnp.cumsum(lengths_row)
    seq_starts = seq_ends - lengths_row
    inside = (slot_ids[:, None] >= seq_starts[None, :]) & (slot_ids[:, None] < seq_ends[None, :])
    is_valid = jnp.any(inside, axis=1)
    numbers = jnp.arange(lengths_row.shape[0], dtype=jnp.int32)
    seq_number = jnp.sum(jnp.where(inside, numbers[None, :], 0), axis=1)
    first_slot = jnp.sum(jnp.where(inside, seq_starts[None, :], 0), axis=1)
    segment = jnp.where(is_valid, seq_number, lengths_row.shape[0] + slot_ids)
    position = jnp.where(is_valid, slot_ids - first_slot, 0)
    return (segment, position, is_valid)


def dot(left, right):
    return jnp.dot(left, right, preferred_element_type=F32)


def dot_tn(left, right):
    return lax.dot_general(left, right, (((0,), (0,)), ((), ())), preferred_element_type=F32)


def dot_nt(left, right):
    return lax.dot_general(left, right, (((1,), (1,)), ((), ())), preferred_element_type=F32)


ROWS = 256


def masked_scores(query, key, seg_col, seg_row, first, scale):
    scores = dot_nt(query, key) * scale
    shape = scores.shape
    row_slot = first + lax.broadcasted_iota(jnp.int32, shape, 0)
    key_slot = lax.broadcasted_iota(jnp.int32, shape, 1)
    allowed = (seg_col == seg_row) & (key_slot <= row_slot)
    return jnp.where(allowed, scores, MASK_VALUE)


def attention_forward_kernel(scale, q_ref, k_ref, v_ref, segc_ref, segr_ref, valid_ref, ctx_ref, lse_ref, max_ref):
    count = q_ref.shape[0]
    best = jnp.full((1, 1), MASK_VALUE, F32)
    for first in range(0, count, ROWS):
        rows, keys = pl.ds(first, ROWS), pl.ds(0, first + ROWS)
        masked = masked_scores(q_ref[rows, :], k_ref[keys, :], segc_ref[rows, :], segr_ref[:, keys], first, scale)
        row_max = jnp.max(masked, axis=1, keepdims=True)
        exponent = jnp.exp(masked - row_max)
        row_sum = jnp.sum(exponent, axis=1, keepdims=True)
        probs = (exponent * (1.0 / row_sum)).astype(BF16)
        ctx_ref[rows, :] = dot(probs, v_ref[keys, :]).astype(BF16)
        lse_ref[rows, :] = row_max + jnp.log(row_sum)
        counted = jnp.where(valid_ref[rows, :] > 0, row_max, MASK_VALUE)
        best = jnp.maximum(best, jnp.max(counted, axis=0, keepdims=True))
    max_ref[...] = jnp.broadcast_to(best, max_ref.shape)


def attention_forward(query, key, value, segment, valid):
    count, width = query.shape
    return pl.pallas_call(
        functools.partial(attention_forward_kernel, width ** (-0.5)),
        out_shape=(
            jax.ShapeDtypeStruct((count, value.shape[1]), BF16),
            jax.ShapeDtypeStruct((count, 1), F32),
            jax.ShapeDtypeStruct((8, 128), F32),
        ),
        compiler_params=pltpu.CompilerParams(vmem_limit_bytes=48 * 2**20),
        cost_estimate=pl.CostEstimate(flops=count * count * 320, bytes_accessed=4 * 2**20, transcendentals=count * count // 2),
        name="attention_forward",
    )(query, key, value, segment[:, None], segment[None, :], valid[:, None].astype(jnp.int32))


def attention_backward_kernel(
    scale, q_ref, k_ref, v_ref, g_ref, segc_ref, segr_ref, lse_ref, cos_ref, sin_ref, out_ref, dk_sum, dv_sum
):
    half = DR // 2
    count = q_ref.shape[0]
    dk_sum[...] = jnp.zeros_like(dk_sum)
    dv_sum[...] = jnp.zeros_like(dv_sum)
    for first in range(0, count, ROWS):
        rows, keys = pl.ds(first, ROWS), pl.ds(0, first + ROWS)
        query, grad = q_ref[rows, :], g_ref[rows, :]
        masked = masked_scores(query, k_ref[keys, :], segc_ref[rows, :], segr_ref[:, keys], first, scale)
        probs = jnp.exp(masked - lse_ref[rows, :])
        prob_grad = dot_nt(grad, v_ref[keys, :])
        mean = jnp.sum(probs * prob_grad, axis=1, keepdims=True)
        score_grad = (probs * (prob_grad - mean)).astype(BF16)
        query_grad = (dot(score_grad, k_ref[keys, :]) * scale).astype(BF16)
        out_ref[rows, :DN] = query_grad[:, :DN]
        rope = query_grad[:, DN:].astype(F32)
        swapped = jnp.concatenate([rope[:, half:], rope[:, :half]], axis=1)
        rope = rope * cos_ref[rows, :DR] - swapped * sin_ref[rows, :DR]
        out_ref[rows, 2 * DN + DV : 2 * DN + DV + DR] = rope.astype(BF16)
        dk_sum[keys, :] += dot_tn(score_grad, query)
        dv_sum[keys, :] += dot_tn(probs.astype(BF16), grad)
    key_grad = (dk_sum[...] * scale).astype(BF16)
    out_ref[:, DN : 2 * DN] = key_grad[:, :DN]
    out_ref[:, 2 * DN : 2 * DN + DV] = dv_sum[...].astype(BF16)
    out_ref[:, 2 * DN + DV + DR :] = key_grad[:, DN:]


def attention_backward(query, key, value, grad, segment, log_total, cosines, sines):
    count, width = query.shape
    return pl.pallas_call(
        functools.partial(attention_backward_kernel, width ** (-0.5)),
        out_shape=jax.ShapeDtypeStruct((count, 2 * width + value.shape[1]), BF16),
        scratch_shapes=[pltpu.VMEM(key.shape, F32), pltpu.VMEM(value.shape, F32)],
        compiler_params=pltpu.CompilerParams(vmem_limit_bytes=48 * 2**20),
        cost_estimate=pl.CostEstimate(flops=count * count * 832, bytes_accessed=6 * 2**20, transcendentals=count * count // 2),
        name="attention_backward",
    )(query, key, value, grad, segment[:, None], segment[None, :], log_total, cosines, sines)


def swap_halves(values):
    half = DR // 2
    pieces = [values[:, i * half : (i + 1) * half] for i in (1, 0, 3, 2)]
    return jnp.concatenate(pieces, axis=1)


def project_kernel(x_ref, gain_ref, w_ref, gain_kv_ref, expand_ref, cos_ref, sin_ref, normed_ref, q_ref, k_ref, v_ref, raw_ref, latent_ref):
    normed = rms_norm(x_ref[...].astype(F32), gain_ref[...]).astype(BF16)
    normed_ref[...] = normed
    both = dot(normed, w_ref[...])
    raw = both[:, :KVR]
    raw_ref[...] = raw
    latent = rms_norm(raw, gain_kv_ref[...]).astype(BF16)
    latent_ref[...] = latent
    expanded = dot(latent, expand_ref[...])
    rope = both[:, KVR + DN :]
    rope = rope * cos_ref[...] + swap_halves(rope) * sin_ref[...]
    q_ref[...] = jnp.concatenate([both[:, KVR : KVR + DN], rope[:, :DR]], axis=1).astype(BF16)
    k_ref[...] = jnp.concatenate([expanded[:, :DN], rope[:, DR:]], axis=1).astype(BF16)
    v_ref[...] = expanded[:, DN:].astype(BF16)


def project(rows, gain, weight, gain_kv, expand, cosines, sines):
    count = rows.shape[0]
    tile = 256

    def by_rows(columns):
        return pl.BlockSpec((tile, columns), lambda i: (i, 0))

    def whole(array):
        return pl.BlockSpec(array.shape, lambda i: (0, 0))

    outs = [(D, BF16), (DN + DR, BF16), (DN + DR, BF16), (DV, BF16), (KVR, F32), (KVR, BF16)]
    return pl.pallas_call(
        project_kernel,
        grid=(count // tile,),
        in_specs=[
            by_rows(D),
            whole(gain[None]),
            whole(weight),
            whole(gain_kv[None]),
            whole(expand),
            by_rows(2 * DR),
            by_rows(2 * DR),
        ],
        out_specs=tuple(by_rows(c) for c, _ in outs),
        out_shape=tuple(jax.ShapeDtypeStruct((count, c), t) for c, t in outs),
        compiler_params=pltpu.CompilerParams(vmem_limit_bytes=48 * 2**20),
        cost_estimate=pl.CostEstimate(flops=2 * count * D * 900, bytes_accessed=24 * 2**20, transcendentals=count),
        name="project",
    )(rows, gain[None], weight, gain_kv[None], expand, cosines, sines)


BLOCKS = 4


def silu_grads(gate, up, grad):
    sig = jax.nn.sigmoid(gate)
    return grad * up * sig * (1.0 + gate * (1.0 - sig)), grad * gate * sig


def pick_of(place_ref, b, capacity):
    tok = place_ref.shape[1]
    return lax.broadcasted_iota(jnp.int32, (capacity, tok), 0) == place_ref[b : b + 1, :]


def as_weights(match):
    return jnp.where(match, 1.0, 0.0).astype(BF16)


def spread_kernel(
    ffn_ref, up_ref, place_ref, gate_ref, in_ref, out_ref,
    x_ref, rg_ref, hidden_ref, grad_ref, gout_ref, gin_ref,
    sum_out, sum_in,
):
    step = pl.program_id(0)
    blocks, tok = place_ref.shape
    capacity = x_ref.shape[0] // blocks
    units = out_ref.shape[0]
    for b in range(blocks):
        match = pick_of(place_ref, b, capacity)
        pick = as_weights(match)
        gate = jnp.sum(jnp.where(match, gate_ref[b : b + 1, :], 0.0), axis=1, keepdims=True)
        tokens, rows = pl.ds(b * tok, tok), pl.ds(b * capacity, capacity)
        x_ref[rows, :] = dot(pick, ffn_ref[tokens, :]).astype(BF16)
        rg_ref[rows, :] = (gate * dot(pick, up_ref[tokens, :])).astype(BF16)
    both = dot(ffn_ref[...], in_ref[...])
    gate, up = both[:, :units], both[:, units:]
    hidden = (gate * jax.nn.sigmoid(gate) * up).astype(BF16)
    hidden_ref[...] = hidden
    grads = silu_grads(gate, up, dot_nt(up_ref[...], out_ref[...]))
    grad = jnp.concatenate(grads, axis=1).astype(BF16)
    grad_ref[...] = grad

    @pl.when(step == 0)
    def _():
        sum_out[...] = jnp.zeros_like(sum_out)
        sum_in[...] = jnp.zeros_like(sum_in)

    sum_out[...] += dot_tn(hidden, up_ref[...])
    sum_in[...] += dot_tn(grad, ffn_ref[...])

    @pl.when(step == pl.num_programs(0) - 1)
    def _():
        gout_ref[...] = sum_out[...].astype(BF16)
        gin_ref[...] = sum_in[...].astype(BF16)


def by_rows(size, columns):
    return pl.BlockSpec((size, columns), lambda i: (i, 0))


def whole(array):
    return pl.BlockSpec(array.shape, lambda i: (0, 0), pipeline_mode=pl.Buffered(1))


def by_step(tok):
    return pl.BlockSpec((None, BLOCKS, tok), lambda i: (i, 0, 0))


def in_steps(rows):
    return rows.reshape(-1, BLOCKS, rows.shape[1])


def spread(ffn, upstream, place, gates, shared_in, shared_out, capacity):
    count = ffn.shape[0]
    seq, tok = place.shape
    steps = seq // BLOCKS
    units = shared_out.shape[0]
    t, rows = BLOCKS * tok, BLOCKS * capacity
    outs = [(rows, D), (rows, D), (t, units), (t, 2 * units)]
    fixed = [(units, D), (2 * units, D)]
    flops = 4 * seq * capacity * tok * D + 2 * count * 6 * D * units
    return pl.pallas_call(
        spread_kernel,
        grid=(steps,),
        in_specs=[by_rows(t, D), by_rows(t, D), by_step(tok), by_step(tok), whole(shared_in), whole(shared_out)],
        out_specs=tuple(by_rows(*o) for o in outs) + tuple(pl.BlockSpec(o, lambda i: (0, 0)) for o in fixed),
        out_shape=tuple(jax.ShapeDtypeStruct((r * steps, c), BF16) for r, c in outs)
        + tuple(jax.ShapeDtypeStruct(o, BF16) for o in fixed),
        scratch_shapes=[pltpu.VMEM(o, F32) for o in fixed],
        compiler_params=pltpu.CompilerParams(vmem_limit_bytes=56 * 2**20),
        cost_estimate=pl.CostEstimate(flops=flops, bytes_accessed=40 * 2**20, transcendentals=2 * count * units),
        name="spread",
    )(ffn, upstream, in_steps(place), in_steps(gates), shared_in, shared_out)


def collect_forward_kernel(res_ref, up_ref, place_ref, gate_ref, hidden_ref, out_ref, mixed_ref, dots_ref):
    blocks, tok = place_ref.shape
    capacity = res_ref.shape[0] // blocks
    for b in range(blocks):
        pick = as_weights(pick_of(place_ref, b, capacity))
        tokens, rows = pl.ds(b * tok, tok), pl.ds(b * capacity, capacity)
        mine = dot_tn(pick, res_ref[rows, :])
        dots_ref[tokens, :] = jnp.sum(up_ref[tokens, :].astype(F32) * mine, axis=1, keepdims=True)
        shared = dot(hidden_ref[tokens, :], out_ref[...])
        mixed_ref[tokens, :] = (gate_ref[tokens, :] * mine + shared).astype(BF16)


def collect_forward(results, upstream, place, gates, hidden, shared_out, capacity):
    count = upstream.shape[0]
    seq, tok = place.shape
    steps = seq // BLOCKS
    t, rows = BLOCKS * tok, BLOCKS * capacity
    units = shared_out.shape[0]
    flops = 2 * seq * capacity * tok * D + 2 * count * D * units
    return pl.pallas_call(
        collect_forward_kernel,
        grid=(steps,),
        in_specs=[by_rows(rows, D), by_rows(t, D), by_step(tok), by_rows(t, 1), by_rows(t, units), whole(shared_out)],
        out_specs=(by_rows(t, D), by_rows(t, 1)),
        out_shape=(jax.ShapeDtypeStruct((count, D), BF16), jax.ShapeDtypeStruct((count, 1), F32)),
        compiler_params=pltpu.CompilerParams(vmem_limit_bytes=48 * 2**20),
        cost_estimate=pl.CostEstimate(flops=flops, bytes_accessed=24 * 2**20, transcendentals=0),
        name="collect_forward",
    )(results, upstream, in_steps(place), gates.reshape(-1, 1), hidden, shared_out)


def collect_backward_kernel(rows_ref, place_ref, grad_ref, in_ref, back_ref):
    blocks, tok = place_ref.shape
    capacity = rows_ref.shape[0] // blocks
    shared = dot_nt(grad_ref[...], in_ref[...])
    for b in range(blocks):
        pick = as_weights(pick_of(place_ref, b, capacity))
        tokens, rows = pl.ds(b * tok, tok), pl.ds(b * capacity, capacity)
        mine = dot_tn(pick, rows_ref[rows, :])
        back_ref[tokens, :] = (mine + shared[b * tok : (b + 1) * tok]).astype(BF16)


def collect_backward(row_grads, place, grads, shared_in, capacity):
    count = grads.shape[0]
    seq, tok = place.shape
    steps = seq // BLOCKS
    t, rows = BLOCKS * tok, BLOCKS * capacity
    flops = 2 * seq * capacity * tok * D + 2 * count * D * grads.shape[1]
    return pl.pallas_call(
        collect_backward_kernel,
        grid=(steps,),
        in_specs=[by_rows(rows, D), by_step(tok), by_rows(t, grads.shape[1]), whole(shared_in)],
        out_specs=by_rows(t, D),
        out_shape=jax.ShapeDtypeStruct((count, D), BF16),
        compiler_params=pltpu.CompilerParams(vmem_limit_bytes=48 * 2**20),
        cost_estimate=pl.CostEstimate(flops=flops, bytes_accessed=18 * 2**20, transcendentals=0),
        name="collect_backward",
    )(row_grads, in_steps(place), grads, shared_in)


def turn_kernel(in_ref, out_ref):
    block = in_ref[...].astype(F32)
    out_ref[...] = block.reshape(-1, block.shape[-1]).T


def turn_rows(rows, tile):
    count, columns = rows.shape
    return pl.pallas_call(
        turn_kernel,
        grid=(count // tile,),
        in_specs=[pl.BlockSpec((tile, columns), lambda i: (i, 0))],
        out_specs=pl.BlockSpec((columns, tile), lambda i: (0, i)),
        out_shape=jax.ShapeDtypeStruct((columns, count), F32),
        compiler_params=pltpu.CompilerParams(vmem_limit_bytes=48 * 2**20),
        cost_estimate=pl.CostEstimate(flops=0, bytes_accessed=6 * rows.size, transcendentals=0),
        name="turn_rows",
    )(rows)


def turn_units(parts):
    seq_count, groups, unit, columns = parts.shape
    if unit % 8 or (seq_count * unit) % 128:
        return parts.transpose(3, 1, 0, 2).reshape(columns, -1).astype(F32)
    wide = seq_count * unit
    tile = 256
    return pl.pallas_call(
        turn_kernel,
        grid=(groups, columns // tile),
        in_specs=[pl.BlockSpec((seq_count, None, unit, tile), lambda g, i: (0, g, 0, i))],
        out_specs=pl.BlockSpec((tile, wide), lambda g, i: (i, g)),
        out_shape=jax.ShapeDtypeStruct((columns, groups * wide), F32),
        compiler_params=pltpu.CompilerParams(vmem_limit_bytes=48 * 2**20),
        cost_estimate=pl.CostEstimate(flops=0, bytes_accessed=6 * parts.size, transcendentals=0),
        name="turn_units",
    )(parts)


LINE = 4
MESH = pl.DeviceIdType.MESH


def place():
    rank = lax.axis_index("seq")
    return rank, lax.div(rank, 4), lax.rem(lax.div(rank, 2), 2), lax.rem(rank, 2)


def rank_at(z, y, x, dz, dy, dx):
    across = y + dy * (1 - 2 * y)
    along = x + dx * (1 - 2 * x)
    return (z + dz) * 4 + across * 2 + along


OFFSETS = [(dz, dy, dx) for dz in (0, -1, 1, -2, 2, -3, 3) for dy in (0, 1) for dx in (0, 1)]


def hops(offset):
    return abs(offset[0]) + offset[1] + offset[2]


def onward(order, offset):
    rel = dict(zip("zyx", offset))
    moved = [i for i, dim in enumerate(order) if rel[dim]]
    last = moved[-1] if moved else -1
    steps = []
    if last >= 0 and order[last] == "z":
        steps.append((1 if rel["z"] < 0 else -1, 0, 0))
    for dim in order[last + 1 :]:
        steps += {"z": [(1, 0, 0), (-1, 0, 0)], "y": [(0, 1, 0)], "x": [(0, 0, 1)]}[dim]
    return [s for s in steps if any(0 <= z + offset[0] < LINE and 0 <= z + s[0] < LINE for z in range(LINE))]


def inside(z, dz):
    return (z + dz >= 0) & (z + dz < LINE)


def guarded(z, steps, body):
    steps = [dz for dz in steps if dz]
    if not steps:
        body()
        return
    good = inside(z, steps[0])
    for dz in steps[1:]:
        good = good & inside(z, dz)
    pl.when(good)(body)


def greet_all():
    rank = lax.axis_index("seq")
    count = lax.axis_size("seq")
    barrier = pltpu.get_barrier_semaphore()
    for k in range(1, count):
        peer = lax.rem(rank + k, count)
        pl.semaphore_signal(barrier, inc=1, device_id={"seq": peer}, device_id_type=MESH)
    pl.semaphore_wait(barrier, count - 1)


def gather_kernel(streams, n_main, n_small, *refs):
    n = n_main + n_small
    ins, outs = refs[:n], refs[n : 2 * n]
    send_sems, recv_sems, small_send, small_recv, local_sems = refs[2 * n :]
    rank, z, y, x = place()
    count = lax.axis_size("seq")
    greet_all()
    locals_ = [pltpu.make_async_copy(ins[i], outs[i].at[rank], local_sems.at[i]) for i in range(n)]
    slots = {}

    def copy(stream, offset, step):
        index, first, rows, order = streams[stream]
        part = pl.ds(first, rows)
        source = rank_at(z, y, x, *offset)
        slot = slots.setdefault((stream, offset, step), len(slots))
        block = outs[index].at[source, part]
        own = offset == (0, 0, 0)
        return pltpu.make_async_remote_copy(
            src_ref=ins[index].at[part] if own else block,
            dst_ref=block,
            send_sem=send_sems.at[slot],
            recv_sem=recv_sems.at[stream * count + source],
            device_id={"seq": rank_at(z, y, x, *step)},
            device_id_type=MESH,
        )

    def small_copy(i, k):
        peer = lax.rem(rank + k, count)
        return pltpu.make_async_remote_copy(
            src_ref=ins[n_main + i],
            dst_ref=outs[n_main + i].at[rank],
            send_sem=small_send.at[i * count + k],
            recv_sem=small_recv.at[i * count + rank],
            device_id={"seq": peer},
            device_id_type=MESH,
        )

    def arrived(stream, offset):
        index, first, rows, order = streams[stream]
        source = rank_at(z, y, x, *offset)
        block = outs[index].at[source, pl.ds(first, rows)]
        pltpu.make_async_remote_copy(
            src_ref=block,
            dst_ref=block,
            send_sem=send_sems.at[0],
            recv_sem=recv_sems.at[stream * count + source],
            device_id={"seq": rank},
            device_id_type=MESH,
        ).wait_recv()

    todo = sorted(
        ((stream, offset) for stream in range(len(streams)) for offset in OFFSETS),
        key=lambda it: (hops(it[1]), it[0]),
    )
    for stream, offset in todo:
        def forward(stream=stream, offset=offset):
            if hops(offset):
                arrived(stream, offset)
            for step in onward(streams[stream][3], offset):
                guarded(z, [step[0]], lambda: copy(stream, offset, step).start())
        guarded(z, [offset[0]], forward)
        if stream == len(streams) - 1 and offset == (0, 0, 0):
            for c in locals_:
                c.start()
            for i in range(n_small):
                for k in range(1, count):
                    small_copy(i, k).start()
    for stream, offset in todo:
        for step in onward(streams[stream][3], offset):
            guarded(z, [offset[0], step[0]], lambda: copy(stream, offset, step).wait_send())
    for i in range(n_small):
        for k in range(1, count):
            small_copy(i, k).wait_send()
        for k in range(1, count):
            source = lax.rem(rank + k, count)
            block = outs[n_main + i].at[source]
            pltpu.make_async_remote_copy(
                src_ref=block, dst_ref=block, send_sem=small_send.at[0],
                recv_sem=small_recv.at[i * count + source], device_id={"seq": rank}, device_id_type=MESH,
            ).wait_recv()
    for c in locals_:
        c.wait()


def n_sends(streams):
    return sum(len(onward(s[3], o)) for s in streams for o in OFFSETS)


def gather_all(main, parts, small, collective_id, count=16):
    streams = []
    for i, pieces in enumerate(parts):
        first = 0
        for rows, order in pieces:
            streams.append((i, first, rows, order))
            first += rows
        assert first == main[i].shape[0]
    arrays = list(main) + list(small)
    any_spec = pl.BlockSpec(memory_space=pl.ANY)
    return pl.pallas_call(
        functools.partial(gather_kernel, streams, len(main), len(small)),
        out_shape=tuple(jax.ShapeDtypeStruct((count,) + a.shape, a.dtype) for a in arrays),
        in_specs=[any_spec] * len(arrays),
        out_specs=tuple([any_spec] * len(arrays)),
        scratch_shapes=[
            pltpu.SemaphoreType.DMA((n_sends(streams),)),
            pltpu.SemaphoreType.DMA((len(streams) * count,)),
            pltpu.SemaphoreType.DMA((max(1, len(small)) * count,)),
            pltpu.SemaphoreType.DMA((max(1, len(small)) * count,)),
            pltpu.SemaphoreType.DMA((len(arrays),)),
        ],
        compiler_params=pltpu.CompilerParams(collective_id=collective_id, has_side_effects=True),
        name="gather_all",
    )(*arrays)


def toward(order, offset):
    rel = dict(zip("zyx", offset))
    dim = [d for d in order if rel[d]][-1]
    return {"z": (1 if rel["z"] > 0 else -1, 0, 0), "y": (0, 1, 0), "x": (0, 0, 1)}[dim]


def seen_from(offset, step):
    return (offset[0] - step[0], offset[1] ^ step[1], offset[2] ^ step[2])


def back(step):
    return (-step[0], step[1], step[2])


ADD_ROWS = 16


def slot_table(order):
    table, used = {}, 0
    for dy in (0, 1):
        for dx in (0, 1):
            for kind in ("x", "y", "up", "down"):
                step = {"x": (0, 0, 1), "y": (0, 1, 0), "up": (1, 0, 0), "down": (-1, 0, 0)}[kind]
                met = [o[0] for o in OFFSETS if o[1:] == (dy, dx) and step in onward(order, o)]
                if not met:
                    continue
                if kind == "down":
                    table[dy, dx, "down"] = (used, False)
                    used += 1
                    continue
                spread = any(met)
                table[dy, dx, kind] = (used, spread)
                used += LINE if spread else 1
    return table, used


def slot_at(table, z, offset, step):
    dz, dy, dx = offset
    kind = "x" if step[2] else "y" if step[1] else "down" if step[0] < 0 and dz == 0 else "up"
    first, spread = table[dy, dx, kind]
    return first + (z + dz) if spread else first


def scatter_kernel(streams, n_main, n_small, *refs):
    n = n_main + n_small
    ins, outs = refs[:n], refs[n : 2 * n]
    scratch = refs[2 * n :]
    bufs = scratch[: len(streams)]
    send_sems, recv_sems, small_send, small_recv, local_sems = scratch[len(streams) :]
    rank, z, y, x = place()
    count = lax.axis_size("seq")
    tables, bases, base = [], [], 0
    for stream in streams:
        table, used = slot_table(stream[3])
        tables.append(table)
        bases.append(base)
        base += used
    greet_all()

    def small_copy(i, k):
        peer = lax.rem(rank + k, count)
        return pltpu.make_async_remote_copy(
            src_ref=ins[n_main + i],
            dst_ref=outs[n_main + i].at[rank],
            send_sem=small_send.at[i * count + k],
            recv_sem=small_recv.at[i * count + rank],
            device_id={"seq": peer},
            device_id_type=MESH,
        )

    todo = sorted(
        ((s, offset) for s in range(len(streams)) for offset in OFFSETS),
        key=lambda it: (-hops(it[1]), it[0]),
    )
    send_slot = {key: i for i, key in enumerate(k for k in todo if hops(k[1]))}

    def send_copy(s, offset, source):
        step = toward(streams[s][3], offset)
        k = slot_at(tables[s], z + step[0], seen_from(offset, step), back(step))
        return pltpu.make_async_remote_copy(
            src_ref=source,
            dst_ref=bufs[s].at[k],
            send_sem=send_sems.at[send_slot[s, offset]],
            recv_sem=recv_sems.at[bases[s] + k],
            device_id={"seq": rank_at(z, y, x, *step)},
            device_id_type=MESH,
        )

    def wait_child(s, k):
        pltpu.make_async_remote_copy(
            src_ref=bufs[s].at[k],
            dst_ref=bufs[s].at[k],
            send_sem=send_sems.at[0],
            recv_sem=recv_sems.at[bases[s] + k],
            device_id={"seq": rank},
            device_id_type=MESH,
        ).wait_recv()

    for s, offset in todo:
        index, first, rows, order = streams[s]
        children = onward(order, offset)
        dest = rank_at(z, y, x, *offset)
        always = [c for c in children if not c[0]]
        sometimes = [c for c in children if c[0]]

        def run(present, s=s, offset=offset, index=index, first=first, rows=rows, dest=dest):
            own = ins[index].at[dest, pl.ds(first, rows)]
            if not present:
                send_copy(s, offset, own).start()
                return
            slots = [slot_at(tables[s], z, offset, step) for step in present]
            for k in slots:
                wait_child(s, k)
            final = not hops(offset)
            target = outs[index].at[pl.ds(first, rows)] if final else bufs[s].at[slots[0]]

            def add(i, carry):
                part = pl.ds(pl.multiple_of(i * ADD_ROWS, ADD_ROWS), ADD_ROWS)
                total = own[part, :].astype(F32)
                for k in slots:
                    total = total + bufs[s][k, part, :].astype(F32)
                target[part, :] = total.astype(target.dtype)
                return carry

            lax.fori_loop(0, rows // ADD_ROWS, add, 0)
            if not final:
                send_copy(s, offset, target).start()

        def cases(run=run, always=always, sometimes=sometimes):
            if not sometimes:
                run(always)
                return
            for mask in range(2 ** len(sometimes)):
                present = [c for i, c in enumerate(sometimes) if mask >> i & 1]
                good = None
                for i, c in enumerate(sometimes):
                    here = inside(z, c[0]) if mask >> i & 1 else jnp.logical_not(inside(z, c[0]))
                    good = here if good is None else good & here
                pl.when(good)(functools.partial(run, present + always))

        guarded(z, [offset[0]], cases)
        if (s, offset) == todo[0]:
            for i in range(n_small):
                for k in range(1, count):
                    small_copy(i, k).start()
                pltpu.make_async_copy(ins[n_main + i], outs[n_main + i].at[rank], local_sems.at[i]).start()
    for s, offset in todo:
        if hops(offset):
            index, first, rows, order = streams[s]
            own = ins[index].at[rank_at(z, y, x, *offset), pl.ds(first, rows)]
            guarded(z, [offset[0]], lambda: send_copy(s, offset, own).wait_send())
    for i in range(n_small):
        for k in range(1, count):
            small_copy(i, k).wait_send()
        for k in range(1, count):
            source = lax.rem(rank + k, count)
            block = outs[n_main + i].at[source]
            pltpu.make_async_remote_copy(
                src_ref=block,
                dst_ref=block,
                send_sem=small_send.at[0],
                recv_sem=small_recv.at[i * count + source],
                device_id={"seq": rank},
                device_id_type=MESH,
            ).wait_recv()
        pltpu.make_async_copy(ins[n_main + i], outs[n_main + i].at[rank], local_sems.at[i]).wait()


def scatter_sum(main, parts, small, collective_id, count=16):
    streams = []
    for i, pieces in enumerate(parts):
        first = 0
        for rows, order in pieces:
            streams.append((i, first, rows, order))
            first += rows
        assert first == main[i].shape[1]
    arrays = list(main) + list(small)
    any_spec = pl.BlockSpec(memory_space=pl.ANY)
    vmem = pl.BlockSpec(memory_space=pltpu.VMEM)
    places = [slot_table(stream[3])[1] for stream in streams]
    buffers = [
        pltpu.VMEM((used, rows, main[index].shape[2]), main[index].dtype)
        for used, (index, first, rows, order) in zip(places, streams)
    ]
    return pl.pallas_call(
        functools.partial(scatter_kernel, streams, len(main), len(small)),
        out_shape=tuple(
            [jax.ShapeDtypeStruct(a.shape[1:], F32) for a in main]
            + [jax.ShapeDtypeStruct((count,) + a.shape, a.dtype) for a in small]
        ),
        in_specs=[vmem] * len(main) + [any_spec] * len(small),
        out_specs=tuple([vmem] * len(main) + [any_spec] * len(small)),
        scratch_shapes=buffers
        + [
            pltpu.SemaphoreType.DMA((len(streams) * len(OFFSETS),)),
            pltpu.SemaphoreType.DMA((sum(places),)),
            pltpu.SemaphoreType.DMA((max(1, len(small)) * count,)),
            pltpu.SemaphoreType.DMA((max(1, len(small)) * count,)),
            pltpu.SemaphoreType.DMA((max(1, len(small)),)),
        ],
        compiler_params=pltpu.CompilerParams(
            collective_id=collective_id, has_side_effects=True, vmem_limit_bytes=60 * 2**20
        ),
        name="scatter_sum",
    )(*arrays)


def gather_seq(rows):
    return lax.all_gather(rows, "seq", axis=0, tiled=True)


def scatter_seq(partial):
    return lax.psum_scatter(partial, "seq", scatter_dimension=0, tiled=True)


def gather_fsdp(rows, axis=0):
    return lax.all_gather(rows, "fsdp", axis=axis, tiled=True)


def scatter_fsdp(partial, axis=0):
    count, me = lax.axis_size("fsdp"), lax.axis_index("fsdp")
    size = partial.shape[axis] // count
    total = lax.dynamic_slice_in_dim(partial, me * size, size, axis).astype(F32)
    for k in range(1, count):
        piece = lax.dynamic_slice_in_dim(partial, lax.rem(me + k, count) * size, size, axis)
        total = total + shift_fsdp(piece, k).astype(F32)
    return total


def shift_fsdp(rows, k):
    count = lax.axis_size("fsdp")
    return lax.ppermute(rows, "fsdp", [(i, (i + k) % count) for i in range(count)])


ROW_PARTS = [(48, "zxy"), (48, "zyx"), (16, "xyz"), (16, "yxz")]


def split_rows(rows):
    tile = 16
    tiles = rows // tile
    short = tiles // 8
    long = (tiles - 2 * short) // 2
    sizes = [tiles - 2 * short - long, long, short, short]
    orders = ["zxy", "zyx", "xyz", "yxz"]
    return [(n * tile, order) for n, order in zip(sizes, orders) if n]


def on_device(
    tokens,
    cotangent,
    lengths,
    routes,
    g_attn,
    w_q,
    w_kva,
    g_kv,
    w_kvb,
    w_o,
    g_ffn,
    w_router,
    w_shared_in,
    w_shared_out,
    w_expert_in,
    w_expert_out,
):
    seq_count = lax.axis_size("seq")
    fsdp_count = lax.axis_size("fsdp")
    rank = lax.axis_index("seq")
    tok_count = tokens.shape[0]
    group_size = tok_count * seq_count
    query_width = DN + DR
    kv_width = DN + DV
    experts = seq_count
    capacity = min(tok_count, 2 * tok_count * TOP // experts)
    buffer_rows = seq_count * capacity
    unit = SH // (seq_count * fsdp_count)
    units = unit * fsdp_count
    row_part = w_q.shape[0]

    def own(rows, axis=0):
        return lax.dynamic_slice_in_dim(rows, rank * tok_count, tok_count, axis)

    expert_ids = jnp.arange(experts, dtype=jnp.int32)
    route_mask = jnp.any(routes[None] == expert_ids[:, None, None], axis=2).astype(BF16)
    token_all, mask_all = gather_all([tokens], [ROW_PARTS], [route_mask], 1)
    token_all = token_all.reshape(group_size, D)

    small = gather_fsdp(jnp.concatenate([g_attn, g_kv, g_ffn, w_router.reshape(-1)])[None])
    cuts = [0, g_attn.size, g_kv.size, g_ffn.size, w_router.size]
    ends = [sum(cuts[: i + 1]) for i in range(len(cuts))]
    gain_attn = small[:, ends[0] : ends[1]].reshape(-1).astype(F32)
    gain_latent = small[:, ends[1] : ends[2]].reshape(-1).astype(F32)
    gain_ffn = small[:, ends[2] : ends[3]].reshape(-1).astype(F32)
    router_weight = small[:, ends[3] : ends[4]].reshape(D, experts)
    head_query_part = lax.dynamic_slice_in_dim(w_q, rank * query_width, query_width, 1)
    lanes = -(-units // 128) * 128
    unit_slices = [
        lax.dynamic_slice_in_dim(w_shared_in, i * (SH // fsdp_count) + rank * unit, unit, 1)
        for i in range(2 * fsdp_count)
    ]
    filler = jnp.zeros((row_part, lanes - units), BF16)
    shared_in_part = jnp.concatenate(
        unit_slices[:fsdp_count] + [filler] + unit_slices[fsdp_count:] + [filler], axis=1
    )
    head_expand = gather_fsdp(lax.dynamic_slice_in_dim(w_kvb, rank * kv_width, kv_width, 1))
    head_weights = gather_fsdp(
        jnp.concatenate([w_kva[:, :KVR], head_query_part, w_kva[:, KVR:]], axis=1)
    )
    shared_in = gather_fsdp(shared_in_part)
    shared_out = gather_fsdp(lax.dynamic_slice_in_dim(w_shared_out, rank * unit, unit, 0))
    shared_out = jnp.pad(shared_out, ((0, lanes - units), (0, 0)))
    output_weight = gather_fsdp(w_o)
    expert_in = gather_fsdp(w_expert_in[0])
    expert_out = gather_fsdp(w_expert_out[0])
    query_weight = gather_fsdp(w_q)
    expand_weight = gather_fsdp(w_kvb)

    slot_ids = jnp.arange(group_size, dtype=jnp.int32)
    segment, position, valid_all = layout(lengths[0], slot_ids)
    angles = own(position)[:, None].astype(F32) * frequencies(DR)[None, :]
    wide_angles = position[:, None].astype(F32) * jnp.tile(frequencies(DR), 4)[None, :]
    cosines = jnp.cos(wide_angles)
    signs = jnp.where(jnp.arange(2 * DR) % DR < DR // 2, -1.0, 1.0).astype(F32)
    sines = jnp.sin(wide_angles) * signs[None, :]

    upstream_own = jnp.where(own(valid_all)[:, None], cotangent, 0).astype(BF16)
    upstream_all = gather_seq(upstream_own)

    normed_all, query, key, value, latent_full, latent_all = project(
        token_all, gain_attn, head_weights, gain_latent, head_expand, cosines, sines
    )
    context, log_total, head_largest = attention_forward(query, key, value, segment, valid_all)
    context_low = lax.all_to_all(context, "seq", split_axis=0, concat_axis=1, tiled=True)
    inputs = tokens.astype(F32)
    middle = inputs + dot(context_low, output_weight)
    ffn_low = rms_norm(middle, gain_ffn).astype(BF16)
    ffn_all, largest_all = gather_all([ffn_low], [ROW_PARTS], [head_largest], 2)
    ffn_all = ffn_all.reshape(group_size, D)
    head_max = largest_all[:, 0, :]
    for k in range(1, fsdp_count):
        head_max = jnp.maximum(head_max, shift_fsdp(largest_all[:, 0, :], k))
    global_max = head_max[:, 0]

    router_probs = jax.nn.softmax(dot(ffn_all, router_weight), axis=-1)
    chosen = lax.dynamic_slice_in_dim(mask_all, rank, 1, 1).reshape(seq_count, tok_count) > 0
    gates = lax.dynamic_slice_in_dim(router_probs, rank, 1, 1).reshape(seq_count, tok_count)
    place = jnp.cumsum(chosen.astype(jnp.int32), axis=1) - 1
    place = jnp.where(chosen, place, capacity)

    arrived, result_grad, shared_hidden, shared_grad, grad_shared_out, grad_shared_in = spread(
        ffn_all, upstream_all, place, gates, shared_in, shared_out, capacity
    )
    part_shared_out = scatter_fsdp(grad_shared_out[:units]).astype(BF16)
    part_shared_in = jnp.concatenate([grad_shared_in[:units], grad_shared_in[lanes : lanes + units]], axis=0)
    part_shared_in = scatter_fsdp(part_shared_in, 1).astype(BF16)
    sum_shared_out = gather_seq(part_shared_out).astype(F32)
    sum_shared_in = turn_units(
        gather_seq(part_shared_in).reshape(seq_count, 2 * fsdp_count, unit, row_part)
    )

    gate_up = dot(arrived, expert_in).astype(BF16)
    gate_part, up_part = gate_up[:, :FF].astype(F32), gate_up[:, FF:].astype(F32)
    hidden = (jax.nn.silu(gate_part) * up_part).astype(BF16)
    result = dot(hidden, expert_out).astype(BF16)
    d_hidden = dot_nt(result_grad, expert_out)
    d_gate_up = jnp.concatenate(silu_grads(gate_part, up_part, d_hidden), axis=1).astype(BF16)
    row_grad = dot_nt(d_gate_up, expert_in).astype(BF16)
    mixed_part, gate_grad = collect_forward(
        result, upstream_all, place, gates, shared_hidden, shared_out, capacity
    )
    ffn_part = collect_backward(row_grad, place, shared_grad, shared_in, capacity)
    mixed_sum, ffn_sum, prob_grads = scatter_sum(
        [part.reshape(seq_count, tok_count, D) for part in (mixed_part, ffn_part)],
        [ROW_PARTS, ROW_PARTS],
        [gate_grad.reshape(seq_count, tok_count)],
        3,
    )
    mixed = (middle + mixed_sum).astype(BF16)
    prob_grads = prob_grads.reshape(experts, group_size).T

    logit_grads = (
        router_probs * (prob_grads - jnp.sum(router_probs * prob_grads, axis=-1, keepdims=True))
    ).astype(BF16)
    grad_router = dot_tn(ffn_all, logit_grads)
    sum_router = scatter_fsdp(grad_router.astype(BF16))
    ffn_grad = ffn_sum + dot_nt(own(logit_grads), router_weight)

    ffn_pull = jax.vjp(rms_norm, middle, gain_ffn)[1]
    middle_norm_grad, grad_gain_ffn = ffn_pull(ffn_grad)
    middle_grad = upstream_own.astype(F32) + middle_norm_grad
    middle_low = middle_grad.astype(BF16)
    context_grad = dot_nt(middle_low, output_weight).astype(BF16)
    head_grad = lax.all_to_all(context_grad, "seq", split_axis=1, concat_axis=0, tiled=True)
    grad_output = scatter_fsdp(dot_tn(context_low, middle_low).astype(BF16)).astype(BF16)
    output_rows = row_part // seq_count
    (part_output,) = scatter_sum(
        [grad_output.reshape(seq_count, output_rows, D)], [split_rows(output_rows)], [], 5
    )

    head_back = attention_backward(query, key, value, head_grad, segment, log_total, cosines, sines)
    head_back, arrived, result_grad, hidden, d_gate_up = lax.optimization_barrier(
        (head_back, arrived, result_grad, hidden, d_gate_up)
    )
    back = lax.all_to_all(
        head_back.reshape(seq_count, tok_count, -1), "seq", split_axis=0, concat_axis=0, tiled=True
    )
    grad_expert_out = dot_tn(hidden, result_grad).astype(BF16)
    grad_expert_in = dot_tn(arrived, d_gate_up).astype(BF16)
    rope_at = 2 * DN + DV
    head_pre_grad = jnp.concatenate([head_back[:, :DN], head_back[:, rope_at : rope_at + DR]], axis=1)
    grad_query = dot_tn(head_pre_grad, normed_all).astype(BF16)
    grad_expand = dot_tn(head_back[:, DN:rope_at], latent_all).astype(BF16)
    back, grad_expert_out, grad_expert_in, grad_query, grad_expand = lax.optimization_barrier(
        (back, grad_expert_out, grad_expert_in, grad_query, grad_expand)
    )
    sum_expert_in = scatter_fsdp(grad_expert_in)[None]
    sum_expert_out = scatter_fsdp(grad_expert_out)[None]
    part_query = scatter_fsdp(grad_query, 1).astype(BF16)
    part_expand = scatter_fsdp(grad_expand, 1).astype(BF16)

    back = back.transpose(1, 0, 2)
    pre_grad = jnp.concatenate([back[..., :DN], back[..., rope_at : rope_at + DR]], axis=-1)
    pre_grad = pre_grad.reshape(tok_count, H * query_width)
    expand_grad = back[..., DN:rope_at].reshape(tok_count, H * kv_width)
    latent_grad = dot_nt(expand_grad, expand_weight)
    rope_grad = rotate(jnp.sum(back[..., rope_at + DR :].astype(F32), axis=1), -angles)
    latent_pull = jax.vjp(rms_norm, own(latent_full), gain_latent)[1]
    compressed_grad, grad_gain_latent = latent_pull(latent_grad)
    full_grad = jnp.concatenate([compressed_grad, rope_grad], axis=1).astype(BF16)
    full_all = gather_seq(full_grad)
    sum_latent = scatter_fsdp(dot_tn(normed_all, full_all).astype(BF16))
    spread_grad = jnp.pad(full_grad[:, :KVR], ((0, 0), (0, query_width + DR)))
    spread_grad = spread_grad + jnp.pad(full_grad[:, KVR:], ((0, 0), (KVR + query_width, 0)))
    normed_grad = dot_nt(pre_grad, query_weight) + dot_nt(spread_grad, head_weights)
    input_pull = jax.vjp(rms_norm, inputs, gain_attn)[1]
    input_norm_grad, grad_gain_attn = input_pull(normed_grad)
    grad_inputs = middle_grad + input_norm_grad

    gain_grads = jnp.concatenate([grad_gain_attn, grad_gain_latent, grad_gain_ffn]).reshape(-1, 128)
    gain_grads = jnp.pad(gain_grads, ((0, -gain_grads.shape[0] % 8), (0, 0)))
    weight_parts = [part_query, part_output.astype(BF16), part_expand]
    *sums, gain_all = gather_all(weight_parts, [split_rows(p.shape[0]) for p in weight_parts], [gain_grads], 4)
    sum_query = turn_rows(sums[0].reshape(-1, row_part), 384)
    sum_output = sums[1].reshape(w_o.shape).astype(F32)
    sum_expand = turn_rows(sums[2].reshape(-1, w_kvb.shape[0]), 512)
    gain_seq = jnp.sum(gain_all, axis=0)
    gain_sum = gain_seq
    for k in range(1, fsdp_count):
        gain_sum = gain_sum + shift_fsdp(gain_seq, k)
    gain_sum = gain_sum.reshape(-1)
    fsdp_rank = lax.axis_index("fsdp")

    def own_part(first, like):
        return lax.dynamic_slice_in_dim(gain_sum, first + fsdp_rank * like.size, like.size, 0)

    sum_gain_attn = own_part(0, g_attn)
    sum_gain_latent = own_part(D, g_kv)
    sum_gain_ffn = own_part(D + KVR, g_ffn)

    clip_gamma = CLIP_LIMIT / jnp.maximum(global_max, CLIP_LIMIT)
    clip_root = jnp.sqrt(clip_gamma)
    query_factor = jnp.concatenate(
        [
            jnp.broadcast_to(clip_root[:, None], (H, DN)),
            jnp.broadcast_to(clip_gamma[:, None], (H, DR)),
        ],
        axis=1,
    ).reshape(1, -1)
    clipped_query = (w_q.astype(F32) * query_factor).astype(BF16)
    return (
        mixed,
        grad_inputs,
        sum_gain_attn,
        sum_query,
        sum_latent,
        sum_gain_latent,
        sum_expand,
        sum_output,
        sum_gain_ffn,
        sum_router,
        sum_shared_in,
        sum_shared_out,
        sum_expert_in,
        sum_expert_out,
        clipped_query,
    )


def solution(mesh):
    in_specs = (
        P(("fsdp", "seq"), None),
        P(("fsdp", "seq"), None),
        P("fsdp", None),
        P(("fsdp", "seq"), None),
        P("fsdp"),
        P("fsdp", None),
        P("fsdp", None),
        P("fsdp"),
        P("fsdp", None),
        P("fsdp", None),
        P("fsdp"),
        P("fsdp", None),
        P("fsdp", None),
        P("fsdp", None),
        P("seq", "fsdp", None),
        P("seq", "fsdp", None),
    )
    out_specs = (
        P(("fsdp", "seq"), None),
        P(("fsdp", "seq"), None),
        P("fsdp"),
        P("fsdp", None),
        P("fsdp", None),
        P("fsdp"),
        P("fsdp", None),
        P("fsdp", None),
        P("fsdp"),
        P("fsdp", None),
        P("fsdp", None),
        P("fsdp", None),
        P("seq", "fsdp", None),
        P("seq", "fsdp", None),
        P("fsdp", None),
    )
    return jax.shard_map(
        on_device, mesh=mesh, in_specs=in_specs, out_specs=out_specs, check_vma=False
    )
```

```python
import functools

import jax
import jax.numpy as jnp
from jax import lax
from jax.experimental import pallas as pl
from jax.experimental.pallas import tpu as pltpu
from jax.sharding import PartitionSpec as P

D = 2048
H = 16
DN = 128
DR = 64
DV = 128
KVR = 512
FF = 1408
TOP = 6
SH = 2816

EPSILON = 1e-06
CLIP_LIMIT = 8.0
ROPE_BASE = 10000.0
MASK_VALUE = -1e30
BF16 = jnp.bfloat16
F32 = jnp.float32


def rms_norm(values, gain_vector):
    return (
        values
        * lax.rsqrt(jnp.mean(values * values, axis=-1, keepdims=True) + EPSILON)
        * gain_vector
    )


def rotate(values, angles):
    half_width = values.shape[-1] // 2
    first_half = values[..., :half_width]
    second_half = values[..., half_width:]
    cosine = jnp.cos(angles)
    sine_part = jnp.sin(angles)
    return jnp.concatenate(
        [
            first_half * cosine - second_half * sine_part,
            second_half * cosine + first_half * sine_part,
        ],
        axis=-1,
    )


def frequencies(count):
    exponent = jnp.arange(count // 2, dtype=jnp.float32) * 2.0 / count
    return ROPE_BASE ** (-exponent)


def layout(lengths_row, slot_ids):
    seq_ends = jnp.cumsum(lengths_row)
    seq_starts = seq_ends - lengths_row
    inside = (slot_ids[:, None] >= seq_starts[None, :]) & (slot_ids[:, None] < seq_ends[None, :])
    is_valid = jnp.any(inside, axis=1)
    numbers = jnp.arange(lengths_row.shape[0], dtype=jnp.int32)
    seq_number = jnp.sum(jnp.where(inside, numbers[None, :], 0), axis=1)
    first_slot = jnp.sum(jnp.where(inside, seq_starts[None, :], 0), axis=1)
    segment = jnp.where(is_valid, seq_number, lengths_row.shape[0] + slot_ids)
    position = jnp.where(is_valid, slot_ids - first_slot, 0)
    return (segment, position, is_valid)


def dot(left, right):
    return jnp.dot(left, right, preferred_element_type=F32)


def dot_tn(left, right):
    return lax.dot_general(left, right, (((0,), (0,)), ((), ())), preferred_element_type=F32)


def dot_nt(left, right):
    return lax.dot_general(left, right, (((1,), (1,)), ((), ())), preferred_element_type=F32)


ROWS = 256


def masked_scores(query, key, seg_col, seg_row, first, scale):
    scores = dot_nt(query, key) * scale
    shape = scores.shape
    row_slot = first + lax.broadcasted_iota(jnp.int32, shape, 0)
    key_slot = lax.broadcasted_iota(jnp.int32, shape, 1)
    allowed = (seg_col == seg_row) & (key_slot <= row_slot)
    return jnp.where(allowed, scores, MASK_VALUE)


def attention_forward_kernel(scale, q_ref, k_ref, v_ref, segc_ref, segr_ref, valid_ref, ctx_ref, lse_ref, max_ref):
    count = q_ref.shape[0]
    best = jnp.full((1, 1), MASK_VALUE, F32)
    for first in range(0, count, ROWS):
        rows, keys = pl.ds(first, ROWS), pl.ds(0, first + ROWS)
        masked = masked_scores(q_ref[rows, :], k_ref[keys, :], segc_ref[rows, :], segr_ref[:, keys], first, scale)
        row_max = jnp.max(masked, axis=1, keepdims=True)
        exponent = jnp.exp(masked - row_max)
        row_sum = jnp.sum(exponent, axis=1, keepdims=True)
        probs = (exponent * (1.0 / row_sum)).astype(BF16)
        ctx_ref[rows, :] = dot(probs, v_ref[keys, :]).astype(BF16)
        lse_ref[rows, :] = row_max + jnp.log(row_sum)
        counted = jnp.where(valid_ref[rows, :] > 0, row_max, MASK_VALUE)
        best = jnp.maximum(best, jnp.max(counted, axis=0, keepdims=True))
    max_ref[...] = jnp.broadcast_to(best, max_ref.shape)


def attention_forward(query, key, value, segment, valid):
    count, width = query.shape
    return pl.pallas_call(
        functools.partial(attention_forward_kernel, width ** (-0.5)),
        out_shape=(
            jax.ShapeDtypeStruct((count, value.shape[1]), BF16),
            jax.ShapeDtypeStruct((count, 1), F32),
            jax.ShapeDtypeStruct((8, 128), F32),
        ),
        compiler_params=pltpu.CompilerParams(vmem_limit_bytes=48 * 2**20),
        cost_estimate=pl.CostEstimate(flops=count * count * 320, bytes_accessed=4 * 2**20, transcendentals=count * count // 2),
        name="attention_forward",
    )(query, key, value, segment[:, None], segment[None, :], valid[:, None].astype(jnp.int32))


def attention_backward_kernel(
    scale, q_ref, k_ref, v_ref, g_ref, segc_ref, segr_ref, lse_ref, cos_ref, sin_ref, out_ref, dk_sum, dv_sum
):
    half = DR // 2
    count = q_ref.shape[0]
    dk_sum[...] = jnp.zeros_like(dk_sum)
    dv_sum[...] = jnp.zeros_like(dv_sum)
    for first in range(0, count, ROWS):
        rows, keys = pl.ds(first, ROWS), pl.ds(0, first + ROWS)
        query, grad = q_ref[rows, :], g_ref[rows, :]
        masked = masked_scores(query, k_ref[keys, :], segc_ref[rows, :], segr_ref[:, keys], first, scale)
        probs = jnp.exp(masked - lse_ref[rows, :])
        prob_grad = dot_nt(grad, v_ref[keys, :])
        mean = jnp.sum(probs * prob_grad, axis=1, keepdims=True)
        score_grad = (probs * (prob_grad - mean)).astype(BF16)
        query_grad = (dot(score_grad, k_ref[keys, :]) * scale).astype(BF16)
        out_ref[rows, :DN] = query_grad[:, :DN]
        rope = query_grad[:, DN:].astype(F32)
        swapped = jnp.concatenate([rope[:, half:], rope[:, :half]], axis=1)
        rope = rope * cos_ref[rows, :DR] - swapped * sin_ref[rows, :DR]
        out_ref[rows, 2 * DN + DV : 2 * DN + DV + DR] = rope.astype(BF16)
        dk_sum[keys, :] += dot_tn(score_grad, query)
        dv_sum[keys, :] += dot_tn(probs.astype(BF16), grad)
    key_grad = (dk_sum[...] * scale).astype(BF16)
    out_ref[:, DN : 2 * DN] = key_grad[:, :DN]
    out_ref[:, 2 * DN : 2 * DN + DV] = dv_sum[...].astype(BF16)
    out_ref[:, 2 * DN + DV + DR :] = key_grad[:, DN:]


def attention_backward(query, key, value, grad, segment, log_total, cosines, sines):
    count, width = query.shape
    return pl.pallas_call(
        functools.partial(attention_backward_kernel, width ** (-0.5)),
        out_shape=jax.ShapeDtypeStruct((count, 2 * width + value.shape[1]), BF16),
        scratch_shapes=[pltpu.VMEM(key.shape, F32), pltpu.VMEM(value.shape, F32)],
        compiler_params=pltpu.CompilerParams(vmem_limit_bytes=48 * 2**20),
        cost_estimate=pl.CostEstimate(flops=count * count * 832, bytes_accessed=6 * 2**20, transcendentals=count * count // 2),
        name="attention_backward",
    )(query, key, value, grad, segment[:, None], segment[None, :], log_total, cosines, sines)


def swap_halves(values):
    half = DR // 2
    pieces = [values[:, i * half : (i + 1) * half] for i in (1, 0, 3, 2)]
    return jnp.concatenate(pieces, axis=1)


def project_kernel(x_ref, gain_ref, w_ref, gain_kv_ref, expand_ref, cos_ref, sin_ref, normed_ref, q_ref, k_ref, v_ref, raw_ref, latent_ref):
    normed = rms_norm(x_ref[...].astype(F32), gain_ref[...]).astype(BF16)
    normed_ref[...] = normed
    both = dot(normed, w_ref[...])
    raw = both[:, :KVR]
    raw_ref[...] = raw
    latent = rms_norm(raw, gain_kv_ref[...]).astype(BF16)
    latent_ref[...] = latent
    expanded = dot(latent, expand_ref[...])
    rope = both[:, KVR + DN :]
    rope = rope * cos_ref[...] + swap_halves(rope) * sin_ref[...]
    q_ref[...] = jnp.concatenate([both[:, KVR : KVR + DN], rope[:, :DR]], axis=1).astype(BF16)
    k_ref[...] = jnp.concatenate([expanded[:, :DN], rope[:, DR:]], axis=1).astype(BF16)
    v_ref[...] = expanded[:, DN:].astype(BF16)


def project(rows, gain, weight, gain_kv, expand, cosines, sines):
    count = rows.shape[0]
    tile = 256

    def by_rows(columns):
        return pl.BlockSpec((tile, columns), lambda i: (i, 0))

    def whole(array):
        return pl.BlockSpec(array.shape, lambda i: (0, 0))

    outs = [(D, BF16), (DN + DR, BF16), (DN + DR, BF16), (DV, BF16), (KVR, F32), (KVR, BF16)]
    return pl.pallas_call(
        project_kernel,
        grid=(count // tile,),
        in_specs=[
            by_rows(D),
            whole(gain[None]),
            whole(weight),
            whole(gain_kv[None]),
            whole(expand),
            by_rows(2 * DR),
            by_rows(2 * DR),
        ],
        out_specs=tuple(by_rows(c) for c, _ in outs),
        out_shape=tuple(jax.ShapeDtypeStruct((count, c), t) for c, t in outs),
        compiler_params=pltpu.CompilerParams(vmem_limit_bytes=48 * 2**20),
        cost_estimate=pl.CostEstimate(flops=2 * count * D * 900, bytes_accessed=24 * 2**20, transcendentals=count),
        name="project",
    )(rows, gain[None], weight, gain_kv[None], expand, cosines, sines)


BLOCKS = 4


def silu_grads(gate, up, grad):
    sig = jax.nn.sigmoid(gate)
    return grad * up * sig * (1.0 + gate * (1.0 - sig)), grad * gate * sig


def pick_of(place_ref, b, capacity):
    tok = place_ref.shape[1]
    return lax.broadcasted_iota(jnp.int32, (capacity, tok), 0) == place_ref[b : b + 1, :]


def as_weights(match):
    return jnp.where(match, 1.0, 0.0).astype(BF16)


def spread_kernel(
    ffn_ref, up_ref, place_ref, gate_ref, in_ref, out_ref,
    x_ref, rg_ref, hidden_ref, grad_ref, gout_ref, gin_ref,
    sum_out, sum_in,
):
    step = pl.program_id(0)
    blocks, tok = place_ref.shape
    capacity = x_ref.shape[0] // blocks
    units = out_ref.shape[0]
    for b in range(blocks):
        match = pick_of(place_ref, b, capacity)
        pick = as_weights(match)
        gate = jnp.sum(jnp.where(match, gate_ref[b : b + 1, :], 0.0), axis=1, keepdims=True)
        tokens, rows = pl.ds(b * tok, tok), pl.ds(b * capacity, capacity)
        x_ref[rows, :] = dot(pick, ffn_ref[tokens, :]).astype(BF16)
        rg_ref[rows, :] = (gate * dot(pick, up_ref[tokens, :])).astype(BF16)
    both = dot(ffn_ref[...], in_ref[...])
    gate, up = both[:, :units], both[:, units:]
    hidden = (gate * jax.nn.sigmoid(gate) * up).astype(BF16)
    hidden_ref[...] = hidden
    grads = silu_grads(gate, up, dot_nt(up_ref[...], out_ref[...]))
    grad = jnp.concatenate(grads, axis=1).astype(BF16)
    grad_ref[...] = grad

    @pl.when(step == 0)
    def _():
        sum_out[...] = jnp.zeros_like(sum_out)
        sum_in[...] = jnp.zeros_like(sum_in)

    sum_out[...] += dot_tn(hidden, up_ref[...])
    sum_in[...] += dot_tn(grad, ffn_ref[...])

    @pl.when(step == pl.num_programs(0) - 1)
    def _():
        gout_ref[...] = sum_out[...].astype(BF16)
        gin_ref[...] = sum_in[...].astype(BF16)


def by_rows(size, columns):
    return pl.BlockSpec((size, columns), lambda i: (i, 0))


def whole(array):
    return pl.BlockSpec(array.shape, lambda i: (0, 0), pipeline_mode=pl.Buffered(1))


def by_step(tok):
    return pl.BlockSpec((None, BLOCKS, tok), lambda i: (i, 0, 0))


def in_steps(rows):
    return rows.reshape(-1, BLOCKS, rows.shape[1])


def spread(ffn, upstream, place, gates, shared_in, shared_out, capacity):
    count = ffn.shape[0]
    seq, tok = place.shape
    steps = seq // BLOCKS
    units = shared_out.shape[0]
    t, rows = BLOCKS * tok, BLOCKS * capacity
    outs = [(rows, D), (rows, D), (t, units), (t, 2 * units)]
    fixed = [(units, D), (2 * units, D)]
    flops = 4 * seq * capacity * tok * D + 2 * count * 6 * D * units
    return pl.pallas_call(
        spread_kernel,
        grid=(steps,),
        in_specs=[by_rows(t, D), by_rows(t, D), by_step(tok), by_step(tok), whole(shared_in), whole(shared_out)],
        out_specs=tuple(by_rows(*o) for o in outs) + tuple(pl.BlockSpec(o, lambda i: (0, 0)) for o in fixed),
        out_shape=tuple(jax.ShapeDtypeStruct((r * steps, c), BF16) for r, c in outs)
        + tuple(jax.ShapeDtypeStruct(o, BF16) for o in fixed),
        scratch_shapes=[pltpu.VMEM(o, F32) for o in fixed],
        compiler_params=pltpu.CompilerParams(vmem_limit_bytes=56 * 2**20),
        cost_estimate=pl.CostEstimate(flops=flops, bytes_accessed=40 * 2**20, transcendentals=2 * count * units),
        name="spread",
    )(ffn, upstream, in_steps(place), in_steps(gates), shared_in, shared_out)


def collect_forward_kernel(res_ref, up_ref, place_ref, gate_ref, hidden_ref, out_ref, mixed_ref, dots_ref):
    blocks, tok = place_ref.shape
    capacity = res_ref.shape[0] // blocks
    for b in range(blocks):
        pick = as_weights(pick_of(place_ref, b, capacity))
        tokens, rows = pl.ds(b * tok, tok), pl.ds(b * capacity, capacity)
        mine = dot_tn(pick, res_ref[rows, :])
        dots_ref[tokens, :] = jnp.sum(up_ref[tokens, :].astype(F32) * mine, axis=1, keepdims=True)
        shared = dot(hidden_ref[tokens, :], out_ref[...])
        mixed_ref[tokens, :] = (gate_ref[tokens, :] * mine + shared).astype(BF16)


def collect_forward(results, upstream, place, gates, hidden, shared_out, capacity):
    count = upstream.shape[0]
    seq, tok = place.shape
    steps = seq // BLOCKS
    t, rows = BLOCKS * tok, BLOCKS * capacity
    units = shared_out.shape[0]
    flops = 2 * seq * capacity * tok * D + 2 * count * D * units
    return pl.pallas_call(
        collect_forward_kernel,
        grid=(steps,),
        in_specs=[by_rows(rows, D), by_rows(t, D), by_step(tok), by_rows(t, 1), by_rows(t, units), whole(shared_out)],
        out_specs=(by_rows(t, D), by_rows(t, 1)),
        out_shape=(jax.ShapeDtypeStruct((count, D), BF16), jax.ShapeDtypeStruct((count, 1), F32)),
        compiler_params=pltpu.CompilerParams(vmem_limit_bytes=48 * 2**20),
        cost_estimate=pl.CostEstimate(flops=flops, bytes_accessed=24 * 2**20, transcendentals=0),
        name="collect_forward",
    )(results, upstream, in_steps(place), gates.reshape(-1, 1), hidden, shared_out)


def collect_backward_kernel(rows_ref, place_ref, grad_ref, in_ref, back_ref):
    blocks, tok = place_ref.shape
    capacity = rows_ref.shape[0] // blocks
    shared = dot_nt(grad_ref[...], in_ref[...])
    for b in range(blocks):
        pick = as_weights(pick_of(place_ref, b, capacity))
        tokens, rows = pl.ds(b * tok, tok), pl.ds(b * capacity, capacity)
        mine = dot_tn(pick, rows_ref[rows, :])
        back_ref[tokens, :] = (mine + shared[b * tok : (b + 1) * tok]).astype(BF16)


def collect_backward(row_grads, place, grads, shared_in, capacity):
    count = grads.shape[0]
    seq, tok = place.shape
    steps = seq // BLOCKS
    t, rows = BLOCKS * tok, BLOCKS * capacity
    flops = 2 * seq * capacity * tok * D + 2 * count * D * grads.shape[1]
    return pl.pallas_call(
        collect_backward_kernel,
        grid=(steps,),
        in_specs=[by_rows(rows, D), by_step(tok), by_rows(t, grads.shape[1]), whole(shared_in)],
        out_specs=by_rows(t, D),
        out_shape=jax.ShapeDtypeStruct((count, D), BF16),
        compiler_params=pltpu.CompilerParams(vmem_limit_bytes=48 * 2**20),
        cost_estimate=pl.CostEstimate(flops=flops, bytes_accessed=18 * 2**20, transcendentals=0),
        name="collect_backward",
    )(row_grads, in_steps(place), grads, shared_in)


def turn_kernel(in_ref, out_ref):
    block = in_ref[...].astype(F32)
    out_ref[...] = block.reshape(-1, block.shape[-1]).T


def turn_rows(rows, tile):
    count, columns = rows.shape
    return pl.pallas_call(
        turn_kernel,
        grid=(count // tile,),
        in_specs=[pl.BlockSpec((tile, columns), lambda i: (i, 0))],
        out_specs=pl.BlockSpec((columns, tile), lambda i: (0, i)),
        out_shape=jax.ShapeDtypeStruct((columns, count), F32),
        compiler_params=pltpu.CompilerParams(vmem_limit_bytes=48 * 2**20),
        cost_estimate=pl.CostEstimate(flops=0, bytes_accessed=6 * rows.size, transcendentals=0),
        name="turn_rows",
    )(rows)


def turn_units(parts):
    seq_count, groups, unit, columns = parts.shape
    if unit % 8 or (seq_count * unit) % 128:
        return parts.transpose(3, 1, 0, 2).reshape(columns, -1).astype(F32)
    wide = seq_count * unit
    tile = 256
    return pl.pallas_call(
        turn_kernel,
        grid=(groups, columns // tile),
        in_specs=[pl.BlockSpec((seq_count, None, unit, tile), lambda g, i: (0, g, 0, i))],
        out_specs=pl.BlockSpec((tile, wide), lambda g, i: (i, g)),
        out_shape=jax.ShapeDtypeStruct((columns, groups * wide), F32),
        compiler_params=pltpu.CompilerParams(vmem_limit_bytes=48 * 2**20),
        cost_estimate=pl.CostEstimate(flops=0, bytes_accessed=6 * parts.size, transcendentals=0),
        name="turn_units",
    )(parts)


LINE = 4
MESH = pl.DeviceIdType.MESH


def place():
    rank = lax.axis_index("seq")
    return rank, lax.div(rank, 4), lax.rem(lax.div(rank, 2), 2), lax.rem(rank, 2)


def rank_at(z, y, x, dz, dy, dx):
    across = y + dy * (1 - 2 * y)
    along = x + dx * (1 - 2 * x)
    return (z + dz) * 4 + across * 2 + along


OFFSETS = [(dz, dy, dx) for dz in (0, -1, 1, -2, 2, -3, 3) for dy in (0, 1) for dx in (0, 1)]


def hops(offset):
    return abs(offset[0]) + offset[1] + offset[2]


def onward(order, offset):
    rel = dict(zip("zyx", offset))
    moved = [i for i, dim in enumerate(order) if rel[dim]]
    last = moved[-1] if moved else -1
    steps = []
    if last >= 0 and order[last] == "z":
        steps.append((1 if rel["z"] < 0 else -1, 0, 0))
    for dim in order[last + 1 :]:
        steps += {"z": [(1, 0, 0), (-1, 0, 0)], "y": [(0, 1, 0)], "x": [(0, 0, 1)]}[dim]
    return [s for s in steps if any(0 <= z + offset[0] < LINE and 0 <= z + s[0] < LINE for z in range(LINE))]


def inside(z, dz):
    return (z + dz >= 0) & (z + dz < LINE)


def guarded(z, steps, body):
    steps = [dz for dz in steps if dz]
    if not steps:
        body()
        return
    good = inside(z, steps[0])
    for dz in steps[1:]:
        good = good & inside(z, dz)
    pl.when(good)(body)


def greet_all():
    rank = lax.axis_index("seq")
    count = lax.axis_size("seq")
    barrier = pltpu.get_barrier_semaphore()
    for k in range(1, count):
        peer = lax.rem(rank + k, count)
        pl.semaphore_signal(barrier, inc=1, device_id={"seq": peer}, device_id_type=MESH)
    pl.semaphore_wait(barrier, count - 1)


def gather_kernel(streams, n_main, n_small, *refs):
    n = n_main + n_small
    ins, outs = refs[:n], refs[n : 2 * n]
    send_sems, recv_sems, small_send, small_recv, local_sems = refs[2 * n :]
    rank, z, y, x = place()
    count = lax.axis_size("seq")
    greet_all()
    locals_ = [pltpu.make_async_copy(ins[i], outs[i].at[rank], local_sems.at[i]) for i in range(n)]
    slots = {}

    def copy(stream, offset, step):
        index, first, rows, order = streams[stream]
        part = pl.ds(first, rows)
        source = rank_at(z, y, x, *offset)
        slot = slots.setdefault((stream, offset, step), len(slots))
        block = outs[index].at[source, part]
        own = offset == (0, 0, 0)
        return pltpu.make_async_remote_copy(
            src_ref=ins[index].at[part] if own else block,
            dst_ref=block,
            send_sem=send_sems.at[slot],
            recv_sem=recv_sems.at[stream * count + source],
            device_id={"seq": rank_at(z, y, x, *step)},
            device_id_type=MESH,
        )

    def small_copy(i, k):
        peer = lax.rem(rank + k, count)
        return pltpu.make_async_remote_copy(
            src_ref=ins[n_main + i],
            dst_ref=outs[n_main + i].at[rank],
            send_sem=small_send.at[i * count + k],
            recv_sem=small_recv.at[i * count + rank],
            device_id={"seq": peer},
            device_id_type=MESH,
        )

    def arrived(stream, offset):
        index, first, rows, order = streams[stream]
        source = rank_at(z, y, x, *offset)
        block = outs[index].at[source, pl.ds(first, rows)]
        pltpu.make_async_remote_copy(
            src_ref=block,
            dst_ref=block,
            send_sem=send_sems.at[0],
            recv_sem=recv_sems.at[stream * count + source],
            device_id={"seq": rank},
            device_id_type=MESH,
        ).wait_recv()

    todo = sorted(
        ((stream, offset) for stream in range(len(streams)) for offset in OFFSETS),
        key=lambda it: (hops(it[1]), it[0]),
    )
    for stream, offset in todo:
        def forward(stream=stream, offset=offset):
            if hops(offset):
                arrived(stream, offset)
            for step in onward(streams[stream][3], offset):
                guarded(z, [step[0]], lambda: copy(stream, offset, step).start())
        guarded(z, [offset[0]], forward)
        if stream == len(streams) - 1 and offset == (0, 0, 0):
            for c in locals_:
                c.start()
            for i in range(n_small):
                for k in range(1, count):
                    small_copy(i, k).start()
    for stream, offset in todo:
        for step in onward(streams[stream][3], offset):
            guarded(z, [offset[0], step[0]], lambda: copy(stream, offset, step).wait_send())
    for i in range(n_small):
        for k in range(1, count):
            small_copy(i, k).wait_send()
        for k in range(1, count):
            source = lax.rem(rank + k, count)
            block = outs[n_main + i].at[source]
            pltpu.make_async_remote_copy(
                src_ref=block, dst_ref=block, send_sem=small_send.at[0],
                recv_sem=small_recv.at[i * count + source], device_id={"seq": rank}, device_id_type=MESH,
            ).wait_recv()
    for c in locals_:
        c.wait()


def n_sends(streams):
    return sum(len(onward(s[3], o)) for s in streams for o in OFFSETS)


def gather_all(main, parts, small, collective_id, count=16):
    streams = []
    for i, pieces in enumerate(parts):
        first = 0
        for rows, order in pieces:
            streams.append((i, first, rows, order))
            first += rows
        assert first == main[i].shape[0]
    arrays = list(main) + list(small)
    any_spec = pl.BlockSpec(memory_space=pl.ANY)
    return pl.pallas_call(
        functools.partial(gather_kernel, streams, len(main), len(small)),
        out_shape=tuple(jax.ShapeDtypeStruct((count,) + a.shape, a.dtype) for a in arrays),
        in_specs=[any_spec] * len(arrays),
        out_specs=tuple([any_spec] * len(arrays)),
        scratch_shapes=[
            pltpu.SemaphoreType.DMA((n_sends(streams),)),
            pltpu.SemaphoreType.DMA((len(streams) * count,)),
            pltpu.SemaphoreType.DMA((max(1, len(small)) * count,)),
            pltpu.SemaphoreType.DMA((max(1, len(small)) * count,)),
            pltpu.SemaphoreType.DMA((len(arrays),)),
        ],
        compiler_params=pltpu.CompilerParams(collective_id=collective_id, has_side_effects=True),
        name="gather_all",
    )(*arrays)


def toward(order, offset):
    rel = dict(zip("zyx", offset))
    dim = [d for d in order if rel[d]][-1]
    return {"z": (1 if rel["z"] > 0 else -1, 0, 0), "y": (0, 1, 0), "x": (0, 0, 1)}[dim]


def seen_from(offset, step):
    return (offset[0] - step[0], offset[1] ^ step[1], offset[2] ^ step[2])


def back(step):
    return (-step[0], step[1], step[2])


ADD_ROWS = 16


def slot_table(order):
    table, used = {}, 0
    for dy in (0, 1):
        for dx in (0, 1):
            for kind in ("x", "y", "up", "down"):
                step = {"x": (0, 0, 1), "y": (0, 1, 0), "up": (1, 0, 0), "down": (-1, 0, 0)}[kind]
                met = [o[0] for o in OFFSETS if o[1:] == (dy, dx) and step in onward(order, o)]
                if not met:
                    continue
                if kind == "down":
                    table[dy, dx, "down"] = (used, False)
                    used += 1
                    continue
                spread = any(met)
                table[dy, dx, kind] = (used, spread)
                used += LINE if spread else 1
    return table, used


def slot_at(table, z, offset, step):
    dz, dy, dx = offset
    kind = "x" if step[2] else "y" if step[1] else "down" if step[0] < 0 and dz == 0 else "up"
    first, spread = table[dy, dx, kind]
    return first + (z + dz) if spread else first


def scatter_kernel(streams, n_main, n_small, *refs):
    n = n_main + n_small
    ins, outs = refs[:n], refs[n : 2 * n]
    scratch = refs[2 * n :]
    bufs = scratch[: len(streams)]
    send_sems, recv_sems, small_send, small_recv, local_sems = scratch[len(streams) :]
    rank, z, y, x = place()
    count = lax.axis_size("seq")
    tables, bases, base = [], [], 0
    for stream in streams:
        table, used = slot_table(stream[3])
        tables.append(table)
        bases.append(base)
        base += used
    greet_all()

    def small_copy(i, k):
        peer = lax.rem(rank + k, count)
        return pltpu.make_async_remote_copy(
            src_ref=ins[n_main + i],
            dst_ref=outs[n_main + i].at[rank],
            send_sem=small_send.at[i * count + k],
            recv_sem=small_recv.at[i * count + rank],
            device_id={"seq": peer},
            device_id_type=MESH,
        )

    todo = sorted(
        ((s, offset) for s in range(len(streams)) for offset in OFFSETS),
        key=lambda it: (-hops(it[1]), it[0]),
    )
    send_slot = {key: i for i, key in enumerate(k for k in todo if hops(k[1]))}

    def send_copy(s, offset, source):
        step = toward(streams[s][3], offset)
        k = slot_at(tables[s], z + step[0], seen_from(offset, step), back(step))
        return pltpu.make_async_remote_copy(
            src_ref=source,
            dst_ref=bufs[s].at[k],
            send_sem=send_sems.at[send_slot[s, offset]],
            recv_sem=recv_sems.at[bases[s] + k],
            device_id={"seq": rank_at(z, y, x, *step)},
            device_id_type=MESH,
        )

    def wait_child(s, k):
        pltpu.make_async_remote_copy(
            src_ref=bufs[s].at[k],
            dst_ref=bufs[s].at[k],
            send_sem=send_sems.at[0],
            recv_sem=recv_sems.at[bases[s] + k],
            device_id={"seq": rank},
            device_id_type=MESH,
        ).wait_recv()

    for s, offset in todo:
        index, first, rows, order = streams[s]
        children = onward(order, offset)
        dest = rank_at(z, y, x, *offset)
        always = [c for c in children if not c[0]]
        sometimes = [c for c in children if c[0]]

        def run(present, s=s, offset=offset, index=index, first=first, rows=rows, dest=dest):
            own = ins[index].at[dest, pl.ds(first, rows)]
            if not present:
                send_copy(s, offset, own).start()
                return
            slots = [slot_at(tables[s], z, offset, step) for step in present]
            for k in slots:
                wait_child(s, k)
            final = not hops(offset)
            target = outs[index].at[pl.ds(first, rows)] if final else bufs[s].at[slots[0]]

            def add(i, carry):
                part = pl.ds(pl.multiple_of(i * ADD_ROWS, ADD_ROWS), ADD_ROWS)
                total = own[part, :].astype(F32)
                for k in slots:
                    total = total + bufs[s][k, part, :].astype(F32)
                target[part, :] = total.astype(target.dtype)
                return carry

            lax.fori_loop(0, rows // ADD_ROWS, add, 0)
            if not final:
                send_copy(s, offset, target).start()

        def cases(run=run, always=always, sometimes=sometimes):
            if not sometimes:
                run(always)
                return
            for mask in range(2 ** len(sometimes)):
                present = [c for i, c in enumerate(sometimes) if mask >> i & 1]
                good = None
                for i, c in enumerate(sometimes):
                    here = inside(z, c[0]) if mask >> i & 1 else jnp.logical_not(inside(z, c[0]))
                    good = here if good is None else good & here
                pl.when(good)(functools.partial(run, present + always))

        guarded(z, [offset[0]], cases)
        if (s, offset) == todo[0]:
            for i in range(n_small):
                for k in range(1, count):
                    small_copy(i, k).start()
                pltpu.make_async_copy(ins[n_main + i], outs[n_main + i].at[rank], local_sems.at[i]).start()
    for s, offset in todo:
        if hops(offset):
            index, first, rows, order = streams[s]
            own = ins[index].at[rank_at(z, y, x, *offset), pl.ds(first, rows)]
            guarded(z, [offset[0]], lambda: send_copy(s, offset, own).wait_send())
    for i in range(n_small):
        for k in range(1, count):
            small_copy(i, k).wait_send()
        for k in range(1, count):
            source = lax.rem(rank + k, count)
            block = outs[n_main + i].at[source]
            pltpu.make_async_remote_copy(
                src_ref=block,
                dst_ref=block,
                send_sem=small_send.at[0],
                recv_sem=small_recv.at[i * count + source],
                device_id={"seq": rank},
                device_id_type=MESH,
            ).wait_recv()
        pltpu.make_async_copy(ins[n_main + i], outs[n_main + i].at[rank], local_sems.at[i]).wait()


def scatter_sum(main, parts, small, collective_id, count=16):
    streams = []
    for i, pieces in enumerate(parts):
        first = 0
        for rows, order in pieces:
            streams.append((i, first, rows, order))
            first += rows
        assert first == main[i].shape[1]
    arrays = list(main) + list(small)
    any_spec = pl.BlockSpec(memory_space=pl.ANY)
    vmem = pl.BlockSpec(memory_space=pltpu.VMEM)
    places = [slot_table(stream[3])[1] for stream in streams]
    buffers = [
        pltpu.VMEM((used, rows, main[index].shape[2]), main[index].dtype)
        for used, (index, first, rows, order) in zip(places, streams)
    ]
    return pl.pallas_call(
        functools.partial(scatter_kernel, streams, len(main), len(small)),
        out_shape=tuple(
            [jax.ShapeDtypeStruct(a.shape[1:], F32) for a in main]
            + [jax.ShapeDtypeStruct((count,) + a.shape, a.dtype) for a in small]
        ),
        in_specs=[vmem] * len(main) + [any_spec] * len(small),
        out_specs=tuple([vmem] * len(main) + [any_spec] * len(small)),
        scratch_shapes=buffers
        + [
            pltpu.SemaphoreType.DMA((len(streams) * len(OFFSETS),)),
            pltpu.SemaphoreType.DMA((sum(places),)),
            pltpu.SemaphoreType.DMA((max(1, len(small)) * count,)),
            pltpu.SemaphoreType.DMA((max(1, len(small)) * count,)),
            pltpu.SemaphoreType.DMA((max(1, len(small)),)),
        ],
        compiler_params=pltpu.CompilerParams(
            collective_id=collective_id, has_side_effects=True, vmem_limit_bytes=60 * 2**20
        ),
        name="scatter_sum",
    )(*arrays)


def gather_seq(rows):
    return lax.all_gather(rows, "seq", axis=0, tiled=True)


def scatter_seq(partial):
    return lax.psum_scatter(partial, "seq", scatter_dimension=0, tiled=True)


def gather_fsdp(rows, axis=0):
    return lax.all_gather(rows, "fsdp", axis=axis, tiled=True)


def scatter_fsdp(partial, axis=0):
    count, me = lax.axis_size("fsdp"), lax.axis_index("fsdp")
    size = partial.shape[axis] // count
    total = lax.dynamic_slice_in_dim(partial, me * size, size, axis).astype(F32)
    for k in range(1, count):
        piece = lax.dynamic_slice_in_dim(partial, lax.rem(me + k, count) * size, size, axis)
        total = total + shift_fsdp(piece, k).astype(F32)
    return total


def shift_fsdp(rows, k):
    count = lax.axis_size("fsdp")
    return lax.ppermute(rows, "fsdp", [(i, (i + k) % count) for i in range(count)])


def sum_everywhere(rows):
    count = lax.axis_size("seq")
    total = rows
    bit = 1
    while bit < count:
        total = total + lax.ppermute(total, "seq", [(i, i ^ bit) for i in range(count)])
        bit *= 2
    kept = total
    for k in range(1, lax.axis_size("fsdp")):
        total = total + shift_fsdp(kept, k)
    return total


ROW_PARTS = [(48, "zxy"), (48, "zyx"), (16, "xyz"), (16, "yxz")]


def split_rows(rows):
    tile = 16
    tiles = rows // tile
    short = tiles // 8
    long = (tiles - 2 * short) // 2
    sizes = [tiles - 2 * short - long, long, short, short]
    orders = ["zxy", "zyx", "xyz", "yxz"]
    return [(n * tile, order) for n, order in zip(sizes, orders) if n]


def on_device(
    tokens,
    cotangent,
    lengths,
    routes,
    g_attn,
    w_q,
    w_kva,
    g_kv,
    w_kvb,
    w_o,
    g_ffn,
    w_router,
    w_shared_in,
    w_shared_out,
    w_expert_in,
    w_expert_out,
):
    seq_count = lax.axis_size("seq")
    fsdp_count = lax.axis_size("fsdp")
    rank = lax.axis_index("seq")
    tok_count = tokens.shape[0]
    group_size = tok_count * seq_count
    query_width = DN + DR
    kv_width = DN + DV
    experts = seq_count
    capacity = min(tok_count, 2 * tok_count * TOP // experts)
    buffer_rows = seq_count * capacity
    unit = SH // (seq_count * fsdp_count)
    units = unit * fsdp_count
    row_part = w_q.shape[0]

    def own(rows, axis=0):
        return lax.dynamic_slice_in_dim(rows, rank * tok_count, tok_count, axis)

    expert_ids = jnp.arange(experts, dtype=jnp.int32)
    route_mask = jnp.any(routes[None] == expert_ids[:, None, None], axis=2).astype(BF16)
    token_all, mask_all = gather_all([tokens], [ROW_PARTS], [route_mask], 1)
    token_all = token_all.reshape(group_size, D)

    small = gather_fsdp(jnp.concatenate([g_attn, g_kv, g_ffn, w_router.reshape(-1)])[None])
    cuts = [0, g_attn.size, g_kv.size, g_ffn.size, w_router.size]
    ends = [sum(cuts[: i + 1]) for i in range(len(cuts))]
    gain_attn = small[:, ends[0] : ends[1]].reshape(-1).astype(F32)
    gain_latent = small[:, ends[1] : ends[2]].reshape(-1).astype(F32)
    gain_ffn = small[:, ends[2] : ends[3]].reshape(-1).astype(F32)
    router_weight = small[:, ends[3] : ends[4]].reshape(D, experts)
    head_query_part = lax.dynamic_slice_in_dim(w_q, rank * query_width, query_width, 1)
    head_expand = gather_fsdp(lax.dynamic_slice_in_dim(w_kvb, rank * kv_width, kv_width, 1))
    head_weights = gather_fsdp(
        jnp.concatenate([w_kva[:, :KVR], head_query_part, w_kva[:, KVR:]], axis=1)
    )
    output_weight = gather_fsdp(w_o)
    expert_in = gather_fsdp(w_expert_in[0])
    expert_out = gather_fsdp(w_expert_out[0])
    query_weight = gather_fsdp(w_q)
    expand_weight = gather_fsdp(w_kvb)

    slot_ids = jnp.arange(group_size, dtype=jnp.int32)
    segment, position, valid_all = layout(lengths[0], slot_ids)
    angles = own(position)[:, None].astype(F32) * frequencies(DR)[None, :]
    wide_angles = position[:, None].astype(F32) * jnp.tile(frequencies(DR), 4)[None, :]
    cosines = jnp.cos(wide_angles)
    signs = jnp.where(jnp.arange(2 * DR) % DR < DR // 2, -1.0, 1.0).astype(F32)
    sines = jnp.sin(wide_angles) * signs[None, :]

    upstream_own = jnp.where(own(valid_all)[:, None], cotangent, 0).astype(BF16)
    upstream_all = gather_seq(upstream_own)

    normed_all, query, key, value, latent_full, latent_all = project(
        token_all, gain_attn, head_weights, gain_latent, head_expand, cosines, sines
    )
    context, log_total, head_largest = attention_forward(query, key, value, segment, valid_all)
    late_rank, context, upstream_all = lax.optimization_barrier((rank, context, upstream_all))
    lanes = -(-units // 128) * 128
    unit_slices = [
        lax.dynamic_slice_in_dim(w_shared_in, i * (SH // fsdp_count) + late_rank * unit, unit, 1)
        for i in range(2 * fsdp_count)
    ]
    filler = jnp.zeros((row_part, lanes - units), BF16)
    shared_in_part = jnp.concatenate(
        unit_slices[:fsdp_count] + [filler] + unit_slices[fsdp_count:] + [filler], axis=1
    )
    shared_in = gather_fsdp(shared_in_part)
    shared_out = gather_fsdp(lax.dynamic_slice_in_dim(w_shared_out, late_rank * unit, unit, 0))
    shared_out = jnp.pad(shared_out, ((0, lanes - units), (0, 0)))

    context_low = lax.all_to_all(context, "seq", split_axis=0, concat_axis=1, tiled=True)
    inputs = tokens.astype(F32)
    middle = inputs + dot(context_low, output_weight)
    ffn_low = rms_norm(middle, gain_ffn).astype(BF16)
    ffn_all, largest_all = gather_all([ffn_low], [ROW_PARTS], [head_largest], 2)
    ffn_all = ffn_all.reshape(group_size, D)
    head_max = largest_all[:, 0, :]
    for k in range(1, fsdp_count):
        head_max = jnp.maximum(head_max, shift_fsdp(largest_all[:, 0, :], k))
    global_max = head_max[:, 0]

    router_probs = jax.nn.softmax(dot(ffn_all, router_weight), axis=-1)
    chosen = lax.dynamic_slice_in_dim(mask_all, rank, 1, 1).reshape(seq_count, tok_count) > 0
    gates = lax.dynamic_slice_in_dim(router_probs, rank, 1, 1).reshape(seq_count, tok_count)
    place = jnp.cumsum(chosen.astype(jnp.int32), axis=1) - 1
    place = jnp.where(chosen, place, capacity)

    arrived, result_grad, shared_hidden, shared_grad, grad_shared_out, grad_shared_in = spread(
        ffn_all, upstream_all, place, gates, shared_in, shared_out, capacity
    )
    part_shared_out = scatter_fsdp(grad_shared_out[:units]).astype(BF16)
    part_shared_in = jnp.concatenate([grad_shared_in[:units], grad_shared_in[lanes : lanes + units]], axis=0)
    part_shared_in = scatter_fsdp(part_shared_in, 1).astype(BF16)
    arrived, part_shared_out, part_shared_in = lax.optimization_barrier(
        (arrived, part_shared_out, part_shared_in)
    )
    all_shared_out = gather_seq(part_shared_out)
    all_shared_in = gather_seq(part_shared_in)

    gate_up = dot(arrived, expert_in).astype(BF16)
    gate_part, up_part = gate_up[:, :FF].astype(F32), gate_up[:, FF:].astype(F32)
    hidden = (jax.nn.silu(gate_part) * up_part).astype(BF16)
    result = dot(hidden, expert_out).astype(BF16)
    d_hidden = dot_nt(result_grad, expert_out)
    d_gate, d_up = [g.astype(BF16) for g in silu_grads(gate_part, up_part, d_hidden)]
    row_grad = dot_nt(jnp.concatenate([d_gate, d_up], axis=1), expert_in).astype(BF16)
    mixed_part, gate_grad = collect_forward(
        result, upstream_all, place, gates, shared_hidden, shared_out, capacity
    )
    ffn_part = collect_backward(row_grad, place, shared_grad, shared_in, capacity)
    mixed_part, ffn_part, all_shared_out = lax.optimization_barrier((mixed_part, ffn_part, all_shared_out))
    mixed_sum, ffn_sum, prob_grads = scatter_sum(
        [part.reshape(seq_count, tok_count, D) for part in (mixed_part, ffn_part)],
        [ROW_PARTS, ROW_PARTS],
        [gate_grad.reshape(seq_count, tok_count)],
        3,
    )
    mixed = (middle + mixed_sum).astype(BF16)
    prob_grads = prob_grads.reshape(experts, group_size).T

    logit_grads = (
        router_probs * (prob_grads - jnp.sum(router_probs * prob_grads, axis=-1, keepdims=True))
    ).astype(BF16)
    grad_router = dot_tn(ffn_all, logit_grads)
    sum_router = scatter_fsdp(grad_router.astype(BF16))
    ffn_grad = ffn_sum + dot_nt(own(logit_grads), router_weight)

    ffn_pull = jax.vjp(rms_norm, middle, gain_ffn)[1]
    middle_norm_grad, grad_gain_ffn = ffn_pull(ffn_grad)
    middle_grad = upstream_own.astype(F32) + middle_norm_grad
    middle_low = middle_grad.astype(BF16)
    context_grad = dot_nt(middle_low, output_weight).astype(BF16)
    head_grad = lax.all_to_all(context_grad, "seq", split_axis=1, concat_axis=0, tiled=True)
    grad_output = scatter_fsdp(dot_tn(context_low, middle_low).astype(BF16)).astype(BF16)
    output_rows = row_part // seq_count
    (part_output,) = scatter_sum(
        [grad_output.reshape(seq_count, output_rows, D)], [split_rows(output_rows)], [], 5
    )

    head_grad, all_shared_in = lax.optimization_barrier((head_grad, all_shared_in))
    head_back = attention_backward(query, key, value, head_grad, segment, log_total, cosines, sines)
    head_back, arrived, result_grad, hidden, d_gate, d_up = lax.optimization_barrier(
        (head_back, arrived, result_grad, hidden, d_gate, d_up)
    )
    back = lax.all_to_all(
        head_back.reshape(seq_count, tok_count, -1), "seq", split_axis=0, concat_axis=0, tiled=True
    )
    grad_expert_out = dot_tn(hidden, result_grad).astype(BF16)
    grad_expert_in = dot_tn(arrived, jnp.concatenate([d_gate, d_up], axis=1)).astype(BF16)
    rope_at = 2 * DN + DV
    head_pre_grad = jnp.concatenate([head_back[:, :DN], head_back[:, rope_at : rope_at + DR]], axis=1)
    grad_query = dot_tn(head_pre_grad, normed_all).astype(BF16)
    grad_expand = dot_tn(head_back[:, DN:rope_at], latent_all).astype(BF16)
    back, grad_expert_out, grad_expert_in, grad_query, grad_expand = lax.optimization_barrier(
        (back, grad_expert_out, grad_expert_in, grad_query, grad_expand)
    )
    sum_expert_in = scatter_fsdp(grad_expert_in)[None]
    sum_expert_out = scatter_fsdp(grad_expert_out)[None]
    part_query = scatter_fsdp(grad_query, 1).astype(BF16)
    part_expand = scatter_fsdp(grad_expand, 1).astype(BF16)

    back = back.transpose(1, 0, 2)
    pre_grad = jnp.concatenate([back[..., :DN], back[..., rope_at : rope_at + DR]], axis=-1)
    pre_grad = pre_grad.reshape(tok_count, H * query_width)
    expand_grad = back[..., DN:rope_at].reshape(tok_count, H * kv_width)
    latent_grad = dot_nt(expand_grad, expand_weight)
    rope_grad = rotate(jnp.sum(back[..., rope_at + DR :].astype(F32), axis=1), -angles)
    latent_pull = jax.vjp(rms_norm, own(latent_full), gain_latent)[1]
    compressed_grad, grad_gain_latent = latent_pull(latent_grad)
    full_grad = jnp.concatenate([compressed_grad, rope_grad], axis=1).astype(BF16)
    full_all = gather_seq(full_grad)
    sum_latent = scatter_fsdp(dot_tn(normed_all, full_all).astype(BF16))
    spread_grad = jnp.pad(full_grad[:, :KVR], ((0, 0), (0, query_width + DR)))
    spread_grad = spread_grad + jnp.pad(full_grad[:, KVR:], ((0, 0), (KVR + query_width, 0)))
    normed_grad = dot_nt(pre_grad, query_weight) + dot_nt(spread_grad, head_weights)
    input_pull = jax.vjp(rms_norm, inputs, gain_attn)[1]
    input_norm_grad, grad_gain_attn = input_pull(normed_grad)
    grad_inputs = middle_grad + input_norm_grad

    gain_sum = sum_everywhere(
        jnp.concatenate([grad_gain_attn, grad_gain_latent, grad_gain_ffn]).reshape(-1, 128)
    ).reshape(-1)
    sum_shared_out = all_shared_out.astype(F32)
    sum_shared_in = turn_units(all_shared_in.reshape(seq_count, 2 * fsdp_count, unit, row_part))
    sum_query = turn_rows(gather_seq(part_query), 384)
    sum_expand = turn_rows(gather_seq(part_expand), 512)
    sum_output = gather_seq(part_output.astype(BF16)).astype(F32)
    fsdp_rank = lax.axis_index("fsdp")

    def own_part(first, like):
        return lax.dynamic_slice_in_dim(gain_sum, first + fsdp_rank * like.size, like.size, 0)

    sum_gain_attn = own_part(0, g_attn)
    sum_gain_latent = own_part(D, g_kv)
    sum_gain_ffn = own_part(D + KVR, g_ffn)

    clip_gamma = CLIP_LIMIT / jnp.maximum(global_max, CLIP_LIMIT)
    clip_root = jnp.sqrt(clip_gamma)
    query_factor = jnp.concatenate(
        [
            jnp.broadcast_to(clip_root[:, None], (H, DN)),
            jnp.broadcast_to(clip_gamma[:, None], (H, DR)),
        ],
        axis=1,
    ).reshape(1, -1)
    clipped_query = (w_q.astype(F32) * query_factor).astype(BF16)
    return (
        mixed,
        grad_inputs,
        sum_gain_attn,
        sum_query,
        sum_latent,
        sum_gain_latent,
        sum_expand,
        sum_output,
        sum_gain_ffn,
        sum_router,
        sum_shared_in,
        sum_shared_out,
        sum_expert_in,
        sum_expert_out,
        clipped_query,
    )


def solution(mesh):
    in_specs = (
        P(("fsdp", "seq"), None),
        P(("fsdp", "seq"), None),
        P("fsdp", None),
        P(("fsdp", "seq"), None),
        P("fsdp"),
        P("fsdp", None),
        P("fsdp", None),
        P("fsdp"),
        P("fsdp", None),
        P("fsdp", None),
        P("fsdp"),
        P("fsdp", None),
        P("fsdp", None),
        P("fsdp", None),
        P("seq", "fsdp", None),
        P("seq", "fsdp", None),
    )
    out_specs = (
        P(("fsdp", "seq"), None),
        P(("fsdp", "seq"), None),
        P("fsdp"),
        P("fsdp", None),
        P("fsdp", None),
        P("fsdp"),
        P("fsdp", None),
        P("fsdp", None),
        P("fsdp"),
        P("fsdp", None),
        P("fsdp", None),
        P("fsdp", None),
        P("seq", "fsdp", None),
        P("seq", "fsdp", None),
        P("fsdp", None),
    )
    return jax.shard_map(
        on_device, mesh=mesh, in_specs=in_specs, out_specs=out_specs, check_vma=False
    )
```

```python
import functools

import jax
import jax.numpy as jnp
from jax import lax
from jax.experimental import pallas as pl
from jax.experimental.pallas import tpu as pltpu
from jax.sharding import PartitionSpec as P

D = 2048
H = 16
DN = 128
DR = 64
DV = 128
KVR = 512
FF = 1408
TOP = 6
SH = 2816

EPSILON = 1e-06
CLIP_LIMIT = 8.0
ROPE_BASE = 10000.0
MASK_VALUE = -1e30
BF16 = jnp.bfloat16
F32 = jnp.float32


def rms_norm(values, gain_vector):
    return (
        values
        * lax.rsqrt(jnp.mean(values * values, axis=-1, keepdims=True) + EPSILON)
        * gain_vector
    )


def rotate(values, angles):
    half_width = values.shape[-1] // 2
    first_half = values[..., :half_width]
    second_half = values[..., half_width:]
    cosine = jnp.cos(angles)
    sine_part = jnp.sin(angles)
    return jnp.concatenate(
        [
            first_half * cosine - second_half * sine_part,
            second_half * cosine + first_half * sine_part,
        ],
        axis=-1,
    )


def frequencies(count):
    exponent = jnp.arange(count // 2, dtype=jnp.float32) * 2.0 / count
    return ROPE_BASE ** (-exponent)


def layout(lengths_row, slot_ids):
    seq_ends = jnp.cumsum(lengths_row)
    seq_starts = seq_ends - lengths_row
    inside = (slot_ids[:, None] >= seq_starts[None, :]) & (slot_ids[:, None] < seq_ends[None, :])
    is_valid = jnp.any(inside, axis=1)
    numbers = jnp.arange(lengths_row.shape[0], dtype=jnp.int32)
    seq_number = jnp.sum(jnp.where(inside, numbers[None, :], 0), axis=1)
    first_slot = jnp.sum(jnp.where(inside, seq_starts[None, :], 0), axis=1)
    segment = jnp.where(is_valid, seq_number, lengths_row.shape[0] + slot_ids)
    position = jnp.where(is_valid, slot_ids - first_slot, 0)
    return (segment, position, is_valid)


def dot(left, right):
    return jnp.dot(left, right, preferred_element_type=F32)


def dot_tn(left, right):
    return lax.dot_general(left, right, (((0,), (0,)), ((), ())), preferred_element_type=F32)


def dot_nt(left, right):
    return lax.dot_general(left, right, (((1,), (1,)), ((), ())), preferred_element_type=F32)


ROWS = 256


def masked_scores(query, key, seg_col, seg_row, first, scale):
    scores = dot_nt(query, key) * scale
    shape = scores.shape
    row_slot = first + lax.broadcasted_iota(jnp.int32, shape, 0)
    key_slot = lax.broadcasted_iota(jnp.int32, shape, 1)
    allowed = (seg_col == seg_row) & (key_slot <= row_slot)
    return jnp.where(allowed, scores, MASK_VALUE)


def attention_forward_kernel(scale, q_ref, k_ref, v_ref, segc_ref, segr_ref, valid_ref, ctx_ref, lse_ref, max_ref):
    count = q_ref.shape[0]
    best = jnp.full((1, 1), MASK_VALUE, F32)
    for first in range(0, count, ROWS):
        rows, keys = pl.ds(first, ROWS), pl.ds(0, first + ROWS)
        masked = masked_scores(q_ref[rows, :], k_ref[keys, :], segc_ref[rows, :], segr_ref[:, keys], first, scale)
        row_max = jnp.max(masked, axis=1, keepdims=True)
        exponent = jnp.exp(masked - row_max)
        row_sum = jnp.sum(exponent, axis=1, keepdims=True)
        probs = (exponent * (1.0 / row_sum)).astype(BF16)
        ctx_ref[rows, :] = dot(probs, v_ref[keys, :]).astype(BF16)
        lse_ref[rows, :] = row_max + jnp.log(row_sum)
        counted = jnp.where(valid_ref[rows, :] > 0, row_max, MASK_VALUE)
        best = jnp.maximum(best, jnp.max(counted, axis=0, keepdims=True))
    max_ref[...] = jnp.broadcast_to(best, max_ref.shape)


def attention_forward(query, key, value, segment, valid):
    count, width = query.shape
    return pl.pallas_call(
        functools.partial(attention_forward_kernel, width ** (-0.5)),
        out_shape=(
            jax.ShapeDtypeStruct((count, value.shape[1]), BF16),
            jax.ShapeDtypeStruct((count, 1), F32),
            jax.ShapeDtypeStruct((8, 128), F32),
        ),
        compiler_params=pltpu.CompilerParams(vmem_limit_bytes=48 * 2**20),
        cost_estimate=pl.CostEstimate(flops=count * count * 320, bytes_accessed=4 * 2**20, transcendentals=count * count // 2),
        name="attention_forward",
    )(query, key, value, segment[:, None], segment[None, :], valid[:, None].astype(jnp.int32))


def attention_backward_kernel(
    scale, q_ref, k_ref, v_ref, g_ref, segc_ref, segr_ref, lse_ref, cos_ref, sin_ref, out_ref, dk_sum, dv_sum
):
    half = DR // 2
    count = q_ref.shape[0]
    dk_sum[...] = jnp.zeros_like(dk_sum)
    dv_sum[...] = jnp.zeros_like(dv_sum)
    for first in range(0, count, ROWS):
        rows, keys = pl.ds(first, ROWS), pl.ds(0, first + ROWS)
        query, grad = q_ref[rows, :], g_ref[rows, :]
        masked = masked_scores(query, k_ref[keys, :], segc_ref[rows, :], segr_ref[:, keys], first, scale)
        probs = jnp.exp(masked - lse_ref[rows, :])
        prob_grad = dot_nt(grad, v_ref[keys, :])
        mean = jnp.sum(probs * prob_grad, axis=1, keepdims=True)
        score_grad = (probs * (prob_grad - mean)).astype(BF16)
        query_grad = (dot(score_grad, k_ref[keys, :]) * scale).astype(BF16)
        out_ref[rows, :DN] = query_grad[:, :DN]
        rope = query_grad[:, DN:].astype(F32)
        swapped = jnp.concatenate([rope[:, half:], rope[:, :half]], axis=1)
        rope = rope * cos_ref[rows, :DR] - swapped * sin_ref[rows, :DR]
        out_ref[rows, 2 * DN + DV : 2 * DN + DV + DR] = rope.astype(BF16)
        dk_sum[keys, :] += dot_tn(score_grad, query)
        dv_sum[keys, :] += dot_tn(probs.astype(BF16), grad)
    key_grad = (dk_sum[...] * scale).astype(BF16)
    out_ref[:, DN : 2 * DN] = key_grad[:, :DN]
    out_ref[:, 2 * DN : 2 * DN + DV] = dv_sum[...].astype(BF16)
    out_ref[:, 2 * DN + DV + DR :] = key_grad[:, DN:]


def attention_backward(query, key, value, grad, segment, log_total, cosines, sines):
    count, width = query.shape
    return pl.pallas_call(
        functools.partial(attention_backward_kernel, width ** (-0.5)),
        out_shape=jax.ShapeDtypeStruct((count, 2 * width + value.shape[1]), BF16),
        scratch_shapes=[pltpu.VMEM(key.shape, F32), pltpu.VMEM(value.shape, F32)],
        compiler_params=pltpu.CompilerParams(vmem_limit_bytes=48 * 2**20),
        cost_estimate=pl.CostEstimate(flops=count * count * 832, bytes_accessed=6 * 2**20, transcendentals=count * count // 2),
        name="attention_backward",
    )(query, key, value, grad, segment[:, None], segment[None, :], log_total, cosines, sines)


def swap_halves(values):
    half = DR // 2
    pieces = [values[:, i * half : (i + 1) * half] for i in (1, 0, 3, 2)]
    return jnp.concatenate(pieces, axis=1)


def project_kernel(x_ref, gain_ref, w_ref, gain_kv_ref, expand_ref, cos_ref, sin_ref, normed_ref, q_ref, k_ref, v_ref, raw_ref, latent_ref):
    normed = rms_norm(x_ref[...].astype(F32), gain_ref[...]).astype(BF16)
    normed_ref[...] = normed
    both = dot(normed, w_ref[...])
    raw = both[:, :KVR]
    raw_ref[...] = raw
    latent = rms_norm(raw, gain_kv_ref[...]).astype(BF16)
    latent_ref[...] = latent
    expanded = dot(latent, expand_ref[...])
    rope = both[:, KVR + DN :]
    rope = rope * cos_ref[...] + swap_halves(rope) * sin_ref[...]
    q_ref[...] = jnp.concatenate([both[:, KVR : KVR + DN], rope[:, :DR]], axis=1).astype(BF16)
    k_ref[...] = jnp.concatenate([expanded[:, :DN], rope[:, DR:]], axis=1).astype(BF16)
    v_ref[...] = expanded[:, DN:].astype(BF16)


def project(rows, gain, weight, gain_kv, expand, cosines, sines):
    count = rows.shape[0]
    tile = 256

    def by_rows(columns):
        return pl.BlockSpec((tile, columns), lambda i: (i, 0))

    def whole(array):
        return pl.BlockSpec(array.shape, lambda i: (0, 0))

    outs = [(D, BF16), (DN + DR, BF16), (DN + DR, BF16), (DV, BF16), (KVR, F32), (KVR, BF16)]
    return pl.pallas_call(
        project_kernel,
        grid=(count // tile,),
        in_specs=[
            by_rows(D),
            whole(gain[None]),
            whole(weight),
            whole(gain_kv[None]),
            whole(expand),
            by_rows(2 * DR),
            by_rows(2 * DR),
        ],
        out_specs=tuple(by_rows(c) for c, _ in outs),
        out_shape=tuple(jax.ShapeDtypeStruct((count, c), t) for c, t in outs),
        compiler_params=pltpu.CompilerParams(vmem_limit_bytes=48 * 2**20),
        cost_estimate=pl.CostEstimate(flops=2 * count * D * 900, bytes_accessed=24 * 2**20, transcendentals=count),
        name="project",
    )(rows, gain[None], weight, gain_kv[None], expand, cosines, sines)


BLOCKS = 4


def silu_grads(gate, up, grad):
    sig = jax.nn.sigmoid(gate)
    return grad * up * sig * (1.0 + gate * (1.0 - sig)), grad * gate * sig


def pick_of(place_ref, b, capacity):
    tok = place_ref.shape[1]
    return lax.broadcasted_iota(jnp.int32, (capacity, tok), 0) == place_ref[b : b + 1, :]


def as_weights(match):
    return jnp.where(match, 1.0, 0.0).astype(BF16)


def spread_kernel(
    ffn_ref, up_ref, place_ref, gate_ref, in_ref, out_ref,
    x_ref, rg_ref, hidden_ref, grad_ref, gout_ref, gin_ref,
    sum_out, sum_in,
):
    step = pl.program_id(0)
    blocks, tok = place_ref.shape
    capacity = x_ref.shape[0] // blocks
    units = out_ref.shape[0]
    for b in range(blocks):
        match = pick_of(place_ref, b, capacity)
        pick = as_weights(match)
        gate = jnp.sum(jnp.where(match, gate_ref[b : b + 1, :], 0.0), axis=1, keepdims=True)
        tokens, rows = pl.ds(b * tok, tok), pl.ds(b * capacity, capacity)
        x_ref[rows, :] = dot(pick, ffn_ref[tokens, :]).astype(BF16)
        rg_ref[rows, :] = (gate * dot(pick, up_ref[tokens, :])).astype(BF16)
    both = dot(ffn_ref[...], in_ref[...])
    gate, up = both[:, :units], both[:, units:]
    hidden = (gate * jax.nn.sigmoid(gate) * up).astype(BF16)
    hidden_ref[...] = hidden
    grads = silu_grads(gate, up, dot_nt(up_ref[...], out_ref[...]))
    grad = jnp.concatenate(grads, axis=1).astype(BF16)
    grad_ref[...] = grad

    @pl.when(step == 0)
    def _():
        sum_out[...] = jnp.zeros_like(sum_out)
        sum_in[...] = jnp.zeros_like(sum_in)

    sum_out[...] += dot_tn(hidden, up_ref[...])
    sum_in[...] += dot_tn(grad, ffn_ref[...])

    @pl.when(step == pl.num_programs(0) - 1)
    def _():
        gout_ref[...] = sum_out[...].astype(BF16)
        gin_ref[...] = sum_in[...].astype(BF16)


def by_rows(size, columns):
    return pl.BlockSpec((size, columns), lambda i: (i, 0))


def whole(array):
    return pl.BlockSpec(array.shape, lambda i: (0, 0), pipeline_mode=pl.Buffered(1))


def by_step(tok):
    return pl.BlockSpec((None, BLOCKS, tok), lambda i: (i, 0, 0))


def in_steps(rows):
    return rows.reshape(-1, BLOCKS, rows.shape[1])


def spread(ffn, upstream, place, gates, shared_in, shared_out, capacity):
    count = ffn.shape[0]
    seq, tok = place.shape
    steps = seq // BLOCKS
    units = shared_out.shape[0]
    t, rows = BLOCKS * tok, BLOCKS * capacity
    outs = [(rows, D), (rows, D), (t, units), (t, 2 * units)]
    fixed = [(units, D), (2 * units, D)]
    flops = 4 * seq * capacity * tok * D + 2 * count * 6 * D * units
    return pl.pallas_call(
        spread_kernel,
        grid=(steps,),
        in_specs=[by_rows(t, D), by_rows(t, D), by_step(tok), by_step(tok), whole(shared_in), whole(shared_out)],
        out_specs=tuple(by_rows(*o) for o in outs) + tuple(pl.BlockSpec(o, lambda i: (0, 0)) for o in fixed),
        out_shape=tuple(jax.ShapeDtypeStruct((r * steps, c), BF16) for r, c in outs)
        + tuple(jax.ShapeDtypeStruct(o, BF16) for o in fixed),
        scratch_shapes=[pltpu.VMEM(o, F32) for o in fixed],
        compiler_params=pltpu.CompilerParams(vmem_limit_bytes=56 * 2**20),
        cost_estimate=pl.CostEstimate(flops=flops, bytes_accessed=40 * 2**20, transcendentals=2 * count * units),
        name="spread",
    )(ffn, upstream, in_steps(place), in_steps(gates), shared_in, shared_out)


def collect_forward_kernel(res_ref, up_ref, place_ref, gate_ref, hidden_ref, out_ref, mixed_ref, dots_ref):
    blocks, tok = place_ref.shape
    capacity = res_ref.shape[0] // blocks
    for b in range(blocks):
        pick = as_weights(pick_of(place_ref, b, capacity))
        tokens, rows = pl.ds(b * tok, tok), pl.ds(b * capacity, capacity)
        mine = dot_tn(pick, res_ref[rows, :])
        dots_ref[tokens, :] = jnp.sum(up_ref[tokens, :].astype(F32) * mine, axis=1, keepdims=True)
        shared = dot(hidden_ref[tokens, :], out_ref[...])
        mixed_ref[tokens, :] = (gate_ref[tokens, :] * mine + shared).astype(BF16)


def collect_forward(results, upstream, place, gates, hidden, shared_out, capacity):
    count = upstream.shape[0]
    seq, tok = place.shape
    steps = seq // BLOCKS
    t, rows = BLOCKS * tok, BLOCKS * capacity
    units = shared_out.shape[0]
    flops = 2 * seq * capacity * tok * D + 2 * count * D * units
    return pl.pallas_call(
        collect_forward_kernel,
        grid=(steps,),
        in_specs=[by_rows(rows, D), by_rows(t, D), by_step(tok), by_rows(t, 1), by_rows(t, units), whole(shared_out)],
        out_specs=(by_rows(t, D), by_rows(t, 1)),
        out_shape=(jax.ShapeDtypeStruct((count, D), BF16), jax.ShapeDtypeStruct((count, 1), F32)),
        compiler_params=pltpu.CompilerParams(vmem_limit_bytes=48 * 2**20),
        cost_estimate=pl.CostEstimate(flops=flops, bytes_accessed=24 * 2**20, transcendentals=0),
        name="collect_forward",
    )(results, upstream, in_steps(place), gates.reshape(-1, 1), hidden, shared_out)


def collect_backward_kernel(rows_ref, place_ref, grad_ref, in_ref, back_ref):
    blocks, tok = place_ref.shape
    capacity = rows_ref.shape[0] // blocks
    shared = dot_nt(grad_ref[...], in_ref[...])
    for b in range(blocks):
        pick = as_weights(pick_of(place_ref, b, capacity))
        tokens, rows = pl.ds(b * tok, tok), pl.ds(b * capacity, capacity)
        mine = dot_tn(pick, rows_ref[rows, :])
        back_ref[tokens, :] = (mine + shared[b * tok : (b + 1) * tok]).astype(BF16)


def collect_backward(row_grads, place, grads, shared_in, capacity):
    count = grads.shape[0]
    seq, tok = place.shape
    steps = seq // BLOCKS
    t, rows = BLOCKS * tok, BLOCKS * capacity
    flops = 2 * seq * capacity * tok * D + 2 * count * D * grads.shape[1]
    return pl.pallas_call(
        collect_backward_kernel,
        grid=(steps,),
        in_specs=[by_rows(rows, D), by_step(tok), by_rows(t, grads.shape[1]), whole(shared_in)],
        out_specs=by_rows(t, D),
        out_shape=jax.ShapeDtypeStruct((count, D), BF16),
        compiler_params=pltpu.CompilerParams(vmem_limit_bytes=48 * 2**20),
        cost_estimate=pl.CostEstimate(flops=flops, bytes_accessed=18 * 2**20, transcendentals=0),
        name="collect_backward",
    )(row_grads, in_steps(place), grads, shared_in)


def turn_kernel(in_ref, out_ref):
    block = in_ref[...].astype(F32)
    out_ref[...] = block.reshape(-1, block.shape[-1]).T


def turn_rows(rows, tile):
    count, columns = rows.shape
    return pl.pallas_call(
        turn_kernel,
        grid=(count // tile,),
        in_specs=[pl.BlockSpec((tile, columns), lambda i: (i, 0))],
        out_specs=pl.BlockSpec((columns, tile), lambda i: (0, i)),
        out_shape=jax.ShapeDtypeStruct((columns, count), F32),
        compiler_params=pltpu.CompilerParams(vmem_limit_bytes=48 * 2**20),
        cost_estimate=pl.CostEstimate(flops=0, bytes_accessed=6 * rows.size, transcendentals=0),
        name="turn_rows",
    )(rows)


def turn_units(parts):
    seq_count, groups, unit, columns = parts.shape
    if unit % 8 or (seq_count * unit) % 128:
        return parts.transpose(3, 1, 0, 2).reshape(columns, -1).astype(F32)
    wide = seq_count * unit
    tile = 256
    return pl.pallas_call(
        turn_kernel,
        grid=(groups, columns // tile),
        in_specs=[pl.BlockSpec((seq_count, None, unit, tile), lambda g, i: (0, g, 0, i))],
        out_specs=pl.BlockSpec((tile, wide), lambda g, i: (i, g)),
        out_shape=jax.ShapeDtypeStruct((columns, groups * wide), F32),
        compiler_params=pltpu.CompilerParams(vmem_limit_bytes=48 * 2**20),
        cost_estimate=pl.CostEstimate(flops=0, bytes_accessed=6 * parts.size, transcendentals=0),
        name="turn_units",
    )(parts)


LINE = 4
MESH = pl.DeviceIdType.MESH


def place():
    rank = lax.axis_index("seq")
    return rank, lax.div(rank, 4), lax.rem(lax.div(rank, 2), 2), lax.rem(rank, 2)


def rank_at(z, y, x, dz, dy, dx):
    across = y + dy * (1 - 2 * y)
    along = x + dx * (1 - 2 * x)
    return (z + dz) * 4 + across * 2 + along


OFFSETS = [(dz, dy, dx) for dz in (0, -1, 1, -2, 2, -3, 3) for dy in (0, 1) for dx in (0, 1)]


def hops(offset):
    return abs(offset[0]) + offset[1] + offset[2]


def onward(order, offset):
    rel = dict(zip("zyx", offset))
    moved = [i for i, dim in enumerate(order) if rel[dim]]
    last = moved[-1] if moved else -1
    steps = []
    if last >= 0 and order[last] == "z":
        steps.append((1 if rel["z"] < 0 else -1, 0, 0))
    for dim in order[last + 1 :]:
        steps += {"z": [(1, 0, 0), (-1, 0, 0)], "y": [(0, 1, 0)], "x": [(0, 0, 1)]}[dim]
    return [s for s in steps if any(0 <= z + offset[0] < LINE and 0 <= z + s[0] < LINE for z in range(LINE))]


def inside(z, dz):
    return (z + dz >= 0) & (z + dz < LINE)


def guarded(z, steps, body):
    steps = [dz for dz in steps if dz]
    if not steps:
        body()
        return
    good = inside(z, steps[0])
    for dz in steps[1:]:
        good = good & inside(z, dz)
    pl.when(good)(body)


def greet_all():
    rank = lax.axis_index("seq")
    count = lax.axis_size("seq")
    barrier = pltpu.get_barrier_semaphore()
    for k in range(1, count):
        peer = lax.rem(rank + k, count)
        pl.semaphore_signal(barrier, inc=1, device_id={"seq": peer}, device_id_type=MESH)
    pl.semaphore_wait(barrier, count - 1)


def gather_events(streams, ins, outs, send_sems, recv_sems):
    rank, z, y, x = place()
    count = lax.axis_size("seq")
    slots = {}

    def copy(stream, offset, step):
        index, first, rows, order = streams[stream]
        part = pl.ds(first, rows)
        source = rank_at(z, y, x, *offset)
        slot = slots.setdefault((stream, offset, step), len(slots))
        block = outs[index].at[source, part]
        own = offset == (0, 0, 0)
        return pltpu.make_async_remote_copy(
            src_ref=ins[index].at[part] if own else block,
            dst_ref=block,
            send_sem=send_sems.at[slot],
            recv_sem=recv_sems.at[stream * count + source],
            device_id={"seq": rank_at(z, y, x, *step)},
            device_id_type=MESH,
        )

    def arrived(stream, offset):
        index, first, rows, order = streams[stream]
        source = rank_at(z, y, x, *offset)
        block = outs[index].at[source, pl.ds(first, rows)]
        pltpu.make_async_remote_copy(
            src_ref=block,
            dst_ref=block,
            send_sem=send_sems.at[0],
            recv_sem=recv_sems.at[stream * count + source],
            device_id={"seq": rank},
            device_id_type=MESH,
        ).wait_recv()

    todo = sorted(
        ((stream, offset) for stream in range(len(streams)) for offset in OFFSETS),
        key=lambda it: (hops(it[1]), it[0]),
    )

    def act(stream, offset):
        def forward():
            if hops(offset):
                arrived(stream, offset)
            for step in onward(streams[stream][3], offset):
                guarded(z, [step[0]], lambda: copy(stream, offset, step).start())

        guarded(z, [offset[0]], forward)

    def finish():
        for stream, offset in todo:
            for step in onward(streams[stream][3], offset):
                guarded(z, [offset[0], step[0]], lambda: copy(stream, offset, step).wait_send())

    return [functools.partial(act, *it) for it in todo], finish


def gather_kernel(streams, n_main, n_small, *refs):
    n = n_main + n_small
    ins, outs = refs[:n], refs[n : 2 * n]
    send_sems, recv_sems, small_send, small_recv, local_sems = refs[2 * n :]
    rank = lax.axis_index("seq")
    count = lax.axis_size("seq")
    greet_all()
    locals_ = [pltpu.make_async_copy(ins[i], outs[i].at[rank], local_sems.at[i]) for i in range(n)]

    def small_copy(i, k):
        peer = lax.rem(rank + k, count)
        return pltpu.make_async_remote_copy(
            src_ref=ins[n_main + i],
            dst_ref=outs[n_main + i].at[rank],
            send_sem=small_send.at[i * count + k],
            recv_sem=small_recv.at[i * count + rank],
            device_id={"seq": peer},
            device_id_type=MESH,
        )

    actions, finish = gather_events(streams, ins, outs, send_sems, recv_sems)
    for i, action in enumerate(actions):
        action()
        if i == len(streams) - 1:
            for c in locals_:
                c.start()
            for s in range(n_small):
                for k in range(1, count):
                    small_copy(s, k).start()
    finish()
    for i in range(n_small):
        for k in range(1, count):
            small_copy(i, k).wait_send()
        for k in range(1, count):
            source = lax.rem(rank + k, count)
            block = outs[n_main + i].at[source]
            pltpu.make_async_remote_copy(
                src_ref=block,
                dst_ref=block,
                send_sem=small_send.at[0],
                recv_sem=small_recv.at[i * count + source],
                device_id={"seq": rank},
                device_id_type=MESH,
            ).wait_recv()
    for c in locals_:
        c.wait()


def n_sends(streams):
    return sum(len(onward(s[3], o)) for s in streams for o in OFFSETS)


def streams_of(main, parts):
    streams = []
    for i, pieces in enumerate(parts):
        first = 0
        for rows, order in pieces:
            streams.append((i, first, rows, order))
            first += rows
    return streams


def gather_all(main, parts, small, collective_id, count=16):
    streams = streams_of(main, parts)
    arrays = list(main) + list(small)
    any_spec = pl.BlockSpec(memory_space=pl.ANY)
    return pl.pallas_call(
        functools.partial(gather_kernel, streams, len(main), len(small)),
        out_shape=tuple(jax.ShapeDtypeStruct((count,) + a.shape, a.dtype) for a in arrays),
        in_specs=[any_spec] * len(arrays),
        out_specs=tuple([any_spec] * len(arrays)),
        scratch_shapes=[
            pltpu.SemaphoreType.DMA((n_sends(streams),)),
            pltpu.SemaphoreType.DMA((len(streams) * count,)),
            pltpu.SemaphoreType.DMA((max(1, len(small)) * count,)),
            pltpu.SemaphoreType.DMA((max(1, len(small)) * count,)),
            pltpu.SemaphoreType.DMA((len(arrays),)),
        ],
        compiler_params=pltpu.CompilerParams(collective_id=collective_id, has_side_effects=True),
        name="gather_all",
    )(*arrays)


def toward(order, offset):
    rel = dict(zip("zyx", offset))
    dim = [d for d in order if rel[d]][-1]
    return {"z": (1 if rel["z"] > 0 else -1, 0, 0), "y": (0, 1, 0), "x": (0, 0, 1)}[dim]


def seen_from(offset, step):
    return (offset[0] - step[0], offset[1] ^ step[1], offset[2] ^ step[2])


def back(step):
    return (-step[0], step[1], step[2])


ADD_ROWS = 16


def slot_table(order):
    table, used = {}, 0
    for dy in (0, 1):
        for dx in (0, 1):
            for kind in ("x", "y", "up", "down"):
                step = {"x": (0, 0, 1), "y": (0, 1, 0), "up": (1, 0, 0), "down": (-1, 0, 0)}[kind]
                met = [o[0] for o in OFFSETS if o[1:] == (dy, dx) and step in onward(order, o)]
                if not met:
                    continue
                if kind == "down":
                    table[dy, dx, "down"] = (used, False)
                    used += 1
                    continue
                spread = any(met)
                table[dy, dx, kind] = (used, spread)
                used += LINE if spread else 1
    return table, used


def slot_at(table, z, offset, step):
    dz, dy, dx = offset
    kind = "x" if step[2] else "y" if step[1] else "down" if step[0] < 0 and dz == 0 else "up"
    first, spread = table[dy, dx, kind]
    return first + (z + dz) if spread else first


def scatter_kernel(streams, n_main, n_small, *refs):
    n = n_main + n_small
    ins, outs = refs[:n], refs[n : 2 * n]
    scratch = refs[2 * n :]
    bufs = scratch[: len(streams)]
    send_sems, recv_sems, small_send, small_recv, local_sems = scratch[len(streams) :]
    rank, z, y, x = place()
    count = lax.axis_size("seq")
    tables, bases, base = [], [], 0
    for stream in streams:
        table, used = slot_table(stream[3])
        tables.append(table)
        bases.append(base)
        base += used
    greet_all()

    def small_copy(i, k):
        peer = lax.rem(rank + k, count)
        return pltpu.make_async_remote_copy(
            src_ref=ins[n_main + i],
            dst_ref=outs[n_main + i].at[rank],
            send_sem=small_send.at[i * count + k],
            recv_sem=small_recv.at[i * count + rank],
            device_id={"seq": peer},
            device_id_type=MESH,
        )

    todo = sorted(
        ((s, offset) for s in range(len(streams)) for offset in OFFSETS),
        key=lambda it: (-hops(it[1]), it[0]),
    )
    send_slot = {key: i for i, key in enumerate(k for k in todo if hops(k[1]))}

    def send_copy(s, offset, source):
        step = toward(streams[s][3], offset)
        k = slot_at(tables[s], z + step[0], seen_from(offset, step), back(step))
        return pltpu.make_async_remote_copy(
            src_ref=source,
            dst_ref=bufs[s].at[k],
            send_sem=send_sems.at[send_slot[s, offset]],
            recv_sem=recv_sems.at[bases[s] + k],
            device_id={"seq": rank_at(z, y, x, *step)},
            device_id_type=MESH,
        )

    def wait_child(s, k):
        pltpu.make_async_remote_copy(
            src_ref=bufs[s].at[k],
            dst_ref=bufs[s].at[k],
            send_sem=send_sems.at[0],
            recv_sem=recv_sems.at[bases[s] + k],
            device_id={"seq": rank},
            device_id_type=MESH,
        ).wait_recv()

    for s, offset in todo:
        index, first, rows, order = streams[s]
        children = onward(order, offset)
        dest = rank_at(z, y, x, *offset)
        always = [c for c in children if not c[0]]
        sometimes = [c for c in children if c[0]]

        def run(present, s=s, offset=offset, index=index, first=first, rows=rows, dest=dest):
            own = ins[index].at[dest, pl.ds(first, rows)]
            if not present:
                send_copy(s, offset, own).start()
                return
            slots = [slot_at(tables[s], z, offset, step) for step in present]
            for k in slots:
                wait_child(s, k)
            final = not hops(offset)
            target = outs[index].at[pl.ds(first, rows)] if final else bufs[s].at[slots[0]]

            def add(i, carry):
                part = pl.ds(pl.multiple_of(i * ADD_ROWS, ADD_ROWS), ADD_ROWS)
                total = own[part, :].astype(F32)
                for k in slots:
                    total = total + bufs[s][k, part, :].astype(F32)
                target[part, :] = total.astype(target.dtype)
                return carry

            lax.fori_loop(0, rows // ADD_ROWS, add, 0)
            if not final:
                send_copy(s, offset, target).start()

        def cases(run=run, always=always, sometimes=sometimes):
            if not sometimes:
                run(always)
                return
            for mask in range(2 ** len(sometimes)):
                present = [c for i, c in enumerate(sometimes) if mask >> i & 1]
                good = None
                for i, c in enumerate(sometimes):
                    here = inside(z, c[0]) if mask >> i & 1 else jnp.logical_not(inside(z, c[0]))
                    good = here if good is None else good & here
                pl.when(good)(functools.partial(run, present + always))

        guarded(z, [offset[0]], cases)
        if (s, offset) == todo[0]:
            for i in range(n_small):
                for k in range(1, count):
                    small_copy(i, k).start()
                pltpu.make_async_copy(ins[n_main + i], outs[n_main + i].at[rank], local_sems.at[i]).start()
    for s, offset in todo:
        if hops(offset):
            index, first, rows, order = streams[s]
            own = ins[index].at[rank_at(z, y, x, *offset), pl.ds(first, rows)]
            guarded(z, [offset[0]], lambda: send_copy(s, offset, own).wait_send())
    for i in range(n_small):
        for k in range(1, count):
            small_copy(i, k).wait_send()
        for k in range(1, count):
            source = lax.rem(rank + k, count)
            block = outs[n_main + i].at[source]
            pltpu.make_async_remote_copy(
                src_ref=block,
                dst_ref=block,
                send_sem=small_send.at[0],
                recv_sem=small_recv.at[i * count + source],
                device_id={"seq": rank},
                device_id_type=MESH,
            ).wait_recv()
        pltpu.make_async_copy(ins[n_main + i], outs[n_main + i].at[rank], local_sems.at[i]).wait()


def scatter_sum(main, parts, small, collective_id, count=16):
    streams = streams_of(main, parts)
    arrays = list(main) + list(small)
    any_spec = pl.BlockSpec(memory_space=pl.ANY)
    vmem = pl.BlockSpec(memory_space=pltpu.VMEM)
    places = [slot_table(stream[3])[1] for stream in streams]
    buffers = [
        pltpu.VMEM((used, rows, main[index].shape[2]), main[index].dtype)
        for used, (index, first, rows, order) in zip(places, streams)
    ]
    return pl.pallas_call(
        functools.partial(scatter_kernel, streams, len(main), len(small)),
        out_shape=tuple(
            [jax.ShapeDtypeStruct(a.shape[1:], F32) for a in main]
            + [jax.ShapeDtypeStruct((count,) + a.shape, a.dtype) for a in small]
        ),
        in_specs=[vmem] * len(main) + [any_spec] * len(small),
        out_specs=tuple([vmem] * len(main) + [any_spec] * len(small)),
        scratch_shapes=buffers
        + [
            pltpu.SemaphoreType.DMA((len(streams) * len(OFFSETS),)),
            pltpu.SemaphoreType.DMA((sum(places),)),
            pltpu.SemaphoreType.DMA((max(1, len(small)) * count,)),
            pltpu.SemaphoreType.DMA((max(1, len(small)) * count,)),
            pltpu.SemaphoreType.DMA((max(1, len(small)),)),
        ],
        compiler_params=pltpu.CompilerParams(
            collective_id=collective_id, has_side_effects=True, vmem_limit_bytes=60 * 2**20
        ),
        name="scatter_sum",
    )(*arrays)


COLS = 256
PACE = 2


def expert_kernel(
    streams, n_main, x_ref, rg_ref, in_col_ref, out_row_ref, out_col_ref, in_row_ref, *refs
):
    ins, refs = refs[:n_main], refs[n_main:]
    res_ref, back_ref, hidden_out, gate_out, up_out, refs = *refs[:5], refs[5:]
    outs, refs = refs[:n_main], refs[n_main:]
    gu, hidden, dgu, send_sems, recv_sems, local_sems, out_sems = refs
    rank = lax.axis_index("seq")
    i = pl.program_id(0)
    spans = -(-FF // COLS)
    ends = [2 * FF // COLS, 2 * FF // COLS + spans]
    ends += [ends[1] + D // COLS, ends[1] + 2 * D // COLS]
    actions, finish = gather_events(streams, ins, outs, send_sems, recv_sems)
    own = [pltpu.make_async_copy(ins[k], outs[k].at[rank], local_sems.at[k]) for k in range(n_main)]
    kept = [
        pltpu.make_async_copy(hidden, hidden_out, out_sems.at[0]),
        pltpu.make_async_copy(dgu.at[:, pl.ds(0, FF)], gate_out, out_sems.at[1]),
        pltpu.make_async_copy(dgu.at[:, pl.ds(FF, FF)], up_out, out_sems.at[2]),
    ]

    @pl.when(i == 0)
    def _():
        greet_all()
        for action in actions[: len(streams)]:
            action()
        for copy in own:
            copy.start()

    @pl.when(i < ends[0])
    def _():
        cols = pl.ds(pl.multiple_of(i * COLS, COLS), COLS)
        gu[:, cols] = dot(x_ref[...], in_col_ref[...]).astype(BF16)

    def back_span(first, width):
        grad = dot_nt(rg_ref[...], out_row_ref[:width, :])
        at, to = pl.ds(first, width), pl.ds(pl.multiple_of(FF + first, 128), width)
        gate, up = gu[:, at].astype(F32), gu[:, to].astype(F32)
        hidden[:, at] = (gate * jax.nn.sigmoid(gate) * up).astype(BF16)
        gate_grad, up_grad = silu_grads(gate, up, grad)
        dgu[:, at] = gate_grad.astype(BF16)
        dgu[:, to] = up_grad.astype(BF16)

    full = FF // COLS

    @pl.when((i >= ends[0]) & (i < ends[0] + full))
    def _():
        back_span(pl.multiple_of((i - ends[0]) * COLS, COLS), COLS)

    if FF % COLS:

        @pl.when(i == ends[0] + full)
        def _():
            back_span(full * COLS, FF % COLS)

    @pl.when(i == ends[1])
    def _():
        for copy in kept:
            copy.start()

    @pl.when((i >= ends[1]) & (i < ends[2]))
    def _():
        res_ref[...] = dot(hidden[...], out_col_ref[...]).astype(BF16)

    @pl.when(i >= ends[2])
    def _():
        back_ref[...] = dot_nt(dgu[...], in_row_ref[...]).astype(BF16)

    done = len(streams)
    for step in range(ends[3] - 1):
        some = actions[done : done + PACE]
        done += len(some)
        if some:

            @pl.when(i == step)
            def _(some=some):
                for action in some:
                    action()

    @pl.when(i == ends[3] - 1)
    def _():
        for action in actions[done:]:
            action()
        finish()
        for copy in own + kept:
            copy.wait()


def expert_block(x, rg, w_in, w_out, main, parts, collective_id, count=16):
    rows = x.shape[0]
    streams = streams_of(main, parts)
    spans = -(-FF // COLS)
    first = 2 * FF // COLS
    second = first + spans
    third = second + D // COLS
    steps = third + D // COLS

    def held(array):
        return pl.BlockSpec(array.shape, lambda i: (0, 0), pipeline_mode=pl.Buffered(1))

    def during(start, stop):
        return lambda i: jnp.minimum(jnp.maximum(i - start, 0), stop - start - 1)

    one, two, three, four = during(0, first), during(first, second), during(second, third), during(third, steps)
    any_spec = pl.BlockSpec(memory_space=pl.ANY)
    n = len(main)
    results = pl.pallas_call(
        functools.partial(expert_kernel, streams, n),
        grid=(steps,),
        in_specs=[
            held(x),
            held(rg),
            pl.BlockSpec((D, COLS), lambda i: (0, one(i))),
            pl.BlockSpec((COLS, D), lambda i: (two(i), 0)),
            pl.BlockSpec((FF, COLS), lambda i: (0, three(i))),
            pl.BlockSpec((COLS, 2 * FF), lambda i: (four(i), 0)),
        ]
        + [any_spec] * n,
        out_specs=(
            pl.BlockSpec((rows, COLS), lambda i: (0, three(i))),
            pl.BlockSpec((rows, COLS), lambda i: (0, four(i))),
            any_spec,
            any_spec,
            any_spec,
        )
        + (any_spec,) * n,
        out_shape=(
            jax.ShapeDtypeStruct((rows, D), BF16),
            jax.ShapeDtypeStruct((rows, D), BF16),
            jax.ShapeDtypeStruct((rows, FF), BF16),
            jax.ShapeDtypeStruct((rows, FF), BF16),
            jax.ShapeDtypeStruct((rows, FF), BF16),
        )
        + tuple(jax.ShapeDtypeStruct((count,) + a.shape, a.dtype) for a in main),
        scratch_shapes=[
            pltpu.VMEM((rows, 2 * FF), BF16),
            pltpu.VMEM((rows, FF), BF16),
            pltpu.VMEM((rows, 2 * FF), BF16),
            pltpu.SemaphoreType.DMA((n_sends(streams),)),
            pltpu.SemaphoreType.DMA((len(streams) * count,)),
            pltpu.SemaphoreType.DMA((n,)),
            pltpu.SemaphoreType.DMA((3,)),
        ],
        compiler_params=pltpu.CompilerParams(
            collective_id=collective_id, has_side_effects=True, vmem_limit_bytes=60 * 2**20
        ),
        cost_estimate=pl.CostEstimate(flops=12 * rows * D * FF, bytes_accessed=100 * 2**20, transcendentals=2 * rows * FF),
        name="expert_block",
    )(x, rg, w_in, w_out, w_out, w_in, *main)
    return results[:5], results[5:]


def gather_seq(rows):
    return lax.all_gather(rows, "seq", axis=0, tiled=True)


def scatter_seq(partial):
    return lax.psum_scatter(partial, "seq", scatter_dimension=0, tiled=True)


def gather_fsdp(rows, axis=0):
    return lax.all_gather(rows, "fsdp", axis=axis, tiled=True)


def scatter_fsdp(partial, axis=0):
    count, me = lax.axis_size("fsdp"), lax.axis_index("fsdp")
    size = partial.shape[axis] // count
    total = lax.dynamic_slice_in_dim(partial, me * size, size, axis).astype(F32)
    for k in range(1, count):
        piece = lax.dynamic_slice_in_dim(partial, lax.rem(me + k, count) * size, size, axis)
        total = total + shift_fsdp(piece, k).astype(F32)
    return total


def shift_fsdp(rows, k):
    count = lax.axis_size("fsdp")
    return lax.ppermute(rows, "fsdp", [(i, (i + k) % count) for i in range(count)])


def sum_everywhere(rows):
    count = lax.axis_size("seq")
    total = rows
    bit = 1
    while bit < count:
        total = total + lax.ppermute(total, "seq", [(i, i ^ bit) for i in range(count)])
        bit *= 2
    kept = total
    for k in range(1, lax.axis_size("fsdp")):
        total = total + shift_fsdp(kept, k)
    return total


ROW_PARTS = [(48, "zxy"), (48, "zyx"), (16, "xyz"), (16, "yxz")]


def split_rows(rows, part=8):
    tile = 16
    tiles = rows // tile
    short = tiles // part
    long = (tiles - 2 * short) // 2
    sizes = [tiles - 2 * short - long, long, short, short]
    orders = ["zxy", "zyx", "xyz", "yxz"]
    return [(n * tile, order) for n, order in zip(sizes, orders) if n]


def on_device(
    tokens,
    cotangent,
    lengths,
    routes,
    g_attn,
    w_q,
    w_kva,
    g_kv,
    w_kvb,
    w_o,
    g_ffn,
    w_router,
    w_shared_in,
    w_shared_out,
    w_expert_in,
    w_expert_out,
):
    seq_count = lax.axis_size("seq")
    fsdp_count = lax.axis_size("fsdp")
    rank = lax.axis_index("seq")
    tok_count = tokens.shape[0]
    group_size = tok_count * seq_count
    query_width = DN + DR
    kv_width = DN + DV
    experts = seq_count
    capacity = min(tok_count, 2 * tok_count * TOP // experts)
    buffer_rows = seq_count * capacity
    unit = SH // (seq_count * fsdp_count)
    units = unit * fsdp_count
    row_part = w_q.shape[0]

    def own(rows, axis=0):
        return lax.dynamic_slice_in_dim(rows, rank * tok_count, tok_count, axis)

    expert_ids = jnp.arange(experts, dtype=jnp.int32)
    route_mask = jnp.any(routes[None] == expert_ids[:, None, None], axis=2).astype(BF16)
    token_all, mask_all = gather_all([tokens], [ROW_PARTS], [route_mask], 1)
    token_all = token_all.reshape(group_size, D)

    small = gather_fsdp(jnp.concatenate([g_attn, g_kv, g_ffn, w_router.reshape(-1)])[None])
    cuts = [0, g_attn.size, g_kv.size, g_ffn.size, w_router.size]
    ends = [sum(cuts[: i + 1]) for i in range(len(cuts))]
    gain_attn = small[:, ends[0] : ends[1]].reshape(-1).astype(F32)
    gain_latent = small[:, ends[1] : ends[2]].reshape(-1).astype(F32)
    gain_ffn = small[:, ends[2] : ends[3]].reshape(-1).astype(F32)
    router_weight = small[:, ends[3] : ends[4]].reshape(D, experts)
    head_query_part = lax.dynamic_slice_in_dim(w_q, rank * query_width, query_width, 1)
    head_expand = gather_fsdp(lax.dynamic_slice_in_dim(w_kvb, rank * kv_width, kv_width, 1))
    head_weights = gather_fsdp(
        jnp.concatenate([w_kva[:, :KVR], head_query_part, w_kva[:, KVR:]], axis=1)
    )
    output_weight = gather_fsdp(w_o)
    expert_in = gather_fsdp(w_expert_in[0])
    expert_out = gather_fsdp(w_expert_out[0])
    query_weight = gather_fsdp(w_q)
    expand_weight = gather_fsdp(w_kvb)

    slot_ids = jnp.arange(group_size, dtype=jnp.int32)
    segment, position, valid_all = layout(lengths[0], slot_ids)
    angles = own(position)[:, None].astype(F32) * frequencies(DR)[None, :]
    wide_angles = position[:, None].astype(F32) * jnp.tile(frequencies(DR), 4)[None, :]
    cosines = jnp.cos(wide_angles)
    signs = jnp.where(jnp.arange(2 * DR) % DR < DR // 2, -1.0, 1.0).astype(F32)
    sines = jnp.sin(wide_angles) * signs[None, :]

    upstream_own = jnp.where(own(valid_all)[:, None], cotangent, 0).astype(BF16)
    upstream_all = gather_seq(upstream_own)

    normed_all, query, key, value, latent_full, latent_all = project(
        token_all, gain_attn, head_weights, gain_latent, head_expand, cosines, sines
    )
    context, log_total, head_largest = attention_forward(query, key, value, segment, valid_all)
    late_rank, context, upstream_all = lax.optimization_barrier((rank, context, upstream_all))
    lanes = -(-units // 128) * 128
    unit_slices = [
        lax.dynamic_slice_in_dim(w_shared_in, i * (SH // fsdp_count) + late_rank * unit, unit, 1)
        for i in range(2 * fsdp_count)
    ]
    filler = jnp.zeros((row_part, lanes - units), BF16)
    shared_in_part = jnp.concatenate(
        unit_slices[:fsdp_count] + [filler] + unit_slices[fsdp_count:] + [filler], axis=1
    )
    shared_in = gather_fsdp(shared_in_part)
    shared_out = gather_fsdp(lax.dynamic_slice_in_dim(w_shared_out, late_rank * unit, unit, 0))
    shared_out = jnp.pad(shared_out, ((0, lanes - units), (0, 0)))

    context_low = lax.all_to_all(context, "seq", split_axis=0, concat_axis=1, tiled=True)
    inputs = tokens.astype(F32)
    middle = inputs + dot(context_low, output_weight)
    ffn_low = rms_norm(middle, gain_ffn).astype(BF16)
    ffn_all, largest_all = gather_all([ffn_low], [ROW_PARTS], [head_largest], 2)
    ffn_all = ffn_all.reshape(group_size, D)
    head_max = largest_all[:, 0, :]
    for k in range(1, fsdp_count):
        head_max = jnp.maximum(head_max, shift_fsdp(largest_all[:, 0, :], k))
    global_max = head_max[:, 0]

    router_probs = jax.nn.softmax(dot(ffn_all, router_weight), axis=-1)
    chosen = lax.dynamic_slice_in_dim(mask_all, rank, 1, 1).reshape(seq_count, tok_count) > 0
    gates = lax.dynamic_slice_in_dim(router_probs, rank, 1, 1).reshape(seq_count, tok_count)
    place = jnp.cumsum(chosen.astype(jnp.int32), axis=1) - 1
    place = jnp.where(chosen, place, capacity)

    arrived, result_grad, shared_hidden, shared_grad, grad_shared_out, grad_shared_in = spread(
        ffn_all, upstream_all, place, gates, shared_in, shared_out, capacity
    )
    part_shared_out = scatter_fsdp(grad_shared_out[:units]).astype(BF16)
    part_shared_in = jnp.concatenate([grad_shared_in[:units], grad_shared_in[lanes : lanes + units]], axis=0)
    part_shared_in = scatter_fsdp(part_shared_in, 1).astype(BF16)
    part_shared_out = jnp.pad(part_shared_out, ((0, -unit % 16), (0, 0)))

    (result, row_grad, hidden, d_gate, d_up), (all_shared_in, all_shared_out) = expert_block(
        arrived,
        result_grad,
        expert_in,
        expert_out,
        [part_shared_in, part_shared_out],
        [split_rows(part_shared_in.shape[0], 6), split_rows(part_shared_out.shape[0], 6)],
        4,
    )
    mixed_part, gate_grad = collect_forward(
        result, upstream_all, place, gates, shared_hidden, shared_out, capacity
    )
    ffn_part = collect_backward(row_grad, place, shared_grad, shared_in, capacity)
    mixed_part, query_weight, expand_weight = lax.optimization_barrier(
        (mixed_part, query_weight, expand_weight)
    )
    mixed_sum, ffn_sum, prob_grads = scatter_sum(
        [part.reshape(seq_count, tok_count, D) for part in (mixed_part, ffn_part)],
        [ROW_PARTS, ROW_PARTS],
        [gate_grad.reshape(seq_count, tok_count)],
        3,
    )
    mixed = (middle + mixed_sum).astype(BF16)
    prob_grads = prob_grads.reshape(experts, group_size).T

    logit_grads = (
        router_probs * (prob_grads - jnp.sum(router_probs * prob_grads, axis=-1, keepdims=True))
    ).astype(BF16)
    grad_router = dot_tn(ffn_all, logit_grads)
    sum_router = scatter_fsdp(grad_router.astype(BF16))
    ffn_grad = ffn_sum + dot_nt(own(logit_grads), router_weight)

    ffn_pull = jax.vjp(rms_norm, middle, gain_ffn)[1]
    middle_norm_grad, grad_gain_ffn = ffn_pull(ffn_grad)
    middle_grad = upstream_own.astype(F32) + middle_norm_grad
    middle_low = middle_grad.astype(BF16)
    context_grad = dot_nt(middle_low, output_weight).astype(BF16)
    head_grad = lax.all_to_all(context_grad, "seq", split_axis=1, concat_axis=0, tiled=True)
    grad_output = scatter_fsdp(dot_tn(context_low, middle_low).astype(BF16)).astype(BF16)
    output_rows = row_part // seq_count
    (part_output,) = scatter_sum(
        [grad_output.reshape(seq_count, output_rows, D)], [split_rows(output_rows)], [], 5
    )

    head_grad, part_output = lax.optimization_barrier((head_grad, part_output.astype(BF16)))
    all_output = gather_seq(part_output)
    head_back = attention_backward(query, key, value, head_grad, segment, log_total, cosines, sines)
    head_back, arrived, result_grad, hidden, d_gate, d_up = lax.optimization_barrier(
        (head_back, arrived, result_grad, hidden, d_gate, d_up)
    )
    back = lax.all_to_all(
        head_back.reshape(seq_count, tok_count, -1), "seq", split_axis=0, concat_axis=0, tiled=True
    )
    grad_expert_out = dot_tn(hidden, result_grad).astype(BF16)
    grad_expert_in = dot_tn(arrived, jnp.concatenate([d_gate, d_up], axis=1)).astype(BF16)
    rope_at = 2 * DN + DV
    head_pre_grad = jnp.concatenate([head_back[:, :DN], head_back[:, rope_at : rope_at + DR]], axis=1)
    grad_query = dot_tn(head_pre_grad, normed_all).astype(BF16)
    grad_expand = dot_tn(head_back[:, DN:rope_at], latent_all).astype(BF16)
    part_query = scatter_fsdp(grad_query, 1).astype(BF16)
    part_expand = scatter_fsdp(grad_expand, 1).astype(BF16)
    all_query = gather_seq(part_query)
    all_expand = gather_seq(part_expand)
    back, grad_expert_out, grad_expert_in, part_query, part_expand = lax.optimization_barrier(
        (back, grad_expert_out, grad_expert_in, part_query, part_expand)
    )
    sum_expert_in = scatter_fsdp(grad_expert_in)[None]
    sum_expert_out = scatter_fsdp(grad_expert_out)[None]

    back = back.transpose(1, 0, 2)
    pre_grad = jnp.concatenate([back[..., :DN], back[..., rope_at : rope_at + DR]], axis=-1)
    pre_grad = pre_grad.reshape(tok_count, H * query_width)
    expand_grad = back[..., DN:rope_at].reshape(tok_count, H * kv_width)
    latent_grad = dot_nt(expand_grad, expand_weight)
    rope_grad = rotate(jnp.sum(back[..., rope_at + DR :].astype(F32), axis=1), -angles)
    latent_pull = jax.vjp(rms_norm, own(latent_full), gain_latent)[1]
    compressed_grad, grad_gain_latent = latent_pull(latent_grad)
    full_grad = jnp.concatenate([compressed_grad, rope_grad], axis=1).astype(BF16)
    full_grad, all_output = lax.optimization_barrier((full_grad, all_output))
    full_all = gather_seq(full_grad)
    sum_latent = scatter_fsdp(dot_tn(normed_all, full_all).astype(BF16))
    spread_grad = jnp.pad(full_grad[:, :KVR], ((0, 0), (0, query_width + DR)))
    spread_grad = spread_grad + jnp.pad(full_grad[:, KVR:], ((0, 0), (KVR + query_width, 0)))
    normed_grad = dot_nt(pre_grad, query_weight) + dot_nt(spread_grad, head_weights)
    normed_grad, all_query = lax.optimization_barrier((normed_grad, all_query))
    input_pull = jax.vjp(rms_norm, inputs, gain_attn)[1]
    input_norm_grad, grad_gain_attn = input_pull(normed_grad)
    grad_inputs = middle_grad + input_norm_grad

    gain_sum = sum_everywhere(
        jnp.concatenate([grad_gain_attn, grad_gain_latent, grad_gain_ffn]).reshape(-1, 128)
    ).reshape(-1)
    sum_shared_out = all_shared_out[:, :unit].reshape(w_shared_out.shape).astype(F32)
    sum_shared_in = turn_units(all_shared_in.reshape(seq_count, 2 * fsdp_count, unit, row_part))
    sum_query = turn_rows(all_query, 384)
    sum_expand = turn_rows(all_expand, 512)
    sum_output = all_output.astype(F32)
    fsdp_rank = lax.axis_index("fsdp")

    def own_part(first, like):
        return lax.dynamic_slice_in_dim(gain_sum, first + fsdp_rank * like.size, like.size, 0)

    sum_gain_attn = own_part(0, g_attn)
    sum_gain_latent = own_part(D, g_kv)
    sum_gain_ffn = own_part(D + KVR, g_ffn)

    clip_gamma = CLIP_LIMIT / jnp.maximum(global_max, CLIP_LIMIT)
    clip_root = jnp.sqrt(clip_gamma)
    query_factor = jnp.concatenate(
        [
            jnp.broadcast_to(clip_root[:, None], (H, DN)),
            jnp.broadcast_to(clip_gamma[:, None], (H, DR)),
        ],
        axis=1,
    ).reshape(1, -1)
    clipped_query = (w_q.astype(F32) * query_factor).astype(BF16)
    return (
        mixed,
        grad_inputs,
        sum_gain_attn,
        sum_query,
        sum_latent,
        sum_gain_latent,
        sum_expand,
        sum_output,
        sum_gain_ffn,
        sum_router,
        sum_shared_in,
        sum_shared_out,
        sum_expert_in,
        sum_expert_out,
        clipped_query,
    )


def solution(mesh):
    in_specs = (
        P(("fsdp", "seq"), None),
        P(("fsdp", "seq"), None),
        P("fsdp", None),
        P(("fsdp", "seq"), None),
        P("fsdp"),
        P("fsdp", None),
        P("fsdp", None),
        P("fsdp"),
        P("fsdp", None),
        P("fsdp", None),
        P("fsdp"),
        P("fsdp", None),
        P("fsdp", None),
        P("fsdp", None),
        P("seq", "fsdp", None),
        P("seq", "fsdp", None),
    )
    out_specs = (
        P(("fsdp", "seq"), None),
        P(("fsdp", "seq"), None),
        P("fsdp"),
        P("fsdp", None),
        P("fsdp", None),
        P("fsdp"),
        P("fsdp", None),
        P("fsdp", None),
        P("fsdp"),
        P("fsdp", None),
        P("fsdp", None),
        P("fsdp", None),
        P("seq", "fsdp", None),
        P("seq", "fsdp", None),
        P("fsdp", None),
    )
    return jax.shard_map(
        on_device, mesh=mesh, in_specs=in_specs, out_specs=out_specs, check_vma=False
    )
```

```python
import functools

import jax
import jax.numpy as jnp
from jax import lax
from jax.experimental import pallas as pl
from jax.experimental.pallas import tpu as pltpu
from jax.sharding import PartitionSpec as P

D = 2048
H = 16
DN = 128
DR = 64
DV = 128
KVR = 512
FF = 1408
TOP = 6
SH = 2816

EPSILON = 1e-06
CLIP_LIMIT = 8.0
ROPE_BASE = 10000.0
MASK_VALUE = -1e30
BF16 = jnp.bfloat16
F32 = jnp.float32


def rms_norm(values, gain_vector):
    return (
        values
        * lax.rsqrt(jnp.mean(values * values, axis=-1, keepdims=True) + EPSILON)
        * gain_vector
    )


def rotate(values, angles):
    half_width = values.shape[-1] // 2
    first_half = values[..., :half_width]
    second_half = values[..., half_width:]
    cosine = jnp.cos(angles)
    sine_part = jnp.sin(angles)
    return jnp.concatenate(
        [
            first_half * cosine - second_half * sine_part,
            second_half * cosine + first_half * sine_part,
        ],
        axis=-1,
    )


def frequencies(count):
    exponent = jnp.arange(count // 2, dtype=jnp.float32) * 2.0 / count
    return ROPE_BASE ** (-exponent)


def layout(lengths_row, slot_ids):
    seq_ends = jnp.cumsum(lengths_row)
    seq_starts = seq_ends - lengths_row
    inside = (slot_ids[:, None] >= seq_starts[None, :]) & (slot_ids[:, None] < seq_ends[None, :])
    is_valid = jnp.any(inside, axis=1)
    numbers = jnp.arange(lengths_row.shape[0], dtype=jnp.int32)
    seq_number = jnp.sum(jnp.where(inside, numbers[None, :], 0), axis=1)
    first_slot = jnp.sum(jnp.where(inside, seq_starts[None, :], 0), axis=1)
    segment = jnp.where(is_valid, seq_number, lengths_row.shape[0] + slot_ids)
    position = jnp.where(is_valid, slot_ids - first_slot, 0)
    return (segment, position, is_valid)


def dot(left, right):
    return jnp.dot(left, right, preferred_element_type=F32)


def dot_tn(left, right):
    return lax.dot_general(left, right, (((0,), (0,)), ((), ())), preferred_element_type=F32)


def dot_nt(left, right):
    return lax.dot_general(left, right, (((1,), (1,)), ((), ())), preferred_element_type=F32)


ROWS = 256


def masked_scores(query, key, seg_col, seg_row, first, scale):
    scores = dot_nt(query, key) * scale
    shape = scores.shape
    row_slot = first + lax.broadcasted_iota(jnp.int32, shape, 0)
    key_slot = lax.broadcasted_iota(jnp.int32, shape, 1)
    allowed = (seg_col == seg_row) & (key_slot <= row_slot)
    return jnp.where(allowed, scores, MASK_VALUE)


def attention_forward_kernel(scale, q_ref, k_ref, v_ref, segc_ref, segr_ref, valid_ref, ctx_ref, lse_ref, max_ref):
    count = q_ref.shape[0]
    best = jnp.full((1, 1), MASK_VALUE, F32)
    for first in range(0, count, ROWS):
        rows, keys = pl.ds(first, ROWS), pl.ds(0, first + ROWS)
        masked = masked_scores(q_ref[rows, :], k_ref[keys, :], segc_ref[rows, :], segr_ref[:, keys], first, scale)
        row_max = jnp.max(masked, axis=1, keepdims=True)
        exponent = jnp.exp(masked - row_max)
        row_sum = jnp.sum(exponent, axis=1, keepdims=True)
        probs = (exponent * (1.0 / row_sum)).astype(BF16)
        ctx_ref[rows, :] = dot(probs, v_ref[keys, :]).astype(BF16)
        lse_ref[rows, :] = row_max + jnp.log(row_sum)
        counted = jnp.where(valid_ref[rows, :] > 0, row_max, MASK_VALUE)
        best = jnp.maximum(best, jnp.max(counted, axis=0, keepdims=True))
    max_ref[...] = jnp.broadcast_to(best, max_ref.shape)


def attention_forward(query, key, value, segment, valid):
    count, width = query.shape
    return pl.pallas_call(
        functools.partial(attention_forward_kernel, width ** (-0.5)),
        out_shape=(
            jax.ShapeDtypeStruct((count, value.shape[1]), BF16),
            jax.ShapeDtypeStruct((count, 1), F32),
            jax.ShapeDtypeStruct((8, 128), F32),
        ),
        compiler_params=pltpu.CompilerParams(vmem_limit_bytes=48 * 2**20),
        cost_estimate=pl.CostEstimate(flops=count * count * 320, bytes_accessed=4 * 2**20, transcendentals=count * count // 2),
        name="attention_forward",
    )(query, key, value, segment[:, None], segment[None, :], valid[:, None].astype(jnp.int32))


def attention_backward_kernel(
    scale, q_ref, k_ref, v_ref, g_ref, segc_ref, segr_ref, lse_ref, cos_ref, sin_ref, out_ref, dk_sum, dv_sum
):
    half = DR // 2
    count = q_ref.shape[0]
    dk_sum[...] = jnp.zeros_like(dk_sum)
    dv_sum[...] = jnp.zeros_like(dv_sum)
    for first in range(0, count, ROWS):
        rows, keys = pl.ds(first, ROWS), pl.ds(0, first + ROWS)
        query, grad = q_ref[rows, :], g_ref[rows, :]
        masked = masked_scores(query, k_ref[keys, :], segc_ref[rows, :], segr_ref[:, keys], first, scale)
        probs = jnp.exp(masked - lse_ref[rows, :])
        prob_grad = dot_nt(grad, v_ref[keys, :])
        mean = jnp.sum(probs * prob_grad, axis=1, keepdims=True)
        score_grad = (probs * (prob_grad - mean)).astype(BF16)
        query_grad = (dot(score_grad, k_ref[keys, :]) * scale).astype(BF16)
        out_ref[rows, :DN] = query_grad[:, :DN]
        rope = query_grad[:, DN:].astype(F32)
        swapped = jnp.concatenate([rope[:, half:], rope[:, :half]], axis=1)
        rope = rope * cos_ref[rows, :DR] - swapped * sin_ref[rows, :DR]
        out_ref[rows, 2 * DN + DV : 2 * DN + DV + DR] = rope.astype(BF16)
        dk_sum[keys, :] += dot_tn(score_grad, query)
        dv_sum[keys, :] += dot_tn(probs.astype(BF16), grad)
    key_grad = (dk_sum[...] * scale).astype(BF16)
    out_ref[:, DN : 2 * DN] = key_grad[:, :DN]
    out_ref[:, 2 * DN : 2 * DN + DV] = dv_sum[...].astype(BF16)
    out_ref[:, 2 * DN + DV + DR :] = key_grad[:, DN:]


def attention_backward(query, key, value, grad, segment, log_total, cosines, sines):
    count, width = query.shape
    return pl.pallas_call(
        functools.partial(attention_backward_kernel, width ** (-0.5)),
        out_shape=jax.ShapeDtypeStruct((count, 2 * width + value.shape[1]), BF16),
        scratch_shapes=[pltpu.VMEM(key.shape, F32), pltpu.VMEM(value.shape, F32)],
        compiler_params=pltpu.CompilerParams(vmem_limit_bytes=48 * 2**20),
        cost_estimate=pl.CostEstimate(flops=count * count * 832, bytes_accessed=6 * 2**20, transcendentals=count * count // 2),
        name="attention_backward",
    )(query, key, value, grad, segment[:, None], segment[None, :], log_total, cosines, sines)


def swap_halves(values):
    half = DR // 2
    pieces = [values[:, i * half : (i + 1) * half] for i in (1, 0, 3, 2)]
    return jnp.concatenate(pieces, axis=1)


def project_kernel(x_ref, gain_ref, w_ref, gain_kv_ref, expand_ref, cos_ref, sin_ref, normed_ref, q_ref, k_ref, v_ref, raw_ref, latent_ref):
    normed = rms_norm(x_ref[...].astype(F32), gain_ref[...]).astype(BF16)
    normed_ref[...] = normed
    both = dot(normed, w_ref[...])
    raw = both[:, :KVR]
    raw_ref[...] = raw
    latent = rms_norm(raw, gain_kv_ref[...]).astype(BF16)
    latent_ref[...] = latent
    expanded = dot(latent, expand_ref[...])
    rope = both[:, KVR + DN :]
    rope = rope * cos_ref[...] + swap_halves(rope) * sin_ref[...]
    q_ref[...] = jnp.concatenate([both[:, KVR : KVR + DN], rope[:, :DR]], axis=1).astype(BF16)
    k_ref[...] = jnp.concatenate([expanded[:, :DN], rope[:, DR:]], axis=1).astype(BF16)
    v_ref[...] = expanded[:, DN:].astype(BF16)


def project(rows, gain, weight, gain_kv, expand, cosines, sines):
    count = rows.shape[0]
    tile = 256

    def by_rows(columns):
        return pl.BlockSpec((tile, columns), lambda i: (i, 0))

    def whole(array):
        return pl.BlockSpec(array.shape, lambda i: (0, 0))

    outs = [(D, BF16), (DN + DR, BF16), (DN + DR, BF16), (DV, BF16), (KVR, F32), (KVR, BF16)]
    return pl.pallas_call(
        project_kernel,
        grid=(count // tile,),
        in_specs=[
            by_rows(D),
            whole(gain[None]),
            whole(weight),
            whole(gain_kv[None]),
            whole(expand),
            by_rows(2 * DR),
            by_rows(2 * DR),
        ],
        out_specs=tuple(by_rows(c) for c, _ in outs),
        out_shape=tuple(jax.ShapeDtypeStruct((count, c), t) for c, t in outs),
        compiler_params=pltpu.CompilerParams(vmem_limit_bytes=48 * 2**20),
        cost_estimate=pl.CostEstimate(flops=2 * count * D * 900, bytes_accessed=24 * 2**20, transcendentals=count),
        name="project",
    )(rows, gain[None], weight, gain_kv[None], expand, cosines, sines)


BLOCKS = 4


def silu_grads(gate, up, grad):
    sig = jax.nn.sigmoid(gate)
    return grad * up * sig * (1.0 + gate * (1.0 - sig)), grad * gate * sig


def pick_of(place_ref, b, capacity):
    tok = place_ref.shape[1]
    return lax.broadcasted_iota(jnp.int32, (capacity, tok), 0) == place_ref[b : b + 1, :]


def as_weights(match):
    return jnp.where(match, 1.0, 0.0).astype(BF16)


def spread_kernel(
    ffn_ref, up_ref, place_ref, gate_ref, in_ref, out_ref,
    x_ref, rg_ref, hidden_ref, grad_ref, gout_ref, gin_ref,
    sum_out, sum_in,
):
    step = pl.program_id(0)
    blocks, tok = place_ref.shape
    capacity = x_ref.shape[0] // blocks
    units = out_ref.shape[0]
    for b in range(blocks):
        match = pick_of(place_ref, b, capacity)
        pick = as_weights(match)
        gate = jnp.sum(jnp.where(match, gate_ref[b : b + 1, :], 0.0), axis=1, keepdims=True)
        tokens, rows = pl.ds(b * tok, tok), pl.ds(b * capacity, capacity)
        x_ref[rows, :] = dot(pick, ffn_ref[tokens, :]).astype(BF16)
        rg_ref[rows, :] = (gate * dot(pick, up_ref[tokens, :])).astype(BF16)
    both = dot(ffn_ref[...], in_ref[...])
    gate, up = both[:, :units], both[:, units:]
    hidden = (gate * jax.nn.sigmoid(gate) * up).astype(BF16)
    hidden_ref[...] = hidden
    grads = silu_grads(gate, up, dot_nt(up_ref[...], out_ref[...]))
    grad = jnp.concatenate(grads, axis=1).astype(BF16)
    grad_ref[...] = grad

    @pl.when(step == 0)
    def _():
        sum_out[...] = jnp.zeros_like(sum_out)
        sum_in[...] = jnp.zeros_like(sum_in)

    sum_out[...] += dot_tn(hidden, up_ref[...])
    sum_in[...] += dot_tn(grad, ffn_ref[...])

    @pl.when(step == pl.num_programs(0) - 1)
    def _():
        gout_ref[...] = sum_out[...].astype(BF16)
        gin_ref[...] = sum_in[...].astype(BF16)


def by_rows(size, columns):
    return pl.BlockSpec((size, columns), lambda i: (i, 0))


def whole(array):
    return pl.BlockSpec(array.shape, lambda i: (0, 0), pipeline_mode=pl.Buffered(1))


def by_step(tok):
    return pl.BlockSpec((None, BLOCKS, tok), lambda i: (i, 0, 0))


def in_steps(rows):
    return rows.reshape(-1, BLOCKS, rows.shape[1])


def spread(ffn, upstream, place, gates, shared_in, shared_out, capacity):
    count = ffn.shape[0]
    seq, tok = place.shape
    steps = seq // BLOCKS
    units = shared_out.shape[0]
    t, rows = BLOCKS * tok, BLOCKS * capacity
    outs = [(rows, D), (rows, D), (t, units), (t, 2 * units)]
    fixed = [(units, D), (2 * units, D)]
    flops = 4 * seq * capacity * tok * D + 2 * count * 6 * D * units
    return pl.pallas_call(
        spread_kernel,
        grid=(steps,),
        in_specs=[by_rows(t, D), by_rows(t, D), by_step(tok), by_step(tok), whole(shared_in), whole(shared_out)],
        out_specs=tuple(by_rows(*o) for o in outs) + tuple(pl.BlockSpec(o, lambda i: (0, 0)) for o in fixed),
        out_shape=tuple(jax.ShapeDtypeStruct((r * steps, c), BF16) for r, c in outs)
        + tuple(jax.ShapeDtypeStruct(o, BF16) for o in fixed),
        scratch_shapes=[pltpu.VMEM(o, F32) for o in fixed],
        compiler_params=pltpu.CompilerParams(vmem_limit_bytes=56 * 2**20),
        cost_estimate=pl.CostEstimate(flops=flops, bytes_accessed=40 * 2**20, transcendentals=2 * count * units),
        name="spread",
    )(ffn, upstream, in_steps(place), in_steps(gates), shared_in, shared_out)


def turn_kernel(in_ref, out_ref):
    block = in_ref[...].astype(F32)
    out_ref[...] = block.reshape(-1, block.shape[-1]).T


def turn_rows(rows, tile):
    count, columns = rows.shape
    return pl.pallas_call(
        turn_kernel,
        grid=(count // tile,),
        in_specs=[pl.BlockSpec((tile, columns), lambda i: (i, 0))],
        out_specs=pl.BlockSpec((columns, tile), lambda i: (0, i)),
        out_shape=jax.ShapeDtypeStruct((columns, count), F32),
        compiler_params=pltpu.CompilerParams(vmem_limit_bytes=48 * 2**20),
        cost_estimate=pl.CostEstimate(flops=0, bytes_accessed=6 * rows.size, transcendentals=0),
        name="turn_rows",
    )(rows)


def turn_units(parts):
    seq_count, groups, unit, columns = parts.shape
    if unit % 8 or (seq_count * unit) % 128:
        return parts.transpose(3, 1, 0, 2).reshape(columns, -1).astype(F32)
    wide = seq_count * unit
    tile = 256
    return pl.pallas_call(
        turn_kernel,
        grid=(groups, columns // tile),
        in_specs=[pl.BlockSpec((seq_count, None, unit, tile), lambda g, i: (0, g, 0, i))],
        out_specs=pl.BlockSpec((tile, wide), lambda g, i: (i, g)),
        out_shape=jax.ShapeDtypeStruct((columns, groups * wide), F32),
        compiler_params=pltpu.CompilerParams(vmem_limit_bytes=48 * 2**20),
        cost_estimate=pl.CostEstimate(flops=0, bytes_accessed=6 * parts.size, transcendentals=0),
        name="turn_units",
    )(parts)


LINE = 4
MESH = pl.DeviceIdType.MESH


def place():
    rank = lax.axis_index("seq")
    return rank, lax.div(rank, 4), lax.rem(lax.div(rank, 2), 2), lax.rem(rank, 2)


def rank_at(z, y, x, dz, dy, dx):
    across = y + dy * (1 - 2 * y)
    along = x + dx * (1 - 2 * x)
    return (z + dz) * 4 + across * 2 + along


OFFSETS = [(dz, dy, dx) for dz in (0, -1, 1, -2, 2, -3, 3) for dy in (0, 1) for dx in (0, 1)]


def hops(offset):
    return abs(offset[0]) + offset[1] + offset[2]


def onward(order, offset):
    rel = dict(zip("zyx", offset))
    moved = [i for i, dim in enumerate(order) if rel[dim]]
    last = moved[-1] if moved else -1
    steps = []
    if last >= 0 and order[last] == "z":
        steps.append((1 if rel["z"] < 0 else -1, 0, 0))
    for dim in order[last + 1 :]:
        steps += {"z": [(1, 0, 0), (-1, 0, 0)], "y": [(0, 1, 0)], "x": [(0, 0, 1)]}[dim]
    return [s for s in steps if any(0 <= z + offset[0] < LINE and 0 <= z + s[0] < LINE for z in range(LINE))]


def inside(z, dz):
    return (z + dz >= 0) & (z + dz < LINE)


def guarded(z, steps, body):
    steps = [dz for dz in steps if dz]
    if not steps:
        body()
        return
    good = inside(z, steps[0])
    for dz in steps[1:]:
        good = good & inside(z, dz)
    pl.when(good)(body)


def greet_all():
    rank = lax.axis_index("seq")
    count = lax.axis_size("seq")
    barrier = pltpu.get_barrier_semaphore()
    for k in range(1, count):
        peer = lax.rem(rank + k, count)
        pl.semaphore_signal(barrier, inc=1, device_id={"seq": peer}, device_id_type=MESH)
    pl.semaphore_wait(barrier, count - 1)


def gather_events(streams, ins, outs, send_sems, recv_sems):
    rank, z, y, x = place()
    count = lax.axis_size("seq")
    slots = {}

    def copy(stream, offset, step):
        index, first, rows, order = streams[stream]
        part = pl.ds(first, rows)
        source = rank_at(z, y, x, *offset)
        slot = slots.setdefault((stream, offset, step), len(slots))
        block = outs[index].at[source, part]
        own = offset == (0, 0, 0)
        return pltpu.make_async_remote_copy(
            src_ref=ins[index].at[part] if own else block,
            dst_ref=block,
            send_sem=send_sems.at[slot],
            recv_sem=recv_sems.at[stream * count + source],
            device_id={"seq": rank_at(z, y, x, *step)},
            device_id_type=MESH,
        )

    def arrived(stream, offset):
        index, first, rows, order = streams[stream]
        source = rank_at(z, y, x, *offset)
        block = outs[index].at[source, pl.ds(first, rows)]
        pltpu.make_async_remote_copy(
            src_ref=block,
            dst_ref=block,
            send_sem=send_sems.at[0],
            recv_sem=recv_sems.at[stream * count + source],
            device_id={"seq": rank},
            device_id_type=MESH,
        ).wait_recv()

    todo = sorted(
        ((stream, offset) for stream in range(len(streams)) for offset in OFFSETS),
        key=lambda it: (hops(it[1]), it[0]),
    )

    def act(stream, offset):
        def forward():
            if hops(offset):
                arrived(stream, offset)
            for step in onward(streams[stream][3], offset):
                guarded(z, [step[0]], lambda: copy(stream, offset, step).start())

        guarded(z, [offset[0]], forward)

    def finish():
        for stream, offset in todo:
            for step in onward(streams[stream][3], offset):
                guarded(z, [offset[0], step[0]], lambda: copy(stream, offset, step).wait_send())

    return [functools.partial(act, *it) for it in todo], finish


def gather_kernel(streams, n_main, n_small, *refs):
    n = n_main + n_small
    ins, outs = refs[:n], refs[n : 2 * n]
    send_sems, recv_sems, small_send, small_recv, local_sems = refs[2 * n :]
    rank = lax.axis_index("seq")
    count = lax.axis_size("seq")
    greet_all()
    locals_ = [pltpu.make_async_copy(ins[i], outs[i].at[rank], local_sems.at[i]) for i in range(n)]

    def small_copy(i, k):
        peer = lax.rem(rank + k, count)
        return pltpu.make_async_remote_copy(
            src_ref=ins[n_main + i],
            dst_ref=outs[n_main + i].at[rank],
            send_sem=small_send.at[i * count + k],
            recv_sem=small_recv.at[i * count + rank],
            device_id={"seq": peer},
            device_id_type=MESH,
        )

    actions, finish = gather_events(streams, ins, outs, send_sems, recv_sems)
    for i, action in enumerate(actions):
        action()
        if i == len(streams) - 1:
            for c in locals_:
                c.start()
            for s in range(n_small):
                for k in range(1, count):
                    small_copy(s, k).start()
    finish()
    for i in range(n_small):
        for k in range(1, count):
            small_copy(i, k).wait_send()
        for k in range(1, count):
            source = lax.rem(rank + k, count)
            block = outs[n_main + i].at[source]
            pltpu.make_async_remote_copy(
                src_ref=block,
                dst_ref=block,
                send_sem=small_send.at[0],
                recv_sem=small_recv.at[i * count + source],
                device_id={"seq": rank},
                device_id_type=MESH,
            ).wait_recv()
    for c in locals_:
        c.wait()


def n_sends(streams):
    return sum(len(onward(s[3], o)) for s in streams for o in OFFSETS)


def streams_of(main, parts):
    streams = []
    for i, pieces in enumerate(parts):
        first = 0
        for rows, order in pieces:
            streams.append((i, first, rows, order))
            first += rows
    return streams


def gather_all(main, parts, small, collective_id, count=16):
    streams = streams_of(main, parts)
    arrays = list(main) + list(small)
    any_spec = pl.BlockSpec(memory_space=pl.ANY)
    return pl.pallas_call(
        functools.partial(gather_kernel, streams, len(main), len(small)),
        out_shape=tuple(jax.ShapeDtypeStruct((count,) + a.shape, a.dtype) for a in arrays),
        in_specs=[any_spec] * len(arrays),
        out_specs=tuple([any_spec] * len(arrays)),
        scratch_shapes=[
            pltpu.SemaphoreType.DMA((n_sends(streams),)),
            pltpu.SemaphoreType.DMA((len(streams) * count,)),
            pltpu.SemaphoreType.DMA((max(1, len(small)) * count,)),
            pltpu.SemaphoreType.DMA((max(1, len(small)) * count,)),
            pltpu.SemaphoreType.DMA((len(arrays),)),
        ],
        compiler_params=pltpu.CompilerParams(collective_id=collective_id, has_side_effects=True),
        name="gather_all",
    )(*arrays)


def toward(order, offset):
    rel = dict(zip("zyx", offset))
    dim = [d for d in order if rel[d]][-1]
    return {"z": (1 if rel["z"] > 0 else -1, 0, 0), "y": (0, 1, 0), "x": (0, 0, 1)}[dim]


def seen_from(offset, step):
    return (offset[0] - step[0], offset[1] ^ step[1], offset[2] ^ step[2])


def back(step):
    return (-step[0], step[1], step[2])


ADD_ROWS = 16


def slot_table(order):
    table, used = {}, 0
    for dy in (0, 1):
        for dx in (0, 1):
            for kind in ("x", "y", "up", "down"):
                step = {"x": (0, 0, 1), "y": (0, 1, 0), "up": (1, 0, 0), "down": (-1, 0, 0)}[kind]
                met = [o[0] for o in OFFSETS if o[1:] == (dy, dx) and step in onward(order, o)]
                if not met:
                    continue
                if kind == "down":
                    table[dy, dx, "down"] = (used, False)
                    used += 1
                    continue
                spread = any(met)
                table[dy, dx, kind] = (used, spread)
                used += LINE if spread else 1
    return table, used


def slot_at(table, z, offset, step):
    dz, dy, dx = offset
    kind = "x" if step[2] else "y" if step[1] else "down" if step[0] < 0 and dz == 0 else "up"
    first, spread = table[dy, dx, kind]
    return first + (z + dz) if spread else first


def scatter_kernel(streams, n_main, n_small, *refs):
    n = n_main + n_small
    ins, outs = refs[:n], refs[n : 2 * n]
    scratch = refs[2 * n :]
    bufs = scratch[: len(streams)]
    send_sems, recv_sems, small_send, small_recv, local_sems = scratch[len(streams) :]
    rank, z, y, x = place()
    count = lax.axis_size("seq")
    tables, bases, base = [], [], 0
    for stream in streams:
        table, used = slot_table(stream[3])
        tables.append(table)
        bases.append(base)
        base += used
    greet_all()

    def small_copy(i, k):
        peer = lax.rem(rank + k, count)
        return pltpu.make_async_remote_copy(
            src_ref=ins[n_main + i],
            dst_ref=outs[n_main + i].at[rank],
            send_sem=small_send.at[i * count + k],
            recv_sem=small_recv.at[i * count + rank],
            device_id={"seq": peer},
            device_id_type=MESH,
        )

    todo = sorted(
        ((s, offset) for s in range(len(streams)) for offset in OFFSETS),
        key=lambda it: (-hops(it[1]), it[0]),
    )
    send_slot = {key: i for i, key in enumerate(k for k in todo if hops(k[1]))}

    def send_copy(s, offset, source):
        step = toward(streams[s][3], offset)
        k = slot_at(tables[s], z + step[0], seen_from(offset, step), back(step))
        return pltpu.make_async_remote_copy(
            src_ref=source,
            dst_ref=bufs[s].at[k],
            send_sem=send_sems.at[send_slot[s, offset]],
            recv_sem=recv_sems.at[bases[s] + k],
            device_id={"seq": rank_at(z, y, x, *step)},
            device_id_type=MESH,
        )

    def wait_child(s, k):
        pltpu.make_async_remote_copy(
            src_ref=bufs[s].at[k],
            dst_ref=bufs[s].at[k],
            send_sem=send_sems.at[0],
            recv_sem=recv_sems.at[bases[s] + k],
            device_id={"seq": rank},
            device_id_type=MESH,
        ).wait_recv()

    for s, offset in todo:
        index, first, rows, order = streams[s]
        children = onward(order, offset)
        dest = rank_at(z, y, x, *offset)
        always = [c for c in children if not c[0]]
        sometimes = [c for c in children if c[0]]

        def run(present, s=s, offset=offset, index=index, first=first, rows=rows, dest=dest):
            own = ins[index].at[dest, pl.ds(first, rows)]
            if not present:
                send_copy(s, offset, own).start()
                return
            slots = [slot_at(tables[s], z, offset, step) for step in present]
            for k in slots:
                wait_child(s, k)
            final = not hops(offset)
            target = outs[index].at[pl.ds(first, rows)] if final else bufs[s].at[slots[0]]

            def add(i, carry):
                part = pl.ds(pl.multiple_of(i * ADD_ROWS, ADD_ROWS), ADD_ROWS)
                total = own[part, :].astype(F32)
                for k in slots:
                    total = total + bufs[s][k, part, :].astype(F32)
                target[part, :] = total.astype(target.dtype)
                return carry

            lax.fori_loop(0, rows // ADD_ROWS, add, 0)
            if not final:
                send_copy(s, offset, target).start()

        def cases(run=run, always=always, sometimes=sometimes):
            if not sometimes:
                run(always)
                return
            for mask in range(2 ** len(sometimes)):
                present = [c for i, c in enumerate(sometimes) if mask >> i & 1]
                good = None
                for i, c in enumerate(sometimes):
                    here = inside(z, c[0]) if mask >> i & 1 else jnp.logical_not(inside(z, c[0]))
                    good = here if good is None else good & here
                pl.when(good)(functools.partial(run, present + always))

        guarded(z, [offset[0]], cases)
        if (s, offset) == todo[0]:
            for i in range(n_small):
                for k in range(1, count):
                    small_copy(i, k).start()
                pltpu.make_async_copy(ins[n_main + i], outs[n_main + i].at[rank], local_sems.at[i]).start()
    for s, offset in todo:
        if hops(offset):
            index, first, rows, order = streams[s]
            own = ins[index].at[rank_at(z, y, x, *offset), pl.ds(first, rows)]
            guarded(z, [offset[0]], lambda: send_copy(s, offset, own).wait_send())
    for i in range(n_small):
        for k in range(1, count):
            small_copy(i, k).wait_send()
        for k in range(1, count):
            source = lax.rem(rank + k, count)
            block = outs[n_main + i].at[source]
            pltpu.make_async_remote_copy(
                src_ref=block,
                dst_ref=block,
                send_sem=small_send.at[0],
                recv_sem=small_recv.at[i * count + source],
                device_id={"seq": rank},
                device_id_type=MESH,
            ).wait_recv()
        pltpu.make_async_copy(ins[n_main + i], outs[n_main + i].at[rank], local_sems.at[i]).wait()


def scatter_sum(main, parts, small, collective_id, count=16):
    streams = streams_of(main, parts)
    arrays = list(main) + list(small)
    any_spec = pl.BlockSpec(memory_space=pl.ANY)
    vmem = pl.BlockSpec(memory_space=pltpu.VMEM)
    places = [slot_table(stream[3])[1] for stream in streams]
    buffers = [
        pltpu.VMEM((used, rows, main[index].shape[2]), main[index].dtype)
        for used, (index, first, rows, order) in zip(places, streams)
    ]
    return pl.pallas_call(
        functools.partial(scatter_kernel, streams, len(main), len(small)),
        out_shape=tuple(
            [jax.ShapeDtypeStruct(a.shape[1:], F32) for a in main]
            + [jax.ShapeDtypeStruct((count,) + a.shape, a.dtype) for a in small]
        ),
        in_specs=[vmem] * len(main) + [any_spec] * len(small),
        out_specs=tuple([vmem] * len(main) + [any_spec] * len(small)),
        scratch_shapes=buffers
        + [
            pltpu.SemaphoreType.DMA((len(streams) * len(OFFSETS),)),
            pltpu.SemaphoreType.DMA((sum(places),)),
            pltpu.SemaphoreType.DMA((max(1, len(small)) * count,)),
            pltpu.SemaphoreType.DMA((max(1, len(small)) * count,)),
            pltpu.SemaphoreType.DMA((max(1, len(small)),)),
        ],
        compiler_params=pltpu.CompilerParams(
            collective_id=collective_id, has_side_effects=True, vmem_limit_bytes=60 * 2**20
        ),
        name="scatter_sum",
    )(*arrays)


COLS = 256
PACE = 4


def expert_phases():
    ends, last = [], 0
    for steps in (2 * FF // COLS, -(-FF // COLS), D // COLS, D // COLS):
        last += steps
        ends.append(last)
    return ends


def expert_kernel(
    streams, n_main,
    x_ref, rg_ref, in_col_ref, out_row_ref, out_col_ref, in_row_ref,
    place_ref, gate_ref, shid_ref, sgrad_ref, sout_ref, sin_ref, up_ref, *refs
):
    ins, refs = refs[:n_main], refs[n_main:]
    mixed_ref, back_ref, dots_ref, hidden_out, gate_out, up_out, refs = *refs[:6], refs[6:]
    outs, refs = refs[:n_main], refs[n_main:]
    gu, hidden, dgu, picks, send_sems, recv_sems, local_sems, out_sems = refs
    rank = lax.axis_index("seq")
    i = pl.program_id(0)
    blocks, tok = place_ref.shape
    capacity = x_ref.shape[0] // blocks
    ends = expert_phases()
    actions, finish = gather_events(streams, ins, outs, send_sems, recv_sems)
    own = [pltpu.make_async_copy(ins[k], outs[k].at[rank], local_sems.at[k]) for k in range(n_main)]
    kept = [
        pltpu.make_async_copy(hidden, hidden_out, out_sems.at[0]),
        pltpu.make_async_copy(dgu.at[:, pl.ds(0, FF)], gate_out, out_sems.at[1]),
        pltpu.make_async_copy(dgu.at[:, pl.ds(FF, FF)], up_out, out_sems.at[2]),
    ]

    @pl.when(i == 0)
    def _():
        greet_all()
        for action in actions[: len(streams)]:
            action()
        for copy in own:
            copy.start()
        for b in range(blocks):
            picks[pl.ds(b * capacity, capacity), :] = as_weights(pick_of(place_ref, b, capacity))

    @pl.when(i < ends[0])
    def _():
        cols = pl.ds(pl.multiple_of(i * COLS, COLS), COLS)
        gu[:, cols] = dot(x_ref[...], in_col_ref[...]).astype(BF16)

    def back_span(first, width):
        grad = dot_nt(rg_ref[...], out_row_ref[:width, :])
        at, to = pl.ds(first, width), pl.ds(pl.multiple_of(FF + first, 128), width)
        gate, up = gu[:, at].astype(F32), gu[:, to].astype(F32)
        hidden[:, at] = (gate * jax.nn.sigmoid(gate) * up).astype(BF16)
        gate_grad, up_grad = silu_grads(gate, up, grad)
        dgu[:, at] = gate_grad.astype(BF16)
        dgu[:, to] = up_grad.astype(BF16)

    full = FF // COLS

    @pl.when((i >= ends[0]) & (i < ends[0] + full))
    def _():
        back_span(pl.multiple_of((i - ends[0]) * COLS, COLS), COLS)

    if FF % COLS:

        @pl.when(i == ends[0] + full)
        def _():
            back_span(full * COLS, FF % COLS)

    @pl.when(i == ends[1])
    def _():
        for copy in kept:
            copy.start()
        dots_ref[...] = jnp.zeros_like(dots_ref)

    @pl.when((i >= ends[1]) & (i < ends[2]))
    def _():
        result = dot(hidden[...], out_col_ref[...]).astype(BF16)
        shared = dot(shid_ref[...], sout_ref[...])
        for b in range(blocks):
            tokens, slots = pl.ds(b * tok, tok), pl.ds(b * capacity, capacity)
            mine = dot_tn(picks[slots, :], result[b * capacity : (b + 1) * capacity])
            dots_ref[tokens, :] += jnp.sum(up_ref[tokens, :].astype(F32) * mine, axis=1, keepdims=True)
            both = gate_ref[tokens, :] * mine + shared[b * tok : (b + 1) * tok]
            mixed_ref[tokens, :] = both.astype(BF16)

    @pl.when(i >= ends[2])
    def _():
        row_grad = dot_nt(dgu[...], in_row_ref[...]).astype(BF16)
        shared = dot_nt(sgrad_ref[...], sin_ref[...])
        for b in range(blocks):
            tokens, slots = pl.ds(b * tok, tok), pl.ds(b * capacity, capacity)
            mine = dot_tn(picks[slots, :], row_grad[b * capacity : (b + 1) * capacity])
            back_ref[tokens, :] = (mine + shared[b * tok : (b + 1) * tok]).astype(BF16)

    done = len(streams)
    for step in range(ends[3] - 1):
        some = actions[done : done + PACE]
        done += len(some)
        if some:

            @pl.when(i == step)
            def _(some=some):
                for action in some:
                    action()

    @pl.when(i == ends[3] - 1)
    def _():
        for action in actions[done:]:
            action()
        finish()
        for copy in own + kept:
            copy.wait()


def expert_block(
    x, rg, w_in, w_out, place, gates, shared_hidden, shared_grad, shared_out, shared_in, upstream,
    main, parts, collective_id, count=16,
):
    rows, tokens = x.shape[0], upstream.shape[0]
    units = shared_out.shape[0]
    streams = streams_of(main, parts)
    ends = expert_phases()

    def held(array):
        return pl.BlockSpec(array.shape, lambda i: (0, 0), pipeline_mode=pl.Buffered(1))

    def during(start, stop):
        return lambda i: jnp.minimum(jnp.maximum(i - start, 0), stop - start - 1)

    one, two, three, four = [during(a, b) for a, b in zip([0] + ends[:-1], ends)]
    any_spec = pl.BlockSpec(memory_space=pl.ANY)
    n = len(main)
    gate_column = gates.reshape(-1, 1)
    results = pl.pallas_call(
        functools.partial(expert_kernel, streams, n),
        grid=(ends[-1],),
        in_specs=[
            held(x),
            held(rg),
            pl.BlockSpec((D, COLS), lambda i: (0, one(i))),
            pl.BlockSpec((COLS, D), lambda i: (two(i), 0)),
            pl.BlockSpec((FF, COLS), lambda i: (0, three(i))),
            pl.BlockSpec((COLS, 2 * FF), lambda i: (four(i), 0)),
            held(place),
            held(gate_column),
            held(shared_hidden),
            held(shared_grad),
            pl.BlockSpec((units, COLS), lambda i: (0, three(i))),
            pl.BlockSpec((COLS, 2 * units), lambda i: (four(i), 0)),
            pl.BlockSpec((tokens, COLS), lambda i: (0, three(i))),
        ]
        + [any_spec] * n,
        out_specs=(
            pl.BlockSpec((tokens, COLS), lambda i: (0, three(i))),
            pl.BlockSpec((tokens, COLS), lambda i: (0, four(i))),
            pl.BlockSpec((tokens, 1), lambda i: (0, 0)),
            any_spec,
            any_spec,
            any_spec,
        )
        + (any_spec,) * n,
        out_shape=(
            jax.ShapeDtypeStruct((tokens, D), BF16),
            jax.ShapeDtypeStruct((tokens, D), BF16),
            jax.ShapeDtypeStruct((tokens, 1), F32),
            jax.ShapeDtypeStruct((rows, FF), BF16),
            jax.ShapeDtypeStruct((rows, FF), BF16),
            jax.ShapeDtypeStruct((rows, FF), BF16),
        )
        + tuple(jax.ShapeDtypeStruct((count,) + a.shape, a.dtype) for a in main),
        scratch_shapes=[
            pltpu.VMEM((rows, 2 * FF), BF16),
            pltpu.VMEM((rows, FF), BF16),
            pltpu.VMEM((rows, 2 * FF), BF16),
            pltpu.VMEM((rows, place.shape[1]), BF16),
            pltpu.SemaphoreType.DMA((n_sends(streams),)),
            pltpu.SemaphoreType.DMA((len(streams) * count,)),
            pltpu.SemaphoreType.DMA((n,)),
            pltpu.SemaphoreType.DMA((3,)),
        ],
        compiler_params=pltpu.CompilerParams(
            collective_id=collective_id, has_side_effects=True, vmem_limit_bytes=62 * 2**20
        ),
        cost_estimate=pl.CostEstimate(
            flops=12 * rows * D * FF, bytes_accessed=100 * 2**20, transcendentals=2 * rows * FF
        ),
        name="expert_block",
    )(
        x, rg, w_in, w_out, w_out, w_in,
        place, gate_column, shared_hidden, shared_grad, shared_out, shared_in, upstream, *main,
    )
    return results[:6], results[6:]


def gather_seq(rows):
    return lax.all_gather(rows, "seq", axis=0, tiled=True)


def scatter_seq(partial):
    return lax.psum_scatter(partial, "seq", scatter_dimension=0, tiled=True)


def gather_fsdp(rows, axis=0):
    return lax.all_gather(rows, "fsdp", axis=axis, tiled=True)


def scatter_fsdp(partial, axis=0):
    count, me = lax.axis_size("fsdp"), lax.axis_index("fsdp")
    size = partial.shape[axis] // count
    total = lax.dynamic_slice_in_dim(partial, me * size, size, axis).astype(F32)
    for k in range(1, count):
        piece = lax.dynamic_slice_in_dim(partial, lax.rem(me + k, count) * size, size, axis)
        total = total + shift_fsdp(piece, k).astype(F32)
    return total


def shift_fsdp(rows, k):
    count = lax.axis_size("fsdp")
    return lax.ppermute(rows, "fsdp", [(i, (i + k) % count) for i in range(count)])


ROW_PARTS = [(48, "zxy"), (48, "zyx"), (16, "xyz"), (16, "yxz")]


def split_rows(rows, part=8):
    tile = 16
    tiles = rows // tile
    short = tiles // part
    long = (tiles - 2 * short) // 2
    sizes = [tiles - 2 * short - long, long, short, short]
    orders = ["zxy", "zyx", "xyz", "yxz"]
    return [(n * tile, order) for n, order in zip(sizes, orders) if n]


def on_device(
    tokens,
    cotangent,
    lengths,
    routes,
    g_attn,
    w_q,
    w_kva,
    g_kv,
    w_kvb,
    w_o,
    g_ffn,
    w_router,
    w_shared_in,
    w_shared_out,
    w_expert_in,
    w_expert_out,
):
    seq_count = lax.axis_size("seq")
    fsdp_count = lax.axis_size("fsdp")
    rank = lax.axis_index("seq")
    tok_count = tokens.shape[0]
    group_size = tok_count * seq_count
    query_width = DN + DR
    kv_width = DN + DV
    experts = seq_count
    capacity = min(tok_count, 2 * tok_count * TOP // experts)
    buffer_rows = seq_count * capacity
    unit = SH // (seq_count * fsdp_count)
    units = unit * fsdp_count
    row_part = w_q.shape[0]

    def own(rows, axis=0):
        return lax.dynamic_slice_in_dim(rows, rank * tok_count, tok_count, axis)

    expert_ids = jnp.arange(experts, dtype=jnp.int32)
    route_mask = jnp.any(routes[None] == expert_ids[:, None, None], axis=2).astype(BF16)
    token_all, mask_all = gather_all([tokens], [ROW_PARTS], [route_mask], 1)
    token_all = token_all.reshape(group_size, D)

    small = gather_fsdp(jnp.concatenate([g_attn, g_kv, g_ffn, w_router.reshape(-1)])[None])
    cuts = [0, g_attn.size, g_kv.size, g_ffn.size, w_router.size]
    ends = [sum(cuts[: i + 1]) for i in range(len(cuts))]
    gain_attn = small[:, ends[0] : ends[1]].reshape(-1).astype(F32)
    gain_latent = small[:, ends[1] : ends[2]].reshape(-1).astype(F32)
    gain_ffn = small[:, ends[2] : ends[3]].reshape(-1).astype(F32)
    router_weight = small[:, ends[3] : ends[4]].reshape(D, experts)
    head_query_part = lax.dynamic_slice_in_dim(w_q, rank * query_width, query_width, 1)
    head_expand = gather_fsdp(lax.dynamic_slice_in_dim(w_kvb, rank * kv_width, kv_width, 1))
    head_weights = gather_fsdp(
        jnp.concatenate([w_kva[:, :KVR], head_query_part, w_kva[:, KVR:]], axis=1)
    )
    output_weight = gather_fsdp(w_o)
    expert_in = gather_fsdp(w_expert_in[0])
    expert_out = gather_fsdp(w_expert_out[0])
    query_weight = gather_fsdp(w_q)
    expand_weight = gather_fsdp(w_kvb)

    slot_ids = jnp.arange(group_size, dtype=jnp.int32)
    segment, position, valid_all = layout(lengths[0], slot_ids)
    angles = own(position)[:, None].astype(F32) * frequencies(DR)[None, :]
    wide_angles = position[:, None].astype(F32) * jnp.tile(frequencies(DR), 4)[None, :]
    cosines = jnp.cos(wide_angles)
    signs = jnp.where(jnp.arange(2 * DR) % DR < DR // 2, -1.0, 1.0).astype(F32)
    sines = jnp.sin(wide_angles) * signs[None, :]

    upstream_own = jnp.where(own(valid_all)[:, None], cotangent, 0).astype(BF16)
    upstream_all = gather_seq(upstream_own)

    normed_all, query, key, value, latent_full, latent_all = project(
        token_all, gain_attn, head_weights, gain_latent, head_expand, cosines, sines
    )
    context, log_total, head_largest = attention_forward(query, key, value, segment, valid_all)
    late_rank, context, upstream_all = lax.optimization_barrier((rank, context, upstream_all))
    lanes = -(-units // 128) * 128
    unit_slices = [
        lax.dynamic_slice_in_dim(w_shared_in, i * (SH // fsdp_count) + late_rank * unit, unit, 1)
        for i in range(2 * fsdp_count)
    ]
    filler = jnp.zeros((row_part, lanes - units), BF16)
    shared_in_part = jnp.concatenate(
        unit_slices[:fsdp_count] + [filler] + unit_slices[fsdp_count:] + [filler], axis=1
    )
    shared_in = gather_fsdp(shared_in_part)
    shared_out = gather_fsdp(lax.dynamic_slice_in_dim(w_shared_out, late_rank * unit, unit, 0))
    shared_out = jnp.pad(shared_out, ((0, lanes - units), (0, 0)))

    context_low = lax.all_to_all(context, "seq", split_axis=0, concat_axis=1, tiled=True)
    inputs = tokens.astype(F32)
    middle = inputs + dot(context_low, output_weight)
    ffn_low = rms_norm(middle, gain_ffn).astype(BF16)
    ffn_all, largest_all = gather_all([ffn_low], [ROW_PARTS], [head_largest], 2)
    ffn_all = ffn_all.reshape(group_size, D)
    head_max = largest_all[:, 0, :]
    for k in range(1, fsdp_count):
        head_max = jnp.maximum(head_max, shift_fsdp(largest_all[:, 0, :], k))
    global_max = head_max[:, 0]

    router_probs = jax.nn.softmax(dot(ffn_all, router_weight), axis=-1)
    chosen = lax.dynamic_slice_in_dim(mask_all, rank, 1, 1).reshape(seq_count, tok_count) > 0
    gates = lax.dynamic_slice_in_dim(router_probs, rank, 1, 1).reshape(seq_count, tok_count)
    place = jnp.cumsum(chosen.astype(jnp.int32), axis=1) - 1
    place = jnp.where(chosen, place, capacity)

    arrived, result_grad, shared_hidden, shared_grad, grad_shared_out, grad_shared_in = spread(
        ffn_all, upstream_all, place, gates, shared_in, shared_out, capacity
    )
    part_shared_out = scatter_fsdp(grad_shared_out[:units]).astype(BF16)
    part_shared_in = jnp.concatenate([grad_shared_in[:units], grad_shared_in[lanes : lanes + units]], axis=0)
    part_shared_in = scatter_fsdp(part_shared_in, 1).astype(BF16)
    part_shared_out = jnp.pad(part_shared_out, ((0, -unit % 16), (0, 0)))

    (mixed_part, ffn_part, gate_grad, hidden, d_gate, d_up), (all_shared_in, all_shared_out) = expert_block(
        arrived,
        result_grad,
        expert_in,
        expert_out,
        place,
        gates,
        shared_hidden,
        shared_grad,
        shared_out,
        shared_in,
        upstream_all,
        [part_shared_in, part_shared_out],
        [split_rows(part_shared_in.shape[0], 6), split_rows(part_shared_out.shape[0], 6)],
        4,
    )
    mixed_part, query_weight, expand_weight = lax.optimization_barrier(
        (mixed_part, query_weight, expand_weight)
    )
    mixed_sum, ffn_sum, prob_grads = scatter_sum(
        [part.reshape(seq_count, tok_count, D) for part in (mixed_part, ffn_part)],
        [ROW_PARTS, ROW_PARTS],
        [gate_grad.reshape(seq_count, tok_count)],
        3,
    )
    mixed = (middle + mixed_sum).astype(BF16)
    prob_grads = prob_grads.reshape(experts, group_size).T

    logit_grads = (
        router_probs * (prob_grads - jnp.sum(router_probs * prob_grads, axis=-1, keepdims=True))
    ).astype(BF16)
    grad_router = dot_tn(ffn_all, logit_grads)
    sum_router = scatter_fsdp(grad_router.astype(BF16))
    ffn_grad = ffn_sum + dot_nt(own(logit_grads), router_weight)

    ffn_pull = jax.vjp(rms_norm, middle, gain_ffn)[1]
    middle_norm_grad, grad_gain_ffn = ffn_pull(ffn_grad)
    middle_grad = upstream_own.astype(F32) + middle_norm_grad
    middle_low = middle_grad.astype(BF16)
    context_grad = dot_nt(middle_low, output_weight).astype(BF16)
    head_grad = lax.all_to_all(context_grad, "seq", split_axis=1, concat_axis=0, tiled=True)
    grad_output = scatter_fsdp(dot_tn(context_low, middle_low).astype(BF16)).astype(BF16)
    output_rows = row_part // seq_count
    (part_output,) = scatter_sum(
        [grad_output.reshape(seq_count, output_rows, D)], [split_rows(output_rows)], [], 5
    )

    head_grad, part_output = lax.optimization_barrier((head_grad, part_output.astype(BF16)))
    all_output = gather_seq(part_output)
    head_back = attention_backward(query, key, value, head_grad, segment, log_total, cosines, sines)
    head_back, arrived, result_grad, hidden, d_gate, d_up = lax.optimization_barrier(
        (head_back, arrived, result_grad, hidden, d_gate, d_up)
    )
    back = lax.all_to_all(
        head_back.reshape(seq_count, tok_count, -1), "seq", split_axis=0, concat_axis=0, tiled=True
    )
    grad_expert_out = dot_tn(hidden, result_grad).astype(BF16)
    grad_expert_in = dot_tn(arrived, jnp.concatenate([d_gate, d_up], axis=1)).astype(BF16)
    rope_at = 2 * DN + DV
    head_pre_grad = jnp.concatenate([head_back[:, :DN], head_back[:, rope_at : rope_at + DR]], axis=1)
    grad_query = dot_tn(head_pre_grad, normed_all).astype(BF16)
    grad_expand = dot_tn(head_back[:, DN:rope_at], latent_all).astype(BF16)
    part_query = scatter_fsdp(grad_query, 1).astype(BF16)
    part_expand = scatter_fsdp(grad_expand, 1).astype(BF16)
    back, grad_expert_out, grad_expert_in, part_query, part_expand = lax.optimization_barrier(
        (back, grad_expert_out, grad_expert_in, part_query, part_expand)
    )
    sum_expert_in = scatter_fsdp(grad_expert_in)[None]
    sum_expert_out = scatter_fsdp(grad_expert_out)[None]

    back = back.transpose(1, 0, 2)
    pre_grad = jnp.concatenate([back[..., :DN], back[..., rope_at : rope_at + DR]], axis=-1)
    pre_grad = pre_grad.reshape(tok_count, H * query_width)
    expand_grad = back[..., DN:rope_at].reshape(tok_count, H * kv_width)
    latent_grad = dot_nt(expand_grad, expand_weight)
    rope_grad = rotate(jnp.sum(back[..., rope_at + DR :].astype(F32), axis=1), -angles)
    latent_pull = jax.vjp(rms_norm, own(latent_full), gain_latent)[1]
    compressed_grad, grad_gain_latent = latent_pull(latent_grad)
    full_grad = jnp.concatenate([compressed_grad, rope_grad], axis=1).astype(BF16)
    full_grad, all_output = lax.optimization_barrier((full_grad, all_output))
    spread_grad = jnp.pad(full_grad[:, :KVR], ((0, 0), (0, query_width + DR)))
    spread_grad = spread_grad + jnp.pad(full_grad[:, KVR:], ((0, 0), (KVR + query_width, 0)))
    normed_grad = dot_nt(pre_grad, query_weight) + dot_nt(spread_grad, head_weights)
    input_pull = jax.vjp(rms_norm, inputs, gain_attn)[1]
    input_norm_grad, grad_gain_attn = input_pull(normed_grad)
    grad_inputs = middle_grad + input_norm_grad

    gain_grads = jnp.concatenate([grad_gain_attn, grad_gain_latent, grad_gain_ffn]).reshape(-1, 128)
    gain_grads = jnp.pad(gain_grads, ((0, -gain_grads.shape[0] % 8), (0, 0)))
    last_parts = [part_query, part_expand, full_grad]
    all_query, all_expand, full_all, gain_all = gather_all(
        last_parts, [split_rows(part.shape[0]) for part in last_parts], [gain_grads], 6
    )
    full_all = full_all.reshape(group_size, -1)
    sum_latent = scatter_fsdp(dot_tn(normed_all, full_all).astype(BF16))
    gain_seq = jnp.sum(gain_all, axis=0)
    gain_sum = gain_seq
    for k in range(1, fsdp_count):
        gain_sum = gain_sum + shift_fsdp(gain_seq, k)
    gain_sum = gain_sum.reshape(-1)
    sum_shared_out = all_shared_out[:, :unit].reshape(w_shared_out.shape).astype(F32)
    sum_shared_in = turn_units(all_shared_in.reshape(seq_count, 2 * fsdp_count, unit, row_part))
    sum_query = turn_rows(all_query.reshape(-1, row_part), 384)
    sum_expand = turn_rows(all_expand.reshape(-1, w_kvb.shape[0]), 512)
    sum_output = all_output.astype(F32)
    fsdp_rank = lax.axis_index("fsdp")

    def own_part(first, like):
        return lax.dynamic_slice_in_dim(gain_sum, first + fsdp_rank * like.size, like.size, 0)

    sum_gain_attn = own_part(0, g_attn)
    sum_gain_latent = own_part(D, g_kv)
    sum_gain_ffn = own_part(D + KVR, g_ffn)

    clip_gamma = CLIP_LIMIT / jnp.maximum(global_max, CLIP_LIMIT)
    clip_root = jnp.sqrt(clip_gamma)
    query_factor = jnp.concatenate(
        [
            jnp.broadcast_to(clip_root[:, None], (H, DN)),
            jnp.broadcast_to(clip_gamma[:, None], (H, DR)),
        ],
        axis=1,
    ).reshape(1, -1)
    clipped_query = (w_q.astype(F32) * query_factor).astype(BF16)
    return (
        mixed,
        grad_inputs,
        sum_gain_attn,
        sum_query,
        sum_latent,
        sum_gain_latent,
        sum_expand,
        sum_output,
        sum_gain_ffn,
        sum_router,
        sum_shared_in,
        sum_shared_out,
        sum_expert_in,
        sum_expert_out,
        clipped_query,
    )


def solution(mesh):
    in_specs = (
        P(("fsdp", "seq"), None),
        P(("fsdp", "seq"), None),
        P("fsdp", None),
        P(("fsdp", "seq"), None),
        P("fsdp"),
        P("fsdp", None),
        P("fsdp", None),
        P("fsdp"),
        P("fsdp", None),
        P("fsdp", None),
        P("fsdp"),
        P("fsdp", None),
        P("fsdp", None),
        P("fsdp", None),
        P("seq", "fsdp", None),
        P("seq", "fsdp", None),
    )
    out_specs = (
        P(("fsdp", "seq"), None),
        P(("fsdp", "seq"), None),
        P("fsdp"),
        P("fsdp", None),
        P("fsdp", None),
        P("fsdp"),
        P("fsdp", None),
        P("fsdp", None),
        P("fsdp"),
        P("fsdp", None),
        P("fsdp", None),
        P("fsdp", None),
        P("seq", "fsdp", None),
        P("seq", "fsdp", None),
        P("fsdp", None),
    )
    return jax.shard_map(
        on_device, mesh=mesh, in_specs=in_specs, out_specs=out_specs, check_vma=False
    )
```

```python
import functools

import jax
import jax.numpy as jnp
from jax import lax
from jax.experimental import pallas as pl
from jax.experimental.pallas import tpu as pltpu
from jax.sharding import PartitionSpec as P

D = 2048
H = 16
DN = 128
DR = 64
DV = 128
KVR = 512
FF = 1408
TOP = 6
SH = 2816

EPSILON = 1e-06
CLIP_LIMIT = 8.0
ROPE_BASE = 10000.0
MASK_VALUE = -1e30
BF16 = jnp.bfloat16
F32 = jnp.float32


def rms_norm(values, gain_vector):
    return (
        values
        * lax.rsqrt(jnp.mean(values * values, axis=-1, keepdims=True) + EPSILON)
        * gain_vector
    )


def rotate(values, angles):
    half_width = values.shape[-1] // 2
    first_half = values[..., :half_width]
    second_half = values[..., half_width:]
    cosine = jnp.cos(angles)
    sine_part = jnp.sin(angles)
    return jnp.concatenate(
        [
            first_half * cosine - second_half * sine_part,
            second_half * cosine + first_half * sine_part,
        ],
        axis=-1,
    )


def frequencies(count):
    exponent = jnp.arange(count // 2, dtype=jnp.float32) * 2.0 / count
    return ROPE_BASE ** (-exponent)


def layout(lengths_row, slot_ids):
    seq_ends = jnp.cumsum(lengths_row)
    seq_starts = seq_ends - lengths_row
    inside = (slot_ids[:, None] >= seq_starts[None, :]) & (slot_ids[:, None] < seq_ends[None, :])
    is_valid = jnp.any(inside, axis=1)
    numbers = jnp.arange(lengths_row.shape[0], dtype=jnp.int32)
    seq_number = jnp.sum(jnp.where(inside, numbers[None, :], 0), axis=1)
    first_slot = jnp.sum(jnp.where(inside, seq_starts[None, :], 0), axis=1)
    segment = jnp.where(is_valid, seq_number, lengths_row.shape[0] + slot_ids)
    position = jnp.where(is_valid, slot_ids - first_slot, 0)
    return (segment, position, is_valid)


def dot(left, right):
    return jnp.dot(left, right, preferred_element_type=F32)


def dot_tn(left, right):
    return lax.dot_general(left, right, (((0,), (0,)), ((), ())), preferred_element_type=F32)


def dot_nt(left, right):
    return lax.dot_general(left, right, (((1,), (1,)), ((), ())), preferred_element_type=F32)


ROWS = 256


def masked_scores(query, key, seg_col, seg_row, first, scale):
    scores = dot_nt(query, key) * scale
    shape = scores.shape
    row_slot = first + lax.broadcasted_iota(jnp.int32, shape, 0)
    key_slot = lax.broadcasted_iota(jnp.int32, shape, 1)
    allowed = (seg_col == seg_row) & (key_slot <= row_slot)
    return jnp.where(allowed, scores, MASK_VALUE)


def attention_forward_kernel(scale, q_ref, k_ref, v_ref, segc_ref, segr_ref, valid_ref, ctx_ref, lse_ref, max_ref):
    count = q_ref.shape[0]
    best = jnp.full((1, 1), MASK_VALUE, F32)
    for first in range(0, count, ROWS):
        rows, keys = pl.ds(first, ROWS), pl.ds(0, first + ROWS)
        masked = masked_scores(q_ref[rows, :], k_ref[keys, :], segc_ref[rows, :], segr_ref[:, keys], first, scale)
        row_max = jnp.max(masked, axis=1, keepdims=True)
        exponent = jnp.exp(masked - row_max)
        row_sum = jnp.sum(exponent, axis=1, keepdims=True)
        probs = (exponent * (1.0 / row_sum)).astype(BF16)
        ctx_ref[rows, :] = dot(probs, v_ref[keys, :]).astype(BF16)
        lse_ref[rows, :] = row_max + jnp.log(row_sum)
        counted = jnp.where(valid_ref[rows, :] > 0, row_max, MASK_VALUE)
        best = jnp.maximum(best, jnp.max(counted, axis=0, keepdims=True))
    max_ref[...] = jnp.broadcast_to(best, max_ref.shape)


def attention_forward(query, key, value, segment, valid):
    count, width = query.shape
    return pl.pallas_call(
        functools.partial(attention_forward_kernel, width ** (-0.5)),
        out_shape=(
            jax.ShapeDtypeStruct((count, value.shape[1]), BF16),
            jax.ShapeDtypeStruct((count, 1), F32),
            jax.ShapeDtypeStruct((8, 128), F32),
        ),
        compiler_params=pltpu.CompilerParams(vmem_limit_bytes=48 * 2**20),
        cost_estimate=pl.CostEstimate(flops=count * count * 320, bytes_accessed=4 * 2**20, transcendentals=count * count // 2),
        name="attention_forward",
    )(query, key, value, segment[:, None], segment[None, :], valid[:, None].astype(jnp.int32))


def attention_backward_kernel(
    scale, q_ref, k_ref, v_ref, g_ref, segc_ref, segr_ref, lse_ref, cos_ref, sin_ref, out_ref, dk_sum, dv_sum
):
    half = DR // 2
    count = q_ref.shape[0]
    dk_sum[...] = jnp.zeros_like(dk_sum)
    dv_sum[...] = jnp.zeros_like(dv_sum)
    for first in range(0, count, ROWS):
        rows, keys = pl.ds(first, ROWS), pl.ds(0, first + ROWS)
        query, grad = q_ref[rows, :], g_ref[rows, :]
        masked = masked_scores(query, k_ref[keys, :], segc_ref[rows, :], segr_ref[:, keys], first, scale)
        probs = jnp.exp(masked - lse_ref[rows, :])
        prob_grad = dot_nt(grad, v_ref[keys, :])
        mean = jnp.sum(probs * prob_grad, axis=1, keepdims=True)
        score_grad = (probs * (prob_grad - mean)).astype(BF16)
        query_grad = (dot(score_grad, k_ref[keys, :]) * scale).astype(BF16)
        out_ref[rows, :DN] = query_grad[:, :DN]
        rope = query_grad[:, DN:].astype(F32)
        swapped = jnp.concatenate([rope[:, half:], rope[:, :half]], axis=1)
        rope = rope * cos_ref[rows, :DR] - swapped * sin_ref[rows, :DR]
        out_ref[rows, 2 * DN + DV : 2 * DN + DV + DR] = rope.astype(BF16)
        dk_sum[keys, :] += dot_tn(score_grad, query)
        dv_sum[keys, :] += dot_tn(probs.astype(BF16), grad)
    key_grad = (dk_sum[...] * scale).astype(BF16)
    out_ref[:, DN : 2 * DN] = key_grad[:, :DN]
    out_ref[:, 2 * DN : 2 * DN + DV] = dv_sum[...].astype(BF16)
    out_ref[:, 2 * DN + DV + DR :] = key_grad[:, DN:]


def attention_backward(query, key, value, grad, segment, log_total, cosines, sines):
    count, width = query.shape
    return pl.pallas_call(
        functools.partial(attention_backward_kernel, width ** (-0.5)),
        out_shape=jax.ShapeDtypeStruct((count, 2 * width + value.shape[1]), BF16),
        scratch_shapes=[pltpu.VMEM(key.shape, F32), pltpu.VMEM(value.shape, F32)],
        compiler_params=pltpu.CompilerParams(vmem_limit_bytes=48 * 2**20),
        cost_estimate=pl.CostEstimate(flops=count * count * 832, bytes_accessed=6 * 2**20, transcendentals=count * count // 2),
        name="attention_backward",
    )(query, key, value, grad, segment[:, None], segment[None, :], log_total, cosines, sines)


def swap_halves(values):
    half = DR // 2
    pieces = [values[:, i * half : (i + 1) * half] for i in (1, 0, 3, 2)]
    return jnp.concatenate(pieces, axis=1)


def project_kernel(x_ref, gain_ref, w_ref, gain_kv_ref, expand_ref, cos_ref, sin_ref, normed_ref, q_ref, k_ref, v_ref, raw_ref, latent_ref):
    normed = rms_norm(x_ref[...].astype(F32), gain_ref[...]).astype(BF16)
    normed_ref[...] = normed
    both = dot(normed, w_ref[...])
    raw = both[:, :KVR]
    raw_ref[...] = raw
    latent = rms_norm(raw, gain_kv_ref[...]).astype(BF16)
    latent_ref[...] = latent
    expanded = dot(latent, expand_ref[...])
    rope = both[:, KVR + DN :]
    rope = rope * cos_ref[...] + swap_halves(rope) * sin_ref[...]
    q_ref[...] = jnp.concatenate([both[:, KVR : KVR + DN], rope[:, :DR]], axis=1).astype(BF16)
    k_ref[...] = jnp.concatenate([expanded[:, :DN], rope[:, DR:]], axis=1).astype(BF16)
    v_ref[...] = expanded[:, DN:].astype(BF16)


def project(rows, gain, weight, gain_kv, expand, cosines, sines):
    count = rows.shape[0]
    tile = 256

    def by_rows(columns):
        return pl.BlockSpec((tile, columns), lambda i: (i, 0))

    def whole(array):
        return pl.BlockSpec(array.shape, lambda i: (0, 0))

    outs = [(D, BF16), (DN + DR, BF16), (DN + DR, BF16), (DV, BF16), (KVR, F32), (KVR, BF16)]
    return pl.pallas_call(
        project_kernel,
        grid=(count // tile,),
        in_specs=[
            by_rows(D),
            whole(gain[None]),
            whole(weight),
            whole(gain_kv[None]),
            whole(expand),
            by_rows(2 * DR),
            by_rows(2 * DR),
        ],
        out_specs=tuple(by_rows(c) for c, _ in outs),
        out_shape=tuple(jax.ShapeDtypeStruct((count, c), t) for c, t in outs),
        compiler_params=pltpu.CompilerParams(vmem_limit_bytes=48 * 2**20),
        cost_estimate=pl.CostEstimate(flops=2 * count * D * 900, bytes_accessed=24 * 2**20, transcendentals=count),
        name="project",
    )(rows, gain[None], weight, gain_kv[None], expand, cosines, sines)


BLOCKS = 4


def silu_grads(gate, up, grad):
    sig = jax.nn.sigmoid(gate)
    return grad * up * sig * (1.0 + gate * (1.0 - sig)), grad * gate * sig


def pick_of(place_ref, b, capacity):
    tok = place_ref.shape[1]
    return lax.broadcasted_iota(jnp.int32, (capacity, tok), 0) == place_ref[b : b + 1, :]


def as_weights(match):
    return jnp.where(match, 1.0, 0.0).astype(BF16)


def spread_kernel(
    ffn_ref, up_ref, place_ref, gate_ref, in_ref, out_ref,
    x_ref, rg_ref, hidden_ref, grad_ref, gout_ref, gin_ref,
    sum_out, sum_in,
):
    step = pl.program_id(0)
    blocks, tok = place_ref.shape
    capacity = x_ref.shape[0] // blocks
    units = out_ref.shape[0]
    for b in range(blocks):
        match = pick_of(place_ref, b, capacity)
        pick = as_weights(match)
        gate = jnp.sum(jnp.where(match, gate_ref[b : b + 1, :], 0.0), axis=1, keepdims=True)
        tokens, rows = pl.ds(b * tok, tok), pl.ds(b * capacity, capacity)
        x_ref[rows, :] = dot(pick, ffn_ref[tokens, :]).astype(BF16)
        rg_ref[rows, :] = (gate * dot(pick, up_ref[tokens, :])).astype(BF16)
    both = dot(ffn_ref[...], in_ref[...])
    gate, up = both[:, :units], both[:, units:]
    hidden = (gate * jax.nn.sigmoid(gate) * up).astype(BF16)
    hidden_ref[...] = hidden
    grads = silu_grads(gate, up, dot_nt(up_ref[...], out_ref[...]))
    grad = jnp.concatenate(grads, axis=1).astype(BF16)
    grad_ref[...] = grad

    @pl.when(step == 0)
    def _():
        sum_out[...] = jnp.zeros_like(sum_out)
        sum_in[...] = jnp.zeros_like(sum_in)

    sum_out[...] += dot_tn(hidden, up_ref[...])
    sum_in[...] += dot_tn(grad, ffn_ref[...])

    @pl.when(step == pl.num_programs(0) - 1)
    def _():
        gout_ref[...] = sum_out[...].astype(BF16)
        gin_ref[...] = sum_in[...].astype(BF16)


def by_rows(size, columns):
    return pl.BlockSpec((size, columns), lambda i: (i, 0))


def whole(array):
    return pl.BlockSpec(array.shape, lambda i: (0, 0), pipeline_mode=pl.Buffered(1))


def by_step(tok):
    return pl.BlockSpec((None, BLOCKS, tok), lambda i: (i, 0, 0))


def in_steps(rows):
    return rows.reshape(-1, BLOCKS, rows.shape[1])


def spread(ffn, upstream, place, gates, shared_in, shared_out, capacity):
    count = ffn.shape[0]
    seq, tok = place.shape
    steps = seq // BLOCKS
    units = shared_out.shape[0]
    t, rows = BLOCKS * tok, BLOCKS * capacity
    outs = [(rows, D), (rows, D), (t, units), (t, 2 * units)]
    fixed = [(units, D), (2 * units, D)]
    flops = 4 * seq * capacity * tok * D + 2 * count * 6 * D * units
    return pl.pallas_call(
        spread_kernel,
        grid=(steps,),
        in_specs=[by_rows(t, D), by_rows(t, D), by_step(tok), by_step(tok), whole(shared_in), whole(shared_out)],
        out_specs=tuple(by_rows(*o) for o in outs) + tuple(pl.BlockSpec(o, lambda i: (0, 0)) for o in fixed),
        out_shape=tuple(jax.ShapeDtypeStruct((r * steps, c), BF16) for r, c in outs)
        + tuple(jax.ShapeDtypeStruct(o, BF16) for o in fixed),
        scratch_shapes=[pltpu.VMEM(o, F32) for o in fixed],
        compiler_params=pltpu.CompilerParams(vmem_limit_bytes=56 * 2**20),
        cost_estimate=pl.CostEstimate(flops=flops, bytes_accessed=40 * 2**20, transcendentals=2 * count * units),
        name="spread",
    )(ffn, upstream, in_steps(place), in_steps(gates), shared_in, shared_out)


def turn_kernel(in_ref, out_ref):
    block = in_ref[...].astype(F32)
    out_ref[...] = block.reshape(-1, block.shape[-1]).T


def turn_rows(rows, tile):
    count, columns = rows.shape
    return pl.pallas_call(
        turn_kernel,
        grid=(count // tile,),
        in_specs=[pl.BlockSpec((tile, columns), lambda i: (i, 0))],
        out_specs=pl.BlockSpec((columns, tile), lambda i: (0, i)),
        out_shape=jax.ShapeDtypeStruct((columns, count), F32),
        compiler_params=pltpu.CompilerParams(vmem_limit_bytes=48 * 2**20),
        cost_estimate=pl.CostEstimate(flops=0, bytes_accessed=6 * rows.size, transcendentals=0),
        name="turn_rows",
    )(rows)


LINE = 4
MESH = pl.DeviceIdType.MESH


def place():
    rank = lax.axis_index("seq")
    return rank, lax.div(rank, 4), lax.rem(lax.div(rank, 2), 2), lax.rem(rank, 2)


def rank_at(z, y, x, dz, dy, dx):
    across = y + dy * (1 - 2 * y)
    along = x + dx * (1 - 2 * x)
    return (z + dz) * 4 + across * 2 + along


OFFSETS = [(dz, dy, dx) for dz in (0, -1, 1, -2, 2, -3, 3) for dy in (0, 1) for dx in (0, 1)]


def hops(offset):
    return abs(offset[0]) + offset[1] + offset[2]


def onward(order, offset):
    rel = dict(zip("zyx", offset))
    moved = [i for i, dim in enumerate(order) if rel[dim]]
    last = moved[-1] if moved else -1
    steps = []
    if last >= 0 and order[last] == "z":
        steps.append((1 if rel["z"] < 0 else -1, 0, 0))
    for dim in order[last + 1 :]:
        steps += {"z": [(1, 0, 0), (-1, 0, 0)], "y": [(0, 1, 0)], "x": [(0, 0, 1)]}[dim]
    return [s for s in steps if any(0 <= z + offset[0] < LINE and 0 <= z + s[0] < LINE for z in range(LINE))]


def inside(z, dz):
    return (z + dz >= 0) & (z + dz < LINE)


def guarded(z, steps, body):
    steps = [dz for dz in steps if dz]
    if not steps:
        body()
        return
    good = inside(z, steps[0])
    for dz in steps[1:]:
        good = good & inside(z, dz)
    pl.when(good)(body)


def greet_all():
    rank = lax.axis_index("seq")
    count = lax.axis_size("seq")
    barrier = pltpu.get_barrier_semaphore()
    for k in range(1, count):
        peer = lax.rem(rank + k, count)
        pl.semaphore_signal(barrier, inc=1, device_id={"seq": peer}, device_id_type=MESH)
    pl.semaphore_wait(barrier, count - 1)


def gather_events(streams, ins, outs, send_sems, recv_sems):
    rank, z, y, x = place()
    count = lax.axis_size("seq")
    slots = {}

    def copy(stream, offset, step):
        index, first, rows, order = streams[stream]
        part = pl.ds(first, rows)
        source = rank_at(z, y, x, *offset)
        slot = slots.setdefault((stream, offset, step), len(slots))
        block = outs[index].at[source, part]
        own = offset == (0, 0, 0)
        return pltpu.make_async_remote_copy(
            src_ref=ins[index].at[part] if own else block,
            dst_ref=block,
            send_sem=send_sems.at[slot],
            recv_sem=recv_sems.at[stream * count + source],
            device_id={"seq": rank_at(z, y, x, *step)},
            device_id_type=MESH,
        )

    def arrived(stream, offset):
        index, first, rows, order = streams[stream]
        source = rank_at(z, y, x, *offset)
        block = outs[index].at[source, pl.ds(first, rows)]
        pltpu.make_async_remote_copy(
            src_ref=block,
            dst_ref=block,
            send_sem=send_sems.at[0],
            recv_sem=recv_sems.at[stream * count + source],
            device_id={"seq": rank},
            device_id_type=MESH,
        ).wait_recv()

    todo = sorted(
        ((stream, offset) for stream in range(len(streams)) for offset in OFFSETS),
        key=lambda it: (hops(it[1]), it[0]),
    )

    def act(stream, offset):
        def forward():
            if hops(offset):
                arrived(stream, offset)
            for step in onward(streams[stream][3], offset):
                guarded(z, [step[0]], lambda: copy(stream, offset, step).start())

        guarded(z, [offset[0]], forward)

    def finish():
        for stream, offset in todo:
            for step in onward(streams[stream][3], offset):
                guarded(z, [offset[0], step[0]], lambda: copy(stream, offset, step).wait_send())

    return [functools.partial(act, *it) for it in todo], finish


def small_events(ins, outs, small_send, small_recv):
    rank, count = lax.axis_index("seq"), lax.axis_size("seq")

    def copy(i, k):
        peer = lax.rem(rank + k, count)
        return pltpu.make_async_remote_copy(
            src_ref=ins[i],
            dst_ref=outs[i].at[rank],
            send_sem=small_send.at[i * count + k],
            recv_sem=small_recv.at[i * count + rank],
            device_id={"seq": peer},
            device_id_type=MESH,
        )

    def send():
        for i in range(len(ins)):
            for k in range(1, count):
                copy(i, k).start()

    def finish():
        for i in range(len(ins)):
            for k in range(1, count):
                copy(i, k).wait_send()
            for k in range(1, count):
                source = lax.rem(rank + k, count)
                block = outs[i].at[source]
                pltpu.make_async_remote_copy(
                    src_ref=block,
                    dst_ref=block,
                    send_sem=small_send.at[0],
                    recv_sem=small_recv.at[i * count + source],
                    device_id={"seq": rank},
                    device_id_type=MESH,
                ).wait_recv()

    return send, finish


def gather_kernel(streams, n_main, n_small, *refs):
    n = n_main + n_small
    ins, outs = refs[:n], refs[n : 2 * n]
    send_sems, recv_sems, small_send, small_recv, local_sems = refs[2 * n :]
    rank = lax.axis_index("seq")
    count = lax.axis_size("seq")
    greet_all()
    locals_ = [pltpu.make_async_copy(ins[i], outs[i].at[rank], local_sems.at[i]) for i in range(n)]
    actions, finish = gather_events(streams, ins, outs, send_sems, recv_sems)
    send_small, finish_small = small_events(ins[n_main:], outs[n_main:], small_send, small_recv)
    for i, action in enumerate(actions):
        action()
        if i == len(streams) - 1:
            for c in locals_:
                c.start()
            send_small()
    finish()
    finish_small()
    for c in locals_:
        c.wait()


def n_sends(streams):
    return sum(len(onward(s[3], o)) for s in streams for o in OFFSETS)


def gather_scratch(streams, n_small, n, count):
    return [
        pltpu.SemaphoreType.DMA((n_sends(streams),)),
        pltpu.SemaphoreType.DMA((len(streams) * count,)),
        pltpu.SemaphoreType.DMA((max(1, n_small) * count,)),
        pltpu.SemaphoreType.DMA((max(1, n_small) * count,)),
        pltpu.SemaphoreType.DMA((n,)),
    ]


def streams_of(main, parts):
    streams = []
    for i, pieces in enumerate(parts):
        first = 0
        for rows, order in pieces:
            streams.append((i, first, rows, order))
            first += rows
    return streams


def gather_all(main, parts, small, collective_id, count=16):
    streams = streams_of(main, parts)
    arrays = list(main) + list(small)
    any_spec = pl.BlockSpec(memory_space=pl.ANY)
    return pl.pallas_call(
        functools.partial(gather_kernel, streams, len(main), len(small)),
        out_shape=tuple(jax.ShapeDtypeStruct((count,) + a.shape, a.dtype) for a in arrays),
        in_specs=[any_spec] * len(arrays),
        out_specs=tuple([any_spec] * len(arrays)),
        scratch_shapes=gather_scratch(streams, len(small), len(arrays), count),
        compiler_params=pltpu.CompilerParams(collective_id=collective_id, has_side_effects=True),
        name="gather_all",
    )(*arrays)


def toward(order, offset):
    rel = dict(zip("zyx", offset))
    dim = [d for d in order if rel[d]][-1]
    return {"z": (1 if rel["z"] > 0 else -1, 0, 0), "y": (0, 1, 0), "x": (0, 0, 1)}[dim]


def seen_from(offset, step):
    return (offset[0] - step[0], offset[1] ^ step[1], offset[2] ^ step[2])


def back(step):
    return (-step[0], step[1], step[2])


ADD_ROWS = 16


def slot_table(order):
    table, used = {}, 0
    for dy in (0, 1):
        for dx in (0, 1):
            for kind in ("x", "y", "up", "down"):
                step = {"x": (0, 0, 1), "y": (0, 1, 0), "up": (1, 0, 0), "down": (-1, 0, 0)}[kind]
                met = [o[0] for o in OFFSETS if o[1:] == (dy, dx) and step in onward(order, o)]
                if not met:
                    continue
                if kind == "down":
                    table[dy, dx, "down"] = (used, False)
                    used += 1
                    continue
                spread = any(met)
                table[dy, dx, kind] = (used, spread)
                used += LINE if spread else 1
    return table, used


def slot_at(table, z, offset, step):
    dz, dy, dx = offset
    kind = "x" if step[2] else "y" if step[1] else "down" if step[0] < 0 and dz == 0 else "up"
    first, spread = table[dy, dx, kind]
    return first + (z + dz) if spread else first


def scatter_kernel(streams, n_main, n_small, *refs):
    n = n_main + n_small
    ins, outs = refs[:n], refs[n : 2 * n]
    scratch = refs[2 * n :]
    bufs = scratch[: len(streams)]
    send_sems, recv_sems, small_send, small_recv, local_sems = scratch[len(streams) :]
    rank, z, y, x = place()
    count = lax.axis_size("seq")
    tables, bases, base = [], [], 0
    for stream in streams:
        table, used = slot_table(stream[3])
        tables.append(table)
        bases.append(base)
        base += used
    greet_all()

    def small_copy(i, k):
        peer = lax.rem(rank + k, count)
        return pltpu.make_async_remote_copy(
            src_ref=ins[n_main + i],
            dst_ref=outs[n_main + i].at[rank],
            send_sem=small_send.at[i * count + k],
            recv_sem=small_recv.at[i * count + rank],
            device_id={"seq": peer},
            device_id_type=MESH,
        )

    todo = sorted(
        ((s, offset) for s in range(len(streams)) for offset in OFFSETS),
        key=lambda it: (-hops(it[1]), it[0]),
    )
    send_slot = {key: i for i, key in enumerate(k for k in todo if hops(k[1]))}

    def send_copy(s, offset, source):
        step = toward(streams[s][3], offset)
        k = slot_at(tables[s], z + step[0], seen_from(offset, step), back(step))
        return pltpu.make_async_remote_copy(
            src_ref=source,
            dst_ref=bufs[s].at[k],
            send_sem=send_sems.at[send_slot[s, offset]],
            recv_sem=recv_sems.at[bases[s] + k],
            device_id={"seq": rank_at(z, y, x, *step)},
            device_id_type=MESH,
        )

    def wait_child(s, k):
        pltpu.make_async_remote_copy(
            src_ref=bufs[s].at[k],
            dst_ref=bufs[s].at[k],
            send_sem=send_sems.at[0],
            recv_sem=recv_sems.at[bases[s] + k],
            device_id={"seq": rank},
            device_id_type=MESH,
        ).wait_recv()

    for s, offset in todo:
        index, first, rows, order = streams[s]
        children = onward(order, offset)
        dest = rank_at(z, y, x, *offset)
        always = [c for c in children if not c[0]]
        sometimes = [c for c in children if c[0]]

        def run(present, s=s, offset=offset, index=index, first=first, rows=rows, dest=dest):
            own = ins[index].at[dest, pl.ds(first, rows)]
            if not present:
                send_copy(s, offset, own).start()
                return
            slots = [slot_at(tables[s], z, offset, step) for step in present]
            for k in slots:
                wait_child(s, k)
            final = not hops(offset)
            target = outs[index].at[pl.ds(first, rows)] if final else bufs[s].at[slots[0]]

            def add(i, carry):
                part = pl.ds(pl.multiple_of(i * ADD_ROWS, ADD_ROWS), ADD_ROWS)
                total = own[part, :].astype(F32)
                for k in slots:
                    total = total + bufs[s][k, part, :].astype(F32)
                target[part, :] = total.astype(target.dtype)
                return carry

            lax.fori_loop(0, rows // ADD_ROWS, add, 0)
            if not final:
                send_copy(s, offset, target).start()

        def cases(run=run, always=always, sometimes=sometimes):
            if not sometimes:
                run(always)
                return
            for mask in range(2 ** len(sometimes)):
                present = [c for i, c in enumerate(sometimes) if mask >> i & 1]
                good = None
                for i, c in enumerate(sometimes):
                    here = inside(z, c[0]) if mask >> i & 1 else jnp.logical_not(inside(z, c[0]))
                    good = here if good is None else good & here
                pl.when(good)(functools.partial(run, present + always))

        guarded(z, [offset[0]], cases)
        if (s, offset) == todo[0]:
            for i in range(n_small):
                for k in range(1, count):
                    small_copy(i, k).start()
                pltpu.make_async_copy(ins[n_main + i], outs[n_main + i].at[rank], local_sems.at[i]).start()
    for s, offset in todo:
        if hops(offset):
            index, first, rows, order = streams[s]
            own = ins[index].at[rank_at(z, y, x, *offset), pl.ds(first, rows)]
            guarded(z, [offset[0]], lambda: send_copy(s, offset, own).wait_send())
    for i in range(n_small):
        for k in range(1, count):
            small_copy(i, k).wait_send()
        for k in range(1, count):
            source = lax.rem(rank + k, count)
            block = outs[n_main + i].at[source]
            pltpu.make_async_remote_copy(
                src_ref=block,
                dst_ref=block,
                send_sem=small_send.at[0],
                recv_sem=small_recv.at[i * count + source],
                device_id={"seq": rank},
                device_id_type=MESH,
            ).wait_recv()
        pltpu.make_async_copy(ins[n_main + i], outs[n_main + i].at[rank], local_sems.at[i]).wait()


def scatter_sum(main, parts, small, collective_id, count=16):
    streams = streams_of(main, parts)
    arrays = list(main) + list(small)
    any_spec = pl.BlockSpec(memory_space=pl.ANY)
    vmem = pl.BlockSpec(memory_space=pltpu.VMEM)
    places = [slot_table(stream[3])[1] for stream in streams]
    buffers = [
        pltpu.VMEM((used, rows, main[index].shape[2]), main[index].dtype)
        for used, (index, first, rows, order) in zip(places, streams)
    ]
    return pl.pallas_call(
        functools.partial(scatter_kernel, streams, len(main), len(small)),
        out_shape=tuple(
            [jax.ShapeDtypeStruct(a.shape[1:], F32) for a in main]
            + [jax.ShapeDtypeStruct((count,) + a.shape, a.dtype) for a in small]
        ),
        in_specs=[vmem] * len(main) + [any_spec] * len(small),
        out_specs=tuple([vmem] * len(main) + [any_spec] * len(small)),
        scratch_shapes=buffers
        + [
            pltpu.SemaphoreType.DMA((len(streams) * len(OFFSETS),)),
            pltpu.SemaphoreType.DMA((sum(places),)),
            pltpu.SemaphoreType.DMA((max(1, len(small)) * count,)),
            pltpu.SemaphoreType.DMA((max(1, len(small)) * count,)),
            pltpu.SemaphoreType.DMA((max(1, len(small)),)),
        ],
        compiler_params=pltpu.CompilerParams(
            collective_id=collective_id, has_side_effects=True, vmem_limit_bytes=60 * 2**20
        ),
        name="scatter_sum",
    )(*arrays)


COLS = 256
PACE = 3


def expert_phases():
    ends, last = [], 0
    for steps in (2 * FF // COLS, -(-FF // COLS), D // COLS, D // COLS):
        last += steps
        ends.append(last)
    return ends


def expert_kernel(
    streams, n_main,
    x_ref, rg_ref, in_col_ref, out_row_ref, out_col_ref, in_row_ref,
    place_ref, gate_ref, shid_ref, sgrad_ref, sout_ref, sin_ref, up_ref, *refs
):
    ins, refs = refs[:n_main], refs[n_main:]
    mixed_ref, back_ref, dots_ref, hidden_out, gate_out, up_out, refs = *refs[:6], refs[6:]
    outs, refs = refs[:n_main], refs[n_main:]
    gu, hidden, dgu, picks, send_sems, recv_sems, local_sems, out_sems = refs
    rank = lax.axis_index("seq")
    i = pl.program_id(0)
    blocks, tok = place_ref.shape
    capacity = x_ref.shape[0] // blocks
    ends = expert_phases()
    actions, finish = gather_events(streams, ins, outs, send_sems, recv_sems)
    own = [pltpu.make_async_copy(ins[k], outs[k].at[rank], local_sems.at[k]) for k in range(n_main)]
    kept = [
        pltpu.make_async_copy(hidden, hidden_out, out_sems.at[0]),
        pltpu.make_async_copy(dgu.at[:, pl.ds(0, FF)], gate_out, out_sems.at[1]),
        pltpu.make_async_copy(dgu.at[:, pl.ds(FF, FF)], up_out, out_sems.at[2]),
    ]

    @pl.when(i == 0)
    def _():
        greet_all()
        for action in actions[: len(streams)]:
            action()
        for copy in own:
            copy.start()
        for b in range(blocks):
            picks[pl.ds(b * capacity, capacity), :] = as_weights(pick_of(place_ref, b, capacity))

    @pl.when(i < ends[0])
    def _():
        cols = pl.ds(pl.multiple_of(i * COLS, COLS), COLS)
        gu[:, cols] = dot(x_ref[...], in_col_ref[...]).astype(BF16)

    def back_span(first, width):
        grad = dot_nt(rg_ref[...], out_row_ref[:width, :])
        at, to = pl.ds(first, width), pl.ds(pl.multiple_of(FF + first, 128), width)
        gate, up = gu[:, at].astype(F32), gu[:, to].astype(F32)
        hidden[:, at] = (gate * jax.nn.sigmoid(gate) * up).astype(BF16)
        gate_grad, up_grad = silu_grads(gate, up, grad)
        dgu[:, at] = gate_grad.astype(BF16)
        dgu[:, to] = up_grad.astype(BF16)

    full = FF // COLS

    @pl.when((i >= ends[0]) & (i < ends[0] + full))
    def _():
        back_span(pl.multiple_of((i - ends[0]) * COLS, COLS), COLS)

    if FF % COLS:

        @pl.when(i == ends[0] + full)
        def _():
            back_span(full * COLS, FF % COLS)

    @pl.when(i == ends[1])
    def _():
        for copy in kept:
            copy.start()
        dots_ref[...] = jnp.zeros_like(dots_ref)

    @pl.when((i >= ends[1]) & (i < ends[2]))
    def _():
        result = dot(hidden[...], out_col_ref[...]).astype(BF16)
        shared = dot(shid_ref[...], sout_ref[...])
        for b in range(blocks):
            tokens, slots = pl.ds(b * tok, tok), pl.ds(b * capacity, capacity)
            mine = dot_tn(picks[slots, :], result[b * capacity : (b + 1) * capacity])
            dots_ref[tokens, :] += jnp.sum(up_ref[tokens, :].astype(F32) * mine, axis=1, keepdims=True)
            both = gate_ref[tokens, :] * mine + shared[b * tok : (b + 1) * tok]
            mixed_ref[tokens, :] = both.astype(BF16)

    @pl.when(i >= ends[2])
    def _():
        row_grad = dot_nt(dgu[...], in_row_ref[...]).astype(BF16)
        shared = dot_nt(sgrad_ref[...], sin_ref[...])
        for b in range(blocks):
            tokens, slots = pl.ds(b * tok, tok), pl.ds(b * capacity, capacity)
            mine = dot_tn(picks[slots, :], row_grad[b * capacity : (b + 1) * capacity])
            back_ref[tokens, :] = (mine + shared[b * tok : (b + 1) * tok]).astype(BF16)

    done = len(streams)
    for step in range(ends[3] - 1):
        some = actions[done : done + PACE]
        done += len(some)
        if some:

            @pl.when(i == step)
            def _(some=some):
                for action in some:
                    action()

    @pl.when(i == ends[3] - 1)
    def _():
        for action in actions[done:]:
            action()
        finish()
        for copy in own + kept:
            copy.wait()


def expert_block(
    x, rg, w_in, w_out, place, gates, shared_hidden, shared_grad, shared_out, shared_in, upstream,
    main, parts, collective_id, count=16,
):
    rows, tokens = x.shape[0], upstream.shape[0]
    units = shared_out.shape[0]
    streams = streams_of(main, parts)
    ends = expert_phases()

    def held(array):
        return pl.BlockSpec(array.shape, lambda i: (0, 0), pipeline_mode=pl.Buffered(1))

    def during(start, stop):
        return lambda i: jnp.minimum(jnp.maximum(i - start, 0), stop - start - 1)

    one, two, three, four = [during(a, b) for a, b in zip([0] + ends[:-1], ends)]
    any_spec = pl.BlockSpec(memory_space=pl.ANY)
    n = len(main)
    gate_column = gates.reshape(-1, 1)
    results = pl.pallas_call(
        functools.partial(expert_kernel, streams, n),
        grid=(ends[-1],),
        in_specs=[
            held(x),
            held(rg),
            pl.BlockSpec((D, COLS), lambda i: (0, one(i))),
            pl.BlockSpec((COLS, D), lambda i: (two(i), 0)),
            pl.BlockSpec((FF, COLS), lambda i: (0, three(i))),
            pl.BlockSpec((COLS, 2 * FF), lambda i: (four(i), 0)),
            held(place),
            held(gate_column),
            held(shared_hidden),
            held(shared_grad),
            pl.BlockSpec((units, COLS), lambda i: (0, three(i))),
            pl.BlockSpec((COLS, 2 * units), lambda i: (four(i), 0)),
            pl.BlockSpec((tokens, COLS), lambda i: (0, three(i))),
        ]
        + [any_spec] * n,
        out_specs=(
            pl.BlockSpec((tokens, COLS), lambda i: (0, three(i))),
            pl.BlockSpec((tokens, COLS), lambda i: (0, four(i))),
            pl.BlockSpec((tokens, 1), lambda i: (0, 0)),
            any_spec,
            any_spec,
            any_spec,
        )
        + (any_spec,) * n,
        out_shape=(
            jax.ShapeDtypeStruct((tokens, D), BF16),
            jax.ShapeDtypeStruct((tokens, D), BF16),
            jax.ShapeDtypeStruct((tokens, 1), F32),
            jax.ShapeDtypeStruct((rows, FF), BF16),
            jax.ShapeDtypeStruct((rows, FF), BF16),
            jax.ShapeDtypeStruct((rows, FF), BF16),
        )
        + tuple(jax.ShapeDtypeStruct((count,) + a.shape, a.dtype) for a in main),
        scratch_shapes=[
            pltpu.VMEM((rows, 2 * FF), BF16),
            pltpu.VMEM((rows, FF), BF16),
            pltpu.VMEM((rows, 2 * FF), BF16),
            pltpu.VMEM((rows, place.shape[1]), BF16),
            pltpu.SemaphoreType.DMA((n_sends(streams),)),
            pltpu.SemaphoreType.DMA((len(streams) * count,)),
            pltpu.SemaphoreType.DMA((n,)),
            pltpu.SemaphoreType.DMA((3,)),
        ],
        compiler_params=pltpu.CompilerParams(
            collective_id=collective_id, has_side_effects=True, vmem_limit_bytes=62 * 2**20
        ),
        cost_estimate=pl.CostEstimate(
            flops=12 * rows * D * FF, bytes_accessed=100 * 2**20, transcendentals=2 * rows * FF
        ),
        name="expert_block",
    )(
        x, rg, w_in, w_out, w_out, w_in,
        place, gate_column, shared_hidden, shared_grad, shared_out, shared_in, upstream, *main,
    )
    return results[:6], results[6:]


def turn_gather_kernel(streams, n_main, n_small, steps, *refs):
    n = n_main + n_small
    parts_ref, ins, refs = refs[0], refs[1 : n + 1], refs[n + 1 :]
    turned_ref, outs, refs = refs[0], refs[1 : n + 1], refs[n + 1 :]
    send_sems, recv_sems, small_send, small_recv, local_sems = refs
    i = pl.program_id(0)
    rank = lax.axis_index("seq")
    actions, finish = gather_events(streams, ins, outs, send_sems, recv_sems)
    own = [pltpu.make_async_copy(ins[k], outs[k].at[rank], local_sems.at[k]) for k in range(n)]
    send_small, finish_small = small_events(ins[n_main:], outs[n_main:], small_send, small_recv)

    @pl.when(i == 0)
    def _():
        greet_all()
        for action in actions[: len(streams)]:
            action()
        for copy in own:
            copy.start()
        send_small()

    block = parts_ref[...].astype(F32)
    turned_ref[...] = block.reshape(-1, block.shape[-1]).T
    rest = actions[len(streams) :]
    for step in range(steps):

        @pl.when(i == step)
        def _(step=step):
            for action in rest[step * len(rest) // steps : (step + 1) * len(rest) // steps]:
                action()

    @pl.when(i == steps - 1)
    def _():
        finish()
        finish_small()
        for copy in own:
            copy.wait()


def turn_and_gather(turned, main, parts, small, collective_id, count=16):
    seq_count, groups, unit, columns = turned.shape
    wide = seq_count * unit
    if unit % 8 or wide % 128 or columns % 256:
        rows = turned.transpose(3, 1, 0, 2).reshape(columns, -1).astype(F32)
        return (rows, *gather_all(main, parts, small, collective_id, count))
    tile = 256
    across = columns // tile
    streams = streams_of(main, parts)
    arrays = list(main) + list(small)
    any_spec = pl.BlockSpec(memory_space=pl.ANY)
    return pl.pallas_call(
        functools.partial(turn_gather_kernel, streams, len(main), len(small), groups * across),
        grid=(groups * across,),
        in_specs=[pl.BlockSpec((seq_count, None, unit, tile), lambda i: (0, i // across, 0, i % across))]
        + [any_spec] * len(arrays),
        out_specs=(pl.BlockSpec((tile, wide), lambda i: (i % across, i // across)),)
        + (any_spec,) * len(arrays),
        out_shape=(jax.ShapeDtypeStruct((columns, groups * wide), F32),)
        + tuple(jax.ShapeDtypeStruct((count,) + a.shape, a.dtype) for a in arrays),
        scratch_shapes=gather_scratch(streams, len(small), len(arrays), count),
        compiler_params=pltpu.CompilerParams(
            collective_id=collective_id, has_side_effects=True, vmem_limit_bytes=40 * 2**20
        ),
        name="turn_and_gather",
    )(turned, *arrays)


def gather_seq(rows):
    return lax.all_gather(rows, "seq", axis=0, tiled=True)


def scatter_seq(partial):
    return lax.psum_scatter(partial, "seq", scatter_dimension=0, tiled=True)


def gather_fsdp(rows, axis=0):
    return lax.all_gather(rows, "fsdp", axis=axis, tiled=True)


def scatter_fsdp(partial, axis=0):
    count, me = lax.axis_size("fsdp"), lax.axis_index("fsdp")
    size = partial.shape[axis] // count
    total = lax.dynamic_slice_in_dim(partial, me * size, size, axis).astype(F32)
    for k in range(1, count):
        piece = lax.dynamic_slice_in_dim(partial, lax.rem(me + k, count) * size, size, axis)
        total = total + shift_fsdp(piece, k).astype(F32)
    return total


def shift_fsdp(rows, k):
    count = lax.axis_size("fsdp")
    return lax.ppermute(rows, "fsdp", [(i, (i + k) % count) for i in range(count)])


ROW_PARTS = [(48, "zxy"), (48, "zyx"), (16, "xyz"), (16, "yxz")]


def split_rows(rows, part=8):
    tile = 16
    tiles = rows // tile
    short = tiles // part
    long = (tiles - 2 * short) // 2
    sizes = [tiles - 2 * short - long, long, short, short]
    orders = ["zxy", "zyx", "xyz", "yxz"]
    return [(n * tile, order) for n, order in zip(sizes, orders) if n]


def in_halves(rows):
    return split_rows(rows, rows)


def on_device(
    tokens,
    cotangent,
    lengths,
    routes,
    g_attn,
    w_q,
    w_kva,
    g_kv,
    w_kvb,
    w_o,
    g_ffn,
    w_router,
    w_shared_in,
    w_shared_out,
    w_expert_in,
    w_expert_out,
):
    seq_count = lax.axis_size("seq")
    fsdp_count = lax.axis_size("fsdp")
    rank = lax.axis_index("seq")
    tok_count = tokens.shape[0]
    group_size = tok_count * seq_count
    query_width = DN + DR
    kv_width = DN + DV
    experts = seq_count
    capacity = min(tok_count, 2 * tok_count * TOP // experts)
    buffer_rows = seq_count * capacity
    unit = SH // (seq_count * fsdp_count)
    units = unit * fsdp_count
    row_part = w_q.shape[0]

    def own(rows, axis=0):
        return lax.dynamic_slice_in_dim(rows, rank * tok_count, tok_count, axis)

    expert_ids = jnp.arange(experts, dtype=jnp.int32)
    route_mask = jnp.any(routes[None] == expert_ids[:, None, None], axis=2).astype(BF16)
    token_all, mask_all = gather_all([tokens], [ROW_PARTS], [route_mask], 1)
    token_all = token_all.reshape(group_size, D)

    small = gather_fsdp(jnp.concatenate([g_attn, g_kv, g_ffn, w_router.reshape(-1)])[None])
    cuts = [0, g_attn.size, g_kv.size, g_ffn.size, w_router.size]
    ends = [sum(cuts[: i + 1]) for i in range(len(cuts))]
    gain_attn = small[:, ends[0] : ends[1]].reshape(-1).astype(F32)
    gain_latent = small[:, ends[1] : ends[2]].reshape(-1).astype(F32)
    gain_ffn = small[:, ends[2] : ends[3]].reshape(-1).astype(F32)
    router_weight = small[:, ends[3] : ends[4]].reshape(D, experts)
    head_query_part = lax.dynamic_slice_in_dim(w_q, rank * query_width, query_width, 1)
    head_expand = gather_fsdp(lax.dynamic_slice_in_dim(w_kvb, rank * kv_width, kv_width, 1))
    head_weights = gather_fsdp(
        jnp.concatenate([w_kva[:, :KVR], head_query_part, w_kva[:, KVR:]], axis=1)
    )
    output_weight = gather_fsdp(w_o)
    expert_in = gather_fsdp(w_expert_in[0])
    expert_out = gather_fsdp(w_expert_out[0])
    query_weight = gather_fsdp(w_q)
    expand_weight = gather_fsdp(w_kvb)

    slot_ids = jnp.arange(group_size, dtype=jnp.int32)
    segment, position, valid_all = layout(lengths[0], slot_ids)
    angles = own(position)[:, None].astype(F32) * frequencies(DR)[None, :]
    wide_angles = position[:, None].astype(F32) * jnp.tile(frequencies(DR), 4)[None, :]
    cosines = jnp.cos(wide_angles)
    signs = jnp.where(jnp.arange(2 * DR) % DR < DR // 2, -1.0, 1.0).astype(F32)
    sines = jnp.sin(wide_angles) * signs[None, :]

    upstream_own = jnp.where(own(valid_all)[:, None], cotangent, 0).astype(BF16)
    upstream_all = gather_seq(upstream_own)

    normed_all, query, key, value, latent_full, latent_all = project(
        token_all, gain_attn, head_weights, gain_latent, head_expand, cosines, sines
    )
    context, log_total, head_largest = attention_forward(query, key, value, segment, valid_all)
    late_rank, context, upstream_all = lax.optimization_barrier((rank, context, upstream_all))
    lanes = -(-units // 128) * 128
    unit_slices = [
        lax.dynamic_slice_in_dim(w_shared_in, i * (SH // fsdp_count) + late_rank * unit, unit, 1)
        for i in range(2 * fsdp_count)
    ]
    filler = jnp.zeros((row_part, lanes - units), BF16)
    shared_in_part = jnp.concatenate(
        unit_slices[:fsdp_count] + [filler] + unit_slices[fsdp_count:] + [filler], axis=1
    )
    shared_in = gather_fsdp(shared_in_part)
    shared_out = gather_fsdp(lax.dynamic_slice_in_dim(w_shared_out, late_rank * unit, unit, 0))
    shared_out = jnp.pad(shared_out, ((0, lanes - units), (0, 0)))

    context_low = lax.all_to_all(context, "seq", split_axis=0, concat_axis=1, tiled=True)
    inputs = tokens.astype(F32)
    middle = inputs + dot(context_low, output_weight)
    ffn_low = rms_norm(middle, gain_ffn).astype(BF16)
    ffn_all, largest_all = gather_all([ffn_low], [ROW_PARTS], [head_largest], 2)
    ffn_all = ffn_all.reshape(group_size, D)
    head_max = largest_all[:, 0, :]
    for k in range(1, fsdp_count):
        head_max = jnp.maximum(head_max, shift_fsdp(largest_all[:, 0, :], k))
    global_max = head_max[:, 0]

    router_probs = jax.nn.softmax(dot(ffn_all, router_weight), axis=-1)
    chosen = lax.dynamic_slice_in_dim(mask_all, rank, 1, 1).reshape(seq_count, tok_count) > 0
    gates = lax.dynamic_slice_in_dim(router_probs, rank, 1, 1).reshape(seq_count, tok_count)
    place = jnp.cumsum(chosen.astype(jnp.int32), axis=1) - 1
    place = jnp.where(chosen, place, capacity)

    arrived, result_grad, shared_hidden, shared_grad, grad_shared_out, grad_shared_in = spread(
        ffn_all, upstream_all, place, gates, shared_in, shared_out, capacity
    )
    part_shared_out = scatter_fsdp(grad_shared_out[:units]).astype(BF16)
    part_shared_in = jnp.concatenate([grad_shared_in[:units], grad_shared_in[lanes : lanes + units]], axis=0)
    part_shared_in = scatter_fsdp(part_shared_in, 1).astype(BF16)
    part_shared_out = jnp.pad(part_shared_out, ((0, -unit % 16), (0, 0)))

    (mixed_part, ffn_part, gate_grad, hidden, d_gate, d_up), (all_shared_in, all_shared_out) = expert_block(
        arrived,
        result_grad,
        expert_in,
        expert_out,
        place,
        gates,
        shared_hidden,
        shared_grad,
        shared_out,
        shared_in,
        upstream_all,
        [part_shared_in, part_shared_out],
        [split_rows(part_shared_in.shape[0], 5), in_halves(part_shared_out.shape[0])],
        4,
    )
    mixed_part, query_weight, expand_weight = lax.optimization_barrier(
        (mixed_part, query_weight, expand_weight)
    )
    mixed_sum, ffn_sum, prob_grads = scatter_sum(
        [part.reshape(seq_count, tok_count, D) for part in (mixed_part, ffn_part)],
        [ROW_PARTS, ROW_PARTS],
        [gate_grad.reshape(seq_count, tok_count)],
        3,
    )
    mixed = (middle + mixed_sum).astype(BF16)
    prob_grads = prob_grads.reshape(experts, group_size).T

    logit_grads = (
        router_probs * (prob_grads - jnp.sum(router_probs * prob_grads, axis=-1, keepdims=True))
    ).astype(BF16)
    grad_router = dot_tn(ffn_all, logit_grads)
    sum_router = scatter_fsdp(grad_router.astype(BF16))
    ffn_grad = ffn_sum + dot_nt(own(logit_grads), router_weight)

    ffn_pull = jax.vjp(rms_norm, middle, gain_ffn)[1]
    middle_norm_grad, grad_gain_ffn = ffn_pull(ffn_grad)
    middle_grad = upstream_own.astype(F32) + middle_norm_grad
    middle_low = middle_grad.astype(BF16)
    context_grad = dot_nt(middle_low, output_weight).astype(BF16)
    head_grad = lax.all_to_all(context_grad, "seq", split_axis=1, concat_axis=0, tiled=True)
    grad_output = scatter_fsdp(dot_tn(context_low, middle_low).astype(BF16)).astype(BF16)
    output_rows = row_part // seq_count
    (part_output,) = scatter_sum(
        [grad_output.reshape(seq_count, output_rows, D)], [split_rows(output_rows)], [], 5
    )

    head_grad, part_output = lax.optimization_barrier((head_grad, part_output.astype(BF16)))
    all_output = gather_seq(part_output)
    head_back = attention_backward(query, key, value, head_grad, segment, log_total, cosines, sines)
    head_back, arrived, result_grad, hidden, d_gate, d_up = lax.optimization_barrier(
        (head_back, arrived, result_grad, hidden, d_gate, d_up)
    )
    back = lax.all_to_all(
        head_back.reshape(seq_count, tok_count, -1), "seq", split_axis=0, concat_axis=0, tiled=True
    )
    grad_expert_out = dot_tn(hidden, result_grad).astype(BF16)
    grad_expert_in = dot_tn(arrived, jnp.concatenate([d_gate, d_up], axis=1)).astype(BF16)
    rope_at = 2 * DN + DV
    head_pre_grad = jnp.concatenate([head_back[:, :DN], head_back[:, rope_at : rope_at + DR]], axis=1)
    grad_query = dot_tn(head_pre_grad, normed_all).astype(BF16)
    grad_expand = dot_tn(head_back[:, DN:rope_at], latent_all).astype(BF16)
    part_query = scatter_fsdp(grad_query, 1).astype(BF16)
    part_expand = scatter_fsdp(grad_expand, 1).astype(BF16)
    back, grad_expert_out, grad_expert_in, part_query, part_expand = lax.optimization_barrier(
        (back, grad_expert_out, grad_expert_in, part_query, part_expand)
    )
    sum_expert_in = scatter_fsdp(grad_expert_in)[None]
    sum_expert_out = scatter_fsdp(grad_expert_out)[None]

    back = back.transpose(1, 0, 2)
    pre_grad = jnp.concatenate([back[..., :DN], back[..., rope_at : rope_at + DR]], axis=-1)
    pre_grad = pre_grad.reshape(tok_count, H * query_width)
    expand_grad = back[..., DN:rope_at].reshape(tok_count, H * kv_width)
    latent_grad = dot_nt(expand_grad, expand_weight)
    rope_grad = rotate(jnp.sum(back[..., rope_at + DR :].astype(F32), axis=1), -angles)
    latent_pull = jax.vjp(rms_norm, own(latent_full), gain_latent)[1]
    compressed_grad, grad_gain_latent = latent_pull(latent_grad)
    full_grad = jnp.concatenate([compressed_grad, rope_grad], axis=1).astype(BF16)
    spread_grad = jnp.pad(full_grad[:, :KVR], ((0, 0), (0, query_width + DR)))
    spread_grad = spread_grad + jnp.pad(full_grad[:, KVR:], ((0, 0), (KVR + query_width, 0)))
    normed_grad = dot_nt(pre_grad, query_weight) + dot_nt(spread_grad, head_weights)
    input_pull = jax.vjp(rms_norm, inputs, gain_attn)[1]
    input_norm_grad, grad_gain_attn = input_pull(normed_grad)
    grad_inputs = middle_grad + input_norm_grad

    full_grad, all_output = lax.optimization_barrier((full_grad, all_output))
    gain_grads = jnp.concatenate([grad_gain_attn, grad_gain_latent, grad_gain_ffn]).reshape(-1, 128)
    gain_grads = jnp.pad(gain_grads, ((0, -gain_grads.shape[0] % 8), (0, 0)))
    sum_shared_in, all_query, all_expand, full_all, gain_all = turn_and_gather(
        all_shared_in.reshape(seq_count, 2 * fsdp_count, unit, row_part),
        [part_query, part_expand, full_grad],
        [split_rows(part.shape[0]) for part in (part_query, part_expand, full_grad)],
        [gain_grads],
        6,
    )
    full_all = full_all.reshape(group_size, -1)
    sum_latent = scatter_fsdp(dot_tn(normed_all, full_all).astype(BF16))
    gain_seq = jnp.sum(gain_all, axis=0)
    gain_sum = gain_seq
    for k in range(1, fsdp_count):
        gain_sum = gain_sum + shift_fsdp(gain_seq, k)
    gain_sum = gain_sum.reshape(-1)
    sum_shared_out = all_shared_out[:, :unit].reshape(w_shared_out.shape).astype(F32)
    sum_query = turn_rows(all_query.reshape(-1, row_part), 384)
    sum_expand = turn_rows(all_expand.reshape(-1, w_kvb.shape[0]), 512)
    sum_output = all_output.astype(F32)
    fsdp_rank = lax.axis_index("fsdp")

    def own_part(first, like):
        return lax.dynamic_slice_in_dim(gain_sum, first + fsdp_rank * like.size, like.size, 0)

    sum_gain_attn = own_part(0, g_attn)
    sum_gain_latent = own_part(D, g_kv)
    sum_gain_ffn = own_part(D + KVR, g_ffn)

    clip_gamma = CLIP_LIMIT / jnp.maximum(global_max, CLIP_LIMIT)
    clip_root = jnp.sqrt(clip_gamma)
    query_factor = jnp.concatenate(
        [
            jnp.broadcast_to(clip_root[:, None], (H, DN)),
            jnp.broadcast_to(clip_gamma[:, None], (H, DR)),
        ],
        axis=1,
    ).reshape(1, -1)
    clipped_query = (w_q.astype(F32) * query_factor).astype(BF16)
    return (
        mixed,
        grad_inputs,
        sum_gain_attn,
        sum_query,
        sum_latent,
        sum_gain_latent,
        sum_expand,
        sum_output,
        sum_gain_ffn,
        sum_router,
        sum_shared_in,
        sum_shared_out,
        sum_expert_in,
        sum_expert_out,
        clipped_query,
    )


def solution(mesh):
    in_specs = (
        P(("fsdp", "seq"), None),
        P(("fsdp", "seq"), None),
        P("fsdp", None),
        P(("fsdp", "seq"), None),
        P("fsdp"),
        P("fsdp", None),
        P("fsdp", None),
        P("fsdp"),
        P("fsdp", None),
        P("fsdp", None),
        P("fsdp"),
        P("fsdp", None),
        P("fsdp", None),
        P("fsdp", None),
        P("seq", "fsdp", None),
        P("seq", "fsdp", None),
    )
    out_specs = (
        P(("fsdp", "seq"), None),
        P(("fsdp", "seq"), None),
        P("fsdp"),
        P("fsdp", None),
        P("fsdp", None),
        P("fsdp"),
        P("fsdp", None),
        P("fsdp", None),
        P("fsdp"),
        P("fsdp", None),
        P("fsdp", None),
        P("fsdp", None),
        P("seq", "fsdp", None),
        P("seq", "fsdp", None),
        P("fsdp", None),
    )
    return jax.shard_map(
        on_device, mesh=mesh, in_specs=in_specs, out_specs=out_specs, check_vma=False
    )
```

```python
import functools

import jax
import jax.numpy as jnp
from jax import lax
from jax.experimental import pallas as pl
from jax.experimental.pallas import tpu as pltpu
from jax.sharding import PartitionSpec as P

D = 2048
H = 16
DN = 128
DR = 64
DV = 128
KVR = 512
FF = 1408
TOP = 6
SH = 2816

EPSILON = 1e-06
CLIP_LIMIT = 8.0
ROPE_BASE = 10000.0
MASK_VALUE = -1e30
BF16 = jnp.bfloat16
F32 = jnp.float32


def rms_norm(values, gain_vector):
    return (
        values
        * lax.rsqrt(jnp.mean(values * values, axis=-1, keepdims=True) + EPSILON)
        * gain_vector
    )


def rotate(values, angles):
    half_width = values.shape[-1] // 2
    first_half = values[..., :half_width]
    second_half = values[..., half_width:]
    cosine = jnp.cos(angles)
    sine_part = jnp.sin(angles)
    return jnp.concatenate(
        [
            first_half * cosine - second_half * sine_part,
            second_half * cosine + first_half * sine_part,
        ],
        axis=-1,
    )


def frequencies(count):
    exponent = jnp.arange(count // 2, dtype=jnp.float32) * 2.0 / count
    return ROPE_BASE ** (-exponent)


def layout(lengths_row, slot_ids):
    seq_ends = jnp.cumsum(lengths_row)
    seq_starts = seq_ends - lengths_row
    inside = (slot_ids[:, None] >= seq_starts[None, :]) & (slot_ids[:, None] < seq_ends[None, :])
    is_valid = jnp.any(inside, axis=1)
    numbers = jnp.arange(lengths_row.shape[0], dtype=jnp.int32)
    seq_number = jnp.sum(jnp.where(inside, numbers[None, :], 0), axis=1)
    first_slot = jnp.sum(jnp.where(inside, seq_starts[None, :], 0), axis=1)
    segment = jnp.where(is_valid, seq_number, lengths_row.shape[0] + slot_ids)
    position = jnp.where(is_valid, slot_ids - first_slot, 0)
    return (segment, position, is_valid)


def dot(left, right):
    return jnp.dot(left, right, preferred_element_type=F32)


def dot_tn(left, right):
    return lax.dot_general(left, right, (((0,), (0,)), ((), ())), preferred_element_type=F32)


def dot_nt(left, right):
    return lax.dot_general(left, right, (((1,), (1,)), ((), ())), preferred_element_type=F32)


ROWS = 256


def masked_scores(query, key, seg_col, seg_row, first, scale):
    scores = dot_nt(query, key) * scale
    shape = scores.shape
    row_slot = first + lax.broadcasted_iota(jnp.int32, shape, 0)
    key_slot = lax.broadcasted_iota(jnp.int32, shape, 1)
    allowed = (seg_col == seg_row) & (key_slot <= row_slot)
    return jnp.where(allowed, scores, MASK_VALUE)


def attention_forward_kernel(scale, q_ref, k_ref, v_ref, segc_ref, segr_ref, valid_ref, ctx_ref, lse_ref, max_ref):
    count = q_ref.shape[0]
    best = jnp.full((1, 1), MASK_VALUE, F32)
    for first in range(0, count, ROWS):
        rows, keys = pl.ds(first, ROWS), pl.ds(0, first + ROWS)
        masked = masked_scores(q_ref[rows, :], k_ref[keys, :], segc_ref[rows, :], segr_ref[:, keys], first, scale)
        row_max = jnp.max(masked, axis=1, keepdims=True)
        exponent = jnp.exp(masked - row_max)
        row_sum = jnp.sum(exponent, axis=1, keepdims=True)
        probs = (exponent * (1.0 / row_sum)).astype(BF16)
        ctx_ref[rows, :] = dot(probs, v_ref[keys, :]).astype(BF16)
        lse_ref[rows, :] = row_max + jnp.log(row_sum)
        counted = jnp.where(valid_ref[rows, :] > 0, row_max, MASK_VALUE)
        best = jnp.maximum(best, jnp.max(counted, axis=0, keepdims=True))
    max_ref[...] = jnp.broadcast_to(best, max_ref.shape)


def attention_forward(query, key, value, segment, valid):
    count, width = query.shape
    return pl.pallas_call(
        functools.partial(attention_forward_kernel, width ** (-0.5)),
        out_shape=(
            jax.ShapeDtypeStruct((count, value.shape[1]), BF16),
            jax.ShapeDtypeStruct((count, 1), F32),
            jax.ShapeDtypeStruct((8, 128), F32),
        ),
        compiler_params=pltpu.CompilerParams(vmem_limit_bytes=48 * 2**20),
        cost_estimate=pl.CostEstimate(flops=count * count * 320, bytes_accessed=4 * 2**20, transcendentals=count * count // 2),
        name="attention_forward",
    )(query, key, value, segment[:, None], segment[None, :], valid[:, None].astype(jnp.int32))


def attention_backward_kernel(
    scale, q_ref, k_ref, v_ref, g_ref, segc_ref, segr_ref, lse_ref, cos_ref, sin_ref, out_ref, dk_sum, dv_sum
):
    half = DR // 2
    count = q_ref.shape[0]
    dk_sum[...] = jnp.zeros_like(dk_sum)
    dv_sum[...] = jnp.zeros_like(dv_sum)
    for first in range(0, count, ROWS):
        rows, keys = pl.ds(first, ROWS), pl.ds(0, first + ROWS)
        query, grad = q_ref[rows, :], g_ref[rows, :]
        masked = masked_scores(query, k_ref[keys, :], segc_ref[rows, :], segr_ref[:, keys], first, scale)
        probs = jnp.exp(masked - lse_ref[rows, :])
        prob_grad = dot_nt(grad, v_ref[keys, :])
        mean = jnp.sum(probs * prob_grad, axis=1, keepdims=True)
        score_grad = (probs * (prob_grad - mean)).astype(BF16)
        query_grad = (dot(score_grad, k_ref[keys, :]) * scale).astype(BF16)
        out_ref[rows, :DN] = query_grad[:, :DN]
        rope = query_grad[:, DN:].astype(F32)
        swapped = jnp.concatenate([rope[:, half:], rope[:, :half]], axis=1)
        rope = rope * cos_ref[rows, :DR] - swapped * sin_ref[rows, :DR]
        out_ref[rows, 2 * DN + DV : 2 * DN + DV + DR] = rope.astype(BF16)
        dk_sum[keys, :] += dot_tn(score_grad, query)
        dv_sum[keys, :] += dot_tn(probs.astype(BF16), grad)
    key_grad = (dk_sum[...] * scale).astype(BF16)
    out_ref[:, DN : 2 * DN] = key_grad[:, :DN]
    out_ref[:, 2 * DN : 2 * DN + DV] = dv_sum[...].astype(BF16)
    out_ref[:, 2 * DN + DV + DR :] = key_grad[:, DN:]


def attention_backward(query, key, value, grad, segment, log_total, cosines, sines):
    count, width = query.shape
    return pl.pallas_call(
        functools.partial(attention_backward_kernel, width ** (-0.5)),
        out_shape=jax.ShapeDtypeStruct((count, 2 * width + value.shape[1]), BF16),
        scratch_shapes=[pltpu.VMEM(key.shape, F32), pltpu.VMEM(value.shape, F32)],
        compiler_params=pltpu.CompilerParams(vmem_limit_bytes=48 * 2**20),
        cost_estimate=pl.CostEstimate(flops=count * count * 832, bytes_accessed=6 * 2**20, transcendentals=count * count // 2),
        name="attention_backward",
    )(query, key, value, grad, segment[:, None], segment[None, :], log_total, cosines, sines)


def swap_halves(values):
    half = DR // 2
    pieces = [values[:, i * half : (i + 1) * half] for i in (1, 0, 3, 2)]
    return jnp.concatenate(pieces, axis=1)


def project_kernel(x_ref, gain_ref, w_ref, gain_kv_ref, expand_ref, cos_ref, sin_ref, normed_ref, q_ref, k_ref, v_ref, raw_ref, latent_ref):
    normed = rms_norm(x_ref[...].astype(F32), gain_ref[...]).astype(BF16)
    normed_ref[...] = normed
    both = dot(normed, w_ref[...])
    raw = both[:, :KVR]
    raw_ref[...] = raw
    latent = rms_norm(raw, gain_kv_ref[...]).astype(BF16)
    latent_ref[...] = latent
    expanded = dot(latent, expand_ref[...])
    rope = both[:, KVR + DN :]
    rope = rope * cos_ref[...] + swap_halves(rope) * sin_ref[...]
    q_ref[...] = jnp.concatenate([both[:, KVR : KVR + DN], rope[:, :DR]], axis=1).astype(BF16)
    k_ref[...] = jnp.concatenate([expanded[:, :DN], rope[:, DR:]], axis=1).astype(BF16)
    v_ref[...] = expanded[:, DN:].astype(BF16)


def project(rows, gain, weight, gain_kv, expand, cosines, sines):
    count = rows.shape[0]
    tile = 256

    def by_rows(columns):
        return pl.BlockSpec((tile, columns), lambda i: (i, 0))

    def whole(array):
        return pl.BlockSpec(array.shape, lambda i: (0, 0))

    outs = [(D, BF16), (DN + DR, BF16), (DN + DR, BF16), (DV, BF16), (KVR, F32), (KVR, BF16)]
    return pl.pallas_call(
        project_kernel,
        grid=(count // tile,),
        in_specs=[
            by_rows(D),
            whole(gain[None]),
            whole(weight),
            whole(gain_kv[None]),
            whole(expand),
            by_rows(2 * DR),
            by_rows(2 * DR),
        ],
        out_specs=tuple(by_rows(c) for c, _ in outs),
        out_shape=tuple(jax.ShapeDtypeStruct((count, c), t) for c, t in outs),
        compiler_params=pltpu.CompilerParams(vmem_limit_bytes=48 * 2**20),
        cost_estimate=pl.CostEstimate(flops=2 * count * D * 900, bytes_accessed=24 * 2**20, transcendentals=count),
        name="project",
    )(rows, gain[None], weight, gain_kv[None], expand, cosines, sines)


BLOCKS = 4


def silu_grads(gate, up, grad):
    sig = jax.nn.sigmoid(gate)
    return grad * up * sig * (1.0 + gate * (1.0 - sig)), grad * gate * sig


def pick_of(place_ref, b, capacity):
    tok = place_ref.shape[1]
    return lax.broadcasted_iota(jnp.int32, (capacity, tok), 0) == place_ref[b : b + 1, :]


def as_weights(match):
    return jnp.where(match, 1.0, 0.0).astype(BF16)


def spread_kernel(
    ffn_ref, up_ref, place_ref, gate_ref, in_ref, out_ref,
    x_ref, rg_ref, hidden_ref, grad_ref, gout_ref, gin_ref,
    sum_out, sum_in,
):
    step = pl.program_id(0)
    blocks, tok = place_ref.shape
    capacity = x_ref.shape[0] // blocks
    units = out_ref.shape[0]
    for b in range(blocks):
        match = pick_of(place_ref, b, capacity)
        pick = as_weights(match)
        gate = jnp.sum(jnp.where(match, gate_ref[b : b + 1, :], 0.0), axis=1, keepdims=True)
        tokens, rows = pl.ds(b * tok, tok), pl.ds(b * capacity, capacity)
        x_ref[rows, :] = dot(pick, ffn_ref[tokens, :]).astype(BF16)
        rg_ref[rows, :] = (gate * dot(pick, up_ref[tokens, :])).astype(BF16)
    both = dot(ffn_ref[...], in_ref[...])
    gate, up = both[:, :units], both[:, units:]
    hidden = (gate * jax.nn.sigmoid(gate) * up).astype(BF16)
    hidden_ref[...] = hidden
    grads = silu_grads(gate, up, dot_nt(up_ref[...], out_ref[...]))
    grad = jnp.concatenate(grads, axis=1).astype(BF16)
    grad_ref[...] = grad

    @pl.when(step == 0)
    def _():
        sum_out[...] = jnp.zeros_like(sum_out)
        sum_in[...] = jnp.zeros_like(sum_in)

    sum_out[...] += dot_tn(hidden, up_ref[...])
    sum_in[...] += dot_tn(grad, ffn_ref[...])

    @pl.when(step == pl.num_programs(0) - 1)
    def _():
        gout_ref[...] = sum_out[...].astype(BF16)
        gin_ref[...] = sum_in[...].astype(BF16)


def by_rows(size, columns):
    return pl.BlockSpec((size, columns), lambda i: (i, 0))


def whole(array):
    return pl.BlockSpec(array.shape, lambda i: (0, 0), pipeline_mode=pl.Buffered(1))


def by_step(tok):
    return pl.BlockSpec((None, BLOCKS, tok), lambda i: (i, 0, 0))


def in_steps(rows):
    return rows.reshape(-1, BLOCKS, rows.shape[1])


def spread(ffn, upstream, place, gates, shared_in, shared_out, capacity):
    count = ffn.shape[0]
    seq, tok = place.shape
    steps = seq // BLOCKS
    units = shared_out.shape[0]
    t, rows = BLOCKS * tok, BLOCKS * capacity
    outs = [(rows, D), (rows, D), (t, units), (t, 2 * units)]
    fixed = [(units, D), (2 * units, D)]
    flops = 4 * seq * capacity * tok * D + 2 * count * 6 * D * units
    return pl.pallas_call(
        spread_kernel,
        grid=(steps,),
        in_specs=[by_rows(t, D), by_rows(t, D), by_step(tok), by_step(tok), whole(shared_in), whole(shared_out)],
        out_specs=tuple(by_rows(*o) for o in outs) + tuple(pl.BlockSpec(o, lambda i: (0, 0)) for o in fixed),
        out_shape=tuple(jax.ShapeDtypeStruct((r * steps, c), BF16) for r, c in outs)
        + tuple(jax.ShapeDtypeStruct(o, BF16) for o in fixed),
        scratch_shapes=[pltpu.VMEM(o, F32) for o in fixed],
        compiler_params=pltpu.CompilerParams(vmem_limit_bytes=56 * 2**20),
        cost_estimate=pl.CostEstimate(flops=flops, bytes_accessed=40 * 2**20, transcendentals=2 * count * units),
        name="spread",
    )(ffn, upstream, in_steps(place), in_steps(gates), shared_in, shared_out)


def turn_kernel(in_ref, out_ref):
    block = in_ref[...].astype(F32)
    out_ref[...] = block.reshape(-1, block.shape[-1]).T


def turn_rows(rows, tile):
    count, columns = rows.shape
    return pl.pallas_call(
        turn_kernel,
        grid=(count // tile,),
        in_specs=[pl.BlockSpec((tile, columns), lambda i: (i, 0))],
        out_specs=pl.BlockSpec((columns, tile), lambda i: (0, i)),
        out_shape=jax.ShapeDtypeStruct((columns, count), F32),
        compiler_params=pltpu.CompilerParams(vmem_limit_bytes=48 * 2**20),
        cost_estimate=pl.CostEstimate(flops=0, bytes_accessed=6 * rows.size, transcendentals=0),
        name="turn_rows",
    )(rows)


LINE = 4
MESH = pl.DeviceIdType.MESH


def place():
    rank = lax.axis_index("seq")
    return rank, lax.div(rank, 4), lax.rem(lax.div(rank, 2), 2), lax.rem(rank, 2)


def rank_at(z, y, x, dz, dy, dx):
    across = y + dy * (1 - 2 * y)
    along = x + dx * (1 - 2 * x)
    return (z + dz) * 4 + across * 2 + along


OFFSETS = [(dz, dy, dx) for dz in (0, -1, 1, -2, 2, -3, 3) for dy in (0, 1) for dx in (0, 1)]


def hops(offset):
    return abs(offset[0]) + offset[1] + offset[2]


def onward(order, offset):
    rel = dict(zip("zyx", offset))
    moved = [i for i, dim in enumerate(order) if rel[dim]]
    last = moved[-1] if moved else -1
    steps = []
    if last >= 0 and order[last] == "z":
        steps.append((1 if rel["z"] < 0 else -1, 0, 0))
    for dim in order[last + 1 :]:
        steps += {"z": [(1, 0, 0), (-1, 0, 0)], "y": [(0, 1, 0)], "x": [(0, 0, 1)]}[dim]
    return [s for s in steps if any(0 <= z + offset[0] < LINE and 0 <= z + s[0] < LINE for z in range(LINE))]


def inside(z, dz):
    return (z + dz >= 0) & (z + dz < LINE)


def guarded(z, steps, body):
    steps = [dz for dz in steps if dz]
    if not steps:
        body()
        return
    good = inside(z, steps[0])
    for dz in steps[1:]:
        good = good & inside(z, dz)
    pl.when(good)(body)


def greet_all():
    rank = lax.axis_index("seq")
    count = lax.axis_size("seq")
    barrier = pltpu.get_barrier_semaphore()
    for k in range(1, count):
        peer = lax.rem(rank + k, count)
        pl.semaphore_signal(barrier, inc=1, device_id={"seq": peer}, device_id_type=MESH)
    pl.semaphore_wait(barrier, count - 1)


def gather_events(streams, ins, outs, send_sems, recv_sems):
    rank, z, y, x = place()
    count = lax.axis_size("seq")
    slots = {}

    def copy(stream, offset, step):
        index, first, rows, order = streams[stream]
        part = pl.ds(first, rows)
        source = rank_at(z, y, x, *offset)
        slot = slots.setdefault((stream, offset, step), len(slots))
        block = outs[index].at[source, part]
        own = offset == (0, 0, 0)
        return pltpu.make_async_remote_copy(
            src_ref=ins[index].at[part] if own else block,
            dst_ref=block,
            send_sem=send_sems.at[slot],
            recv_sem=recv_sems.at[stream * count + source],
            device_id={"seq": rank_at(z, y, x, *step)},
            device_id_type=MESH,
        )

    def arrived(stream, offset):
        index, first, rows, order = streams[stream]
        source = rank_at(z, y, x, *offset)
        block = outs[index].at[source, pl.ds(first, rows)]
        pltpu.make_async_remote_copy(
            src_ref=block,
            dst_ref=block,
            send_sem=send_sems.at[0],
            recv_sem=recv_sems.at[stream * count + source],
            device_id={"seq": rank},
            device_id_type=MESH,
        ).wait_recv()

    todo = sorted(
        ((stream, offset) for stream in range(len(streams)) for offset in OFFSETS),
        key=lambda it: (hops(it[1]), it[0]),
    )

    def act(stream, offset):
        def forward():
            if hops(offset):
                arrived(stream, offset)
            for step in onward(streams[stream][3], offset):
                guarded(z, [step[0]], lambda: copy(stream, offset, step).start())

        guarded(z, [offset[0]], forward)

    def finish():
        for stream, offset in todo:
            for step in onward(streams[stream][3], offset):
                guarded(z, [offset[0], step[0]], lambda: copy(stream, offset, step).wait_send())

    return [functools.partial(act, *it) for it in todo], finish


def small_events(ins, outs, small_send, small_recv):
    rank, count = lax.axis_index("seq"), lax.axis_size("seq")

    def copy(i, k):
        peer = lax.rem(rank + k, count)
        return pltpu.make_async_remote_copy(
            src_ref=ins[i],
            dst_ref=outs[i].at[rank],
            send_sem=small_send.at[i * count + k],
            recv_sem=small_recv.at[i * count + rank],
            device_id={"seq": peer},
            device_id_type=MESH,
        )

    def send():
        for i in range(len(ins)):
            for k in range(1, count):
                copy(i, k).start()

    def finish():
        for i in range(len(ins)):
            for k in range(1, count):
                copy(i, k).wait_send()
            for k in range(1, count):
                source = lax.rem(rank + k, count)
                block = outs[i].at[source]
                pltpu.make_async_remote_copy(
                    src_ref=block,
                    dst_ref=block,
                    send_sem=small_send.at[0],
                    recv_sem=small_recv.at[i * count + source],
                    device_id={"seq": rank},
                    device_id_type=MESH,
                ).wait_recv()

    return send, finish


def gather_kernel(streams, n_main, n_small, *refs):
    n = n_main + n_small
    ins, outs = refs[:n], refs[n : 2 * n]
    send_sems, recv_sems, small_send, small_recv, local_sems = refs[2 * n :]
    rank = lax.axis_index("seq")
    count = lax.axis_size("seq")
    greet_all()
    locals_ = [pltpu.make_async_copy(ins[i], outs[i].at[rank], local_sems.at[i]) for i in range(n)]
    actions, finish = gather_events(streams, ins, outs, send_sems, recv_sems)
    send_small, finish_small = small_events(ins[n_main:], outs[n_main:], small_send, small_recv)
    for i, action in enumerate(actions):
        action()
        if i == len(streams) - 1:
            for c in locals_:
                c.start()
            send_small()
    finish()
    finish_small()
    for c in locals_:
        c.wait()


def n_sends(streams):
    return sum(len(onward(s[3], o)) for s in streams for o in OFFSETS)


def gather_scratch(streams, n_small, n, count):
    return [
        pltpu.SemaphoreType.DMA((n_sends(streams),)),
        pltpu.SemaphoreType.DMA((len(streams) * count,)),
        pltpu.SemaphoreType.DMA((max(1, n_small) * count,)),
        pltpu.SemaphoreType.DMA((max(1, n_small) * count,)),
        pltpu.SemaphoreType.DMA((n,)),
    ]


def streams_of(main, parts):
    streams = []
    for i, pieces in enumerate(parts):
        first = 0
        for rows, order in pieces:
            streams.append((i, first, rows, order))
            first += rows
    return streams


def gather_all(main, parts, small, collective_id, count=16):
    streams = streams_of(main, parts)
    arrays = list(main) + list(small)
    any_spec = pl.BlockSpec(memory_space=pl.ANY)
    return pl.pallas_call(
        functools.partial(gather_kernel, streams, len(main), len(small)),
        out_shape=tuple(jax.ShapeDtypeStruct((count,) + a.shape, a.dtype) for a in arrays),
        in_specs=[any_spec] * len(arrays),
        out_specs=tuple([any_spec] * len(arrays)),
        scratch_shapes=gather_scratch(streams, len(small), len(arrays), count),
        compiler_params=pltpu.CompilerParams(collective_id=collective_id, has_side_effects=True),
        name="gather_all",
    )(*arrays)


def toward(order, offset):
    rel = dict(zip("zyx", offset))
    dim = [d for d in order if rel[d]][-1]
    return {"z": (1 if rel["z"] > 0 else -1, 0, 0), "y": (0, 1, 0), "x": (0, 0, 1)}[dim]


def seen_from(offset, step):
    return (offset[0] - step[0], offset[1] ^ step[1], offset[2] ^ step[2])


def back(step):
    return (-step[0], step[1], step[2])


ADD_ROWS = 16


def slot_table(order):
    table, used = {}, 0
    for dy in (0, 1):
        for dx in (0, 1):
            for kind in ("x", "y", "up", "down"):
                step = {"x": (0, 0, 1), "y": (0, 1, 0), "up": (1, 0, 0), "down": (-1, 0, 0)}[kind]
                met = [o[0] for o in OFFSETS if o[1:] == (dy, dx) and step in onward(order, o)]
                if not met:
                    continue
                if kind == "down":
                    table[dy, dx, "down"] = (used, False)
                    used += 1
                    continue
                spread = any(met)
                table[dy, dx, kind] = (used, spread)
                used += LINE if spread else 1
    return table, used


def slot_at(table, z, offset, step):
    dz, dy, dx = offset
    kind = "x" if step[2] else "y" if step[1] else "down" if step[0] < 0 and dz == 0 else "up"
    first, spread = table[dy, dx, kind]
    return first + (z + dz) if spread else first


def scatter_kernel(streams, n_main, n_small, *refs):
    n = n_main + n_small
    ins, outs = refs[:n], refs[n : 2 * n]
    scratch = refs[2 * n :]
    bufs = scratch[: len(streams)]
    send_sems, recv_sems, small_send, small_recv, local_sems = scratch[len(streams) :]
    rank, z, y, x = place()
    count = lax.axis_size("seq")
    tables, bases, base = [], [], 0
    for stream in streams:
        table, used = slot_table(stream[3])
        tables.append(table)
        bases.append(base)
        base += used
    greet_all()

    def small_copy(i, k):
        peer = lax.rem(rank + k, count)
        return pltpu.make_async_remote_copy(
            src_ref=ins[n_main + i],
            dst_ref=outs[n_main + i].at[rank],
            send_sem=small_send.at[i * count + k],
            recv_sem=small_recv.at[i * count + rank],
            device_id={"seq": peer},
            device_id_type=MESH,
        )

    todo = sorted(
        ((s, offset) for s in range(len(streams)) for offset in OFFSETS),
        key=lambda it: (-hops(it[1]), it[0]),
    )
    send_slot = {key: i for i, key in enumerate(k for k in todo if hops(k[1]))}

    def send_copy(s, offset, source):
        step = toward(streams[s][3], offset)
        k = slot_at(tables[s], z + step[0], seen_from(offset, step), back(step))
        return pltpu.make_async_remote_copy(
            src_ref=source,
            dst_ref=bufs[s].at[k],
            send_sem=send_sems.at[send_slot[s, offset]],
            recv_sem=recv_sems.at[bases[s] + k],
            device_id={"seq": rank_at(z, y, x, *step)},
            device_id_type=MESH,
        )

    def wait_child(s, k):
        pltpu.make_async_remote_copy(
            src_ref=bufs[s].at[k],
            dst_ref=bufs[s].at[k],
            send_sem=send_sems.at[0],
            recv_sem=recv_sems.at[bases[s] + k],
            device_id={"seq": rank},
            device_id_type=MESH,
        ).wait_recv()

    for s, offset in todo:
        index, first, rows, order = streams[s]
        children = onward(order, offset)
        dest = rank_at(z, y, x, *offset)
        always = [c for c in children if not c[0]]
        sometimes = [c for c in children if c[0]]

        def run(present, s=s, offset=offset, index=index, first=first, rows=rows, dest=dest):
            own = ins[index].at[dest, pl.ds(first, rows)]
            if not present:
                send_copy(s, offset, own).start()
                return
            slots = [slot_at(tables[s], z, offset, step) for step in present]
            for k in slots:
                wait_child(s, k)
            final = not hops(offset)
            target = outs[index].at[pl.ds(first, rows)] if final else bufs[s].at[slots[0]]

            def add(i, carry):
                part = pl.ds(pl.multiple_of(i * ADD_ROWS, ADD_ROWS), ADD_ROWS)
                total = own[part, :].astype(F32)
                for k in slots:
                    total = total + bufs[s][k, part, :].astype(F32)
                target[part, :] = total.astype(target.dtype)
                return carry

            lax.fori_loop(0, rows // ADD_ROWS, add, 0)
            if not final:
                send_copy(s, offset, target).start()

        def cases(run=run, always=always, sometimes=sometimes):
            if not sometimes:
                run(always)
                return
            for mask in range(2 ** len(sometimes)):
                present = [c for i, c in enumerate(sometimes) if mask >> i & 1]
                good = None
                for i, c in enumerate(sometimes):
                    here = inside(z, c[0]) if mask >> i & 1 else jnp.logical_not(inside(z, c[0]))
                    good = here if good is None else good & here
                pl.when(good)(functools.partial(run, present + always))

        guarded(z, [offset[0]], cases)
        if (s, offset) == todo[0]:
            for i in range(n_small):
                for k in range(1, count):
                    small_copy(i, k).start()
                pltpu.make_async_copy(ins[n_main + i], outs[n_main + i].at[rank], local_sems.at[i]).start()
    for s, offset in todo:
        if hops(offset):
            index, first, rows, order = streams[s]
            own = ins[index].at[rank_at(z, y, x, *offset), pl.ds(first, rows)]
            guarded(z, [offset[0]], lambda: send_copy(s, offset, own).wait_send())
    for i in range(n_small):
        for k in range(1, count):
            small_copy(i, k).wait_send()
        for k in range(1, count):
            source = lax.rem(rank + k, count)
            block = outs[n_main + i].at[source]
            pltpu.make_async_remote_copy(
                src_ref=block,
                dst_ref=block,
                send_sem=small_send.at[0],
                recv_sem=small_recv.at[i * count + source],
                device_id={"seq": rank},
                device_id_type=MESH,
            ).wait_recv()
        pltpu.make_async_copy(ins[n_main + i], outs[n_main + i].at[rank], local_sems.at[i]).wait()


def scatter_sum(main, parts, small, collective_id, count=16):
    streams = streams_of(main, parts)
    arrays = list(main) + list(small)
    any_spec = pl.BlockSpec(memory_space=pl.ANY)
    vmem = pl.BlockSpec(memory_space=pltpu.VMEM)
    places = [slot_table(stream[3])[1] for stream in streams]
    buffers = [
        pltpu.VMEM((used, rows, main[index].shape[2]), main[index].dtype)
        for used, (index, first, rows, order) in zip(places, streams)
    ]
    return pl.pallas_call(
        functools.partial(scatter_kernel, streams, len(main), len(small)),
        out_shape=tuple(
            [jax.ShapeDtypeStruct(a.shape[1:], F32) for a in main]
            + [jax.ShapeDtypeStruct((count,) + a.shape, a.dtype) for a in small]
        ),
        in_specs=[vmem] * len(main) + [any_spec] * len(small),
        out_specs=tuple([vmem] * len(main) + [any_spec] * len(small)),
        scratch_shapes=buffers
        + [
            pltpu.SemaphoreType.DMA((len(streams) * len(OFFSETS),)),
            pltpu.SemaphoreType.DMA((sum(places),)),
            pltpu.SemaphoreType.DMA((max(1, len(small)) * count,)),
            pltpu.SemaphoreType.DMA((max(1, len(small)) * count,)),
            pltpu.SemaphoreType.DMA((max(1, len(small)),)),
        ],
        compiler_params=pltpu.CompilerParams(
            collective_id=collective_id, has_side_effects=True, vmem_limit_bytes=60 * 2**20
        ),
        name="scatter_sum",
    )(*arrays)


COLS = 256
PACE = 3


def expert_phases():
    ends, last = [], 0
    for steps in (2 * FF // COLS, -(-FF // COLS), D // COLS, D // COLS):
        last += steps
        ends.append(last)
    return ends


def expert_kernel(
    streams, n_main,
    x_ref, rg_ref, in_col_ref, out_row_ref, out_col_ref, in_row_ref,
    place_ref, gate_ref, shid_ref, sgrad_ref, sout_ref, sin_ref, up_ref, *refs
):
    ins, refs = refs[:n_main], refs[n_main:]
    mixed_ref, back_ref, dots_ref, hidden_out, gate_out, up_out, refs = *refs[:6], refs[6:]
    outs, refs = refs[:n_main], refs[n_main:]
    gu, hidden, dgu, picks, send_sems, recv_sems, local_sems, out_sems = refs
    rank = lax.axis_index("seq")
    i = pl.program_id(0)
    blocks, tok = place_ref.shape
    capacity = x_ref.shape[0] // blocks
    ends = expert_phases()
    actions, finish = gather_events(streams, ins, outs, send_sems, recv_sems)
    own = [pltpu.make_async_copy(ins[k], outs[k].at[rank], local_sems.at[k]) for k in range(n_main)]
    kept = [
        pltpu.make_async_copy(hidden, hidden_out, out_sems.at[0]),
        pltpu.make_async_copy(dgu.at[:, pl.ds(0, FF)], gate_out, out_sems.at[1]),
        pltpu.make_async_copy(dgu.at[:, pl.ds(FF, FF)], up_out, out_sems.at[2]),
    ]

    @pl.when(i == 0)
    def _():
        greet_all()
        for action in actions[: len(streams)]:
            action()
        for copy in own:
            copy.start()
        for b in range(blocks):
            picks[pl.ds(b * capacity, capacity), :] = as_weights(pick_of(place_ref, b, capacity))

    @pl.when(i < ends[0])
    def _():
        cols = pl.ds(pl.multiple_of(i * COLS, COLS), COLS)
        gu[:, cols] = dot(x_ref[...], in_col_ref[...]).astype(BF16)

    def back_span(first, width):
        grad = dot_nt(rg_ref[...], out_row_ref[:width, :])
        at, to = pl.ds(first, width), pl.ds(pl.multiple_of(FF + first, 128), width)
        gate, up = gu[:, at].astype(F32), gu[:, to].astype(F32)
        hidden[:, at] = (gate * jax.nn.sigmoid(gate) * up).astype(BF16)
        gate_grad, up_grad = silu_grads(gate, up, grad)
        dgu[:, at] = gate_grad.astype(BF16)
        dgu[:, to] = up_grad.astype(BF16)

    full = FF // COLS

    @pl.when((i >= ends[0]) & (i < ends[0] + full))
    def _():
        back_span(pl.multiple_of((i - ends[0]) * COLS, COLS), COLS)

    if FF % COLS:

        @pl.when(i == ends[0] + full)
        def _():
            back_span(full * COLS, FF % COLS)

    @pl.when(i == ends[1])
    def _():
        for copy in kept:
            copy.start()
        dots_ref[...] = jnp.zeros_like(dots_ref)

    @pl.when((i >= ends[1]) & (i < ends[2]))
    def _():
        result = dot(hidden[...], out_col_ref[...]).astype(BF16)
        shared = dot(shid_ref[...], sout_ref[...])
        for b in range(blocks):
            tokens, slots = pl.ds(b * tok, tok), pl.ds(b * capacity, capacity)
            mine = dot_tn(picks[slots, :], result[b * capacity : (b + 1) * capacity])
            dots_ref[tokens, :] += jnp.sum(up_ref[tokens, :].astype(F32) * mine, axis=1, keepdims=True)
            both = gate_ref[tokens, :] * mine + shared[b * tok : (b + 1) * tok]
            mixed_ref[tokens, :] = both.astype(BF16)

    @pl.when(i >= ends[2])
    def _():
        row_grad = dot_nt(dgu[...], in_row_ref[...]).astype(BF16)
        shared = dot_nt(sgrad_ref[...], sin_ref[...])
        for b in range(blocks):
            tokens, slots = pl.ds(b * tok, tok), pl.ds(b * capacity, capacity)
            mine = dot_tn(picks[slots, :], row_grad[b * capacity : (b + 1) * capacity])
            back_ref[tokens, :] = (mine + shared[b * tok : (b + 1) * tok]).astype(BF16)

    done = len(streams)
    for step in range(ends[3] - 1):
        some = actions[done : done + PACE]
        done += len(some)
        if some:

            @pl.when(i == step)
            def _(some=some):
                for action in some:
                    action()

    @pl.when(i == ends[3] - 1)
    def _():
        for action in actions[done:]:
            action()
        finish()
        for copy in own + kept:
            copy.wait()


def expert_block(
    x, rg, w_in, w_out, place, gates, shared_hidden, shared_grad, shared_out, shared_in, upstream,
    main, parts, collective_id, count=16,
):
    rows, tokens = x.shape[0], upstream.shape[0]
    units = shared_out.shape[0]
    streams = streams_of(main, parts)
    ends = expert_phases()

    def held(array):
        return pl.BlockSpec(array.shape, lambda i: (0, 0), pipeline_mode=pl.Buffered(1))

    def during(start, stop):
        return lambda i: jnp.minimum(jnp.maximum(i - start, 0), stop - start - 1)

    one, two, three, four = [during(a, b) for a, b in zip([0] + ends[:-1], ends)]
    any_spec = pl.BlockSpec(memory_space=pl.ANY)
    n = len(main)
    gate_column = gates.reshape(-1, 1)
    results = pl.pallas_call(
        functools.partial(expert_kernel, streams, n),
        grid=(ends[-1],),
        in_specs=[
            held(x),
            held(rg),
            pl.BlockSpec((D, COLS), lambda i: (0, one(i))),
            pl.BlockSpec((COLS, D), lambda i: (two(i), 0)),
            pl.BlockSpec((FF, COLS), lambda i: (0, three(i))),
            pl.BlockSpec((COLS, 2 * FF), lambda i: (four(i), 0)),
            held(place),
            held(gate_column),
            held(shared_hidden),
            held(shared_grad),
            pl.BlockSpec((units, COLS), lambda i: (0, three(i))),
            pl.BlockSpec((COLS, 2 * units), lambda i: (four(i), 0)),
            pl.BlockSpec((tokens, COLS), lambda i: (0, three(i))),
        ]
        + [any_spec] * n,
        out_specs=(
            pl.BlockSpec((tokens, COLS), lambda i: (0, three(i))),
            pl.BlockSpec((tokens, COLS), lambda i: (0, four(i))),
            pl.BlockSpec((tokens, 1), lambda i: (0, 0)),
            any_spec,
            any_spec,
            any_spec,
        )
        + (any_spec,) * n,
        out_shape=(
            jax.ShapeDtypeStruct((tokens, D), BF16),
            jax.ShapeDtypeStruct((tokens, D), BF16),
            jax.ShapeDtypeStruct((tokens, 1), F32),
            jax.ShapeDtypeStruct((rows, FF), BF16),
            jax.ShapeDtypeStruct((rows, FF), BF16),
            jax.ShapeDtypeStruct((rows, FF), BF16),
        )
        + tuple(jax.ShapeDtypeStruct((count,) + a.shape, a.dtype) for a in main),
        scratch_shapes=[
            pltpu.VMEM((rows, 2 * FF), BF16),
            pltpu.VMEM((rows, FF), BF16),
            pltpu.VMEM((rows, 2 * FF), BF16),
            pltpu.VMEM((rows, place.shape[1]), BF16),
            pltpu.SemaphoreType.DMA((n_sends(streams),)),
            pltpu.SemaphoreType.DMA((len(streams) * count,)),
            pltpu.SemaphoreType.DMA((n,)),
            pltpu.SemaphoreType.DMA((3,)),
        ],
        compiler_params=pltpu.CompilerParams(
            collective_id=collective_id, has_side_effects=True, vmem_limit_bytes=62 * 2**20
        ),
        cost_estimate=pl.CostEstimate(
            flops=12 * rows * D * FF, bytes_accessed=100 * 2**20, transcendentals=2 * rows * FF
        ),
        name="expert_block",
    )(
        x, rg, w_in, w_out, w_out, w_in,
        place, gate_column, shared_hidden, shared_grad, shared_out, shared_in, upstream, *main,
    )
    return results[:6], results[6:]


def turn_gather_kernel(streams, n_main, n_small, steps, *refs):
    n = n_main + n_small
    parts_ref, ins, refs = refs[0], refs[1 : n + 1], refs[n + 1 :]
    turned_ref, outs, refs = refs[0], refs[1 : n + 1], refs[n + 1 :]
    send_sems, recv_sems, small_send, small_recv, local_sems = refs
    i = pl.program_id(0)
    rank = lax.axis_index("seq")
    actions, finish = gather_events(streams, ins, outs, send_sems, recv_sems)
    own = [pltpu.make_async_copy(ins[k], outs[k].at[rank], local_sems.at[k]) for k in range(n)]
    send_small, finish_small = small_events(ins[n_main:], outs[n_main:], small_send, small_recv)

    @pl.when(i == 0)
    def _():
        greet_all()
        for action in actions[: len(streams)]:
            action()
        for copy in own:
            copy.start()
        send_small()

    block = parts_ref[...].astype(F32)
    turned_ref[...] = block.reshape(-1, block.shape[-1]).T.astype(turned_ref.dtype)
    rest = actions[len(streams) :]
    for step in range(steps):

        @pl.when(i == step)
        def _(step=step):
            for action in rest[step * len(rest) // steps : (step + 1) * len(rest) // steps]:
                action()

    @pl.when(i == steps - 1)
    def _():
        finish()
        finish_small()
        for copy in own:
            copy.wait()


def turn_and_gather(turned, main, parts, small, collective_id, count=16):
    seq_count, groups, unit, columns = turned.shape
    wide = seq_count * unit
    if unit % 8 or wide % 128 or columns % 256:
        rows = turned.transpose(3, 1, 0, 2).reshape(columns, -1)
        return (rows, *gather_all(main, parts, small, collective_id, count))
    tile = 256
    across = columns // tile
    streams = streams_of(main, parts)
    arrays = list(main) + list(small)
    any_spec = pl.BlockSpec(memory_space=pl.ANY)
    return pl.pallas_call(
        functools.partial(turn_gather_kernel, streams, len(main), len(small), groups * across),
        grid=(groups * across,),
        in_specs=[pl.BlockSpec((seq_count, None, unit, tile), lambda i: (0, i // across, 0, i % across))]
        + [any_spec] * len(arrays),
        out_specs=(pl.BlockSpec((tile, wide), lambda i: (i % across, i // across)),)
        + (any_spec,) * len(arrays),
        out_shape=(jax.ShapeDtypeStruct((columns, groups * wide), turned.dtype),)
        + tuple(jax.ShapeDtypeStruct((count,) + a.shape, a.dtype) for a in arrays),
        scratch_shapes=gather_scratch(streams, len(small), len(arrays), count),
        compiler_params=pltpu.CompilerParams(
            collective_id=collective_id, has_side_effects=True, vmem_limit_bytes=40 * 2**20
        ),
        name="turn_and_gather",
    )(turned, *arrays)


def gather_seq(rows):
    return lax.all_gather(rows, "seq", axis=0, tiled=True)


def scatter_seq(partial):
    return lax.psum_scatter(partial, "seq", scatter_dimension=0, tiled=True)


def gather_fsdp(rows, axis=0):
    return lax.all_gather(rows, "fsdp", axis=axis, tiled=True)


def scatter_fsdp(partial, axis=0):
    count, me = lax.axis_size("fsdp"), lax.axis_index("fsdp")
    size = partial.shape[axis] // count
    total = lax.dynamic_slice_in_dim(partial, me * size, size, axis).astype(F32)
    for k in range(1, count):
        piece = lax.dynamic_slice_in_dim(partial, lax.rem(me + k, count) * size, size, axis)
        total = total + shift_fsdp(piece, k).astype(F32)
    return total


def shift_fsdp(rows, k):
    count = lax.axis_size("fsdp")
    return lax.ppermute(rows, "fsdp", [(i, (i + k) % count) for i in range(count)])


ROW_PARTS = [(48, "zxy"), (48, "zyx"), (16, "xyz"), (16, "yxz")]


def split_rows(rows, part=8):
    tile = 16
    tiles = rows // tile
    short = tiles // part
    long = (tiles - 2 * short) // 2
    sizes = [tiles - 2 * short - long, long, short, short]
    orders = ["zxy", "zyx", "xyz", "yxz"]
    return [(n * tile, order) for n, order in zip(sizes, orders) if n]


def in_halves(rows):
    return split_rows(rows, rows)


def on_device(
    tokens,
    cotangent,
    lengths,
    routes,
    g_attn,
    w_q,
    w_kva,
    g_kv,
    w_kvb,
    w_o,
    g_ffn,
    w_router,
    w_shared_in,
    w_shared_out,
    w_expert_in,
    w_expert_out,
):
    seq_count = lax.axis_size("seq")
    fsdp_count = lax.axis_size("fsdp")
    rank = lax.axis_index("seq")
    tok_count = tokens.shape[0]
    group_size = tok_count * seq_count
    query_width = DN + DR
    kv_width = DN + DV
    experts = seq_count
    capacity = min(tok_count, 2 * tok_count * TOP // experts)
    buffer_rows = seq_count * capacity
    unit = SH // (seq_count * fsdp_count)
    units = unit * fsdp_count
    row_part = w_q.shape[0]

    def own(rows, axis=0):
        return lax.dynamic_slice_in_dim(rows, rank * tok_count, tok_count, axis)

    expert_ids = jnp.arange(experts, dtype=jnp.int32)
    route_mask = jnp.any(routes[None] == expert_ids[:, None, None], axis=2).astype(BF16)
    token_all, mask_all = gather_all([tokens], [ROW_PARTS], [route_mask], 1)
    token_all = token_all.reshape(group_size, D)

    small = gather_fsdp(jnp.concatenate([g_attn, g_kv, g_ffn, w_router.reshape(-1)])[None])
    cuts = [0, g_attn.size, g_kv.size, g_ffn.size, w_router.size]
    ends = [sum(cuts[: i + 1]) for i in range(len(cuts))]
    gain_attn = small[:, ends[0] : ends[1]].reshape(-1).astype(F32)
    gain_latent = small[:, ends[1] : ends[2]].reshape(-1).astype(F32)
    gain_ffn = small[:, ends[2] : ends[3]].reshape(-1).astype(F32)
    router_weight = small[:, ends[3] : ends[4]].reshape(D, experts)
    head_query_part = lax.dynamic_slice_in_dim(w_q, rank * query_width, query_width, 1)
    head_expand = gather_fsdp(lax.dynamic_slice_in_dim(w_kvb, rank * kv_width, kv_width, 1))
    head_weights = gather_fsdp(
        jnp.concatenate([w_kva[:, :KVR], head_query_part, w_kva[:, KVR:]], axis=1)
    )
    output_weight = gather_fsdp(w_o)
    expert_in = gather_fsdp(w_expert_in[0])
    expert_out = gather_fsdp(w_expert_out[0])
    query_weight = gather_fsdp(w_q)
    expand_weight = gather_fsdp(w_kvb)

    slot_ids = jnp.arange(group_size, dtype=jnp.int32)
    segment, position, valid_all = layout(lengths[0], slot_ids)
    angles = own(position)[:, None].astype(F32) * frequencies(DR)[None, :]
    wide_angles = position[:, None].astype(F32) * jnp.tile(frequencies(DR), 4)[None, :]
    cosines = jnp.cos(wide_angles)
    signs = jnp.where(jnp.arange(2 * DR) % DR < DR // 2, -1.0, 1.0).astype(F32)
    sines = jnp.sin(wide_angles) * signs[None, :]

    upstream_own = jnp.where(own(valid_all)[:, None], cotangent, 0).astype(BF16)
    upstream_all = gather_seq(upstream_own)

    normed_all, query, key, value, latent_full, latent_all = project(
        token_all, gain_attn, head_weights, gain_latent, head_expand, cosines, sines
    )
    context, log_total, head_largest = attention_forward(query, key, value, segment, valid_all)
    late_rank, context, upstream_all = lax.optimization_barrier((rank, context, upstream_all))
    lanes = -(-units // 128) * 128
    unit_slices = [
        lax.dynamic_slice_in_dim(w_shared_in, i * (SH // fsdp_count) + late_rank * unit, unit, 1)
        for i in range(2 * fsdp_count)
    ]
    filler = jnp.zeros((row_part, lanes - units), BF16)
    shared_in_part = jnp.concatenate(
        unit_slices[:fsdp_count] + [filler] + unit_slices[fsdp_count:] + [filler], axis=1
    )
    shared_in = gather_fsdp(shared_in_part)
    shared_out = gather_fsdp(lax.dynamic_slice_in_dim(w_shared_out, late_rank * unit, unit, 0))
    shared_out = jnp.pad(shared_out, ((0, lanes - units), (0, 0)))

    context_low = lax.all_to_all(context, "seq", split_axis=0, concat_axis=1, tiled=True)
    inputs = tokens.astype(F32)
    middle = inputs + dot(context_low, output_weight)
    ffn_low = rms_norm(middle, gain_ffn).astype(BF16)
    ffn_all, largest_all = gather_all([ffn_low], [ROW_PARTS], [head_largest], 2)
    ffn_all = ffn_all.reshape(group_size, D)
    head_max = largest_all[:, 0, :]
    for k in range(1, fsdp_count):
        head_max = jnp.maximum(head_max, shift_fsdp(largest_all[:, 0, :], k))
    global_max = head_max[:, 0]

    router_probs = jax.nn.softmax(dot(ffn_all, router_weight), axis=-1)
    chosen = lax.dynamic_slice_in_dim(mask_all, rank, 1, 1).reshape(seq_count, tok_count) > 0
    gates = lax.dynamic_slice_in_dim(router_probs, rank, 1, 1).reshape(seq_count, tok_count)
    place = jnp.cumsum(chosen.astype(jnp.int32), axis=1) - 1
    place = jnp.where(chosen, place, capacity)

    arrived, result_grad, shared_hidden, shared_grad, grad_shared_out, grad_shared_in = spread(
        ffn_all, upstream_all, place, gates, shared_in, shared_out, capacity
    )
    part_shared_out = scatter_fsdp(grad_shared_out[:units]).astype(BF16)
    part_shared_in = jnp.concatenate([grad_shared_in[:units], grad_shared_in[lanes : lanes + units]], axis=0)
    part_shared_in = scatter_fsdp(part_shared_in, 1).astype(BF16)
    part_shared_out = jnp.pad(part_shared_out, ((0, -unit % 16), (0, 0)))

    (mixed_part, ffn_part, gate_grad, hidden, d_gate, d_up), (all_shared_in, all_shared_out) = expert_block(
        arrived,
        result_grad,
        expert_in,
        expert_out,
        place,
        gates,
        shared_hidden,
        shared_grad,
        shared_out,
        shared_in,
        upstream_all,
        [part_shared_in, part_shared_out],
        [split_rows(part_shared_in.shape[0], 5), in_halves(part_shared_out.shape[0])],
        4,
    )
    mixed_part, query_weight, expand_weight = lax.optimization_barrier(
        (mixed_part, query_weight, expand_weight)
    )
    mixed_sum, ffn_sum, prob_grads = scatter_sum(
        [part.reshape(seq_count, tok_count, D) for part in (mixed_part, ffn_part)],
        [ROW_PARTS, ROW_PARTS],
        [gate_grad.reshape(seq_count, tok_count)],
        3,
    )
    mixed = (middle + mixed_sum).astype(BF16)
    prob_grads = prob_grads.reshape(experts, group_size).T

    logit_grads = (
        router_probs * (prob_grads - jnp.sum(router_probs * prob_grads, axis=-1, keepdims=True))
    ).astype(BF16)
    grad_router = dot_tn(ffn_all, logit_grads)
    sum_router = scatter_fsdp(grad_router.astype(BF16))
    ffn_grad = ffn_sum + dot_nt(own(logit_grads), router_weight)

    ffn_pull = jax.vjp(rms_norm, middle, gain_ffn)[1]
    middle_norm_grad, grad_gain_ffn = ffn_pull(ffn_grad)
    middle_grad = upstream_own.astype(F32) + middle_norm_grad
    middle_low = middle_grad.astype(BF16)
    context_grad = dot_nt(middle_low, output_weight).astype(BF16)
    head_grad = lax.all_to_all(context_grad, "seq", split_axis=1, concat_axis=0, tiled=True)
    grad_output = scatter_fsdp(dot_tn(context_low, middle_low).astype(BF16)).astype(BF16)
    output_rows = row_part // seq_count
    (part_output,) = scatter_sum(
        [grad_output.reshape(seq_count, output_rows, D)], [split_rows(output_rows)], [], 5
    )

    head_grad, part_output = lax.optimization_barrier((head_grad, part_output.astype(BF16)))
    all_output = gather_seq(part_output)
    head_back = attention_backward(query, key, value, head_grad, segment, log_total, cosines, sines)
    head_back, arrived, result_grad, hidden, d_gate, d_up = lax.optimization_barrier(
        (head_back, arrived, result_grad, hidden, d_gate, d_up)
    )
    back = lax.all_to_all(
        head_back.reshape(seq_count, tok_count, -1), "seq", split_axis=0, concat_axis=0, tiled=True
    )
    grad_expert_out = dot_tn(hidden, result_grad).astype(BF16)
    grad_expert_in = dot_tn(arrived, jnp.concatenate([d_gate, d_up], axis=1)).astype(BF16)
    rope_at = 2 * DN + DV
    head_pre_grad = jnp.concatenate([head_back[:, :DN], head_back[:, rope_at : rope_at + DR]], axis=1)
    grad_query = dot_tn(head_pre_grad, normed_all).astype(BF16)
    grad_expand = dot_tn(head_back[:, DN:rope_at], latent_all).astype(BF16)
    part_query = scatter_fsdp(grad_query, 1).astype(BF16)
    part_expand = scatter_fsdp(grad_expand, 1).astype(BF16)
    grad_expert_in, global_max = lax.optimization_barrier((grad_expert_in, global_max))
    clip_gamma = CLIP_LIMIT / jnp.maximum(global_max, CLIP_LIMIT)
    clip_root = jnp.sqrt(clip_gamma)
    query_factor = jnp.concatenate(
        [
            jnp.broadcast_to(clip_root[:, None], (H, DN)),
            jnp.broadcast_to(clip_gamma[:, None], (H, DR)),
        ],
        axis=1,
    ).reshape(1, -1)
    clipped_query = (w_q.astype(F32) * query_factor).astype(BF16)
    back, grad_expert_out, grad_expert_in, part_query, part_expand, clipped_query = lax.optimization_barrier(
        (back, grad_expert_out, grad_expert_in, part_query, part_expand, clipped_query)
    )
    sum_expert_in = scatter_fsdp(grad_expert_in)[None]
    sum_expert_out = scatter_fsdp(grad_expert_out)[None]

    back = back.transpose(1, 0, 2)
    pre_grad = jnp.concatenate([back[..., :DN], back[..., rope_at : rope_at + DR]], axis=-1)
    pre_grad = pre_grad.reshape(tok_count, H * query_width)
    expand_grad = back[..., DN:rope_at].reshape(tok_count, H * kv_width)
    latent_grad = dot_nt(expand_grad, expand_weight)
    rope_grad = rotate(jnp.sum(back[..., rope_at + DR :].astype(F32), axis=1), -angles)
    latent_pull = jax.vjp(rms_norm, own(latent_full), gain_latent)[1]
    compressed_grad, grad_gain_latent = latent_pull(latent_grad)
    full_grad = jnp.concatenate([compressed_grad, rope_grad], axis=1).astype(BF16)
    spread_grad = jnp.pad(full_grad[:, :KVR], ((0, 0), (0, query_width + DR)))
    spread_grad = spread_grad + jnp.pad(full_grad[:, KVR:], ((0, 0), (KVR + query_width, 0)))
    normed_grad = dot_nt(pre_grad, query_weight) + dot_nt(spread_grad, head_weights)
    input_pull = jax.vjp(rms_norm, inputs, gain_attn)[1]
    input_norm_grad, grad_gain_attn = input_pull(normed_grad)
    grad_inputs = middle_grad + input_norm_grad

    full_grad, all_output, sum_expert_in, sum_expert_out = lax.optimization_barrier(
        (full_grad, all_output, sum_expert_in, sum_expert_out)
    )
    gain_grads = jnp.concatenate([grad_gain_attn, grad_gain_latent, grad_gain_ffn]).reshape(-1, 128)
    gain_grads = jnp.pad(gain_grads, ((0, -gain_grads.shape[0] % 8), (0, 0)))
    sum_shared_in, all_query, all_expand, full_all, gain_all = turn_and_gather(
        all_shared_in.reshape(seq_count, 2 * fsdp_count, unit, row_part),
        [part_query, part_expand, full_grad],
        [split_rows(part.shape[0]) for part in (part_query, part_expand, full_grad)],
        [gain_grads],
        6,
    )
    full_all = full_all.reshape(group_size, -1)
    sum_latent = scatter_fsdp(dot_tn(normed_all, full_all).astype(BF16))
    gain_seq = jnp.sum(gain_all, axis=0)
    gain_sum = gain_seq
    for k in range(1, fsdp_count):
        gain_sum = gain_sum + shift_fsdp(gain_seq, k)
    gain_sum = gain_sum.reshape(-1)
    sum_shared_out = all_shared_out[:, :unit].reshape(w_shared_out.shape).astype(F32)
    sum_shared_in = sum_shared_in.astype(F32)
    sum_query = turn_rows(all_query.reshape(-1, row_part), 384)
    sum_expand = turn_rows(all_expand.reshape(-1, w_kvb.shape[0]), 512)
    sum_output = all_output.astype(F32)
    fsdp_rank = lax.axis_index("fsdp")

    def own_part(first, like):
        return lax.dynamic_slice_in_dim(gain_sum, first + fsdp_rank * like.size, like.size, 0)

    sum_gain_attn = own_part(0, g_attn)
    sum_gain_latent = own_part(D, g_kv)
    sum_gain_ffn = own_part(D + KVR, g_ffn)

    return (
        mixed,
        grad_inputs,
        sum_gain_attn,
        sum_query,
        sum_latent,
        sum_gain_latent,
        sum_expand,
        sum_output,
        sum_gain_ffn,
        sum_router,
        sum_shared_in,
        sum_shared_out,
        sum_expert_in,
        sum_expert_out,
        clipped_query,
    )


def solution(mesh):
    in_specs = (
        P(("fsdp", "seq"), None),
        P(("fsdp", "seq"), None),
        P("fsdp", None),
        P(("fsdp", "seq"), None),
        P("fsdp"),
        P("fsdp", None),
        P("fsdp", None),
        P("fsdp"),
        P("fsdp", None),
        P("fsdp", None),
        P("fsdp"),
        P("fsdp", None),
        P("fsdp", None),
        P("fsdp", None),
        P("seq", "fsdp", None),
        P("seq", "fsdp", None),
    )
    out_specs = (
        P(("fsdp", "seq"), None),
        P(("fsdp", "seq"), None),
        P("fsdp"),
        P("fsdp", None),
        P("fsdp", None),
        P("fsdp"),
        P("fsdp", None),
        P("fsdp", None),
        P("fsdp"),
        P("fsdp", None),
        P("fsdp", None),
        P("fsdp", None),
        P("seq", "fsdp", None),
        P("seq", "fsdp", None),
        P("fsdp", None),
    )
    return jax.shard_map(
        on_device, mesh=mesh, in_specs=in_specs, out_specs=out_specs, check_vma=False
    )
```
